32 devices in a mesh: dp: 16 (over z, y, core), tensor: 2 (over x).
Axes of the slice: x: 2, y: 2, z: 4, core: 2. Of those that a mesh axis runs over, the one named last changes fastest.
Arguments:
- inputs: bfloat16 [256, 64, 512], P(('dp', 'tensor')), may hold values from -6 to 6
- cotangent: bfloat16 [256, 64, 512], P(('dp', 'tensor')), may hold values from -6 to 6
- attention_mask: int32 [256, 64], P(('dp', 'tensor')), may hold values from 0 to 1, as said below
- patch_valid: int32 [256, 64], P(('dp', 'tensor')), may hold values 0 or 1
- buckets: int32 [64, 64], replicated, may hold values from 0 to 31
- mask_embed: float32 [512], replicated, may hold values from -6 to 6
- w_query: bfloat16 [2, 512, 384], P(None, ('dp', 'tensor')), may hold values from -0.125 to 0.125
- w_key: bfloat16 [2, 512, 384], P(None, ('dp', 'tensor')), may hold values from -0.125 to 0.125
- w_value: bfloat16 [2, 512, 384], P(None, ('dp', 'tensor')), may hold values from -0.25 to 0.25
- w_output: bfloat16 [2, 384, 512], P(None, None, ('dp', 'tensor')), may hold values from -0.875 to 0.875
- w_gate: bfloat16 [2, 512, 1024], P(None, None, 'tensor'), may hold values from -0.25 to 0.25
- w_up: bfloat16 [2, 512, 1024], P(None, None, 'tensor'), may hold values from -0.25 to 0.25
- w_down: bfloat16 [2, 1024, 512], P(None, 'tensor'), may hold values from -0.25 to 0.25
- gain_attn: float32 [2, 512], replicated, may hold values from 0.5 to 1.5
- gain_ff: float32 [2, 512], replicated, may hold values from 0.5 to 1.5
- bias_table: float32 [32, 6], replicated, may hold values from -6 to 6
Outputs:
- outputs: bfloat16 [256, 64, 512], P(('dp', 'tensor'))
- grad_inputs: float32 [256, 64, 512], P(('dp', 'tensor'))
- grad_query: float32 [2, 512, 384], P(None, ('dp', 'tensor'))
- grad_key: float32 [2, 512, 384], P(None, ('dp', 'tensor'))
- grad_value: float32 [2, 512, 384], P(None, ('dp', 'tensor'))
- grad_output: float32 [2, 384, 512], P(None, None, ('dp', 'tensor'))
- grad_gate: float32 [2, 512, 1024], P(None, None, 'tensor')
- grad_up: float32 [2, 512, 1024], P(None, None, 'tensor')
- grad_down: float32 [2, 1024, 512], P(None, 'tensor')
- grad_gain_attn: float32 [2, 512], replicated
- grad_gain_ff: float32 [2, 512], replicated
- grad_bias_table: float32 [32, 6], replicated
- grad_mask_embed: float32 [512], replicated
The draws below stay inside these ranges and needn't reach their ends.
Inputs may be any that keep to these rules, and one draw needn't show every extreme that they name: In each series the ones of attention_mask are the last of its 64 slots, one or more of them.
All inputs are finite; a program needn't handle non-finite values. No bound on the sum of `patch_valid` on one device may be relied on, other than what follows from the above.
Results may differ from the reference program's by a relative error of at most 0.03.
The reference program's roundings to bfloat16 on the way count: a program that leaves them out, or rounds other values in their place, can miss the bound.
Values may be sent and summed in bfloat16 or wider, within the bound.
No kernel may reach another device: no remote copies, remote signals or barrier semaphores. Data moves between devices by JAX's collectives and lax.ppermute only.
A program may use at most 128 MiB of HBM per device.

```python
import math
import jax
import jax.numpy as jnp
from jax import lax

D = 512
FF = 1024
HEADS = 6
HEAD_DIM = 64
BUCKETS = 32
INNER = 384
SLOTS = 64
LAYERS = 2
SERIES = 256


def draw_attention_mask(key, part):
    lengths = jax.random.randint(key, (SERIES, 1), 1, SLOTS + 1)
    slot_ids = jnp.arange(SLOTS, dtype=jnp.int32)[None, :]
    return (slot_ids >= SLOTS - lengths).astype(jnp.int32)


def touch_ends(array, own_key, least, top_value):
    dims = array.shape
    spot = [jax.random.randint(jax.random.fold_in(own_key, axis), (), 0, dims[axis]) for axis in range(len(dims))]
    array = array.at[tuple(spot)].set(least)
    longest = dims.index(max(dims))
    spot[longest] = (spot[longest] + 1) % dims[longest]
    return array.at[tuple(spot)].set(top_value)


def strengthened(values, key, source, target, shards_of, factor):
    def block_of(position):
        return (jnp.arange(values.shape[position]) // (values.shape[position] // shards_of)).reshape((-1,) + (1,) * (values.ndim - 1 - position))

    one_side = jax.random.permutation(key, shards_of)[block_of(target)]
    second = (block_of(target) + shards_of // 2) % shards_of
    return jnp.where((block_of(source) == one_side) | (block_of(source) == second), factor * values, values)


def block_levels(stream_key, shape, shards, low, largest):
    def one(axis_at, shards_of):
        steps = jax.random.uniform(jax.random.fold_in(jax.random.fold_in(stream_key, 6), axis_at), (shards_of,), jnp.float32, low / len(shards), largest / len(shards))
        return jnp.repeat(jnp.exp(steps), shape[axis_at] // shards_of).reshape((-1,) + (1,) * (len(shape) - axis_at - 1))

    level = one(*shards[0])
    for cut in shards[1:]:
        level = level * one(*cut)
    return level


def centred(rng, extent, deviation, limit, split=(), kind=jnp.bfloat16):
    values = deviation * jax.random.normal(rng, extent, jnp.float32)
    if split:
        values = values * block_levels(rng, extent, split, -0.22, 0.18)
    return jnp.clip(values, -limit, limit).astype(kind)


def heavy_noise(rng, shape, width, limit, cuts, heavy, held_as=jnp.bfloat16):
    values = width * jax.random.normal(rng, shape, jnp.float32)
    if cuts:
        values = values * block_levels(rng, shape, cuts, -0.22, 0.18)
    return jnp.clip(strengthened(values, jax.random.fold_in(rng, 3), *heavy), -limit, limit).astype(held_as)


def setup_inputs(seed: int = 0) -> dict:
    seeds = jax.random.split(jax.random.key(seed), 17)
    inputs = heavy_noise(seeds[0], (SERIES, SLOTS, D), 1.0, 6.0, ((0, 32),), (0, 2, 32, 2.75))
    cotangent = centred(seeds[1], (SERIES, SLOTS, D), 1.0, 6.0, ((0, 32),))
    attention_mask = draw_attention_mask(jax.random.fold_in(seeds[16], 71), 0)
    patch_valid = touch_ends((jax.random.randint(seeds[3], (SERIES, SLOTS), 0, 8) < 7).astype(jnp.int32), jax.random.fold_in(seeds[3], 1), 0, 1)
    buckets = touch_ends(jax.random.randint(seeds[4], (SLOTS, SLOTS), 0, BUCKETS), jax.random.fold_in(seeds[4], 1), 0, BUCKETS - 1).astype(jnp.int32)
    mask_embed = centred(seeds[5], (D,), 1.0, 6.0, (), jnp.float32)
    w_query = centred(seeds[6], (LAYERS, D, INNER), (4 * D) ** -0.5, 0.125, ((1, 32),))
    w_key = centred(seeds[7], (LAYERS, D, INNER), (4 * D) ** -0.5, 0.125, ((1, 32),))
    w_value = centred(seeds[8], (LAYERS, D, INNER), D ** -0.5, 0.25, ((1, 32),))
    w_output = centred(seeds[9], (LAYERS, INNER, D), (INNER // 8) ** -0.5, 0.875, ((2, 32),))
    w_gate = centred(seeds[10], (LAYERS, D, FF), D ** -0.5, 0.25, ((2, 2),))
    w_up = centred(seeds[11], (LAYERS, D, FF), D ** -0.5, 0.25, ((2, 2),))
    w_down = centred(seeds[12], (LAYERS, FF, D), (FF // 2) ** -0.5, 0.25, ((1, 2),))
    gain_attn = jnp.clip(1.0 + 0.1 * jax.random.normal(seeds[13], (LAYERS, D), jnp.float32), 0.5, 1.5)
    gain_ff = jnp.clip(1.0 + 0.1 * jax.random.normal(seeds[14], (LAYERS, D), jnp.float32), 0.5, 1.5)
    bias_table = centred(seeds[15], (BUCKETS, HEADS), 1.0, 6.0, (), jnp.float32)
    return dict(inputs=inputs, cotangent=cotangent, attention_mask=attention_mask, patch_valid=patch_valid, buckets=buckets, mask_embed=mask_embed, w_query=w_query, w_key=w_key, w_value=w_value, w_output=w_output, w_gate=w_gate, w_up=w_up, w_down=w_down, gain_attn=gain_attn, gain_ff=gain_ff, bias_table=bias_table)


norm_eps = 1e-06
masked_score = -1e+30
precise = lax.Precision.HIGHEST

@jax.custom_vjp
def low(v):
    return lax.optimization_barrier(v.astype(jnp.bfloat16)).astype(jnp.float32)

@jax.custom_vjp
def low_back(v):
    return v

def low_keep(v):
    return (low(v), None)

def low_pass(kept, grad):
    return (grad,)

def back_keep(v):
    return (v, None)

def back_low(kept, grad):
    return (low(grad),)
low.defvjp(low_keep, low_pass)
low_back.defvjp(back_keep, back_low)

def rms_norm(values, gain):
    return values * lax.rsqrt(lax.optimization_barrier(jnp.mean(values * values, axis=-1, keepdims=True)) + norm_eps) * gain

def gelu_mix(gate_act, up_act):
    inner = 0.7978845608028654 * (gate_act + 0.044715 * gate_act * gate_act * gate_act)
    return 0.5 * gate_act * (1.0 + jnp.tanh(inner)) * up_act

def matmul(left, right):
    return jnp.matmul(left, right, precision=precise)

def encode(block_in, mask_embed, w_query, w_key, w_value, w_output, w_gate, w_up, w_down, gain_attn, gain_ff, bias_table, key_mask, valid_rows, buckets):
    series_count = block_in.shape[0]
    residual = jnp.where(valid_rows[:, :, None] == 1, block_in, mask_embed)
    score_bias = jnp.transpose(bias_table[buckets], (2, 0, 1))
    keep_keys = key_mask[:, None, None, :] == 1
    for layer_idx in range(LAYERS):
        normed = low(rms_norm(residual, gain_attn[layer_idx]))
        query_rows = low(low_back(matmul(normed, w_query[layer_idx]))).reshape(series_count, SLOTS, HEADS, HEAD_DIM)
        key_rows = low(low_back(matmul(normed, w_key[layer_idx]))).reshape(series_count, SLOTS, HEADS, HEAD_DIM)
        value_rows = low(low_back(matmul(normed, w_value[layer_idx]))).reshape(series_count, SLOTS, HEADS, HEAD_DIM)
        scores = jnp.einsum('bqhe,bkhe->bhqk', query_rows, key_rows, precision=precise) + score_bias[None]
        scores = low_back(jnp.where(keep_keys, scores, masked_score))
        row_max = lax.optimization_barrier(jnp.max(scores, axis=-1, keepdims=True))
        exp_scores = jnp.exp(scores - row_max)
        probs = exp_scores / lax.optimization_barrier(jnp.sum(exp_scores, axis=-1, keepdims=True))
        attended = jnp.einsum('bhqk,bkhe->bqhe', low(probs), value_rows, precision=precise)
        attended = low(low_back(attended.reshape(series_count, SLOTS, HEADS * HEAD_DIM)))
        residual = residual + low_back(matmul(attended, w_output[layer_idx]))
        ff_input = low(rms_norm(residual, gain_ff[layer_idx]))
        gate_act = low_back(matmul(ff_input, w_gate[layer_idx]))
        up_act = low_back(matmul(ff_input, w_up[layer_idx]))
        hidden = low(gelu_mix(gate_act, up_act))
        residual = residual + low_back(matmul(hidden, w_down[layer_idx]))
    return residual

def reference(inputs, cotangent, attention_mask, patch_valid, buckets, mask_embed, w_query, w_key, w_value, w_output, w_gate, w_up, w_down, gain_attn, gain_ff, bias_table):
    params = tuple((weight.astype(jnp.float32) for weight in (mask_embed, w_query, w_key, w_value, w_output, w_gate, w_up, w_down, gain_attn, gain_ff, bias_table)))
    block_ser = math.gcd(SERIES, 64)
    step_count = SERIES // block_ser
    shaped_in = inputs.astype(jnp.float32).reshape(step_count, block_ser, SLOTS, D)
    shaped_cot = cotangent.astype(jnp.float32).reshape(step_count, block_ser, SLOTS, D)
    shaped_mask = attention_mask.reshape(step_count, block_ser, SLOTS)
    shaped_valid = patch_valid.reshape(step_count, block_ser, SLOTS)

    def one_block(totals, pieces):
        block_in, block_cot, key_mask, valid_rows = pieces

        def forward(block_x, *weights):
            return encode(block_x, *weights, key_mask, valid_rows, buckets)
        result, pull = jax.vjp(forward, block_in, *params)
        grads = pull(block_cot)
        totals = tuple((total_part + grad_part for total_part, grad_part in zip(totals, grads[1:])))
        return (totals, (result.astype(jnp.bfloat16), grads[0]))
    zeros = tuple((jnp.zeros_like(weight) for weight in params))
    totals, (outputs, grad_inputs) = lax.scan(one_block, zeros, (shaped_in, shaped_cot, shaped_mask, shaped_valid))
    return (outputs.reshape(SERIES, SLOTS, D), grad_inputs.reshape(SERIES, SLOTS, D), totals[1], totals[2], totals[3], totals[4], totals[5], totals[6], totals[7], totals[8], totals[9], totals[10], totals[0])
```

```python
import functools
import types

import jax
import jax.numpy as jnp
from jax import lax
from jax.experimental import pallas as pl
from jax.experimental.pallas import tpu as pltpu
from jax.sharding import PartitionSpec as P

norm_eps = 1e-06
masked_score = -1e30
bf16 = jnp.bfloat16
f32 = jnp.float32
axes = ("dp", "tensor")
vmem_bytes = 56 * 1024 * 1024


def dot_nn(left, right):
    return lax.dot_general(left, right, (((1,), (0,)), ((), ())), preferred_element_type=f32)


def dot_nt(left, right):
    return lax.dot_general(left, right, (((1,), (1,)), ((), ())), preferred_element_type=f32)


def dot_tn(left, right):
    return lax.dot_general(left, right, (((0,), (0,)), ((), ())), preferred_element_type=f32)


def inverse_rms(values):
    return lax.rsqrt(jnp.mean(values * values, axis=-1, keepdims=True) + norm_eps)


def norm_back(values, gain, grad_out):
    scale = inverse_rms(values)
    pulled = grad_out * gain
    mean_part = jnp.mean(pulled * values, axis=-1, keepdims=True)
    grad_in = scale * pulled - values * (scale * scale * scale) * mean_part
    return grad_in, jnp.sum(grad_out * values * scale, axis=0, keepdims=True)


def gelu_terms(gate_act):
    square = gate_act * gate_act
    bent = jnp.tanh(0.7978845608028654 * gate_act * (1.0 + 0.044715 * square))
    half = 0.5 * (1.0 + bent)
    slope = half + 0.5 * gate_act * (1.0 - bent * bent) * (
        0.7978845608028654 * (1.0 + 3.0 * 0.044715 * square)
    )
    return gate_act * half, slope


def run(body, name, ins, outs, scratch, flops=0):
    names = list(ins) + list(outs) + list(scratch)

    def kernel(*refs):
        body(types.SimpleNamespace(**dict(zip(names, refs))))

    moved = sum(a.size * a.dtype.itemsize for a, _ in ins.values())
    results = pl.pallas_call(
        kernel,
        name=name,
        in_specs=[pl.BlockSpec(memory_space=space) for _, space in ins.values()],
        out_specs=[pl.BlockSpec(memory_space=pltpu.VMEM) for _ in outs],
        out_shape=[jax.ShapeDtypeStruct(shape, kind) for shape, kind in outs.values()],
        scratch_shapes=list(scratch.values()),
        compiler_params=pltpu.CompilerParams(vmem_limit_bytes=vmem_bytes),
        cost_estimate=pl.CostEstimate(flops=flops, bytes_accessed=moved, transcendentals=0),
    )(*[a for a, _ in ins.values()])
    return types.SimpleNamespace(**dict(zip(outs, results)))


def chunks(extent, size):
    size = min(size, extent)
    return [slice(start, start + size) for start in range(0, extent, size)]


def attention_copies(r, masks, rows):
    copies = []
    for idx, mask in enumerate(masks):
        half, at = divmod(idx, max(1, len(masks) // 2))
        source = (r.attn_near if half == 0 else r.attn_far).at[pl.ds(at * rows, rows)]
        place = (r.place[0] ^ mask) * rows if len(masks) > 1 else 0
        target = r.attn_w.at[pl.ds(pl.multiple_of(place, rows), rows)]
        copies.append(pltpu.make_async_copy(source, target, r.attn_sem))
    return copies


def ff_copies(r, layer_idx):
    copies = []
    for k, own in enumerate((r.w_gate, r.w_up, r.w_down)):
        copies.append(pltpu.make_async_copy(own.at[layer_idx], r.ff_w.at[0, k], r.ff_sem))
    part = r.ff_near.shape[1]
    core = r.place[1]
    for source, which in ((r.ff_near, core), (r.ff_far, 1 - core)):
        for k in range(3):
            target = r.ff_w.at[1, k, pl.ds(pl.multiple_of(which * part, part), part)]
            copies.append(pltpu.make_async_copy(source.at[k], target, r.ff_sem))
    return copies


def start_all(copies):
    for copy in copies:
        copy.start()


def wait_all(whole, sem):
    pltpu.make_async_copy(whole, whole, sem).wait()


def lane_low(rows):
    return lax.broadcasted_iota(jnp.int32, (rows, 128), 1) < 64


def pair_blocks(rows, low, high):
    return jnp.concatenate([rows * low, rows * high], axis=0)


def half_sums(values, is_low):
    first = jnp.sum(jnp.where(is_low, values, 0.0), axis=1, keepdims=True)
    second = jnp.sum(jnp.where(is_low, 0.0, values), axis=1, keepdims=True)
    return jnp.where(is_low, first, second)


def attention_forward(r, x_ref, a_ref, gain_ref, series, slots, inner):
    rows = series * slots
    for part in chunks(rows, 256):
        r.qkv[part, :] = dot_nn(a_ref[part, :], r.attn_w[:, : 3 * inner]).astype(bf16)
    is_low = lane_low(slots)
    low = lane_low(1).astype(f32).astype(bf16)
    high = (1.0 - low.astype(f32)).astype(bf16)

    def one(s):
        here = pl.ds(pl.multiple_of(s * slots, slots), slots)
        keep = r.mask[pl.ds(s, 1), :] == 1
        for start in range(0, inner, 128):
            at = slice(start, start + 128)
            query = r.qkv[here, at]
            keys = r.qkv[here, inner + start : inner + start + 128]
            values = r.qkv[here, 2 * inner + start : 2 * inner + start + 128]
            scores = dot_nt(query, pair_blocks(keys, low, high)) + r.bias[:, at]
            scores = jnp.where(keep, scores, masked_score)
            top_low = jnp.max(jnp.where(is_low, scores, -jnp.inf), axis=1, keepdims=True)
            top_high = jnp.max(jnp.where(is_low, -jnp.inf, scores), axis=1, keepdims=True)
            exps = jnp.exp(scores - jnp.where(is_low, top_low, top_high))
            probs = exps / half_sums(exps, is_low)
            r.probs[here, at] = probs
            r.heads[here, at] = dot_nn(
                probs.astype(bf16), pair_blocks(values, low, high)
            ).astype(bf16)

    @pl.loop(0, series // 2)
    def _(step):
        one(2 * step)
        one(2 * step + 1)

    for part in chunks(rows, 256):
        middle = x_ref[part, :] + dot_nt(r.heads[part, :], r.attn_w[:, 3 * inner :])
        r.middle[part, :] = middle
        r.ff_in[part, :] = (middle * inverse_rms(middle) * gain_ref[...]).astype(bf16)


def ff_forward(r, part):
    total = None
    for half in range(2):
        rows = r.ff_in[part, :]
        gate_act = dot_nn(rows, r.ff_w[half, 0])
        up_act = dot_nn(rows, r.ff_w[half, 1])
        hidden = (gelu_terms(gate_act)[0] * up_act).astype(bf16)
        term = dot_nn(hidden, r.ff_w[half, 2])
        total = term if total is None else total + term
    return total


def prepare_body(r):
    x = jnp.where(r.valid[...] == 1, r.inputs[...].astype(f32), r.embed[...])
    r.x[...] = x
    r.a[...] = (x * inverse_rms(x) * r.gain[...]).astype(bf16)
    buckets = r.buckets[...]
    bias = jnp.zeros(buckets.shape, f32)
    for idx in range(r.table.shape[0]):
        bias = jnp.where(buckets == idx, r.table[idx : idx + 1, :], bias)
    r.bias[...] = bias


def first_body(r, sizes, masks, grain):
    attn = attention_copies(r, masks, grain)
    start_all(attn)
    ff = ff_copies(r, 0)
    start_all(ff)
    wait_all(r.attn_w, r.attn_sem)
    attention_forward(r, r.x, r.a, r.gain_ff, *sizes)
    wait_all(r.ff_w, r.ff_sem)
    for part in chunks(r.x.shape[0], 256):
        x_next = r.middle[part, :] + ff_forward(r, part)
        r.x_next[part, :] = x_next
        r.a_next[part, :] = (x_next * inverse_rms(x_next) * r.gain_next[...]).astype(bf16)


def second_body(r, sizes, masks, grain):
    attn = attention_copies(r, masks, grain)
    start_all(attn)
    wait_all(r.attn_w, r.attn_sem)
    attention_forward(r, r.x, r.a, r.gain_ff, *sizes)


def backward_body(r, sizes, masks, grain, layer_idx, last, piece_masks):
    series, slots, inner = sizes
    rows = series * slots
    attn = attention_copies(r, masks, grain)
    ff = ff_copies(r, layer_idx)
    start_all(ff)
    start_all(attn)
    wait_all(r.ff_w, r.ff_sem)
    r.grad_gain_ff[...] = jnp.zeros(r.grad_gain_ff.shape, f32)
    r.grad_gain_attn[...] = jnp.zeros(r.grad_gain_attn.shape, f32)
    for part in chunks(rows, 256):
        grad = r.grad[part, :].astype(f32)
        rounded = grad.astype(bf16)
        ff_rows = r.ff_in[part, :]
        back = None
        total = None
        for half in range(2):
            gate_act = dot_nn(ff_rows, r.ff_w[half, 0])
            up_act = dot_nn(ff_rows, r.ff_w[half, 1])
            grad_hidden = dot_nt(rounded, r.ff_w[half, 2])
            mixed, slope = gelu_terms(gate_act)
            grad_gate = (grad_hidden * up_act * slope).astype(bf16)
            grad_up = (grad_hidden * mixed).astype(bf16)
            hidden = (mixed * up_act).astype(bf16)
            if half == 0:
                r.hidden[part, :] = hidden
                r.grad_gate[part, :] = grad_gate
                r.grad_up[part, :] = grad_up
            if last:
                term = dot_nn(hidden, r.ff_w[half, 2])
                total = term if total is None else total + term
            term = dot_nt(grad_gate, r.ff_w[half, 0]) + dot_nt(grad_up, r.ff_w[half, 1])
            back = term if back is None else back + term
        middle = r.middle[part, :]
        if last:
            r.outputs[part, :] = (middle + total).astype(bf16)
        grad_mid, gain_part = norm_back(middle, r.gain_ff[...], back)
        r.grad_gain_ff[...] += gain_part
        grad_mid = grad + grad_mid
        r.grad_mid[part, :] = grad_mid
        r.branch[part, :] = grad_mid.astype(bf16)
    wait_all(r.attn_w, r.attn_sem)
    for part in chunks(rows, 256):
        r.grad_heads[part, :] = dot_nn(r.branch[part, :], r.attn_w[:, 3 * inner :]).astype(bf16)
    is_low = lane_low(slots)
    low = lane_low(1).astype(f32).astype(bf16)
    high = (1.0 - low.astype(f32)).astype(bf16)
    if last:
        r.bias_acc[...] = jnp.zeros(r.bias_acc.shape, f32)
    else:
        r.bias_acc[...] = r.bias_before[...]

    def one(s):
        here = pl.ds(pl.multiple_of(s * slots, slots), slots)
        for start in range(0, inner, 128):
            at = slice(start, start + 128)
            key_at = slice(inner + start, inner + start + 128)
            value_at = slice(2 * inner + start, 2 * inner + start + 128)
            query = r.qkv[here, at]
            probs = r.probs[here, at]
            grad_out = r.grad_heads[here, at]
            grad_probs = dot_nt(grad_out, pair_blocks(r.qkv[here, value_at], low, high))
            inner_sum = half_sums(probs * grad_probs, is_low)
            grad_scores = (probs * (grad_probs - inner_sum)).astype(bf16)
            r.bias_acc[:, at] += grad_scores.astype(f32)
            r.grad_qkv[here, at] = dot_nn(
                grad_scores, pair_blocks(r.qkv[here, key_at], low, high)
            ).astype(bf16)
            both = dot_tn(grad_scores, query)
            r.grad_qkv[here, key_at] = jnp.where(is_low, both[:slots], both[slots:]).astype(bf16)
            both = dot_tn(probs.astype(bf16), grad_out)
            r.grad_qkv[here, value_at] = jnp.where(is_low, both[:slots], both[slots:]).astype(bf16)

    @pl.loop(0, series // 2)
    def _(step):
        one(2 * step)
        one(2 * step + 1)

    for at in chunks(3 * inner, inner):
        r.attn_grad[:, at] = dot_tn(r.a[...], r.grad_qkv[:, at])
    r.attn_grad[:, 3 * inner :] = dot_tn(r.branch[...], r.heads[...])
    scatter_pieces(r, r.attn_grad, r.attn_keep, r.attn_send, piece_masks, r.place[2])
    if not last:
        r.grad_embed[...] = jnp.zeros(r.grad_embed.shape, f32)
    for part in chunks(rows, 256):
        grad_normed = dot_nt(r.grad_qkv[part, :], r.attn_w[:, : 3 * inner])
        grad_in, gain_part = norm_back(r.x[part, :], r.gain_attn[...], grad_normed)
        r.grad_gain_attn[...] += gain_part
        grad_in = r.grad_mid[part, :] + grad_in
        if last:
            r.grad_next[part, :] = grad_in
            r.grad_next_low[part, :] = grad_in.astype(bf16)
        else:
            seen = r.valid[part, :] == 1
            r.grad_next[part, :] = jnp.where(seen, grad_in, 0.0)
            r.grad_embed[...] += jnp.sum(jnp.where(seen, 0.0, grad_in), axis=0, keepdims=True)
    if not last:
        head_size = r.bias_acc.shape[1] // r.head_count
        for idx in range(r.table_rows.shape[0]):
            chosen = jnp.where(r.buckets[...] == idx, r.bias_acc[...], 0.0)
            r.table_rows[idx : idx + 1, :] = jnp.sum(chosen, axis=0, keepdims=True)
        lane = lax.broadcasted_iota(jnp.int32, r.grad_table.shape, 1)
        table = jnp.zeros(r.grad_table.shape, f32)
        for head in range(r.head_count):
            cut = r.table_rows[:, head * head_size : (head + 1) * head_size]
            table = jnp.where(lane == head, jnp.sum(cut, axis=1, keepdims=True), table)
        r.grad_table[...] = table


def scatter_pieces(r, whole, keep, send, masks, place):
    count = len(masks)
    grain = whole.shape[-2] // count
    for idx, mask in enumerate(masks):
        target = keep if idx < count // 2 else send
        at = idx % (count // 2)
        source = pl.ds(pl.multiple_of((place ^ mask) * grain, grain), grain)
        if len(whole.shape) == 2:
            target[at] = whole[source, :].astype(bf16)
        else:
            for k in range(whole.shape[0]):
                target[at, k] = whole[k, source, :].astype(bf16)


def weight_body(r, layer_idx, piece_masks):
    copies = [
        pltpu.make_async_copy(own.at[layer_idx], r.ff_w.at[k], r.ff_sem)
        for k, own in enumerate((r.w_gate, r.w_up, r.w_down))
    ]
    start_all(copies)
    wait_all(r.ff_w, r.ff_sem)
    for part in chunks(r.peer_in.shape[0], 256):
        rows = r.peer_in[part, :]
        gate_act = dot_nn(rows, r.ff_w[0])
        up_act = dot_nn(rows, r.ff_w[1])
        grad_hidden = dot_nt(r.peer_grad[part, :], r.ff_w[2])
        mixed, slope = gelu_terms(gate_act)
        r.peer_gate[part, :] = (grad_hidden * up_act * slope).astype(bf16)
        r.peer_up[part, :] = (grad_hidden * mixed).astype(bf16)
        r.peer_hidden[part, :] = (mixed * up_act).astype(bf16)
    r.ff_grad[0] = dot_tn(r.ff_in[...], r.grad_gate[...]) + dot_tn(r.peer_in[...], r.peer_gate[...])
    r.ff_grad[1] = dot_tn(r.ff_in[...], r.grad_up[...]) + dot_tn(r.peer_in[...], r.peer_up[...])
    r.ff_grad[2] = dot_tn(r.hidden[...], r.grad[...]) + dot_tn(r.peer_hidden[...], r.peer_grad[...])
    scatter_pieces(r, r.ff_grad, r.ff_keep, r.ff_send, piece_masks, r.place[3])


def finish_body(r, masks):
    count = len(masks)
    grain = r.near0.shape[2]
    for layer_idx, (near, far) in enumerate(((r.near0, r.far0), (r.near1, r.far1))):
        for idx, mask in enumerate(masks):
            half, at = divmod(idx, count // 2)
            source = far if half else near
            target = pl.ds(pl.multiple_of((r.place[3] ^ mask) * grain, grain), grain)
            for k, out in enumerate((r.gate, r.up, r.down)):
                out[layer_idx, target, :] = source[at, k].astype(f32)


def order_masks(hops):
    masks = [0]
    for hop in reversed(hops):
        masks = masks + [mask ^ hop for mask in masks]
    return masks


def on_device(
    inputs,
    cotangent,
    attention_mask,
    patch_valid,
    buckets,
    mask_embed,
    w_query,
    w_key,
    w_value,
    w_output,
    w_gate,
    w_up,
    w_down,
    gain_attn,
    gain_ff,
    bias_table,
    dp_size,
):
    series, slots, width = inputs.shape
    heads = bias_table.shape[1]
    inner = w_query.shape[2]
    rows = series * slots
    sizes = (series, slots, inner)
    devices = 2 * dp_size
    dp_at = lax.axis_index("dp")
    device_at = 2 * dp_at + lax.axis_index("tensor")
    core_at = lax.rem(dp_at, 2)
    VMEM, ANY, SMEM = pltpu.VMEM, pl.ANY, pltpu.SMEM

    def swap(array, mask):
        return lax.ppermute(array, axes, [(n, n ^ mask) for n in range(devices)])

    bits = [1 << k for k in range(devices.bit_length() - 1)]
    far_first = bits[4:] + bits[2:4][::-1] + bits[:1] + bits[1:2]

    packed = jnp.concatenate(
        [w_query, w_key, w_value, jnp.swapaxes(w_output, 1, 2)], axis=2
    )
    own_rows = packed.shape[1]
    direct = own_rows % 16 == 0

    def gather_attention(block, hops):
        if not direct:
            return lax.all_gather(block, axes, axis=0, tiled=True), None, [0]
        masks = [0]
        for hop in hops[:-1]:
            block = jnp.concatenate([block, swap(block, hop)], axis=0)
            masks = masks + [mask ^ hop for mask in masks]
        return block, swap(block, hops[-1]), masks + [mask ^ hops[-1] for mask in masks]

    def gather_ff(layer_idx):
        part = width // 2
        blocks = [
            lax.dynamic_slice_in_dim(w[layer_idx], core_at * part, part, axis=0)
            for w in (w_gate, w_up, w_down)
        ]
        near = swap(jnp.stack(blocks), 1)
        return near, swap(near, 2)

    attn_pieces = []
    ff_pieces = []
    for layer_idx in range(2):
        attn_pieces.append(gather_attention(packed[layer_idx], far_first))
        ff_pieces.append(gather_ff(layer_idx))
    peer_cotangent = swap(cotangent.reshape(rows, width), 1)

    attn_grain = max(16, width // devices)
    attn_count = width // attn_grain
    ff_grain = max(16, width // dp_size)
    ff_count = width // ff_grain
    place = jnp.stack(
        [
            device_at,
            core_at,
            device_at // (devices // attn_count),
            lax.rem(dp_at, ff_count),
        ]
    ).astype(jnp.int32)

    wide_buckets = jnp.tile(buckets, (1, heads))
    wide_table = jnp.repeat(bias_table, slots, axis=1)
    wide_mask = jnp.tile(attention_mask, (1, 2))
    valid = patch_valid.reshape(rows, 1)
    matrix = (rows, width)

    start = run(
        prepare_body,
        "prepare",
        dict(
            inputs=(inputs.reshape(matrix), VMEM),
            valid=(valid, VMEM),
            embed=(mask_embed[None, :], VMEM),
            gain=(gain_attn[0:1], VMEM),
            buckets=(wide_buckets, VMEM),
            table=(wide_table, VMEM),
        ),
        dict(x=(matrix, f32), a=(matrix, bf16), bias=((slots, heads * slots), f32)),
        {},
    )

    def attn_ins(layer_idx):
        near, far, masks = attn_pieces[layer_idx]
        return dict(attn_near=(near, ANY), attn_far=(near if far is None else far, ANY)), masks

    def ff_ins(layer_idx):
        near, far = ff_pieces[layer_idx]
        return dict(
            w_gate=(w_gate, ANY),
            w_up=(w_up, ANY),
            w_down=(w_down, ANY),
            ff_near=(near, ANY),
            ff_far=(far, ANY),
        )

    attn_scratch = dict(
        attn_w=pltpu.VMEM((width, 4 * inner), bf16), attn_sem=pltpu.SemaphoreType.DMA
    )
    ff_scratch = dict(
        ff_w=pltpu.VMEM((2, 3, width, width), bf16), ff_sem=pltpu.SemaphoreType.DMA
    )
    grain = own_rows if direct else width
    attn_outs = dict(
        qkv=((rows, 3 * inner), bf16),
        probs=((rows, heads * slots), f32),
        heads=((rows, inner), bf16),
        middle=(matrix, f32),
        ff_in=(matrix, bf16),
    )
    attn_flops = 2 * rows * width * 4 * inner
    ff_flops = 2 * rows * width * 6 * width

    pieces, masks = attn_ins(0)
    first = run(
        functools.partial(first_body, sizes=sizes, masks=masks, grain=grain),
        "layer_0_forward",
        dict(
            place=(place, SMEM),
            x=(start.x, VMEM),
            a=(start.a, VMEM),
            bias=(start.bias, VMEM),
            mask=(wide_mask, VMEM),
            gain_ff=(gain_ff[0:1], VMEM),
            gain_next=(gain_attn[1:2], VMEM),
            **pieces,
            **ff_ins(0),
        ),
        dict(**attn_outs, x_next=(matrix, f32), a_next=(matrix, bf16)),
        dict(**attn_scratch, **ff_scratch),
        flops=attn_flops + ff_flops,
    )
    peer_in_0 = swap(first.ff_in, 1)
    pieces, masks = attn_ins(1)
    second = run(
        functools.partial(second_body, sizes=sizes, masks=masks, grain=grain),
        "layer_1_attention",
        dict(
            place=(place, SMEM),
            x=(first.x_next, VMEM),
            a=(first.a_next, VMEM),
            bias=(start.bias, VMEM),
            mask=(wide_mask, VMEM),
            gain_ff=(gain_ff[1:2], VMEM),
            **pieces,
        ),
        attn_outs,
        attn_scratch,
        flops=attn_flops,
    )
    peer_in_1 = swap(second.ff_in, 1)

    attn_hops = [2, 1] + bits[2:]
    attn_low = devices // attn_count
    attn_split = [hop for hop in attn_hops if hop >= attn_low]
    attn_whole = [hop for hop in attn_hops if hop < attn_low]
    ff_hops = bits[1:]
    ff_split = [hop for hop in ff_hops if hop // 2 < ff_count]
    ff_whole = [hop for hop in ff_hops if hop // 2 >= ff_count]
    attn_masks = [mask // attn_low for mask in order_masks(attn_split)]
    ff_masks = [mask // 2 for mask in order_masks(ff_split)]
    attn_half = (attn_count // 2, attn_grain, 4 * inner)
    ff_half = (ff_count // 2, 3, ff_grain, width)

    def backward(layer_idx, kept, x, a, grad, extra_ins, extra_outs, extra_scratch):
        last = layer_idx == 1
        pieces, masks = attn_ins(layer_idx)

        def body(r):
            r.head_count = heads
            backward_body(r, sizes, masks, grain, layer_idx, last, attn_masks)

        return run(
            body,
            "layer_%d_backward" % layer_idx,
            dict(
                place=(place, SMEM),
                x=(x, VMEM),
                a=(a, VMEM),
                grad=(grad, VMEM),
                gain_attn=(gain_attn[layer_idx : layer_idx + 1], VMEM),
                gain_ff=(gain_ff[layer_idx : layer_idx + 1], VMEM),
                qkv=(kept.qkv, VMEM),
                probs=(kept.probs, VMEM),
                heads=(kept.heads, VMEM),
                middle=(kept.middle, VMEM),
                ff_in=(kept.ff_in, VMEM),
                **pieces,
                **ff_ins(layer_idx),
                **extra_ins,
            ),
            dict(
                grad_next=(matrix, f32),
                hidden=(matrix, bf16),
                grad_gate=(matrix, bf16),
                grad_up=(matrix, bf16),
                grad_gain_attn=((1, width), f32),
                grad_gain_ff=((1, width), f32),
                attn_keep=(attn_half, bf16),
                attn_send=(attn_half, bf16),
                **extra_outs,
            ),
            dict(
                grad_mid=pltpu.VMEM(matrix, f32),
                branch=pltpu.VMEM(matrix, bf16),
                grad_heads=pltpu.VMEM((rows, inner), bf16),
                grad_qkv=pltpu.VMEM((rows, 3 * inner), bf16),
                attn_grad=pltpu.VMEM((width, 4 * inner), f32),
                **attn_scratch,
                **ff_scratch,
                **extra_scratch,
            ),
            flops=2 * (attn_flops + ff_flops),
        )

    def weight_grads(layer_idx, kept, back, grad, peer_in, peer_grad):
        return run(
            functools.partial(weight_body, layer_idx=layer_idx, piece_masks=ff_masks),
            "layer_%d_weight_grads" % layer_idx,
            dict(
                place=(place, SMEM),
                ff_in=(kept.ff_in, VMEM),
                grad=(grad, VMEM),
                hidden=(back.hidden, VMEM),
                grad_gate=(back.grad_gate, VMEM),
                grad_up=(back.grad_up, VMEM),
                peer_in=(peer_in, VMEM),
                peer_grad=(peer_grad, VMEM),
                w_gate=(w_gate, ANY),
                w_up=(w_up, ANY),
                w_down=(w_down, ANY),
            ),
            dict(ff_keep=(ff_half, bf16), ff_send=(ff_half, bf16)),
            dict(
                peer_gate=pltpu.VMEM(matrix, bf16),
                peer_up=pltpu.VMEM(matrix, bf16),
                peer_hidden=pltpu.VMEM(matrix, bf16),
                ff_grad=pltpu.VMEM((3, width, width), f32),
                ff_w=pltpu.VMEM((3, width, width), bf16),
                ff_sem=pltpu.SemaphoreType.DMA,
            ),
            flops=ff_flops,
        )

    def add(left, right):
        return (left.astype(f32) + right.astype(f32)).astype(bf16)

    def halve(keep, send, hops):
        for step, hop in enumerate(hops):
            got = swap(send, hop)
            if step + 1 < len(hops):
                cut = keep.shape[0] // 2
                send = add(keep[cut:], got[cut:])
                keep = add(keep[:cut], got[:cut])
            else:
                keep = add(keep, got)
        return keep

    def share(piece, hops):
        for hop in hops[:-1]:
            piece = jnp.concatenate([piece, swap(piece, hop)], axis=0)
        return piece, swap(piece, hops[-1])

    def whole_sum(piece, hops):
        for hop in hops:
            piece = add(piece, swap(piece, hop))
        return piece

    def reduce_ff(part):
        piece = whole_sum(halve(part.ff_keep, part.ff_send, ff_split), ff_whole)
        return share(piece, ff_split[::-1])

    def reduce_attn(part):
        piece = whole_sum(halve(part.attn_keep, part.attn_send, attn_split), attn_whole)[0]
        if own_rows < attn_grain:
            first_row = lax.rem(device_at, attn_low) * own_rows
            piece = lax.dynamic_slice_in_dim(piece, first_row, own_rows, axis=0)
        return piece.astype(f32)

    back_1 = backward(
        1,
        second,
        first.x_next,
        first.a_next,
        cotangent.reshape(matrix),
        {},
        dict(
            outputs=(matrix, bf16),
            grad_next_low=(matrix, bf16),
            bias_acc=((slots, heads * slots), f32),
        ),
        {},
    )
    peer_grad_0 = swap(back_1.grad_next_low, 1)
    part_1 = weight_grads(
        1, second, back_1, cotangent.reshape(matrix), peer_in_1, peer_cotangent
    )
    back_0 = backward(
        0,
        first,
        start.x,
        start.a,
        back_1.grad_next,
        dict(bias_before=(back_1.bias_acc, VMEM), valid=(valid, VMEM), buckets=(wide_buckets, VMEM)),
        dict(grad_embed=((1, width), f32), grad_table=((bias_table.shape[0], 128), f32)),
        dict(
            bias_acc=pltpu.VMEM((slots, heads * slots), f32),
            table_rows=pltpu.VMEM((bias_table.shape[0], heads * slots), f32),
        ),
    )
    part_0 = weight_grads(0, first, back_0, back_1.grad_next_low, peer_in_0, peer_grad_0)

    attn_1 = reduce_attn(back_1)
    ff_1 = reduce_ff(part_1)
    attn_0 = reduce_attn(back_0)
    ff_0 = reduce_ff(part_0)

    small = jnp.concatenate(
        [
            back_0.grad_gain_attn,
            back_1.grad_gain_attn,
            back_0.grad_gain_ff,
            back_1.grad_gain_ff,
            back_0.grad_embed,
            back_0.grad_table[:, :heads].reshape(1, -1),
        ],
        axis=1,
    ).reshape(-1, 1)
    small = jnp.pad(small, ((0, -small.shape[0] % 1024), (0, 0))).reshape(-1, 128)
    for hop in attn_hops:
        small = small + swap(small, hop)
    small = small.reshape(-1)

    done = run(
        functools.partial(
            finish_body,
            masks=[mask // 2 for mask in order_masks(ff_split)],
        ),
        "finish",
        dict(
            place=(place, SMEM),
            near0=(ff_0[0], VMEM),
            far0=(ff_0[1], VMEM),
            near1=(ff_1[0], VMEM),
            far1=(ff_1[1], VMEM),
        ),
        dict(
            gate=((2, width, width), f32),
            up=((2, width, width), f32),
            down=((2, width, width), f32),
        ),
        {},
    )
    attn_grads = jnp.stack([attn_0, attn_1])
    table_size = bias_table.size
    return (
        back_1.outputs.reshape(inputs.shape),
        back_0.grad_next.reshape(inputs.shape),
        attn_grads[:, :, :inner],
        attn_grads[:, :, inner : 2 * inner],
        attn_grads[:, :, 2 * inner : 3 * inner],
        jnp.swapaxes(attn_grads[:, :, 3 * inner :], 1, 2),
        done.gate,
        done.up,
        done.down,
        small[: 2 * width].reshape(2, width),
        small[2 * width : 4 * width].reshape(2, width),
        small[5 * width : 5 * width + table_size].reshape(bias_table.shape),
        small[4 * width : 5 * width],
    )


def solution(mesh):
    placed = (
        P(("dp", "tensor"), None, None),
        P(("dp", "tensor"), None, None),
        P(("dp", "tensor"), None),
        P(("dp", "tensor"), None),
        P(),
        P(),
        P(None, ("dp", "tensor"), None),
        P(None, ("dp", "tensor"), None),
        P(None, ("dp", "tensor"), None),
        P(None, None, ("dp", "tensor")),
        P(None, None, "tensor"),
        P(None, None, "tensor"),
        P(None, "tensor", None),
        P(),
        P(),
        P(),
    )
    return jax.shard_map(
        functools.partial(on_device, dp_size=mesh.shape["dp"]),
        mesh=mesh,
        in_specs=placed,
        out_specs=(
            P(("dp", "tensor"), None, None),
            P(("dp", "tensor"), None, None),
            P(None, ("dp", "tensor"), None),
            P(None, ("dp", "tensor"), None),
            P(None, ("dp", "tensor"), None),
            P(None, None, ("dp", "tensor")),
            P(None, None, "tensor"),
            P(None, None, "tensor"),
            P(None, "tensor", None),
            P(),
            P(),
            P(),
            P(),
        ),
        check_vma=False,
    )
```

```python
import functools
import types

import jax
import jax.numpy as jnp
from jax import lax
from jax.experimental import pallas as pl
from jax.experimental.pallas import tpu as pltpu
from jax.sharding import PartitionSpec as P

norm_eps = 1e-06
masked_score = -1e30
bf16 = jnp.bfloat16
f32 = jnp.float32
axes = ("dp", "tensor")
vmem_bytes = 56 * 1024 * 1024
raw_names = ("attn_near", "attn_far", "ff_near", "ff_far", "w_gate", "w_up", "w_down")


def dot_nn(left, right):
    return lax.dot_general(left, right, (((1,), (0,)), ((), ())), preferred_element_type=f32)


def dot_nt(left, right):
    return lax.dot_general(left, right, (((1,), (1,)), ((), ())), preferred_element_type=f32)


def dot_tn(left, right):
    return lax.dot_general(left, right, (((0,), (0,)), ((), ())), preferred_element_type=f32)


def inverse_rms(values):
    return lax.rsqrt(jnp.mean(values * values, axis=-1, keepdims=True) + norm_eps)


def norm_back(values, gain, grad_out):
    scale = inverse_rms(values)
    pulled = grad_out * gain
    mean_part = jnp.mean(pulled * values, axis=-1, keepdims=True)
    grad_in = scale * pulled - values * (scale * scale * scale) * mean_part
    return grad_in, jnp.sum(grad_out * values * scale, axis=0, keepdims=True)


def gelu_terms(gate_act):
    square = gate_act * gate_act
    bent = jnp.tanh(0.7978845608028654 * gate_act * (1.0 + 0.044715 * square))
    half = 0.5 * (1.0 + bent)
    slope = half + 0.5 * gate_act * (1.0 - bent * bent) * (
        0.7978845608028654 * (1.0 + 3.0 * 0.044715 * square)
    )
    return gate_act * half, slope


def run(body, name, ins, outs, scratch, after=(), flops=0):
    in_names, out_names, scratch_names = list(ins), list(outs), list(scratch)
    staged = [n for n in in_names if n != "place" and n not in raw_names]
    in_sems = {n: i for i, n in enumerate(staged)}
    out_sems = {n: i for i, n in enumerate(out_names)}

    def kernel(*refs):
        refs = list(refs)
        sources = dict(zip(in_names, refs))
        refs = refs[len(in_names) + len(after) :]
        targets = dict(zip(out_names, refs))
        refs = refs[len(out_names) :]
        space = dict(zip(scratch_names, refs))
        refs = refs[len(scratch_names) :]
        buffers = dict(zip(staged + out_names, refs))
        sems_in, sems_out = refs[len(staged) + len(out_names) :]
        r = types.SimpleNamespace(**space, **buffers)
        for n in in_names:
            if n == "place" or n in raw_names:
                setattr(r, n, sources[n])

        def copy_in(n):
            return pltpu.make_async_copy(sources[n], buffers[n], sems_in.at[in_sems[n]])

        def copy_out(n):
            return pltpu.make_async_copy(buffers[n], targets[n], sems_out.at[out_sems[n]])

        r.fetch = lambda *names: [copy_in(n).start() for n in names]
        r.need = lambda *names: [copy_in(n).wait() for n in names]
        r.write = lambda *names: [copy_out(n).start() for n in names]
        r.drain = lambda *names: [copy_out(n).wait() for n in names]
        body(r)

    moved = sum(a.size * a.dtype.itemsize for a in ins.values())
    results = pl.pallas_call(
        kernel,
        name=name,
        in_specs=[
            pl.BlockSpec(memory_space=pltpu.SMEM if n == "place" else pl.ANY) for n in in_names
        ]
        + [pl.BlockSpec(memory_space=pl.ANY) for _ in after],
        out_specs=[pl.BlockSpec(memory_space=pl.ANY) for _ in outs],
        out_shape=[jax.ShapeDtypeStruct(shape, kind) for shape, kind in outs.values()],
        scratch_shapes=list(scratch.values())
        + [pltpu.VMEM(ins[n].shape, ins[n].dtype) for n in staged]
        + [pltpu.VMEM(shape, kind) for shape, kind in outs.values()]
        + [pltpu.SemaphoreType.DMA((max(1, len(staged)),)), pltpu.SemaphoreType.DMA((len(outs),))],
        compiler_params=pltpu.CompilerParams(vmem_limit_bytes=vmem_bytes),
        cost_estimate=pl.CostEstimate(flops=flops, bytes_accessed=moved, transcendentals=0),
    )(*ins.values(), *after)
    return types.SimpleNamespace(**dict(zip(outs, results)))


def chunks(extent, size):
    size = min(size, extent)
    return [slice(start, start + size) for start in range(0, extent, size)]


def attention_copies(r, masks, rows):
    copies = []
    for idx, mask in enumerate(masks):
        half, at = divmod(idx, max(1, len(masks) // 2))
        source = (r.attn_near if half == 0 else r.attn_far).at[pl.ds(at * rows, rows)]
        place = (r.place[0] ^ mask) * rows if len(masks) > 1 else 0
        target = r.attn_w.at[pl.ds(pl.multiple_of(place, rows), rows)]
        copies.append(pltpu.make_async_copy(source, target, r.attn_sem))
    return copies


def ff_copies(r, layer_idx):
    width = r.ff_down.shape[-1]
    copies = []
    for k, own in enumerate((r.w_gate, r.w_up)):
        target = r.ff_gate_up.at[0, :, pl.ds(k * width, width)]
        copies.append(pltpu.make_async_copy(own.at[layer_idx], target, r.ff_sem))
    copies.append(pltpu.make_async_copy(r.w_down.at[layer_idx], r.ff_down.at[0], r.ff_sem))
    part = r.ff_near.shape[1]
    for source, base in ((r.ff_near, 0), (r.ff_far, 1)):
        for m in range(2):
            rows = pl.ds(pl.multiple_of((r.place[1] ^ (2 * m + base)) * part, part), part)
            for k in range(2):
                target = r.ff_gate_up.at[1, rows, pl.ds(k * width, width)]
                copies.append(pltpu.make_async_copy(source.at[3 * m + k], target, r.ff_sem))
            copies.append(
                pltpu.make_async_copy(source.at[3 * m + 2], r.ff_down.at[1, rows], r.ff_sem)
            )
    return copies


def start_all(copies):
    for copy in copies:
        copy.start()


def wait_all(sem, *buffers):
    for whole in buffers:
        pltpu.make_async_copy(whole, whole, sem).wait()


def lane_low(rows):
    return lax.broadcasted_iota(jnp.int32, (rows, 128), 1) < 64


def lane_halves():
    low = lane_low(1).astype(f32)
    return low.astype(bf16), (1.0 - low).astype(bf16)


def pair_blocks(rows, low, high):
    return jnp.concatenate([rows * low, rows * high], axis=0)


def own_blocks(both, is_low):
    half = both.shape[0] // 2
    return jnp.where(is_low, both[:half], both[half:]).astype(bf16)


def attention_forward(r, x_ref, a_ref, sizes):
    series, slots, inner = sizes
    rows = series * slots
    for part in chunks(rows, 256):
        r.qkv[part, :] = dot_nn(a_ref[part, :], r.attn_w[:, : 3 * inner]).astype(bf16)
    r.write("qkv")
    is_low = lane_low(slots)
    low, high = lane_halves()
    for s in range(series):
        here = slice(s * slots, (s + 1) * slots)
        keep = r.mask[here, :] == 1
        for start in range(0, inner, 128):
            at = slice(start, start + 128)
            query = r.qkv[here, at]
            keys = r.qkv[here, inner + start : inner + start + 128]
            scores = dot_nt(keys, pair_blocks(query, low, high)) + r.bias[:, at]
            scores = jnp.where(keep, scores, masked_score)
            exps = jnp.exp(scores - jnp.max(scores, axis=0, keepdims=True))
            r.probs[here, at] = exps / jnp.sum(exps, axis=0, keepdims=True)
    r.write("probs")
    for s in range(series):
        here = slice(s * slots, (s + 1) * slots)
        for start in range(0, inner, 128):
            at = slice(start, start + 128)
            values = r.qkv[here, 2 * inner + start : 2 * inner + start + 128]
            both = dot_tn(r.probs[here, at].astype(bf16), values)
            r.heads[here, at] = own_blocks(both, is_low)
    r.write("heads")
    for part in chunks(rows, 256):
        middle = x_ref[part, :] + dot_nt(r.heads[part, :], r.attn_w[:, 3 * inner :])
        r.middle[part, :] = middle
        r.ff_in[part, :] = (middle * inverse_rms(middle) * r.gain_ff[...]).astype(bf16)
    r.write("middle", "ff_in")


attn_out_names = ("qkv", "probs", "heads", "middle", "ff_in")


def prepare_body(r):
    r.fetch("inputs", "marks", "embed", "gain", "buckets", "table")
    r.need("inputs", "marks", "embed", "gain", "buckets", "table")
    x = jnp.where(r.marks[:, 0:1] == 1, r.inputs[...].astype(f32), r.embed[...])
    r.x[...] = x
    r.a[...] = (x * inverse_rms(x) * r.gain[...]).astype(bf16)
    buckets = r.buckets[...]
    bias = jnp.zeros(buckets.shape, f32)
    for idx in range(r.table.shape[0]):
        bias = jnp.where(buckets == idx, r.table[idx : idx + 1, :], bias)
    r.bias[...] = bias
    r.mask[...] = jnp.broadcast_to(r.marks[:, 1:2], r.mask.shape)
    r.write("x", "a", "bias", "mask")
    r.drain("x", "a", "bias", "mask")


def first_body(r, sizes, masks, grain):
    r.fetch("a")
    start_all(attention_copies(r, masks, grain))
    r.fetch("bias", "mask", "x", "gain_ff", "gain_next")
    start_all(ff_copies(r, 0))
    r.need("a")
    wait_all(r.attn_sem, r.attn_w)
    r.need("bias", "mask", "x", "gain_ff", "gain_next")
    attention_forward(r, r.x, r.a, sizes)
    wait_all(r.ff_sem, r.ff_gate_up, r.ff_down)
    width = r.x.shape[1]
    for part in chunks(r.x.shape[0], 256):
        x_next = r.middle[part, :]
        for half in range(2):
            both = dot_nn(r.ff_in[part, :], r.ff_gate_up[half])
            hidden = (gelu_terms(both[:, :width])[0] * both[:, width:]).astype(bf16)
            x_next = x_next + dot_nn(hidden, r.ff_down[half])
        r.x_next[part, :] = x_next
        r.a_next[part, :] = (x_next * inverse_rms(x_next) * r.gain_next[...]).astype(bf16)
    r.write("x_next", "a_next")
    r.drain(*attn_out_names, "x_next", "a_next")


def second_body(r, sizes, masks, grain):
    r.fetch("a")
    start_all(attention_copies(r, masks, grain))
    r.fetch("bias", "mask", "x", "gain_ff")
    r.need("a")
    wait_all(r.attn_sem, r.attn_w)
    r.need("bias", "mask", "x", "gain_ff")
    attention_forward(r, r.x, r.a, sizes)
    r.drain(*attn_out_names)


def backward_body(r, sizes, masks, grain, layer_idx, last, piece_masks, heads):
    series, slots, inner = sizes
    rows = series * slots
    width = r.x.shape[1]
    r.fetch("grad", "ff_in", "gain_ff", "gain_attn")
    start_all(ff_copies(r, layer_idx))
    r.fetch("middle")
    start_all(attention_copies(r, masks, grain))
    r.fetch("qkv", "probs", "heads", "a", "x")
    if not last:
        r.fetch("bias_before", "marks", "buckets", "small_before")
    r.need("grad", "ff_in", "gain_ff", "gain_attn")
    if not last:
        r.need("small_before")
        r.small[...] = r.small_before[...]
    wait_all(r.ff_sem, r.ff_gate_up, r.ff_down)
    r.need("middle")
    gain_total = jnp.zeros((1, width), f32)
    for part in chunks(rows, 256):
        grad = r.grad[part, :].astype(f32)
        rounded = grad.astype(bf16)
        ff_rows = r.ff_in[part, :]
        back = None
        middle = r.middle[part, :]
        total = middle
        for half in range(2):
            both = dot_nn(ff_rows, r.ff_gate_up[half])
            grad_hidden = dot_nt(rounded, r.ff_down[half])
            gate_act, up_act = both[:, :width], both[:, width:]
            mixed, slope = gelu_terms(gate_act)
            if half == 0:
                r.grad_gate_up[part, :width] = (grad_hidden * up_act * slope).astype(bf16)
                r.grad_gate_up[part, width:] = (grad_hidden * mixed).astype(bf16)
                pulled = r.grad_gate_up[part, :]
            else:
                r.pulled[:, :width] = (grad_hidden * up_act * slope).astype(bf16)
                r.pulled[:, width:] = (grad_hidden * mixed).astype(bf16)
                pulled = r.pulled[...]
            hidden = (mixed * up_act).astype(bf16)
            if half == 0:
                r.hidden[part, :] = hidden
            if last:
                total = total + dot_nn(hidden, r.ff_down[half])
            term = dot_nt(pulled, r.ff_gate_up[half])
            back = term if back is None else back + term
        if last:
            r.outputs[part, :] = total.astype(bf16)
        grad_mid, gain_part = norm_back(middle, r.gain_ff[...], back)
        gain_total += gain_part
        grad_mid = grad + grad_mid
        r.grad_mid[part, :] = grad_mid
        r.branch[part, :] = grad_mid.astype(bf16)
    if last:
        r.small[...] = jnp.zeros(r.small.shape, f32)
    put_row(r.small, 2 + layer_idx, gain_total)
    r.write("hidden", "grad_gate_up")
    if last:
        r.write("outputs")
    wait_all(r.attn_sem, r.attn_w)
    for part in chunks(rows, 256):
        r.grad_heads[part, :] = dot_nn(r.branch[part, :], r.attn_w[:, 3 * inner :]).astype(bf16)
    r.need("qkv", "probs", "heads", "a", "x")
    if not last:
        r.need("bias_before", "marks", "buckets")
    is_low = lane_low(slots)
    low, high = lane_halves()
    for start in range(0, inner, 128):
        at = slice(start, start + 128)
        bias_total = jnp.zeros((slots, 128), f32) if last else r.bias_before[:, at]
        for s in range(series):
            here = slice(s * slots, (s + 1) * slots)
            probs = r.probs[here, at]
            values = r.qkv[here, 2 * inner + start : 2 * inner + start + 128]
            grad_probs = dot_nt(values, pair_blocks(r.grad_heads[here, at], low, high))
            inner_sum = jnp.sum(probs * grad_probs, axis=0, keepdims=True)
            grad_scores = (probs * (grad_probs - inner_sum)).astype(bf16)
            r.grad_scores[here, at] = grad_scores
            bias_total = bias_total + grad_scores.astype(f32)
        r.bias_acc[:, at] = bias_total
    for s in range(series):
        here = slice(s * slots, (s + 1) * slots)
        for start in range(0, inner, 128):
            at = slice(start, start + 128)
            key_at = slice(inner + start, inner + start + 128)
            value_at = slice(2 * inner + start, 2 * inner + start + 128)
            grad_scores = r.grad_scores[here, at]
            r.grad_qkv[here, key_at] = dot_nn(
                grad_scores, pair_blocks(r.qkv[here, at], low, high)
            ).astype(bf16)
            r.grad_qkv[here, value_at] = dot_nn(
                r.probs[here, at].astype(bf16), pair_blocks(r.grad_heads[here, at], low, high)
            ).astype(bf16)
            r.grad_qkv[here, at] = own_blocks(dot_tn(grad_scores, r.qkv[here, key_at]), is_low)
    r.attn_grad[:, : 3 * inner] = dot_tn(r.a[...], r.grad_qkv[...])
    r.attn_grad[:, 3 * inner :] = dot_tn(r.branch[...], r.heads[...])
    scatter_pieces(r.attn_grad, r.attn_keep, r.attn_send, piece_masks, r.place[2])
    r.write("attn_send", "attn_keep")
    gain_total = jnp.zeros((1, width), f32)
    embed_total = jnp.zeros((1, width), f32)
    for part in chunks(rows, 256):
        grad_normed = dot_nt(r.grad_qkv[part, :], r.attn_w[:, : 3 * inner])
        grad_in, gain_part = norm_back(r.x[part, :], r.gain_attn[...], grad_normed)
        gain_total += gain_part
        grad_in = r.grad_mid[part, :] + grad_in
        if last:
            r.grad_next[part, :] = grad_in
            r.grad_next_low[part, :] = grad_in.astype(bf16)
        else:
            seen = r.marks[part, 0:1] == 1
            r.grad_next[part, :] = jnp.where(seen, grad_in, 0.0)
            embed_total += jnp.sum(jnp.where(seen, 0.0, grad_in), axis=0, keepdims=True)
    put_row(r.small, layer_idx, gain_total)
    r.write("grad_next")
    if last:
        r.write("grad_next_low", "bias_acc", "small")
    else:
        put_row(r.small, 4, embed_total)
        head_size = inner // heads
        for idx in range(r.table_rows.shape[0]):
            chosen = jnp.where(r.buckets[...] == idx, r.bias_acc[...], 0.0)
            r.table_rows[idx : idx + 1, :] = jnp.sum(chosen, axis=0, keepdims=True)
        lane = lax.broadcasted_iota(jnp.int32, (r.table_rows.shape[0], 128), 1)
        table = jnp.zeros(lane.shape, f32)
        for head in range(heads):
            cut = r.table_rows[:, head * head_size : (head + 1) * head_size]
            table = jnp.where(lane == head, jnp.sum(cut, axis=1, keepdims=True), table)
        r.small[small_rows(width) :, :] = table
        r.write("small")
    r.drain("hidden", "grad_gate_up", "attn_send", "attn_keep", "grad_next", "small")
    if last:
        r.drain("outputs", "grad_next_low", "bias_acc")


def small_rows(width):
    return -(-5 * width // 1024) * 8


def put_row(packed, which, row):
    lanes = row.shape[1] // 128
    for k in range(lanes):
        packed[which * lanes + k : which * lanes + k + 1, :] = row[:, k * 128 : (k + 1) * 128]


def scatter_pieces(whole, keep, send, masks, place):
    count = len(masks)
    grain = whole.shape[0] // count
    for idx, mask in enumerate(masks):
        target = keep if idx < count // 2 else send
        source = pl.ds(pl.multiple_of((place ^ mask) * grain, grain), grain)
        target[idx % (count // 2)] = whole[source, :].astype(bf16)


def weight_body(r, layer_idx, piece_masks):
    width = r.ff_in.shape[1]
    rows = r.ff_in.shape[0]
    r.fetch("peer_in", "peer_grad")
    copies = [
        pltpu.make_async_copy(
            own.at[layer_idx], r.ff_gate_up.at[:, pl.ds(k * width, width)], r.ff_sem
        )
        for k, own in enumerate((r.w_gate, r.w_up))
    ]
    copies.append(pltpu.make_async_copy(r.w_down.at[layer_idx], r.ff_down, r.ff_sem))
    start_all(copies)
    r.fetch("ff_in", "grad_gate_up", "hidden", "grad")
    r.need("peer_in", "peer_grad")
    wait_all(r.ff_sem, r.ff_gate_up, r.ff_down)
    for part in chunks(rows, 256):
        both = dot_nn(r.peer_in[part, :], r.ff_gate_up[...])
        grad_hidden = dot_nt(r.peer_grad[part, :], r.ff_down[...])
        gate_act, up_act = both[:, :width], both[:, width:]
        mixed, slope = gelu_terms(gate_act)
        r.peer_gate_up[part, :width] = (grad_hidden * up_act * slope).astype(bf16)
        r.peer_gate_up[part, width:] = (grad_hidden * mixed).astype(bf16)
        r.peer_hidden[part, :] = (mixed * up_act).astype(bf16)
    r.need("ff_in", "grad_gate_up", "hidden", "grad")
    r.ff_grad[:, : 2 * width] = dot_tn(r.ff_in[...], r.grad_gate_up[...]) + dot_tn(
        r.peer_in[...], r.peer_gate_up[...]
    )
    r.ff_grad[:, 2 * width :] = dot_tn(r.hidden[...], r.grad[...]) + dot_tn(
        r.peer_hidden[...], r.peer_grad[...]
    )
    scatter_pieces(r.ff_grad, r.ff_keep, r.ff_send, piece_masks, r.place[3])
    r.write("ff_send", "ff_keep")
    r.drain("ff_send", "ff_keep")


def finish(pieces, masks, layer_idx, place, shape, before=()):
    grain, width = pieces.shape[1], shape[-1]
    count = len(before)

    def kernel(place_ref, source, *refs):
        outs = refs[count : count + 3]
        held, stage, in_sem, out_sem = refs[count + 3 :]
        copy_in = pltpu.make_async_copy(source, held, in_sem)
        copy_in.start()
        copy_in.wait()
        for idx, mask in enumerate(masks):
            rows = pl.ds(pl.multiple_of((place_ref[3] ^ mask) * grain, grain), grain)
            for k, out in enumerate(outs):
                stage[k, idx] = held[idx, :, k * width : (k + 1) * width].astype(f32)
                pltpu.make_async_copy(stage.at[k, idx], out.at[layer_idx, rows], out_sem).start()
        pltpu.make_async_copy(stage, stage, out_sem).wait()

    return pl.pallas_call(
        kernel,
        name="layer_%d_ff_grads" % layer_idx,
        in_specs=[pl.BlockSpec(memory_space=pltpu.SMEM)]
        + [pl.BlockSpec(memory_space=pl.ANY)] * (1 + count),
        out_specs=[pl.BlockSpec(memory_space=pl.ANY)] * 3,
        out_shape=[jax.ShapeDtypeStruct(shape, f32)] * 3,
        input_output_aliases={2 + k: k for k in range(count)},
        scratch_shapes=[
            pltpu.VMEM(pieces.shape, bf16),
            pltpu.VMEM((3, len(masks), grain, width), f32),
            pltpu.SemaphoreType.DMA,
            pltpu.SemaphoreType.DMA,
        ],
        compiler_params=pltpu.CompilerParams(vmem_limit_bytes=vmem_bytes),
    )(place, pieces, *before)


def small_body(r):
    r.fetch("packed")
    r.need("packed")
    lanes = r.embed.shape[1] // 128
    for which in range(5):
        out, row = ((r.gain_attn, which), (r.gain_ff, which - 2), (r.embed, 0))[which // 2]
        for k in range(lanes):
            at = which * lanes + k
            out[row : row + 1, k * 128 : (k + 1) * 128] = r.packed[at : at + 1, :]
    r.table[...] = r.packed[small_rows(r.embed.shape[1]) :, : r.table.shape[1]]
    r.write("gain_attn", "gain_ff", "embed", "table")
    r.drain("gain_attn", "gain_ff", "embed", "table")


def order_masks(hops):
    masks = [0]
    for hop in reversed(hops):
        masks = masks + [mask ^ hop for mask in masks]
    return masks


def tie(value, *others):
    return lax.optimization_barrier((value, *others))[0]


def on_device(
    inputs,
    cotangent,
    attention_mask,
    patch_valid,
    buckets,
    mask_embed,
    w_query,
    w_key,
    w_value,
    w_output,
    w_gate,
    w_up,
    w_down,
    gain_attn,
    gain_ff,
    bias_table,
    dp_size,
):
    series, slots, width = inputs.shape
    heads = bias_table.shape[1]
    inner = w_query.shape[2]
    rows = series * slots
    sizes = (series, slots, inner)
    matrix = (rows, width)
    devices = 2 * dp_size
    dp_at = lax.axis_index("dp")
    device_at = 2 * dp_at + lax.axis_index("tensor")
    cotangent = cotangent.reshape(matrix)

    def swap(array, mask):
        return lax.ppermute(array, axes, [(n, n ^ mask) for n in range(devices)])

    def join(left, right):
        return jnp.concatenate([left, right], axis=0)

    bits = [1 << k for k in range(devices.bit_length() - 1)]

    attn_grain = max(16, width // devices)
    attn_count = width // attn_grain
    ff_grain = max(16, width // dp_size)
    ff_count = width // ff_grain
    quarter_at = lax.rem(dp_at, 4)
    place = jnp.stack(
        [
            device_at,
            quarter_at,
            device_at // (devices // attn_count),
            lax.rem(dp_at, ff_count),
        ]
    ).astype(jnp.int32)

    quarter = width // 4
    packed = jnp.concatenate([w_query, w_key, w_value, jnp.swapaxes(w_output, 1, 2)], axis=2)
    ff_blocks = jnp.concatenate(
        [
            lax.dynamic_slice_in_dim(tie(w, packed), quarter_at * quarter, quarter, axis=1)
            for w in (w_gate, w_up, w_down)
        ],
        axis=0,
    )
    ff_quarter = swap(ff_blocks, 1).reshape(3, 2, quarter, width)

    wide_buckets = jnp.tile(buckets.T, (1, heads))
    wide_table = jnp.repeat(bias_table, slots, axis=1)
    marks = jnp.stack([patch_valid.reshape(rows), attention_mask.reshape(rows)], axis=1)

    start = run(
        prepare_body,
        "prepare",
        dict(
            inputs=inputs.reshape(matrix),
            marks=marks,
            embed=mask_embed[None, :],
            gain=gain_attn[0:1],
            buckets=wide_buckets,
            table=wide_table,
        ),
        dict(
            x=(matrix, f32),
            a=(matrix, bf16),
            bias=((slots, heads * slots), f32),
            mask=((rows, 128), jnp.int32),
        ),
        {},
    )

    own_rows = packed.shape[1]
    direct = own_rows % 16 == 0
    far = bits[2:]
    if direct:
        hops_0 = far[1:][::-1] + far[:1] + [1, 2]
        hops_1 = [1] + far + [2]
        block_0, block_1 = packed[0], packed[1]
        got_0 = got_1 = None
        for step, (hop_0, hop_1) in enumerate(zip(hops_0, hops_1)):
            if step + 1 == len(hops_0):
                break
            got_0, got_1 = swap(block_0, hop_0), swap(block_1, hop_1)
            if step + 2 == len(hops_0):
                before_last = block_0
                got_0 = tie(got_0, start.a)
            block_0, block_1 = join(block_0, got_0), join(block_1, got_1)
        ff_0 = ff_quarter[:, 0]
        ff_0 = join(ff_0, swap(tie(ff_0, before_last), 4))
        ff_1 = tie(ff_quarter[:, 1], block_0)
        ff_1 = join(ff_1, swap(ff_1, 4))
        attn_pieces = [
            (block_0, swap(block_0, 2), order_masks(hops_0[::-1])),
            (block_1, swap(block_1, 2), order_masks(hops_1[::-1])),
        ]
    else:
        ff_0, ff_1 = (
            join(ff_quarter[:, layer_idx], swap(ff_quarter[:, layer_idx], 4))
            for layer_idx in range(2)
        )
        attn_pieces = []
        for layer_idx in range(2):
            whole = lax.all_gather(packed[layer_idx], axes, axis=0, tiled=True)
            attn_pieces.append((whole, whole, [0]))
    ff_pieces = [(ff_0, swap(ff_0, 2)), (ff_1, swap(ff_1, 2))]

    def attn_ins(layer_idx):
        near, far, masks = attn_pieces[layer_idx]
        return dict(attn_near=near, attn_far=far), masks

    def ff_ins(layer_idx):
        near, far = ff_pieces[layer_idx]
        return dict(w_gate=w_gate, w_up=w_up, w_down=w_down, ff_near=near, ff_far=far)

    attn_scratch = dict(
        attn_w=pltpu.VMEM((width, 4 * inner), bf16), attn_sem=pltpu.SemaphoreType.DMA
    )
    ff_scratch = dict(
        ff_gate_up=pltpu.VMEM((2, width, 2 * width), bf16),
        ff_down=pltpu.VMEM((2, width, width), bf16),
        ff_sem=pltpu.SemaphoreType.DMA,
    )
    grain = own_rows if direct else width
    attn_outs = dict(
        qkv=((rows, 3 * inner), bf16),
        probs=((rows, heads * slots), f32),
        heads=((rows, inner), bf16),
        middle=(matrix, f32),
        ff_in=(matrix, bf16),
    )
    attn_flops = 2 * rows * width * 4 * inner
    ff_flops = 2 * rows * width * 6 * width

    pieces, masks = attn_ins(0)
    first = run(
        functools.partial(first_body, sizes=sizes, masks=masks, grain=grain),
        "layer_0_forward",
        dict(
            place=place,
            x=start.x,
            a=start.a,
            bias=start.bias,
            mask=start.mask,
            gain_ff=gain_ff[0:1],
            gain_next=gain_attn[1:2],
            **pieces,
            **ff_ins(0),
        ),
        dict(**attn_outs, x_next=(matrix, f32), a_next=(matrix, bf16)),
        dict(**attn_scratch, **ff_scratch),
        flops=attn_flops + ff_flops,
    )
    peer_in_0 = swap(first.ff_in, 1)
    pieces, masks = attn_ins(1)
    second = run(
        functools.partial(second_body, sizes=sizes, masks=masks, grain=grain),
        "layer_1_attention",
        dict(
            place=place,
            x=first.x_next,
            a=first.a_next,
            bias=start.bias,
            mask=start.mask,
            gain_ff=gain_ff[1:2],
            **pieces,
        ),
        attn_outs,
        attn_scratch,
        flops=attn_flops,
    )
    peer_in_1 = swap(second.ff_in, 1)
    peer_cotangent = swap(tie(cotangent, second.ff_in), 1)

    attn_hops = [2, 1] + bits[2:]
    attn_low = devices // attn_count
    attn_split = [hop for hop in attn_hops if hop >= attn_low]
    attn_whole = [hop for hop in attn_hops if hop < attn_low]
    ff_hops = bits[1:]
    ff_split = [hop for hop in ff_hops if hop // 2 < ff_count]
    ff_whole = [hop for hop in ff_hops if hop // 2 >= ff_count]
    attn_masks = [mask // attn_low for mask in order_masks(attn_split)]
    ff_masks = [mask // 2 for mask in order_masks(ff_split)]
    attn_half = (attn_count // 2, attn_grain, 4 * inner)
    ff_half = (ff_count // 2, ff_grain, 3 * width)
    small_shape = (small_rows(width) + bias_table.shape[0], 128)

    def backward(layer_idx, kept, x, a, grad, extra_ins, extra_outs, extra_scratch, after=()):
        last = layer_idx == 1
        pieces, masks = attn_ins(layer_idx)
        return run(
            functools.partial(
                backward_body,
                sizes=sizes,
                masks=masks,
                grain=grain,
                layer_idx=layer_idx,
                last=last,
                piece_masks=attn_masks,
                heads=heads,
            ),
            "layer_%d_backward" % layer_idx,
            dict(
                place=place,
                x=x,
                a=a,
                grad=grad,
                gain_attn=gain_attn[layer_idx : layer_idx + 1],
                gain_ff=gain_ff[layer_idx : layer_idx + 1],
                qkv=kept.qkv,
                probs=kept.probs,
                heads=kept.heads,
                middle=kept.middle,
                ff_in=kept.ff_in,
                **pieces,
                **ff_ins(layer_idx),
                **extra_ins,
            ),
            dict(
                grad_next=(matrix, f32),
                hidden=(matrix, bf16),
                grad_gate_up=((rows, 2 * width), bf16),
                small=(small_shape, f32),
                attn_keep=(attn_half, bf16),
                attn_send=(attn_half, bf16),
                **extra_outs,
            ),
            dict(
                grad_mid=pltpu.VMEM(matrix, f32),
                branch=pltpu.VMEM(matrix, bf16),
                grad_heads=pltpu.VMEM((rows, inner), bf16),
                grad_qkv=pltpu.VMEM((rows, 3 * inner), bf16),
                grad_scores=pltpu.VMEM((rows, heads * slots), bf16),
                attn_grad=pltpu.VMEM((width, 4 * inner), f32),
                pulled=pltpu.VMEM((256, 2 * width), bf16),
                **attn_scratch,
                **ff_scratch,
                **extra_scratch,
            ),
            after=after,
            flops=2 * (attn_flops + ff_flops),
        )

    def weight_grads(layer_idx, kept, back, grad, peer_in, peer_grad, after=()):
        return run(
            functools.partial(weight_body, layer_idx=layer_idx, piece_masks=ff_masks),
            "layer_%d_weight_grads" % layer_idx,
            dict(
                place=place,
                ff_in=kept.ff_in,
                grad=grad,
                hidden=back.hidden,
                grad_gate_up=back.grad_gate_up,
                peer_in=peer_in,
                peer_grad=peer_grad,
                w_gate=w_gate,
                w_up=w_up,
                w_down=w_down,
            ),
            dict(ff_keep=(ff_half, bf16), ff_send=(ff_half, bf16)),
            dict(
                peer_gate_up=pltpu.VMEM((rows, 2 * width), bf16),
                peer_hidden=pltpu.VMEM(matrix, bf16),
                ff_grad=pltpu.VMEM((width, 3 * width), f32),
                ff_gate_up=pltpu.VMEM((width, 2 * width), bf16),
                ff_down=pltpu.VMEM((width, width), bf16),
                ff_sem=pltpu.SemaphoreType.DMA,
            ),
            after=after,
            flops=ff_flops,
        )

    def add(left, right):
        return (left.astype(f32) + right.astype(f32)).astype(bf16)

    def halving(keep, send, hops, out):
        for step, hop in enumerate(hops):
            got = yield swap(send, hop)
            if step + 1 < len(hops):
                cut = keep.shape[0] // 2
                send = add(keep[cut:], got[cut:])
                keep = add(keep[:cut], got[:cut])
                out["token"] = send
            else:
                out["token"] = keep = add(keep, got)
        out["piece"] = keep

    def summing(piece, hops, out):
        for hop in hops:
            got = yield swap(piece, hop)
            out["token"] = piece = add(piece, got) if piece.dtype == bf16 else piece + got
        out["piece"] = piece

    def sharing(piece, hops, out):
        for step, hop in enumerate(hops):
            got = yield swap(piece, hop)
            if step + 1 < len(hops):
                out["token"] = piece = join(piece, got)
            else:
                out["token"] = got
        out["near"], out["far"] = piece, got

    def attn_chain(part, out):
        yield from halving(part.attn_keep, part.attn_send, attn_split, out)
        yield from summing(out["piece"], attn_whole, out)
        piece = out["piece"][0]
        if own_rows < attn_grain:
            first_row = lax.rem(device_at, attn_low) * own_rows
            piece = lax.dynamic_slice_in_dim(piece, first_row, own_rows, axis=0)
        out["done"] = piece.astype(f32)

    def ff_chain(part, out):
        yield from halving(part.ff_keep, part.ff_send, ff_split, out)
        yield from summing(out["piece"], ff_whole, out)
        yield from sharing(out["piece"], ff_split[::-1], out)
        out["done"] = True

    class Chain:
        def __init__(self, steps, *args):
            self.out = {}
            self.steps = steps(*args, self.out)
            self.arriving = next(self.steps)

        def step(self, token):
            if self.arriving is not None:
                arrived = tie(self.arriving, token)
                self.arriving = None
                try:
                    self.arriving = self.steps.send(arrived)
                except StopIteration:
                    pass
                return self.out["token"]
            return token

    back_1 = backward(
        1,
        second,
        first.x_next,
        first.a_next,
        cotangent,
        {},
        dict(
            outputs=(matrix, bf16),
            grad_next_low=(matrix, bf16),
            bias_acc=((slots, heads * slots), f32),
        ),
        {},
    )
    peer_grad_0 = swap(back_1.grad_next_low, 1)
    part_1 = weight_grads(1, second, back_1, cotangent, peer_in_1, peer_cotangent)
    attn_1 = Chain(attn_chain, back_1)
    ff_1 = Chain(ff_chain, part_1)
    token = attn_1.step(part_1.ff_send)
    back_0 = backward(
        0,
        first,
        start.x,
        start.a,
        back_1.grad_next,
        dict(
            bias_before=back_1.bias_acc,
            marks=marks,
            buckets=wide_buckets,
            small_before=back_1.small,
        ),
        {},
        dict(
            bias_acc=pltpu.VMEM((slots, heads * slots), f32),
            table_rows=pltpu.VMEM((bias_table.shape[0], heads * slots), f32),
        ),
        after=(token,),
    )
    attn_0 = Chain(attn_chain, back_0)
    token = ff_1.step(back_0.attn_send)
    token = attn_1.step(token)
    part_0 = weight_grads(
        0, first, back_0, back_1.grad_next_low, peer_in_0, peer_grad_0, after=(token,)
    )
    ff_0 = Chain(ff_chain, part_0)
    small = Chain(summing, back_0.small, attn_hops)
    token = part_0.ff_send
    done_1 = None
    shape = (2, width, width)
    finish_masks = order_masks(ff_split)
    near_masks = [mask // 2 for mask in finish_masks[: ff_count // 2]]
    far_masks = [mask // 2 for mask in finish_masks[ff_count // 2 :]]
    chains = (ff_0, attn_0, ff_1, attn_1, small)
    while any(chain.arriving is not None for chain in chains):
        if "near" in ff_1.out and done_1 is None:
            pieces = join(ff_1.out["near"], ff_1.out["far"])
            done_1 = finish(pieces, near_masks + far_masks, 1, place, shape)
        for chain in chains:
            token = chain.step(token)
    if done_1 is None:
        pieces = join(ff_1.out["near"], ff_1.out["far"])
        done_1 = finish(pieces, near_masks + far_masks, 1, place, shape)
    near_0 = finish(ff_0.out["near"], near_masks, 0, place, shape, done_1)
    done = finish(ff_0.out["far"], far_masks, 0, place, shape, near_0)
    sums = run(
        small_body,
        "small_sums",
        dict(packed=small.out["piece"]),
        dict(
            gain_attn=((2, width), f32),
            gain_ff=((2, width), f32),
            embed=((1, width), f32),
            table=(bias_table.shape, f32),
        ),
        {},
    )
    attn_0, attn_1 = attn_0.out["done"], attn_1.out["done"]
    attn_grads = jnp.stack([attn_0, attn_1])
    return (
        back_1.outputs.reshape(inputs.shape),
        back_0.grad_next.reshape(inputs.shape),
        attn_grads[:, :, :inner],
        attn_grads[:, :, inner : 2 * inner],
        attn_grads[:, :, 2 * inner : 3 * inner],
        jnp.swapaxes(attn_grads[:, :, 3 * inner :], 1, 2),
        *done,
        sums.gain_attn,
        sums.gain_ff,
        sums.table,
        sums.embed[0],
    )


def solution(mesh):
    placed = (
        P(("dp", "tensor"), None, None),
        P(("dp", "tensor"), None, None),
        P(("dp", "tensor"), None),
        P(("dp", "tensor"), None),
        P(),
        P(),
        P(None, ("dp", "tensor"), None),
        P(None, ("dp", "tensor"), None),
        P(None, ("dp", "tensor"), None),
        P(None, None, ("dp", "tensor")),
        P(None, None, "tensor"),
        P(None, None, "tensor"),
        P(None, "tensor", None),
        P(),
        P(),
        P(),
    )
    return jax.shard_map(
        functools.partial(on_device, dp_size=mesh.shape["dp"]),
        mesh=mesh,
        in_specs=placed,
        out_specs=(
            P(("dp", "tensor"), None, None),
            P(("dp", "tensor"), None, None),
            P(None, ("dp", "tensor"), None),
            P(None, ("dp", "tensor"), None),
            P(None, ("dp", "tensor"), None),
            P(None, None, ("dp", "tensor")),
            P(None, None, "tensor"),
            P(None, None, "tensor"),
            P(None, "tensor", None),
            P(),
            P(),
            P(),
            P(),
        ),
        check_vma=False,
    )
```

```python
import functools
import types

import jax
import jax.numpy as jnp
from jax import lax
from jax.experimental import pallas as pl
from jax.experimental.pallas import tpu as pltpu
from jax.sharding import PartitionSpec as P

norm_eps = 1e-06
masked_score = -1e30
bf16 = jnp.bfloat16
f32 = jnp.float32
axes = ("dp", "tensor")
vmem_bytes = 56 * 1024 * 1024
raw_names = ("attn_near", "attn_far", "ff_near", "ff_far", "w_gate", "w_up", "w_down")


def dot_nn(left, right):
    return lax.dot_general(left, right, (((1,), (0,)), ((), ())), preferred_element_type=f32)


def dot_nt(left, right):
    return lax.dot_general(left, right, (((1,), (1,)), ((), ())), preferred_element_type=f32)


def dot_tn(left, right):
    return lax.dot_general(left, right, (((0,), (0,)), ((), ())), preferred_element_type=f32)


def inverse_rms(values):
    return lax.rsqrt(jnp.mean(values * values, axis=-1, keepdims=True) + norm_eps)


def norm_back(values, gain, grad_out):
    scale = inverse_rms(values)
    pulled = grad_out * gain
    mean_part = jnp.mean(pulled * values, axis=-1, keepdims=True)
    grad_in = scale * pulled - values * (scale * scale * scale) * mean_part
    return grad_in, jnp.sum(grad_out * values * scale, axis=0, keepdims=True)


def gelu_terms(gate_act):
    square = gate_act * gate_act
    bent = jnp.tanh(0.7978845608028654 * gate_act * (1.0 + 0.044715 * square))
    half = 0.5 * (1.0 + bent)
    slope = half + 0.5 * gate_act * (1.0 - bent * bent) * (
        0.7978845608028654 * (1.0 + 3.0 * 0.044715 * square)
    )
    return gate_act * half, slope


def cost(micros):
    return pl.CostEstimate(flops=int(micros * 1.15e9), bytes_accessed=0, transcendentals=0)


def run(body, name, ins, outs, scratch, after=(), micros=1):
    in_names, out_names, scratch_names = list(ins), list(outs), list(scratch)
    staged = [n for n in in_names if n != "place" and n not in raw_names]
    in_sems = {n: i for i, n in enumerate(staged)}
    out_sems = {n: i for i, n in enumerate(out_names)}

    def kernel(*refs):
        refs = list(refs)
        sources = dict(zip(in_names, refs))
        refs = refs[len(in_names) + len(after) :]
        targets = dict(zip(out_names, refs))
        refs = refs[len(out_names) :]
        space = dict(zip(scratch_names, refs))
        refs = refs[len(scratch_names) :]
        buffers = dict(zip(staged + out_names, refs))
        sems_in, sems_out = refs[len(staged) + len(out_names) :]
        r = types.SimpleNamespace(**space, **buffers)
        for n in in_names:
            if n == "place" or n in raw_names:
                setattr(r, n, sources[n])

        def copy_in(n):
            return pltpu.make_async_copy(sources[n], buffers[n], sems_in.at[in_sems[n]])

        def copy_out(n):
            return pltpu.make_async_copy(buffers[n], targets[n], sems_out.at[out_sems[n]])

        r.fetch = lambda *names: [copy_in(n).start() for n in names]
        r.need = lambda *names: [copy_in(n).wait() for n in names]
        r.write = lambda *names: [copy_out(n).start() for n in names]
        r.drain = lambda *names: [copy_out(n).wait() for n in names]
        body(r)

    results = pl.pallas_call(
        kernel,
        name=name,
        in_specs=[
            pl.BlockSpec(memory_space=pltpu.SMEM if n == "place" else pl.ANY) for n in in_names
        ]
        + [pl.BlockSpec(memory_space=pl.ANY) for _ in after],
        out_specs=[pl.BlockSpec(memory_space=pl.ANY) for _ in outs],
        out_shape=[jax.ShapeDtypeStruct(shape, kind) for shape, kind in outs.values()],
        scratch_shapes=list(scratch.values())
        + [pltpu.VMEM(ins[n].shape, ins[n].dtype) for n in staged]
        + [pltpu.VMEM(shape, kind) for shape, kind in outs.values()]
        + [pltpu.SemaphoreType.DMA((max(1, len(staged)),)), pltpu.SemaphoreType.DMA((len(outs),))],
        compiler_params=pltpu.CompilerParams(vmem_limit_bytes=vmem_bytes),
        cost_estimate=cost(micros),
    )(*ins.values(), *after)
    return types.SimpleNamespace(**dict(zip(outs, results)))


def chunks(extent, size):
    size = min(size, extent)
    return [slice(start, start + size) for start in range(0, extent, size)]


def attention_copies(r, masks, rows):
    copies = []
    for idx, mask in enumerate(masks):
        half, at = divmod(idx, max(1, len(masks) // 2))
        source = (r.attn_near if half == 0 else r.attn_far).at[pl.ds(at * rows, rows)]
        place = (r.place[0] ^ mask) * rows if len(masks) > 1 else 0
        target = r.attn_w.at[pl.ds(pl.multiple_of(place, rows), rows)]
        copies.append(pltpu.make_async_copy(source, target, r.attn_sem))
    return copies


def ff_copies(r, layer_idx):
    width = r.ff_down.shape[-1]
    copies = []
    for k, own in enumerate((r.w_gate, r.w_up)):
        target = r.ff_gate_up.at[0, :, pl.ds(k * width, width)]
        copies.append(pltpu.make_async_copy(own.at[layer_idx], target, r.ff_sem))
    copies.append(pltpu.make_async_copy(r.w_down.at[layer_idx], r.ff_down.at[0], r.ff_sem))
    part = r.ff_near.shape[1]
    for source, base in ((r.ff_near, 0), (r.ff_far, 1)):
        for m in range(2):
            rows = pl.ds(pl.multiple_of((r.place[1] ^ (2 * m + base)) * part, part), part)
            for k in range(2):
                target = r.ff_gate_up.at[1, rows, pl.ds(k * width, width)]
                copies.append(pltpu.make_async_copy(source.at[3 * m + k], target, r.ff_sem))
            copies.append(
                pltpu.make_async_copy(source.at[3 * m + 2], r.ff_down.at[1, rows], r.ff_sem)
            )
    return copies


def start_all(copies):
    for copy in copies:
        copy.start()


def wait_all(sem, *buffers):
    for whole in buffers:
        pltpu.make_async_copy(whole, whole, sem).wait()


def lane_low(rows):
    return lax.broadcasted_iota(jnp.int32, (rows, 128), 1) < 64


def lane_halves():
    low = lane_low(1).astype(f32)
    return low.astype(bf16), (1.0 - low).astype(bf16)


def pair_blocks(rows, low, high):
    return jnp.concatenate([rows * low, rows * high], axis=0)


def own_blocks(both, is_low):
    half = both.shape[0] // 2
    return jnp.where(is_low, both[:half], both[half:]).astype(bf16)


def attention_forward(r, x_ref, a_ref, sizes):
    series, slots, inner = sizes
    rows = series * slots
    for part in chunks(rows, 256):
        r.qkv[part, :] = dot_nn(a_ref[part, :], r.attn_w[:, : 3 * inner]).astype(bf16)
    r.write("qkv")
    is_low = lane_low(slots)
    low, high = lane_halves()
    for s in range(series):
        here = slice(s * slots, (s + 1) * slots)
        keep = r.mask[here, :] == 1
        for start in range(0, inner, 128):
            at = slice(start, start + 128)
            query = r.qkv[here, at]
            keys = r.qkv[here, inner + start : inner + start + 128]
            scores = dot_nt(keys, pair_blocks(query, low, high)) + r.bias[:, at]
            scores = jnp.where(keep, scores, masked_score)
            exps = jnp.exp(scores - jnp.max(scores, axis=0, keepdims=True))
            r.probs[here, at] = exps / jnp.sum(exps, axis=0, keepdims=True)
    r.write("probs")
    for s in range(series):
        here = slice(s * slots, (s + 1) * slots)
        for start in range(0, inner, 128):
            at = slice(start, start + 128)
            values = r.qkv[here, 2 * inner + start : 2 * inner + start + 128]
            both = dot_tn(r.probs[here, at].astype(bf16), values)
            r.heads[here, at] = own_blocks(both, is_low)
    r.write("heads")
    for part in chunks(rows, 256):
        middle = x_ref[part, :] + dot_nt(r.heads[part, :], r.attn_w[:, 3 * inner :])
        r.middle[part, :] = middle
        r.ff_in[part, :] = (middle * inverse_rms(middle) * r.gain_ff[...]).astype(bf16)
    r.write("middle", "ff_in")


attn_out_names = ("qkv", "probs", "heads", "middle", "ff_in")


def prepare_body(r):
    r.fetch("inputs", "marks", "embed", "gain", "buckets", "table")
    r.need("inputs", "marks", "embed", "gain", "buckets", "table")
    x = jnp.where(r.marks[:, 0:1] == 1, r.inputs[...].astype(f32), r.embed[...])
    r.x[...] = x
    r.a[...] = (x * inverse_rms(x) * r.gain[...]).astype(bf16)
    buckets = r.buckets[...]
    bias = jnp.zeros(buckets.shape, f32)
    for idx in range(r.table.shape[0]):
        bias = jnp.where(buckets == idx, r.table[idx : idx + 1, :], bias)
    r.bias[...] = bias
    r.mask[...] = jnp.broadcast_to(r.marks[:, 1:2], r.mask.shape)
    r.write("x", "a", "bias", "mask")
    r.drain("x", "a", "bias", "mask")


def first_body(r, sizes, masks, grain):
    r.fetch("a")
    start_all(attention_copies(r, masks, grain))
    r.fetch("bias", "mask", "x", "gain_ff", "gain_next")
    start_all(ff_copies(r, 0))
    r.need("a")
    wait_all(r.attn_sem, r.attn_w)
    r.need("bias", "mask", "x", "gain_ff", "gain_next")
    attention_forward(r, r.x, r.a, sizes)
    wait_all(r.ff_sem, r.ff_gate_up, r.ff_down)
    width = r.x.shape[1]
    for part in chunks(r.x.shape[0], 256):
        x_next = r.middle[part, :]
        for half in range(2):
            both = dot_nn(r.ff_in[part, :], r.ff_gate_up[half])
            hidden = (gelu_terms(both[:, :width])[0] * both[:, width:]).astype(bf16)
            x_next = x_next + dot_nn(hidden, r.ff_down[half])
        r.x_next[part, :] = x_next
        r.a_next[part, :] = (x_next * inverse_rms(x_next) * r.gain_next[...]).astype(bf16)
    r.write("x_next", "a_next")
    r.drain(*attn_out_names, "x_next", "a_next")


def second_body(r, sizes, masks, grain):
    r.fetch("a")
    start_all(attention_copies(r, masks, grain))
    r.fetch("bias", "mask", "x", "gain_ff")
    r.need("a")
    wait_all(r.attn_sem, r.attn_w)
    r.need("bias", "mask", "x", "gain_ff")
    attention_forward(r, r.x, r.a, sizes)
    r.drain(*attn_out_names)


def backward_body(r, sizes, masks, grain, layer_idx, last, piece_masks, heads):
    series, slots, inner = sizes
    rows = series * slots
    width = r.x.shape[1]
    r.fetch("grad", "ff_in", "gain_ff", "gain_attn")
    start_all(ff_copies(r, layer_idx))
    r.fetch("middle")
    start_all(attention_copies(r, masks, grain))
    r.fetch("qkv", "probs", "heads", "a", "x")
    if not last:
        r.fetch("bias_before", "marks", "buckets", "small_before")
    r.need("grad", "ff_in", "gain_ff", "gain_attn")
    if not last:
        r.need("small_before")
        r.small[...] = r.small_before[...]
    wait_all(r.ff_sem, r.ff_gate_up, r.ff_down)
    r.need("middle")
    gain_total = jnp.zeros((1, width), f32)
    for part in chunks(rows, 256):
        grad = r.grad[part, :].astype(f32)
        rounded = grad.astype(bf16)
        ff_rows = r.ff_in[part, :]
        back = None
        middle = r.middle[part, :]
        total = middle
        for half in range(2):
            both = dot_nn(ff_rows, r.ff_gate_up[half])
            grad_hidden = dot_nt(rounded, r.ff_down[half])
            gate_act, up_act = both[:, :width], both[:, width:]
            mixed, slope = gelu_terms(gate_act)
            if half == 0:
                r.grad_gate_up[part, :width] = (grad_hidden * up_act * slope).astype(bf16)
                r.grad_gate_up[part, width:] = (grad_hidden * mixed).astype(bf16)
                pulled = r.grad_gate_up[part, :]
            else:
                r.pulled[:, :width] = (grad_hidden * up_act * slope).astype(bf16)
                r.pulled[:, width:] = (grad_hidden * mixed).astype(bf16)
                pulled = r.pulled[...]
            hidden = (mixed * up_act).astype(bf16)
            if half == 0:
                r.hidden[part, :] = hidden
            if last:
                total = total + dot_nn(hidden, r.ff_down[half])
            term = dot_nt(pulled, r.ff_gate_up[half])
            back = term if back is None else back + term
        if last:
            r.outputs[part, :] = total.astype(bf16)
        grad_mid, gain_part = norm_back(middle, r.gain_ff[...], back)
        gain_total += gain_part
        grad_mid = grad + grad_mid
        r.grad_mid[part, :] = grad_mid
        r.branch[part, :] = grad_mid.astype(bf16)
    if last:
        r.small[...] = jnp.zeros(r.small.shape, f32)
    put_row(r.small, 2 + layer_idx, gain_total)
    r.write("hidden", "grad_gate_up")
    if last:
        r.write("outputs")
    wait_all(r.attn_sem, r.attn_w)
    for part in chunks(rows, 256):
        r.grad_heads[part, :] = dot_nn(r.branch[part, :], r.attn_w[:, 3 * inner :]).astype(bf16)
    r.need("qkv", "probs", "heads", "a", "x")
    if not last:
        r.need("bias_before", "marks", "buckets")
    is_low = lane_low(slots)
    low, high = lane_halves()
    for start in range(0, inner, 128):
        at = slice(start, start + 128)
        bias_total = jnp.zeros((slots, 128), f32) if last else r.bias_before[:, at]
        for s in range(series):
            here = slice(s * slots, (s + 1) * slots)
            probs = r.probs[here, at]
            values = r.qkv[here, 2 * inner + start : 2 * inner + start + 128]
            grad_probs = dot_nt(values, pair_blocks(r.grad_heads[here, at], low, high))
            inner_sum = jnp.sum(probs * grad_probs, axis=0, keepdims=True)
            grad_scores = (probs * (grad_probs - inner_sum)).astype(bf16)
            r.grad_scores[here, at] = grad_scores
            bias_total = bias_total + grad_scores.astype(f32)
        r.bias_acc[:, at] = bias_total
    for s in range(series):
        here = slice(s * slots, (s + 1) * slots)
        for start in range(0, inner, 128):
            at = slice(start, start + 128)
            key_at = slice(inner + start, inner + start + 128)
            value_at = slice(2 * inner + start, 2 * inner + start + 128)
            grad_scores = r.grad_scores[here, at]
            r.grad_qkv[here, key_at] = dot_nn(
                grad_scores, pair_blocks(r.qkv[here, at], low, high)
            ).astype(bf16)
            r.grad_qkv[here, value_at] = dot_nn(
                r.probs[here, at].astype(bf16), pair_blocks(r.grad_heads[here, at], low, high)
            ).astype(bf16)
            r.grad_qkv[here, at] = own_blocks(dot_tn(grad_scores, r.qkv[here, key_at]), is_low)
    r.attn_grad[:, : 3 * inner] = dot_tn(r.a[...], r.grad_qkv[...])
    r.attn_grad[:, 3 * inner :] = dot_tn(r.branch[...], r.heads[...])
    scatter_pieces(r.attn_grad, r.attn_keep, r.attn_send, piece_masks, r.place[2])
    r.write("attn_send", "attn_keep")
    gain_total = jnp.zeros((1, width), f32)
    embed_total = jnp.zeros((1, width), f32)
    for part in chunks(rows, 256):
        grad_normed = dot_nt(r.grad_qkv[part, :], r.attn_w[:, : 3 * inner])
        grad_in, gain_part = norm_back(r.x[part, :], r.gain_attn[...], grad_normed)
        gain_total += gain_part
        grad_in = r.grad_mid[part, :] + grad_in
        if last:
            r.grad_next[part, :] = grad_in
            r.grad_next_low[part, :] = grad_in.astype(bf16)
        else:
            seen = r.marks[part, 0:1] == 1
            r.grad_next[part, :] = jnp.where(seen, grad_in, 0.0)
            embed_total += jnp.sum(jnp.where(seen, 0.0, grad_in), axis=0, keepdims=True)
    put_row(r.small, layer_idx, gain_total)
    r.write("grad_next")
    if last:
        r.write("grad_next_low", "bias_acc", "small")
    else:
        put_row(r.small, 4, embed_total)
        head_size = inner // heads
        for idx in range(r.table_rows.shape[0]):
            chosen = jnp.where(r.buckets[...] == idx, r.bias_acc[...], 0.0)
            r.table_rows[idx : idx + 1, :] = jnp.sum(chosen, axis=0, keepdims=True)
        lane = lax.broadcasted_iota(jnp.int32, (r.table_rows.shape[0], 128), 1)
        table = jnp.zeros(lane.shape, f32)
        for head in range(heads):
            cut = r.table_rows[:, head * head_size : (head + 1) * head_size]
            table = jnp.where(lane == head, jnp.sum(cut, axis=1, keepdims=True), table)
        r.small[small_rows(width) :, :] = table
        r.write("small")
    r.drain("hidden", "grad_gate_up", "attn_send", "attn_keep", "grad_next", "small")
    if last:
        r.drain("outputs", "grad_next_low", "bias_acc")


def small_rows(width):
    return -(-5 * width // 1024) * 8


def put_row(packed, which, row):
    lanes = row.shape[1] // 128
    for k in range(lanes):
        packed[which * lanes + k : which * lanes + k + 1, :] = row[:, k * 128 : (k + 1) * 128]


def scatter_pieces(whole, keep, send, masks, place):
    count = len(masks)
    grain = whole.shape[0] // count
    for idx, mask in enumerate(masks):
        target = keep if idx < count // 2 else send
        source = pl.ds(pl.multiple_of((place ^ mask) * grain, grain), grain)
        target[idx % (count // 2)] = whole[source, :].astype(bf16)


def weight_body(r, layer_idx, piece_masks):
    width = r.ff_in.shape[1]
    rows = r.ff_in.shape[0]
    r.fetch("peer_in", "peer_grad")
    copies = [
        pltpu.make_async_copy(
            own.at[layer_idx], r.ff_gate_up.at[:, pl.ds(k * width, width)], r.ff_sem
        )
        for k, own in enumerate((r.w_gate, r.w_up))
    ]
    copies.append(pltpu.make_async_copy(r.w_down.at[layer_idx], r.ff_down, r.ff_sem))
    start_all(copies)
    r.fetch("ff_in", "grad_gate_up", "hidden", "grad")
    r.need("peer_in", "peer_grad")
    wait_all(r.ff_sem, r.ff_gate_up, r.ff_down)
    for part in chunks(rows, 256):
        both = dot_nn(r.peer_in[part, :], r.ff_gate_up[...])
        grad_hidden = dot_nt(r.peer_grad[part, :], r.ff_down[...])
        gate_act, up_act = both[:, :width], both[:, width:]
        mixed, slope = gelu_terms(gate_act)
        r.peer_gate_up[part, :width] = (grad_hidden * up_act * slope).astype(bf16)
        r.peer_gate_up[part, width:] = (grad_hidden * mixed).astype(bf16)
        r.peer_hidden[part, :] = (mixed * up_act).astype(bf16)
    r.need("ff_in", "grad_gate_up", "hidden", "grad")
    r.ff_grad[:, : 2 * width] = dot_tn(r.ff_in[...], r.grad_gate_up[...]) + dot_tn(
        r.peer_in[...], r.peer_gate_up[...]
    )
    r.ff_grad[:, 2 * width :] = dot_tn(r.hidden[...], r.grad[...]) + dot_tn(
        r.peer_hidden[...], r.peer_grad[...]
    )
    scatter_pieces(r.ff_grad, r.ff_keep, r.ff_send, piece_masks, r.place[3])
    r.write("ff_send", "ff_keep")
    r.drain("ff_send", "ff_keep")


def finish(pieces, masks, layer_idx, place, shape, before=()):
    grain, width = pieces.shape[1], shape[-1]
    count = len(before)

    def kernel(place_ref, source, *refs):
        outs = refs[count : count + 3]
        held, stage, in_sem, out_sem = refs[count + 3 :]
        copy_in = pltpu.make_async_copy(source, held, in_sem)
        copy_in.start()
        copy_in.wait()
        for idx, mask in enumerate(masks):
            rows = pl.ds(pl.multiple_of((place_ref[3] ^ mask) * grain, grain), grain)
            for k, out in enumerate(outs):
                stage[k, idx] = held[idx, :, k * width : (k + 1) * width].astype(f32)
                pltpu.make_async_copy(stage.at[k, idx], out.at[layer_idx, rows], out_sem).start()
        pltpu.make_async_copy(stage, stage, out_sem).wait()

    return pl.pallas_call(
        kernel,
        name="layer_%d_ff_grads" % layer_idx,
        in_specs=[pl.BlockSpec(memory_space=pltpu.SMEM)]
        + [pl.BlockSpec(memory_space=pl.ANY)] * (1 + count),
        out_specs=[pl.BlockSpec(memory_space=pl.ANY)] * 3,
        out_shape=[jax.ShapeDtypeStruct(shape, f32)] * 3,
        input_output_aliases={2 + k: k for k in range(count)},
        scratch_shapes=[
            pltpu.VMEM(pieces.shape, bf16),
            pltpu.VMEM((3, len(masks), grain, width), f32),
            pltpu.SemaphoreType.DMA,
            pltpu.SemaphoreType.DMA,
        ],
        compiler_params=pltpu.CompilerParams(vmem_limit_bytes=vmem_bytes),
        cost_estimate=cost(3),
    )(place, pieces, *before)


def small_body(r):
    r.fetch("packed")
    r.need("packed")
    lanes = r.embed.shape[1] // 128
    for which in range(5):
        out, row = ((r.gain_attn, which), (r.gain_ff, which - 2), (r.embed, 0))[which // 2]
        for k in range(lanes):
            at = which * lanes + k
            out[row : row + 1, k * 128 : (k + 1) * 128] = r.packed[at : at + 1, :]
    r.table[...] = r.packed[small_rows(r.embed.shape[1]) :, : r.table.shape[1]]
    r.write("gain_attn", "gain_ff", "embed", "table")
    r.drain("gain_attn", "gain_ff", "embed", "table")


def order_masks(hops):
    masks = [0]
    for hop in reversed(hops):
        masks = masks + [mask ^ hop for mask in masks]
    return masks


def tie(value, *others):
    return lax.optimization_barrier((value, *others))[0]


def on_device(
    inputs,
    cotangent,
    attention_mask,
    patch_valid,
    buckets,
    mask_embed,
    w_query,
    w_key,
    w_value,
    w_output,
    w_gate,
    w_up,
    w_down,
    gain_attn,
    gain_ff,
    bias_table,
    dp_size,
):
    series, slots, width = inputs.shape
    heads = bias_table.shape[1]
    inner = w_query.shape[2]
    rows = series * slots
    sizes = (series, slots, inner)
    matrix = (rows, width)
    devices = 2 * dp_size
    dp_at = lax.axis_index("dp")
    device_at = 2 * dp_at + lax.axis_index("tensor")
    cotangent = cotangent.reshape(matrix)

    def swap(array, mask):
        return lax.ppermute(array, axes, [(n, n ^ mask) for n in range(devices)])

    def join(left, right):
        return jnp.concatenate([left, right], axis=0)

    bits = [1 << k for k in range(devices.bit_length() - 1)]

    attn_grain = max(16, width // devices)
    attn_count = width // attn_grain
    ff_grain = max(16, width // dp_size)
    ff_count = width // ff_grain
    quarter_at = lax.rem(dp_at, 4)
    place = jnp.stack(
        [
            device_at,
            quarter_at,
            device_at // (devices // attn_count),
            lax.rem(dp_at, ff_count),
        ]
    ).astype(jnp.int32)

    quarter = width // 4
    packed = jnp.concatenate([w_query, w_key, w_value, jnp.swapaxes(w_output, 1, 2)], axis=2)
    ff_blocks = jnp.concatenate(
        [
            lax.dynamic_slice_in_dim(tie(w, packed), quarter_at * quarter, quarter, axis=1)
            for w in (w_gate, w_up, w_down)
        ],
        axis=0,
    )
    ff_quarter = swap(ff_blocks, 1).reshape(3, 2, quarter, width)

    wide_buckets = jnp.tile(buckets.T, (1, heads))
    wide_table = jnp.repeat(bias_table, slots, axis=1)
    marks = jnp.stack([patch_valid.reshape(rows), attention_mask.reshape(rows)], axis=1)

    start = run(
        prepare_body,
        "prepare",
        dict(
            inputs=inputs.reshape(matrix),
            marks=marks,
            embed=mask_embed[None, :],
            gain=gain_attn[0:1],
            buckets=wide_buckets,
            table=wide_table,
        ),
        dict(
            x=(matrix, f32),
            a=(matrix, bf16),
            bias=((slots, heads * slots), f32),
            mask=((rows, 128), jnp.int32),
        ),
        {},
        micros=3,
    )

    own_rows = packed.shape[1]
    direct = own_rows % 16 == 0
    far = bits[2:]
    if direct:
        hops_0 = far[1:][::-1] + far[:1] + [1, 2]
        hops_1 = far[:1] + far[1:][::-1] + [1, 2]
        block_0, block_1 = packed[0], packed[1]
        for hop_0, hop_1 in zip(hops_0[:-2], hops_1[:-2]):
            got_0, got_1 = swap(block_0, hop_0), swap(block_1, hop_1)
            block_0 = join(block_0, got_0)
            block_1 = join(block_1, tie(got_1, block_0))
        got_0 = swap(block_0, 1)
        ff_0 = tie(ff_quarter[:, 0], block_0)
        got_ff_0 = swap(ff_0, 4)
        block_0 = join(block_0, tie(got_0, start.a, ff_0))
        block_1 = tie(block_1, block_0)
        got_1 = swap(block_1, 1)
        ff_0 = join(ff_0, tie(got_ff_0, block_0))
        ff_1 = tie(ff_quarter[:, 1], ff_0)
        ff_1 = join(ff_1, swap(ff_1, 4))
        block_1 = join(block_1, got_1)
        attn_pieces = [
            (block_0, swap(block_0, 2), order_masks(hops_0[::-1])),
            (block_1, swap(block_1, 2), order_masks(hops_1[::-1])),
        ]
    else:
        ff_0, ff_1 = (
            join(ff_quarter[:, layer_idx], swap(ff_quarter[:, layer_idx], 4))
            for layer_idx in range(2)
        )
        attn_pieces = []
        for layer_idx in range(2):
            whole = lax.all_gather(packed[layer_idx], axes, axis=0, tiled=True)
            attn_pieces.append((whole, whole, [0]))
    ff_pieces = [(ff_0, swap(ff_0, 2)), (ff_1, swap(ff_1, 2))]

    def attn_ins(layer_idx):
        near, far, masks = attn_pieces[layer_idx]
        return dict(attn_near=near, attn_far=far), masks

    def ff_ins(layer_idx):
        near, far = ff_pieces[layer_idx]
        return dict(w_gate=w_gate, w_up=w_up, w_down=w_down, ff_near=near, ff_far=far)

    attn_scratch = dict(
        attn_w=pltpu.VMEM((width, 4 * inner), bf16), attn_sem=pltpu.SemaphoreType.DMA
    )
    ff_scratch = dict(
        ff_gate_up=pltpu.VMEM((2, width, 2 * width), bf16),
        ff_down=pltpu.VMEM((2, width, width), bf16),
        ff_sem=pltpu.SemaphoreType.DMA,
    )
    grain = own_rows if direct else width
    attn_outs = dict(
        qkv=((rows, 3 * inner), bf16),
        probs=((rows, heads * slots), f32),
        heads=((rows, inner), bf16),
        middle=(matrix, f32),
        ff_in=(matrix, bf16),
    )

    pieces, masks = attn_ins(0)
    first = run(
        functools.partial(first_body, sizes=sizes, masks=masks, grain=grain),
        "layer_0_forward",
        dict(
            place=place,
            x=start.x,
            a=start.a,
            bias=start.bias,
            mask=start.mask,
            gain_ff=gain_ff[0:1],
            gain_next=gain_attn[1:2],
            **pieces,
            **ff_ins(0),
        ),
        dict(**attn_outs, x_next=(matrix, f32), a_next=(matrix, bf16)),
        dict(**attn_scratch, **ff_scratch),
        micros=9,
    )
    peer_cotangent = swap(tie(cotangent, first.ff_in), 1)
    pieces, masks = attn_ins(1)
    second = run(
        functools.partial(second_body, sizes=sizes, masks=masks, grain=grain),
        "layer_1_attention",
        dict(
            place=place,
            x=first.x_next,
            a=first.a_next,
            bias=start.bias,
            mask=start.mask,
            gain_ff=gain_ff[1:2],
            **pieces,
        ),
        attn_outs,
        attn_scratch,
        micros=6,
    )
    peer_in_1 = swap(second.ff_in, 1)

    attn_hops = [2, 1] + bits[2:]
    attn_low = devices // attn_count
    attn_split = [hop for hop in attn_hops if hop >= attn_low]
    attn_whole = [hop for hop in attn_hops if hop < attn_low]
    ff_hops = bits[1:]
    ff_split = [hop for hop in ff_hops if hop // 2 < ff_count]
    ff_whole = [hop for hop in ff_hops if hop // 2 >= ff_count]
    attn_masks = [mask // attn_low for mask in order_masks(attn_split)]
    ff_masks = [mask // 2 for mask in order_masks(ff_split)]
    attn_half = (attn_count // 2, attn_grain, 4 * inner)
    ff_half = (ff_count // 2, ff_grain, 3 * width)
    small_shape = (small_rows(width) + bias_table.shape[0], 128)

    def backward(layer_idx, kept, x, a, grad, extra_ins, extra_outs, extra_scratch, after=()):
        last = layer_idx == 1
        pieces, masks = attn_ins(layer_idx)
        return run(
            functools.partial(
                backward_body,
                sizes=sizes,
                masks=masks,
                grain=grain,
                layer_idx=layer_idx,
                last=last,
                piece_masks=attn_masks,
                heads=heads,
            ),
            "layer_%d_backward" % layer_idx,
            dict(
                place=place,
                x=x,
                a=a,
                grad=grad,
                gain_attn=gain_attn[layer_idx : layer_idx + 1],
                gain_ff=gain_ff[layer_idx : layer_idx + 1],
                qkv=kept.qkv,
                probs=kept.probs,
                heads=kept.heads,
                middle=kept.middle,
                ff_in=kept.ff_in,
                **pieces,
                **ff_ins(layer_idx),
                **extra_ins,
            ),
            dict(
                grad_next=(matrix, f32),
                hidden=(matrix, bf16),
                grad_gate_up=((rows, 2 * width), bf16),
                small=(small_shape, f32),
                attn_keep=(attn_half, bf16),
                attn_send=(attn_half, bf16),
                **extra_outs,
            ),
            dict(
                grad_mid=pltpu.VMEM(matrix, f32),
                branch=pltpu.VMEM(matrix, bf16),
                grad_heads=pltpu.VMEM((rows, inner), bf16),
                grad_qkv=pltpu.VMEM((rows, 3 * inner), bf16),
                grad_scores=pltpu.VMEM((rows, heads * slots), bf16),
                attn_grad=pltpu.VMEM((width, 4 * inner), f32),
                pulled=pltpu.VMEM((256, 2 * width), bf16),
                **attn_scratch,
                **ff_scratch,
                **extra_scratch,
            ),
            after=after,
            micros=14,
        )

    def weight_grads(layer_idx, kept, back, grad, peer_in, peer_grad, after=()):
        return run(
            functools.partial(weight_body, layer_idx=layer_idx, piece_masks=ff_masks),
            "layer_%d_weight_grads" % layer_idx,
            dict(
                place=place,
                ff_in=kept.ff_in,
                grad=grad,
                hidden=back.hidden,
                grad_gate_up=back.grad_gate_up,
                peer_in=peer_in,
                peer_grad=peer_grad,
                w_gate=w_gate,
                w_up=w_up,
                w_down=w_down,
            ),
            dict(ff_keep=(ff_half, bf16), ff_send=(ff_half, bf16)),
            dict(
                peer_gate_up=pltpu.VMEM((rows, 2 * width), bf16),
                peer_hidden=pltpu.VMEM(matrix, bf16),
                ff_grad=pltpu.VMEM((width, 3 * width), f32),
                ff_gate_up=pltpu.VMEM((width, 2 * width), bf16),
                ff_down=pltpu.VMEM((width, width), bf16),
                ff_sem=pltpu.SemaphoreType.DMA,
            ),
            after=after,
            micros=7,
        )

    def add(left, right):
        return (left.astype(f32) + right.astype(f32)).astype(bf16)

    def halving(keep, send, hops, out):
        for step, hop in enumerate(hops):
            got = yield swap(send, hop)
            if step + 1 < len(hops):
                cut = keep.shape[0] // 2
                send = add(keep[cut:], got[cut:])
                keep = add(keep[:cut], got[:cut])
                out["token"] = send
            else:
                out["token"] = keep = add(keep, got)
        out["piece"] = keep

    def summing(piece, hops, out):
        for hop in hops:
            got = yield swap(piece, hop)
            out["token"] = piece = add(piece, got) if piece.dtype == bf16 else piece + got
        out["piece"] = piece

    def sharing(piece, hops, out):
        for step, hop in enumerate(hops):
            got = yield swap(piece, hop)
            if step + 1 < len(hops):
                out["token"] = piece = join(piece, got)
            else:
                out["token"] = got
        out["near"], out["far"] = piece, got

    def attn_chain(part, out):
        yield from halving(part.attn_keep, part.attn_send, attn_split, out)
        yield from summing(out["piece"], attn_whole, out)
        piece = out["piece"][0]
        if own_rows < attn_grain:
            first_row = lax.rem(device_at, attn_low) * own_rows
            piece = lax.dynamic_slice_in_dim(piece, first_row, own_rows, axis=0)
        out["done"] = piece.astype(f32)

    def ff_chain(part, out):
        yield from halving(part.ff_keep, part.ff_send, ff_split, out)
        yield from summing(out["piece"], ff_whole, out)
        yield from sharing(out["piece"], ff_split[::-1], out)
        out["done"] = True

    class Chain:
        def __init__(self, steps, *args):
            self.out = {}
            self.steps = steps(*args, self.out)
            self.arriving = next(self.steps)

        def step(self, token):
            if self.arriving is not None:
                arrived = tie(self.arriving, token)
                self.arriving = None
                try:
                    self.arriving = self.steps.send(arrived)
                except StopIteration:
                    pass
                return self.out["token"]
            return token

    back_1 = backward(
        1,
        second,
        first.x_next,
        first.a_next,
        cotangent,
        {},
        dict(
            outputs=(matrix, bf16),
            grad_next_low=(matrix, bf16),
            bias_acc=((slots, heads * slots), f32),
        ),
        {},
        after=(peer_cotangent,),
    )
    peer_grad_0 = swap(back_1.grad_next_low, 1)
    part_1 = weight_grads(1, second, back_1, cotangent, peer_in_1, peer_cotangent)
    attn_1 = Chain(attn_chain, back_1)
    ff_1 = Chain(ff_chain, part_1)
    token = attn_1.step(part_1.ff_send)
    token = ff_1.step(token)
    peer_in_0 = swap(tie(first.ff_in, token), 1)
    back_0 = backward(
        0,
        first,
        start.x,
        start.a,
        back_1.grad_next,
        dict(
            bias_before=back_1.bias_acc,
            marks=marks,
            buckets=wide_buckets,
            small_before=back_1.small,
        ),
        {},
        dict(
            bias_acc=pltpu.VMEM((slots, heads * slots), f32),
            table_rows=pltpu.VMEM((bias_table.shape[0], heads * slots), f32),
        ),
        after=(token,),
    )
    attn_0 = Chain(attn_chain, back_0)
    token = ff_1.step(back_0.attn_send)
    token = attn_1.step(token)
    part_0 = weight_grads(
        0, first, back_0, back_1.grad_next_low, peer_in_0, peer_grad_0, after=(token,)
    )
    ff_0 = Chain(ff_chain, part_0)
    small = Chain(summing, back_0.small, attn_hops)
    token = attn_1.step(ff_1.step(part_0.ff_send))
    token = ff_0.step(attn_0.step(token))
    token = small.step(token)
    done_1 = None
    shape = (2, width, width)
    finish_masks = order_masks(ff_split)
    near_masks = [mask // 2 for mask in finish_masks[: ff_count // 2]]
    far_masks = [mask // 2 for mask in finish_masks[ff_count // 2 :]]
    chains = (ff_0, ff_1, attn_0, attn_1, small)
    while any(chain.arriving is not None for chain in chains):
        if "near" in ff_1.out and done_1 is None:
            pieces = join(ff_1.out["near"], ff_1.out["far"])
            done_1 = finish(tie(pieces, token), near_masks + far_masks, 1, place, shape)
            token = done_1[0]
        for chain in chains:
            token = chain.step(token)
    if done_1 is None:
        pieces = join(ff_1.out["near"], ff_1.out["far"])
        done_1 = finish(pieces, near_masks + far_masks, 1, place, shape)
    near_0 = finish(ff_0.out["near"], near_masks, 0, place, shape, done_1)
    done = finish(ff_0.out["far"], far_masks, 0, place, shape, near_0)
    sums = run(
        small_body,
        "small_sums",
        dict(packed=small.out["piece"]),
        dict(
            gain_attn=((2, width), f32),
            gain_ff=((2, width), f32),
            embed=((1, width), f32),
            table=(bias_table.shape, f32),
        ),
        {},
    )
    attn_0, attn_1 = attn_0.out["done"], attn_1.out["done"]
    attn_grads = jnp.stack([attn_0, attn_1])
    return (
        back_1.outputs.reshape(inputs.shape),
        back_0.grad_next.reshape(inputs.shape),
        attn_grads[:, :, :inner],
        attn_grads[:, :, inner : 2 * inner],
        attn_grads[:, :, 2 * inner : 3 * inner],
        jnp.swapaxes(attn_grads[:, :, 3 * inner :], 1, 2),
        *done,
        sums.gain_attn,
        sums.gain_ff,
        sums.table,
        sums.embed[0],
    )


def solution(mesh):
    placed = (
        P(("dp", "tensor"), None, None),
        P(("dp", "tensor"), None, None),
        P(("dp", "tensor"), None),
        P(("dp", "tensor"), None),
        P(),
        P(),
        P(None, ("dp", "tensor"), None),
        P(None, ("dp", "tensor"), None),
        P(None, ("dp", "tensor"), None),
        P(None, None, ("dp", "tensor")),
        P(None, None, "tensor"),
        P(None, None, "tensor"),
        P(None, "tensor", None),
        P(),
        P(),
        P(),
    )
    return jax.shard_map(
        functools.partial(on_device, dp_size=mesh.shape["dp"]),
        mesh=mesh,
        in_specs=placed,
        out_specs=(
            P(("dp", "tensor"), None, None),
            P(("dp", "tensor"), None, None),
            P(None, ("dp", "tensor"), None),
            P(None, ("dp", "tensor"), None),
            P(None, ("dp", "tensor"), None),
            P(None, None, ("dp", "tensor")),
            P(None, None, "tensor"),
            P(None, None, "tensor"),
            P(None, "tensor", None),
            P(),
            P(),
            P(),
            P(),
        ),
        check_vma=False,
    )
```

```python
import functools
import types

import jax
import jax.numpy as jnp
from jax import lax
from jax.experimental import pallas as pl
from jax.experimental.pallas import tpu as pltpu
from jax.sharding import PartitionSpec as P

norm_eps = 1e-06
masked_score = -1e30
bf16 = jnp.bfloat16
f32 = jnp.float32
axes = ("dp", "tensor")
vmem_bytes = 26 * 1024 * 1024
raw_names = ("attn_near", "attn_far", "ff_near", "ff_far", "w_gate", "w_up", "w_down")


def dot_nn(left, right):
    return lax.dot_general(left, right, (((1,), (0,)), ((), ())), preferred_element_type=f32)


def dot_nt(left, right):
    return lax.dot_general(left, right, (((1,), (1,)), ((), ())), preferred_element_type=f32)


def dot_tn(left, right):
    return lax.dot_general(left, right, (((0,), (0,)), ((), ())), preferred_element_type=f32)


def inverse_rms(values):
    return lax.rsqrt(jnp.mean(values * values, axis=-1, keepdims=True) + norm_eps)


def norm_back(values, gain, grad_out):
    scale = inverse_rms(values)
    pulled = grad_out * gain
    mean_part = jnp.mean(pulled * values, axis=-1, keepdims=True)
    grad_in = scale * pulled - values * (scale * scale * scale) * mean_part
    return grad_in, jnp.sum(grad_out * values * scale, axis=0, keepdims=True)


def gelu_terms(gate_act):
    square = gate_act * gate_act
    bent = jnp.tanh(0.7978845608028654 * gate_act * (1.0 + 0.044715 * square))
    half = 0.5 * (1.0 + bent)
    slope = half + 0.5 * gate_act * (1.0 - bent * bent) * (
        0.7978845608028654 * (1.0 + 3.0 * 0.044715 * square)
    )
    return gate_act * half, slope


def cost(micros):
    return pl.CostEstimate(flops=int(micros * 1.15e9), bytes_accessed=0, transcendentals=0)


def run(body, name, ins, outs, scratch, after=(), micros=1):
    in_names, out_names, scratch_names = list(ins), list(outs), list(scratch)
    direct = {n for n in in_names if n == "place" or n in raw_names or isinstance(ins[n], Kept)}
    staged = [n for n in in_names if n not in direct]
    copied = [n for n in out_names if not isinstance(outs[n], Kept)]
    in_sems = {n: i for i, n in enumerate(staged)}
    out_sems = {n: i for i, n in enumerate(copied)}

    def kernel(*refs):
        refs = list(refs)
        sources = dict(zip(in_names, refs))
        refs = refs[len(in_names) + len(after) :]
        targets = dict(zip(out_names, refs))
        refs = refs[len(out_names) :]
        space = dict(zip(scratch_names, refs))
        refs = refs[len(scratch_names) :]
        buffers = dict(zip(staged + copied, refs))
        sems_in, sems_out = refs[len(staged) + len(copied) :]
        kept = {n: ref for n, ref in targets.items() if n not in out_sems}
        r = types.SimpleNamespace(**space, **buffers, **kept)
        for n in direct:
            setattr(r, n, sources[n])

        def copy_in(n):
            return pltpu.make_async_copy(sources[n], buffers[n], sems_in.at[in_sems[n]])

        def copy_out(n):
            return pltpu.make_async_copy(buffers[n], targets[n], sems_out.at[out_sems[n]])

        r.fetch = lambda *names: [copy_in(n).start() for n in names if n in in_sems]
        r.need = lambda *names: [copy_in(n).wait() for n in names if n in in_sems]
        r.write = lambda *names: [copy_out(n).start() for n in names if n in out_sems]
        r.drain = lambda *names: [copy_out(n).wait() for n in names if n in out_sems]
        body(r)

    def in_space(n):
        if n == "place":
            return pltpu.SMEM
        return pltpu.VMEM if isinstance(ins[n], Kept) else pl.ANY

    results = pl.pallas_call(
        kernel,
        name=name,
        in_specs=[pl.BlockSpec(memory_space=in_space(n)) for n in in_names]
        + [pl.BlockSpec(memory_space=pl.ANY) for _ in after],
        out_specs=[
            pl.BlockSpec(memory_space=pltpu.VMEM if isinstance(out, Kept) else pl.ANY)
            for out in outs.values()
        ],
        out_shape=[
            pltpu.VMEM(*out.what) if isinstance(out, Kept) else jax.ShapeDtypeStruct(*out)
            for out in outs.values()
        ],
        scratch_shapes=list(scratch.values())
        + [pltpu.VMEM(ins[n].shape, ins[n].dtype) for n in staged]
        + [pltpu.VMEM(*outs[n]) for n in copied]
        + [
            pltpu.SemaphoreType.DMA((max(1, len(staged)),)),
            pltpu.SemaphoreType.DMA((max(1, len(copied)),)),
        ],
        compiler_params=pltpu.CompilerParams(vmem_limit_bytes=vmem_bytes),
        cost_estimate=cost(micros),
    )(
        *[
            pltpu.with_memory_space_constraint(value.what, pltpu.VMEM)
            if isinstance(value, Kept)
            else value
            for value in ins.values()
        ],
        *after,
    )
    return types.SimpleNamespace(**dict(zip(outs, results)))


class Kept:
    def __init__(self, *what):
        self.what = what[0] if len(what) == 1 else what


def keep_all(names):
    return {name: Kept(value) for name, value in names.items()}


def chunks(extent, size):
    size = min(size, extent)
    return [slice(start, start + size) for start in range(0, extent, size)]


def attention_copies(r, masks, rows):
    copies = []
    for idx, mask in enumerate(masks):
        half, at = divmod(idx, max(1, len(masks) // 2))
        source = (r.attn_near if half == 0 else r.attn_far).at[pl.ds(at * rows, rows)]
        place = (r.place[0] ^ mask) * rows if len(masks) > 1 else 0
        target = r.attn_w.at[pl.ds(pl.multiple_of(place, rows), rows)]
        copies.append(pltpu.make_async_copy(source, target, r.attn_sem))
    return copies


def ff_copies(r, layer_idx):
    width = r.ff_down.shape[-1]
    copies = []
    for k, own in enumerate((r.w_gate, r.w_up)):
        target = r.ff_gate_up.at[0, :, pl.ds(k * width, width)]
        copies.append(pltpu.make_async_copy(own.at[layer_idx], target, r.ff_sem))
    copies.append(pltpu.make_async_copy(r.w_down.at[layer_idx], r.ff_down.at[0], r.ff_sem))
    part = r.ff_near.shape[1]
    for source, base in ((r.ff_near, 0), (r.ff_far, 1)):
        for m in range(2):
            rows = pl.ds(pl.multiple_of((r.place[1] ^ (2 * m + base)) * part, part), part)
            for k in range(2):
                target = r.ff_gate_up.at[1, rows, pl.ds(k * width, width)]
                copies.append(pltpu.make_async_copy(source.at[3 * m + k], target, r.ff_sem))
            copies.append(
                pltpu.make_async_copy(source.at[3 * m + 2], r.ff_down.at[1, rows], r.ff_sem)
            )
    return copies


def start_all(copies):
    for copy in copies:
        copy.start()


def wait_all(sem, *buffers):
    for whole in buffers:
        pltpu.make_async_copy(whole, whole, sem).wait()


def lane_low(rows):
    return lax.broadcasted_iota(jnp.int32, (rows, 128), 1) < 64


def lane_halves():
    low = lane_low(1).astype(f32)
    return low.astype(bf16), (1.0 - low).astype(bf16)


def pair_blocks(rows, low, high):
    return jnp.concatenate([rows * low, rows * high], axis=0)


def own_blocks(both, is_low):
    half = both.shape[0] // 2
    return jnp.where(is_low, both[:half], both[half:]).astype(bf16)


def attention_forward(r, x_ref, a_ref, sizes, layer_idx):
    series, slots, inner = sizes
    rows = series * slots
    for part in chunks(rows, 256):
        r.qkv[part, :] = dot_nn(a_ref[part, :], r.attn_w[:, : 3 * inner]).astype(bf16)
    r.write("qkv")
    is_low = lane_low(slots)
    low, high = lane_halves()
    for s in range(series):
        here = slice(s * slots, (s + 1) * slots)
        keep = r.mask[here, :] == 1
        for start in range(0, inner, 128):
            at = slice(start, start + 128)
            query = r.qkv[here, at]
            keys = r.qkv[here, inner + start : inner + start + 128]
            scores = dot_nt(keys, pair_blocks(query, low, high)) + r.bias[:, at]
            scores = jnp.where(keep, scores, masked_score)
            exps = jnp.exp(scores - jnp.max(scores, axis=0, keepdims=True))
            r.probs[here, at] = exps / jnp.sum(exps, axis=0, keepdims=True)
    r.write("probs")
    for s in range(series):
        here = slice(s * slots, (s + 1) * slots)
        for start in range(0, inner, 128):
            at = slice(start, start + 128)
            values = r.qkv[here, 2 * inner + start : 2 * inner + start + 128]
            both = dot_tn(r.probs[here, at].astype(bf16), values)
            r.heads[here, at] = own_blocks(both, is_low)
    r.write("heads")
    gain = r.gain_ff[layer_idx : layer_idx + 1, :]
    for part in chunks(rows, 256):
        middle = x_ref[part, :] + dot_nt(r.heads[part, :], r.attn_w[:, 3 * inner :])
        r.middle[part, :] = middle
        r.ff_in[part, :] = (middle * inverse_rms(middle) * gain).astype(bf16)
    r.write("middle", "ff_in")


attn_out_names = ("qkv", "probs", "heads", "middle", "ff_in")


def prepare_body(r):
    r.fetch("inputs", "marks", "embed", "gain_attn", "buckets", "table")
    r.need("inputs", "marks", "embed", "gain_attn", "buckets", "table")
    x = jnp.where(r.marks[:, 0:1] == 1, r.inputs[...].astype(f32), r.embed[...])
    r.x[...] = x
    r.a[...] = (x * inverse_rms(x) * r.gain_attn[0:1, :]).astype(bf16)
    buckets = r.buckets[...]
    bias = jnp.zeros(buckets.shape, f32)
    for idx in range(r.table.shape[0]):
        bias = jnp.where(buckets == idx, r.table[idx : idx + 1, :], bias)
    r.bias[...] = bias
    r.mask[...] = jnp.broadcast_to(r.marks[:, 1:2], r.mask.shape)
    r.write("x", "a", "bias", "mask")
    r.drain("x", "a", "bias", "mask")


def first_body(r, sizes, masks, grain):
    r.fetch("a")
    start_all(attention_copies(r, masks, grain))
    r.fetch("bias", "mask", "x", "gain_ff", "gain_attn")
    start_all(ff_copies(r, 0))
    r.need("a")
    wait_all(r.attn_sem, r.attn_w)
    r.need("bias", "mask", "x", "gain_ff", "gain_attn")
    attention_forward(r, r.x, r.a, sizes, 0)
    wait_all(r.ff_sem, r.ff_gate_up, r.ff_down)
    width = r.x.shape[1]
    for part in chunks(r.x.shape[0], 256):
        x_next = r.middle[part, :]
        for half in range(2):
            both = dot_nn(r.ff_in[part, :], r.ff_gate_up[half])
            hidden = (gelu_terms(both[:, :width])[0] * both[:, width:]).astype(bf16)
            x_next = x_next + dot_nn(hidden, r.ff_down[half])
        r.x_next[part, :] = x_next
        r.a_next[part, :] = (x_next * inverse_rms(x_next) * r.gain_attn[1:2, :]).astype(bf16)
    r.write("x_next", "a_next")
    r.drain(*attn_out_names, "x_next", "a_next")


def second_body(r, sizes, masks, grain):
    r.fetch("a")
    start_all(attention_copies(r, masks, grain))
    r.fetch("bias", "mask", "x", "gain_ff")
    r.need("a")
    wait_all(r.attn_sem, r.attn_w)
    r.need("bias", "mask", "x", "gain_ff")
    attention_forward(r, r.x, r.a, sizes, 1)
    r.drain(*attn_out_names)


def backward_body(r, sizes, layer_idx, last, piece_masks, heads):
    series, slots, inner = sizes
    rows = series * slots
    width = r.x.shape[1]
    r.fetch("grad", "ff_in", "gain_ff", "gain_attn")
    if last:
        start_all(ff_copies(r, layer_idx))
    r.fetch("middle")
    r.fetch("qkv", "probs", "heads", "a", "x")
    if not last:
        r.fetch("bias_before", "marks", "buckets", "small_before")
    r.need("grad", "ff_in", "gain_ff", "gain_attn")
    if not last:
        r.need("small_before")
        r.small[...] = r.small_before[...]
    if last:
        wait_all(r.ff_sem, r.ff_gate_up, r.ff_down)
    r.need("middle")
    gain_ff = r.gain_ff[layer_idx : layer_idx + 1, :]
    gain_attn = r.gain_attn[layer_idx : layer_idx + 1, :]
    gain_total = jnp.zeros((1, width), f32)
    for part in chunks(rows, 256):
        grad = r.grad[part, :].astype(f32)
        rounded = grad.astype(bf16)
        ff_rows = r.ff_in[part, :]
        back = None
        middle = r.middle[part, :]
        total = middle
        for half in range(2):
            both = dot_nn(ff_rows, r.ff_gate_up[half])
            grad_hidden = dot_nt(rounded, r.ff_down[half])
            gate_act, up_act = both[:, :width], both[:, width:]
            mixed, slope = gelu_terms(gate_act)
            if half == 0:
                r.grad_gate_up[part, :width] = (grad_hidden * up_act * slope).astype(bf16)
                r.grad_gate_up[part, width:] = (grad_hidden * mixed).astype(bf16)
                pulled = r.grad_gate_up[part, :]
            else:
                r.pulled[:, :width] = (grad_hidden * up_act * slope).astype(bf16)
                r.pulled[:, width:] = (grad_hidden * mixed).astype(bf16)
                pulled = r.pulled[...]
            hidden = (mixed * up_act).astype(bf16)
            if half == 0:
                r.hidden[part, :] = hidden
            if last:
                total = total + dot_nn(hidden, r.ff_down[half])
            term = dot_nt(pulled, r.ff_gate_up[half])
            back = term if back is None else back + term
        if last:
            r.outputs[part, :] = total.astype(bf16)
        grad_mid, gain_part = norm_back(middle, gain_ff, back)
        gain_total += gain_part
        grad_mid = grad + grad_mid
        r.grad_mid[part, :] = grad_mid
        r.branch[part, :] = grad_mid.astype(bf16)
    if last:
        r.small[...] = jnp.zeros(r.small.shape, f32)
    put_row(r.small, 2 + layer_idx, gain_total)
    r.write("hidden", "grad_gate_up")
    if last:
        r.write("outputs")
    for part in chunks(rows, 256):
        r.grad_heads[part, :] = dot_nn(r.branch[part, :], r.attn_w[:, 3 * inner :]).astype(bf16)
    r.need("qkv", "probs", "heads", "a", "x")
    if not last:
        r.need("bias_before", "marks", "buckets")
    is_low = lane_low(slots)
    low, high = lane_halves()
    for start in range(0, inner, 128):
        at = slice(start, start + 128)
        bias_total = jnp.zeros((slots, 128), f32) if last else r.bias_before[:, at]
        for s in range(series):
            here = slice(s * slots, (s + 1) * slots)
            probs = r.probs[here, at]
            values = r.qkv[here, 2 * inner + start : 2 * inner + start + 128]
            grad_probs = dot_nt(values, pair_blocks(r.grad_heads[here, at], low, high))
            inner_sum = jnp.sum(probs * grad_probs, axis=0, keepdims=True)
            grad_scores = (probs * (grad_probs - inner_sum)).astype(bf16)
            r.grad_scores[here, at] = grad_scores
            bias_total = bias_total + grad_scores.astype(f32)
        r.bias_acc[:, at] = bias_total
    for s in range(series):
        here = slice(s * slots, (s + 1) * slots)
        for start in range(0, inner, 128):
            at = slice(start, start + 128)
            key_at = slice(inner + start, inner + start + 128)
            value_at = slice(2 * inner + start, 2 * inner + start + 128)
            grad_scores = r.grad_scores[here, at]
            r.grad_qkv[here, key_at] = dot_nn(
                grad_scores, pair_blocks(r.qkv[here, at], low, high)
            ).astype(bf16)
            r.grad_qkv[here, value_at] = dot_nn(
                r.probs[here, at].astype(bf16), pair_blocks(r.grad_heads[here, at], low, high)
            ).astype(bf16)
            r.grad_qkv[here, at] = own_blocks(dot_tn(grad_scores, r.qkv[here, key_at]), is_low)
    r.attn_grad[:, : 3 * inner] = dot_tn(r.a[...], r.grad_qkv[...])
    r.attn_grad[:, 3 * inner :] = dot_tn(r.branch[...], r.heads[...])
    scatter_pieces(r.attn_grad, r.attn_keep, r.attn_send, piece_masks, r.place[2])
    r.write("attn_send", "attn_keep")
    gain_total = jnp.zeros((1, width), f32)
    embed_total = jnp.zeros((1, width), f32)
    for part in chunks(rows, 256):
        grad_normed = dot_nt(r.grad_qkv[part, :], r.attn_w[:, : 3 * inner])
        grad_in, gain_part = norm_back(r.x[part, :], gain_attn, grad_normed)
        gain_total += gain_part
        grad_in = r.grad_mid[part, :] + grad_in
        if last:
            r.grad_next[part, :] = grad_in
            r.grad_next_low[part, :] = grad_in.astype(bf16)
        else:
            seen = r.marks[part, 0:1] == 1
            r.grad_next[part, :] = jnp.where(seen, grad_in, 0.0)
            embed_total += jnp.sum(jnp.where(seen, 0.0, grad_in), axis=0, keepdims=True)
    put_row(r.small, layer_idx, gain_total)
    r.write("grad_next")
    if last:
        r.write("grad_next_low", "bias_acc", "small")
    else:
        put_row(r.small, 4, embed_total)
        head_size = inner // heads
        for idx in range(r.table_rows.shape[0]):
            chosen = jnp.where(r.buckets[...] == idx, r.bias_acc[...], 0.0)
            r.table_rows[idx : idx + 1, :] = jnp.sum(chosen, axis=0, keepdims=True)
        lane = lax.broadcasted_iota(jnp.int32, (r.table_rows.shape[0], 128), 1)
        table = jnp.zeros(lane.shape, f32)
        for head in range(heads):
            cut = r.table_rows[:, head * head_size : (head + 1) * head_size]
            table = jnp.where(lane == head, jnp.sum(cut, axis=1, keepdims=True), table)
        r.small[small_rows(width) :, :] = table
        r.write("small")
    r.drain("hidden", "grad_gate_up", "attn_send", "attn_keep", "grad_next", "small")
    if last:
        r.drain("outputs", "grad_next_low", "bias_acc")


def small_rows(width):
    return -(-5 * width // 1024) * 8


def put_row(packed, which, row):
    lanes = row.shape[1] // 128
    for k in range(lanes):
        packed[which * lanes + k : which * lanes + k + 1, :] = row[:, k * 128 : (k + 1) * 128]


def scatter_pieces(whole, keep, send, masks, place):
    count = len(masks)
    grain = whole.shape[0] // count
    for idx, mask in enumerate(masks):
        target = keep if idx < count // 2 else send
        source = pl.ds(pl.multiple_of((place ^ mask) * grain, grain), grain)
        target[idx % (count // 2)] = whole[source, :].astype(bf16)


def weight_body(r, piece_masks):
    width = r.ff_in.shape[1]
    rows = r.ff_in.shape[0]
    r.fetch("peer_in", "peer_grad")
    r.fetch("ff_in", "grad_gate_up", "hidden", "grad")
    r.need("peer_in", "peer_grad")
    for part in chunks(rows, 256):
        both = dot_nn(r.peer_in[part, :], r.ff_gate_up[0])
        grad_hidden = dot_nt(r.peer_grad[part, :], r.ff_down[0])
        gate_act, up_act = both[:, :width], both[:, width:]
        mixed, slope = gelu_terms(gate_act)
        r.peer_gate_up[part, :width] = (grad_hidden * up_act * slope).astype(bf16)
        r.peer_gate_up[part, width:] = (grad_hidden * mixed).astype(bf16)
        r.peer_hidden[part, :] = (mixed * up_act).astype(bf16)
    r.need("ff_in", "grad_gate_up", "hidden", "grad")
    r.ff_grad[:, : 2 * width] = dot_tn(r.ff_in[...], r.grad_gate_up[...]) + dot_tn(
        r.peer_in[...], r.peer_gate_up[...]
    )
    r.ff_grad[:, 2 * width :] = dot_tn(r.hidden[...], r.grad[...]) + dot_tn(
        r.peer_hidden[...], r.peer_grad[...]
    )
    scatter_pieces(r.ff_grad, r.ff_keep, r.ff_send, piece_masks, r.place[3])
    r.write("ff_send", "ff_keep")
    r.drain("ff_send", "ff_keep")


def finish(pieces, masks, layer_idx, place, shape, before=()):
    grain, width = pieces.shape[1], shape[-1]
    count = len(before)

    def kernel(place_ref, source, *refs):
        outs = refs[count : count + 3]
        stage, out_sem = refs[count + 3 :]
        for idx, mask in enumerate(masks):
            rows = pl.ds(pl.multiple_of((place_ref[3] ^ mask) * grain, grain), grain)
            for k, out in enumerate(outs):
                stage[k, idx] = source[idx, :, k * width : (k + 1) * width].astype(f32)
                pltpu.make_async_copy(stage.at[k, idx], out.at[layer_idx, rows], out_sem).start()
        pltpu.make_async_copy(stage, stage, out_sem).wait()

    return pl.pallas_call(
        kernel,
        name="layer_%d_ff_grads" % layer_idx,
        in_specs=[
            pl.BlockSpec(memory_space=pltpu.SMEM),
            pl.BlockSpec(memory_space=pltpu.VMEM),
        ]
        + [pl.BlockSpec(memory_space=pl.ANY)] * count,
        out_specs=[pl.BlockSpec(memory_space=pl.ANY)] * 3,
        out_shape=[jax.ShapeDtypeStruct(shape, f32)] * 3,
        input_output_aliases={2 + k: k for k in range(count)},
        scratch_shapes=[
            pltpu.VMEM((3, len(masks), grain, width), f32),
            pltpu.SemaphoreType.DMA,
        ],
        compiler_params=pltpu.CompilerParams(vmem_limit_bytes=vmem_bytes),
        cost_estimate=cost(3),
    )(place, pltpu.with_memory_space_constraint(pieces, pltpu.VMEM), *before)


def small_body(r):
    r.fetch("packed")
    r.need("packed")
    lanes = r.embed.shape[1] // 128
    for which in range(5):
        out, row = ((r.gain_attn, which), (r.gain_ff, which - 2), (r.embed, 0))[which // 2]
        for k in range(lanes):
            at = which * lanes + k
            out[row : row + 1, k * 128 : (k + 1) * 128] = r.packed[at : at + 1, :]
    r.table[...] = r.packed[small_rows(r.embed.shape[1]) :, : r.table.shape[1]]
    r.write("gain_attn", "gain_ff", "embed", "table")
    r.drain("gain_attn", "gain_ff", "embed", "table")


def order_masks(hops):
    masks = [0]
    for hop in reversed(hops):
        masks = masks + [mask ^ hop for mask in masks]
    return masks


def tie(value, *others):
    return lax.optimization_barrier((value, *others))[0]


def on_device(
    inputs,
    cotangent,
    attention_mask,
    patch_valid,
    buckets,
    mask_embed,
    w_query,
    w_key,
    w_value,
    w_output,
    w_gate,
    w_up,
    w_down,
    gain_attn,
    gain_ff,
    bias_table,
    dp_size,
):
    series, slots, width = inputs.shape
    heads = bias_table.shape[1]
    inner = w_query.shape[2]
    rows = series * slots
    sizes = (series, slots, inner)
    matrix = (rows, width)
    devices = 2 * dp_size
    dp_at = lax.axis_index("dp")
    device_at = 2 * dp_at + lax.axis_index("tensor")
    cotangent = cotangent.reshape(matrix)

    def swap(array, mask):
        return lax.ppermute(array, axes, [(n, n ^ mask) for n in range(devices)])

    def join(left, right):
        return jnp.concatenate([left, right], axis=0)

    bits = [1 << k for k in range(devices.bit_length() - 1)]

    attn_grain = max(16, width // devices)
    attn_count = width // attn_grain
    ff_grain = max(16, width // dp_size)
    ff_count = width // ff_grain
    quarter_at = lax.rem(dp_at, 4)
    place = jnp.stack(
        [
            device_at,
            quarter_at,
            device_at // (devices // attn_count),
            lax.rem(dp_at, ff_count),
        ]
    ).astype(jnp.int32)

    quarter = width // 4
    packed = jnp.concatenate([w_query, w_key, w_value, jnp.swapaxes(w_output, 1, 2)], axis=2)
    ff_blocks = jnp.concatenate(
        [
            lax.dynamic_slice_in_dim(tie(w, packed), quarter_at * quarter, quarter, axis=1)
            for w in (w_gate, w_up, w_down)
        ],
        axis=0,
    )
    ff_quarter = swap(ff_blocks, 1).reshape(3, 2, quarter, width)

    def prepare(token):
        table, marked, kept, near = (
            tie(array, token) for array in (bias_table, patch_valid, attention_mask, buckets)
        )
        wide_buckets = jnp.tile(near.T, (1, heads))
        wide_table = jnp.repeat(table, slots, axis=1)
        marks = jnp.stack([marked.reshape(rows), kept.reshape(rows)], axis=1)
        result = run(
            prepare_body,
            "prepare",
            dict(
                inputs=inputs.reshape(matrix),
                marks=marks,
                embed=mask_embed[None, :],
                gain_attn=gain_attn,
                buckets=wide_buckets,
                table=wide_table,
            ),
            dict(
                x=Kept(matrix, f32),
                a=Kept(matrix, bf16),
                bias=Kept((slots, heads * slots), f32),
                mask=Kept((rows, 128), jnp.int32),
            ),
            {},
            micros=3,
        )
        return result, wide_buckets, marks

    own_rows = packed.shape[1]
    direct = own_rows % 16 == 0
    far = bits[2:]
    if direct:
        hops_0 = far[1:][::-1] + far[:1] + [1, 2]
        hops_1 = far[:1] + far[1:][::-1] + [1, 2]
        block_0, block_1 = packed[0], packed[1]
        for hop_0, hop_1 in zip(hops_0[:-2], hops_1[:-2]):
            got_0, got_1 = swap(block_0, hop_0), swap(block_1, hop_1)
            block_0 = join(block_0, got_0)
            block_1 = join(block_1, tie(got_1, block_0))
            if hop_0 == hops_0[0]:
                start, wide_buckets, marks = prepare(block_1)
        got_0 = swap(block_0, 1)
        ff_0 = tie(ff_quarter[:, 0], block_0)
        got_ff_0 = swap(ff_0, 4)
        block_0 = join(block_0, tie(got_0, start.a, ff_0))
        block_1 = tie(block_1, block_0)
        got_1 = swap(block_1, 1)
        ff_0 = join(ff_0, tie(got_ff_0, block_0))
        got_ff_1 = swap(tie(ff_quarter[:, 1], ff_0), 4)
        attn_pieces = [(block_0, swap(block_0, 2), order_masks(hops_0[::-1]))]
        peer_cotangent = swap(tie(cotangent, got_1), 1)
    else:
        ff_0 = join(ff_quarter[:, 0], swap(ff_quarter[:, 0], 4))
        start, wide_buckets, marks = prepare(packed)
        whole = lax.all_gather(packed[0], axes, axis=0, tiled=True)
        attn_pieces = [(whole, whole, [0])]
        peer_cotangent = swap(cotangent, 1)
    ff_pieces = [(ff_0, swap(ff_0, 2))]

    def attn_ins(layer_idx):
        near, far, masks = attn_pieces[layer_idx]
        return dict(attn_near=Kept(near), attn_far=Kept(far)), masks

    def ff_ins(layer_idx):
        near, far = ff_pieces[layer_idx]
        return dict(w_gate=w_gate, w_up=w_up, w_down=w_down, ff_near=Kept(near), ff_far=Kept(far))

    attn_scratch = dict(attn_sem=pltpu.SemaphoreType.DMA)
    ff_scratch = dict(ff_sem=pltpu.SemaphoreType.DMA)
    ff_outs = dict(
        ff_gate_up=Kept((2, width, 2 * width), bf16), ff_down=Kept((2, width, width), bf16)
    )
    grain = own_rows if direct else width
    attn_outs = dict(
        attn_w=Kept((width, 4 * inner), bf16),
        qkv=Kept((rows, 3 * inner), bf16),
        probs=Kept((rows, heads * slots), f32),
        heads=Kept((rows, inner), bf16),
        middle=Kept(matrix, f32),
        ff_in=Kept(matrix, bf16),
    )

    pieces, masks = attn_ins(0)
    first = run(
        functools.partial(first_body, sizes=sizes, masks=masks, grain=grain),
        "layer_0_forward",
        dict(
            place=place,
            x=Kept(start.x),
            a=Kept(start.a),
            bias=Kept(start.bias),
            mask=Kept(start.mask),
            gain_ff=gain_ff,
            gain_attn=gain_attn,
            **pieces,
            **ff_ins(0),
        ),
        dict(**attn_outs, **ff_outs, x_next=Kept(matrix, f32), a_next=Kept(matrix, bf16)),
        dict(**attn_scratch, **ff_scratch),
        micros=9,
    )
    peer_in_0 = swap(first.ff_in, 1)
    if direct:
        block_1 = join(block_1, tie(got_1, first.ff_in))
        attn_pieces.append((block_1, swap(block_1, 2), order_masks(hops_1[::-1])))
        ff_1 = tie(ff_quarter[:, 1], ff_0)
        ff_1 = join(ff_1, tie(got_ff_1, first.ff_in))
    else:
        whole = lax.all_gather(packed[1], axes, axis=0, tiled=True)
        attn_pieces.append((whole, whole, [0]))
        ff_1 = join(ff_quarter[:, 1], swap(ff_quarter[:, 1], 4))
    ff_pieces.append((ff_1, swap(ff_1, 2)))
    pieces, masks = attn_ins(1)
    second = run(
        functools.partial(second_body, sizes=sizes, masks=masks, grain=grain),
        "layer_1_attention",
        dict(
            place=place,
            x=Kept(first.x_next),
            a=Kept(first.a_next),
            bias=Kept(start.bias),
            mask=Kept(start.mask),
            gain_ff=gain_ff,
            **pieces,
        ),
        attn_outs,
        attn_scratch,
        micros=6,
    )
    peer_in_1 = swap(second.ff_in, 1)

    attn_hops = [2, 1] + bits[2:]
    attn_low = devices // attn_count
    attn_split = [hop for hop in attn_hops if hop >= attn_low]
    attn_whole = [hop for hop in attn_hops if hop < attn_low]
    ff_hops = bits[1:]
    ff_split = [hop for hop in ff_hops if hop // 2 < ff_count]
    ff_whole = [hop for hop in ff_hops if hop // 2 >= ff_count]
    attn_masks = [mask // attn_low for mask in order_masks(attn_split)]
    ff_masks = [mask // 2 for mask in order_masks(ff_split)]
    attn_half = (attn_count // 2, attn_grain, 4 * inner)
    ff_half = (ff_count // 2, ff_grain, 3 * width)
    small_shape = (small_rows(width) + bias_table.shape[0], 128)

    def backward(layer_idx, kept, x, a, grad, extra_ins, extra_outs, extra_scratch, after=()):
        last = layer_idx == 1
        ff_given = ff_ins(1) if last else keep_all(
            dict(ff_gate_up=kept.ff_gate_up, ff_down=kept.ff_down)
        )
        return run(
            functools.partial(
                backward_body,
                sizes=sizes,
                layer_idx=layer_idx,
                last=last,
                piece_masks=attn_masks,
                heads=heads,
            ),
            "layer_%d_backward" % layer_idx,
            dict(
                place=place,
                x=Kept(x),
                a=Kept(a),
                grad=grad,
                gain_attn=gain_attn,
                gain_ff=gain_ff,
                attn_w=Kept(kept.attn_w),
                qkv=Kept(kept.qkv),
                probs=Kept(kept.probs),
                heads=Kept(kept.heads),
                middle=Kept(kept.middle),
                ff_in=Kept(kept.ff_in),
                **ff_given,
                **extra_ins,
            ),
            dict(
                hidden=Kept(matrix, bf16),
                grad_gate_up=Kept((rows, 2 * width), bf16),
                small=Kept(small_shape, f32),
                attn_keep=Kept(attn_half, bf16),
                attn_send=Kept(attn_half, bf16),
                **(ff_outs if last else {}),
                **extra_outs,
            ),
            dict(
                grad_mid=pltpu.VMEM(matrix, f32),
                branch=pltpu.VMEM(matrix, bf16),
                grad_heads=pltpu.VMEM((rows, inner), bf16),
                grad_qkv=pltpu.VMEM((rows, 3 * inner), bf16),
                grad_scores=pltpu.VMEM((rows, heads * slots), bf16),
                attn_grad=pltpu.VMEM((width, 4 * inner), f32),
                pulled=pltpu.VMEM((256, 2 * width), bf16),
                **(ff_scratch if last else {}),
                **extra_scratch,
            ),
            after=after,
            micros=14,
        )

    def weight_grads(layer_idx, kept, weights, back, grad, peer_in, peer_grad, after=()):
        return run(
            functools.partial(weight_body, piece_masks=ff_masks),
            "layer_%d_weight_grads" % layer_idx,
            dict(
                place=place,
                ff_in=Kept(kept.ff_in),
                grad=grad,
                hidden=Kept(back.hidden),
                grad_gate_up=Kept(back.grad_gate_up),
                peer_in=Kept(peer_in),
                peer_grad=Kept(peer_grad),
                ff_gate_up=Kept(weights.ff_gate_up),
                ff_down=Kept(weights.ff_down),
            ),
            dict(ff_keep=Kept(ff_half, bf16), ff_send=Kept(ff_half, bf16)),
            dict(
                peer_gate_up=pltpu.VMEM((rows, 2 * width), bf16),
                peer_hidden=pltpu.VMEM(matrix, bf16),
                ff_grad=pltpu.VMEM((width, 3 * width), f32),
            ),
            after=after,
            micros=7,
        )

    def add(left, right):
        return (left.astype(f32) + right.astype(f32)).astype(bf16)

    def halving(keep, send, hops, out):
        for step, hop in enumerate(hops):
            got = yield swap(send, hop)
            if step + 1 < len(hops):
                cut = keep.shape[0] // 2
                send = add(keep[cut:], got[cut:])
                keep = add(keep[:cut], got[:cut])
                out["token"] = send
            else:
                out["token"] = keep = add(keep, got)
        out["piece"] = keep

    def summing(piece, hops, out):
        for hop in hops:
            got = yield swap(piece, hop)
            out["token"] = piece = add(piece, got) if piece.dtype == bf16 else piece + got
        out["piece"] = piece

    def sharing(piece, hops, out):
        for step, hop in enumerate(hops):
            got = yield swap(piece, hop)
            if step + 1 < len(hops):
                out["token"] = piece = join(piece, got)
            else:
                out["token"] = got
        out["near"], out["far"] = piece, got

    def attn_chain(part, out):
        yield from halving(part.attn_keep, part.attn_send, attn_split, out)
        yield from summing(out["piece"], attn_whole, out)
        piece = out["piece"][0]
        if own_rows < attn_grain:
            first_row = lax.rem(device_at, attn_low) * own_rows
            piece = lax.dynamic_slice_in_dim(piece, first_row, own_rows, axis=0)
        out["done"] = piece.astype(f32)

    def ff_chain(part, out):
        yield from halving(part.ff_keep, part.ff_send, ff_split, out)
        yield from summing(out["piece"], ff_whole, out)
        yield from sharing(out["piece"], ff_split[::-1], out)
        out["done"] = True

    class Chain:
        def __init__(self, steps, *args):
            self.out = {}
            self.steps = steps(*args, self.out)
            self.arriving = next(self.steps)

        def step(self, token):
            if self.arriving is not None:
                arrived = tie(self.arriving, token)
                self.arriving = None
                try:
                    self.arriving = self.steps.send(arrived)
                except StopIteration:
                    pass
                return self.out["token"]
            return token

    back_1 = backward(
        1,
        second,
        first.x_next,
        first.a_next,
        cotangent,
        {},
        dict(
            outputs=(matrix, bf16),
            grad_next=Kept(matrix, f32),
            grad_next_low=Kept(matrix, bf16),
            bias_acc=Kept((slots, heads * slots), f32),
        ),
        {},
        after=(peer_cotangent,),
    )
    peer_grad_0 = swap(back_1.grad_next_low, 1)
    part_1 = weight_grads(
        1, second, back_1, back_1, cotangent, peer_in_1, peer_cotangent, after=(peer_in_0,)
    )
    attn_1 = Chain(attn_chain, back_1)
    ff_1 = Chain(ff_chain, part_1)
    token = attn_1.step(part_1.ff_send)
    token = ff_1.step(token)
    back_0 = backward(
        0,
        first,
        start.x,
        start.a,
        Kept(back_1.grad_next),
        dict(
            bias_before=Kept(back_1.bias_acc),
            marks=marks,
            buckets=wide_buckets,
            small_before=Kept(back_1.small),
        ),
        dict(grad_next=(matrix, f32)),
        dict(
            bias_acc=pltpu.VMEM((slots, heads * slots), f32),
            table_rows=pltpu.VMEM((bias_table.shape[0], heads * slots), f32),
        ),
        after=(token,),
    )
    attn_0 = Chain(attn_chain, back_0)
    token = ff_1.step(back_0.attn_send)
    token = attn_1.step(token)
    part_0 = weight_grads(
        0,
        first,
        first,
        back_0,
        Kept(back_1.grad_next_low),
        peer_in_0,
        peer_grad_0,
        after=(token,),
    )
    ff_0 = Chain(ff_chain, part_0)
    small = Chain(summing, back_0.small, attn_hops)
    token = attn_1.step(ff_1.step(part_0.ff_send))
    token = ff_0.step(attn_0.step(token))
    token = small.step(token)
    done_1 = None
    shape = (2, width, width)
    finish_masks = order_masks(ff_split)
    near_masks = [mask // 2 for mask in finish_masks[: ff_count // 2]]
    far_masks = [mask // 2 for mask in finish_masks[ff_count // 2 :]]
    chains = (ff_0, ff_1, attn_0, attn_1, small)
    while any(chain.arriving is not None for chain in chains):
        if "near" in ff_1.out and done_1 is None:
            pieces = join(ff_1.out["near"], ff_1.out["far"])
            done_1 = finish(tie(pieces, token), near_masks + far_masks, 1, place, shape)
            token = done_1[0]
        for chain in chains:
            token = chain.step(token)
    if done_1 is None:
        pieces = join(ff_1.out["near"], ff_1.out["far"])
        done_1 = finish(pieces, near_masks + far_masks, 1, place, shape)
    near_0 = finish(ff_0.out["near"], near_masks, 0, place, shape, done_1)
    done = finish(ff_0.out["far"], far_masks, 0, place, shape, near_0)
    sums = run(
        small_body,
        "small_sums",
        dict(packed=Kept(small.out["piece"])),
        dict(
            gain_attn=((2, width), f32),
            gain_ff=((2, width), f32),
            embed=((1, width), f32),
            table=(bias_table.shape, f32),
        ),
        {},
    )
    attn_0, attn_1 = attn_0.out["done"], attn_1.out["done"]
    attn_grads = jnp.stack([attn_0, attn_1])
    return (
        back_1.outputs.reshape(inputs.shape),
        back_0.grad_next.reshape(inputs.shape),
        attn_grads[:, :, :inner],
        attn_grads[:, :, inner : 2 * inner],
        attn_grads[:, :, 2 * inner : 3 * inner],
        jnp.swapaxes(attn_grads[:, :, 3 * inner :], 1, 2),
        *done,
        sums.gain_attn,
        sums.gain_ff,
        sums.table,
        sums.embed[0],
    )


def solution(mesh):
    placed = (
        P(("dp", "tensor"), None, None),
        P(("dp", "tensor"), None, None),
        P(("dp", "tensor"), None),
        P(("dp", "tensor"), None),
        P(),
        P(),
        P(None, ("dp", "tensor"), None),
        P(None, ("dp", "tensor"), None),
        P(None, ("dp", "tensor"), None),
        P(None, None, ("dp", "tensor")),
        P(None, None, "tensor"),
        P(None, None, "tensor"),
        P(None, "tensor", None),
        P(),
        P(),
        P(),
    )
    return jax.shard_map(
        functools.partial(on_device, dp_size=mesh.shape["dp"]),
        mesh=mesh,
        in_specs=placed,
        out_specs=(
            P(("dp", "tensor"), None, None),
            P(("dp", "tensor"), None, None),
            P(None, ("dp", "tensor"), None),
            P(None, ("dp", "tensor"), None),
            P(None, ("dp", "tensor"), None),
            P(None, None, ("dp", "tensor")),
            P(None, None, "tensor"),
            P(None, None, "tensor"),
            P(None, "tensor", None),
            P(),
            P(),
            P(),
            P(),
        ),
        check_vma=False,
    )
```

```python
import functools
import types

import jax
import jax.numpy as jnp
from jax import lax
from jax.experimental import pallas as pl
from jax.experimental.pallas import tpu as pltpu
from jax.sharding import PartitionSpec as P

norm_eps = 1e-06
masked_score = -1e30
bf16 = jnp.bfloat16
f32 = jnp.float32
axes = ("dp", "tensor")
vmem_bytes = 26 * 1024 * 1024
raw_names = ("attn_near", "attn_far", "ff_near", "ff_far", "w_gate", "w_up", "w_down")


def dot_nn(left, right):
    return lax.dot_general(left, right, (((1,), (0,)), ((), ())), preferred_element_type=f32)


def dot_nt(left, right):
    return lax.dot_general(left, right, (((1,), (1,)), ((), ())), preferred_element_type=f32)


def dot_tn(left, right):
    return lax.dot_general(left, right, (((0,), (0,)), ((), ())), preferred_element_type=f32)


def inverse_rms(values):
    return lax.rsqrt(jnp.mean(values * values, axis=-1, keepdims=True) + norm_eps)


def norm_back(values, gain, grad_out):
    scale = inverse_rms(values)
    pulled = grad_out * gain
    mean_part = jnp.mean(pulled * values, axis=-1, keepdims=True)
    grad_in = scale * pulled - values * (scale * scale * scale) * mean_part
    return grad_in, jnp.sum(grad_out * values * scale, axis=0, keepdims=True)


def gelu_terms(gate_act):
    square = gate_act * gate_act
    bent = jnp.tanh(0.7978845608028654 * gate_act * (1.0 + 0.044715 * square))
    half = 0.5 * (1.0 + bent)
    slope = half + 0.5 * gate_act * (1.0 - bent * bent) * (
        0.7978845608028654 * (1.0 + 3.0 * 0.044715 * square)
    )
    return gate_act * half, slope


def cost(micros):
    return pl.CostEstimate(flops=int(micros * 1.15e9), bytes_accessed=0, transcendentals=0)


def run(body, name, ins, outs, scratch, after=(), micros=1):
    in_names, out_names, scratch_names = list(ins), list(outs), list(scratch)
    direct = {n for n in in_names if n == "place" or n in raw_names or isinstance(ins[n], Kept)}
    staged = [n for n in in_names if n not in direct]
    copied = [n for n in out_names if not isinstance(outs[n], Kept)]
    in_sems = {n: i for i, n in enumerate(staged)}
    out_sems = {n: i for i, n in enumerate(copied)}

    def kernel(*refs):
        refs = list(refs)
        sources = dict(zip(in_names, refs))
        refs = refs[len(in_names) + len(after) :]
        targets = dict(zip(out_names, refs))
        refs = refs[len(out_names) :]
        space = dict(zip(scratch_names, refs))
        refs = refs[len(scratch_names) :]
        buffers = dict(zip(staged + copied, refs))
        sems_in, sems_out = refs[len(staged) + len(copied) :]
        kept = {n: ref for n, ref in targets.items() if n not in out_sems}
        r = types.SimpleNamespace(**space, **buffers, **kept)
        for n in direct:
            setattr(r, n, sources[n])

        def copy_in(n):
            return pltpu.make_async_copy(sources[n], buffers[n], sems_in.at[in_sems[n]])

        def copy_out(n):
            return pltpu.make_async_copy(buffers[n], targets[n], sems_out.at[out_sems[n]])

        r.fetch = lambda *names: [copy_in(n).start() for n in names if n in in_sems]
        r.need = lambda *names: [copy_in(n).wait() for n in names if n in in_sems]
        r.write = lambda *names: [copy_out(n).start() for n in names if n in out_sems]
        r.drain = lambda *names: [copy_out(n).wait() for n in names if n in out_sems]
        body(r)

    def in_space(n):
        if n == "place":
            return pltpu.SMEM
        return pltpu.VMEM if isinstance(ins[n], Kept) else pl.ANY

    results = pl.pallas_call(
        kernel,
        name=name,
        in_specs=[pl.BlockSpec(memory_space=in_space(n)) for n in in_names]
        + [pl.BlockSpec(memory_space=pl.ANY) for _ in after],
        out_specs=[
            pl.BlockSpec(memory_space=pltpu.VMEM if isinstance(out, Kept) else pl.ANY)
            for out in outs.values()
        ],
        out_shape=[
            pltpu.VMEM(*out.what) if isinstance(out, Kept) else jax.ShapeDtypeStruct(*out)
            for out in outs.values()
        ],
        scratch_shapes=list(scratch.values())
        + [pltpu.VMEM(ins[n].shape, ins[n].dtype) for n in staged]
        + [pltpu.VMEM(*outs[n]) for n in copied]
        + [
            pltpu.SemaphoreType.DMA((max(1, len(staged)),)),
            pltpu.SemaphoreType.DMA((max(1, len(copied)),)),
        ],
        compiler_params=pltpu.CompilerParams(vmem_limit_bytes=vmem_bytes),
        cost_estimate=cost(micros),
    )(
        *[
            pltpu.with_memory_space_constraint(value.what, pltpu.VMEM)
            if isinstance(value, Kept)
            else value
            for value in ins.values()
        ],
        *after,
    )
    return types.SimpleNamespace(**dict(zip(outs, results)))


class Kept:
    def __init__(self, *what):
        self.what = what[0] if len(what) == 1 else what


def keep_all(names):
    return {name: Kept(value) for name, value in names.items()}


def chunks(extent, size):
    size = min(size, extent)
    return [slice(start, start + size) for start in range(0, extent, size)]


def attention_copies(r, masks, rows):
    copies = []
    for idx, mask in enumerate(masks):
        half, at = divmod(idx, max(1, len(masks) // 2))
        source = (r.attn_near if half == 0 else r.attn_far).at[pl.ds(at * rows, rows)]
        place = (r.place[0] ^ mask) * rows if len(masks) > 1 else 0
        target = r.attn_w.at[pl.ds(pl.multiple_of(place, rows), rows)]
        copies.append(pltpu.make_async_copy(source, target, r.attn_sem))
    return copies


def ff_copies(r, layer_idx):
    width = r.ff_down.shape[-1]
    copies = []
    for k, own in enumerate((r.w_gate, r.w_up)):
        target = r.ff_gate_up.at[0, :, pl.ds(k * width, width)]
        copies.append(pltpu.make_async_copy(own.at[layer_idx], target, r.ff_sem))
    copies.append(pltpu.make_async_copy(r.w_down.at[layer_idx], r.ff_down.at[0], r.ff_sem))
    part = r.ff_near.shape[1]
    for source, base in ((r.ff_near, 0), (r.ff_far, 1)):
        for m in range(2):
            rows = pl.ds(pl.multiple_of((r.place[1] ^ (2 * m + base)) * part, part), part)
            for k in range(2):
                target = r.ff_gate_up.at[1, rows, pl.ds(k * width, width)]
                copies.append(pltpu.make_async_copy(source.at[3 * m + k], target, r.ff_sem))
            copies.append(
                pltpu.make_async_copy(source.at[3 * m + 2], r.ff_down.at[1, rows], r.ff_sem)
            )
    return copies


def start_all(copies):
    for copy in copies:
        copy.start()


def wait_all(sem, *buffers):
    for whole in buffers:
        pltpu.make_async_copy(whole, whole, sem).wait()


def lane_low(rows):
    return lax.broadcasted_iota(jnp.int32, (rows, 128), 1) < 64


def lane_halves():
    low = lane_low(1).astype(f32)
    return low.astype(bf16), (1.0 - low).astype(bf16)


def pair_blocks(rows, low, high):
    return jnp.concatenate([rows * low, rows * high], axis=0)


def own_blocks(both, is_low):
    half = both.shape[0] // 2
    return jnp.where(is_low, both[:half], both[half:]).astype(bf16)


def attention_forward(r, x_ref, a_ref, sizes, layer_idx):
    series, slots, inner = sizes
    rows = series * slots
    for part in chunks(rows, 256):
        r.qkv[part, :] = dot_nn(a_ref[part, :], r.attn_w[:, : 3 * inner]).astype(bf16)
    is_low = lane_low(slots)
    low, high = lane_halves()
    for s in range(series):
        here = slice(s * slots, (s + 1) * slots)
        keep = r.mask[here, :] == 1
        for start in range(0, inner, 128):
            at = slice(start, start + 128)
            query = r.qkv[here, at]
            keys = r.qkv[here, inner + start : inner + start + 128]
            scores = dot_nt(keys, pair_blocks(query, low, high)) + r.bias[:, at]
            scores = jnp.where(keep, scores, masked_score)
            exps = jnp.exp(scores - jnp.max(scores, axis=0, keepdims=True))
            r.probs[here, at] = exps / jnp.sum(exps, axis=0, keepdims=True)
    for s in range(series):
        here = slice(s * slots, (s + 1) * slots)
        for start in range(0, inner, 128):
            at = slice(start, start + 128)
            values = r.qkv[here, 2 * inner + start : 2 * inner + start + 128]
            both = dot_tn(r.probs[here, at].astype(bf16), values)
            r.heads[here, at] = own_blocks(both, is_low)
    gain = r.gain_ff[layer_idx : layer_idx + 1, :]
    for part in chunks(rows, 256):
        middle = x_ref[part, :] + dot_nt(r.heads[part, :], r.attn_w[:, 3 * inner :])
        r.middle[part, :] = middle
        r.ff_in[part, :] = (middle * inverse_rms(middle) * gain).astype(bf16)


def prepare_body(r):
    r.fetch("inputs", "marks", "embed", "gain_attn", "buckets", "table")
    r.need("inputs", "marks", "embed", "gain_attn", "buckets", "table")
    x = jnp.where(r.marks[:, 0:1] == 1, r.inputs[...].astype(f32), r.embed[...])
    r.x[...] = x
    r.a[...] = (x * inverse_rms(x) * r.gain_attn[0:1, :]).astype(bf16)
    buckets = r.buckets[...]
    bias = jnp.zeros(buckets.shape, f32)
    for idx in range(r.table.shape[0]):
        bias = jnp.where(buckets == idx, r.table[idx : idx + 1, :], bias)
    r.bias[...] = bias
    r.mask[...] = jnp.broadcast_to(r.marks[:, 1:2], r.mask.shape)
    r.write("x", "a", "bias", "mask")
    r.drain("x", "a", "bias", "mask")


def attention_body(r, sizes, masks, grain, layer_idx):
    start_all(attention_copies(r, masks, grain))
    r.fetch("gain_ff")
    r.need("gain_ff")
    wait_all(r.attn_sem, r.attn_w)
    attention_forward(r, r.x, r.a, sizes, layer_idx)


def ff_body(r):
    start_all(ff_copies(r, 0))
    r.fetch("gain_attn")
    r.need("gain_attn")
    wait_all(r.ff_sem, r.ff_gate_up, r.ff_down)
    width = r.middle.shape[1]
    for part in chunks(r.middle.shape[0], 256):
        x_next = r.middle[part, :]
        for half in range(2):
            both = dot_nn(r.ff_in[part, :], r.ff_gate_up[half])
            hidden = (gelu_terms(both[:, :width])[0] * both[:, width:]).astype(bf16)
            x_next = x_next + dot_nn(hidden, r.ff_down[half])
        r.x_next[part, :] = x_next
        r.a_next[part, :] = (x_next * inverse_rms(x_next) * r.gain_attn[1:2, :]).astype(bf16)


def ff_backward(r, layer_idx, last):
    rows, width = r.middle.shape
    r.fetch("grad", "gain_ff")
    if last:
        start_all(ff_copies(r, layer_idx))
    r.need("grad", "gain_ff")
    if last:
        wait_all(r.ff_sem, r.ff_gate_up, r.ff_down)
    gain_ff = r.gain_ff[layer_idx : layer_idx + 1, :]
    gain_total = jnp.zeros((1, width), f32)
    for part in chunks(rows, 256):
        grad = r.grad[part, :].astype(f32)
        rounded = grad.astype(bf16)
        ff_rows = r.ff_in[part, :]
        back = None
        middle = r.middle[part, :]
        total = middle
        for half in range(2):
            both = dot_nn(ff_rows, r.ff_gate_up[half])
            grad_hidden = dot_nt(rounded, r.ff_down[half])
            gate_act, up_act = both[:, :width], both[:, width:]
            mixed, slope = gelu_terms(gate_act)
            if half == 0:
                r.grad_gate_up[part, :width] = (grad_hidden * up_act * slope).astype(bf16)
                r.grad_gate_up[part, width:] = (grad_hidden * mixed).astype(bf16)
                pulled = r.grad_gate_up[part, :]
            else:
                r.pulled[:, :width] = (grad_hidden * up_act * slope).astype(bf16)
                r.pulled[:, width:] = (grad_hidden * mixed).astype(bf16)
                pulled = r.pulled[...]
            hidden = (mixed * up_act).astype(bf16)
            if half == 0:
                r.hidden[part, :] = hidden
            if last:
                total = total + dot_nn(hidden, r.ff_down[half])
            term = dot_nt(pulled, r.ff_gate_up[half])
            back = term if back is None else back + term
        if last:
            r.outputs[part, :] = total.astype(bf16)
        grad_mid, gain_part = norm_back(middle, gain_ff, back)
        gain_total += gain_part
        grad_mid = grad + grad_mid
        r.grad_mid[part, :] = grad_mid
        r.branch[part, :] = grad_mid.astype(bf16)
    if last:
        r.write("outputs")
    return gain_total


def attention_backward(r, sizes, layer_idx, last, piece_masks, heads):
    series, slots, inner = sizes
    rows = series * slots
    width = r.x.shape[1]
    r.fetch("gain_attn")
    if not last:
        r.fetch("marks", "buckets")
    for part in chunks(rows, 256):
        r.grad_heads[part, :] = dot_nn(r.branch[part, :], r.attn_w[:, 3 * inner :]).astype(bf16)
    is_low = lane_low(slots)
    low, high = lane_halves()
    for start in range(0, inner, 128):
        at = slice(start, start + 128)
        bias_total = jnp.zeros((slots, 128), f32) if last else r.bias_before[:, at]
        for s in range(series):
            here = slice(s * slots, (s + 1) * slots)
            probs = r.probs[here, at]
            values = r.qkv[here, 2 * inner + start : 2 * inner + start + 128]
            grad_probs = dot_nt(values, pair_blocks(r.grad_heads[here, at], low, high))
            inner_sum = jnp.sum(probs * grad_probs, axis=0, keepdims=True)
            grad_scores = (probs * (grad_probs - inner_sum)).astype(bf16)
            r.grad_scores[here, at] = grad_scores
            bias_total = bias_total + grad_scores.astype(f32)
        r.bias_acc[:, at] = bias_total
    for s in range(series):
        here = slice(s * slots, (s + 1) * slots)
        for start in range(0, inner, 128):
            at = slice(start, start + 128)
            key_at = slice(inner + start, inner + start + 128)
            value_at = slice(2 * inner + start, 2 * inner + start + 128)
            grad_scores = r.grad_scores[here, at]
            r.grad_qkv[here, key_at] = dot_nn(
                grad_scores, pair_blocks(r.qkv[here, at], low, high)
            ).astype(bf16)
            r.grad_qkv[here, value_at] = dot_nn(
                r.probs[here, at].astype(bf16), pair_blocks(r.grad_heads[here, at], low, high)
            ).astype(bf16)
            r.grad_qkv[here, at] = own_blocks(dot_tn(grad_scores, r.qkv[here, key_at]), is_low)
    r.attn_grad[:, : 3 * inner] = dot_tn(r.a[...], r.grad_qkv[...])
    r.attn_grad[:, 3 * inner :] = dot_tn(r.branch[...], r.heads[...])
    scatter_pieces(r.attn_grad, r.attn_keep, r.attn_send, piece_masks, r.place[2])
    r.need("gain_attn")
    if not last:
        r.need("marks", "buckets")
    gain_attn = r.gain_attn[layer_idx : layer_idx + 1, :]
    gain_total = jnp.zeros((1, width), f32)
    embed_total = jnp.zeros((1, width), f32)
    for part in chunks(rows, 256):
        grad_normed = dot_nt(r.grad_qkv[part, :], r.attn_w[:, : 3 * inner])
        grad_in, gain_part = norm_back(r.x[part, :], gain_attn, grad_normed)
        gain_total += gain_part
        grad_in = r.grad_mid[part, :] + grad_in
        if last:
            r.grad_next[part, :] = grad_in
            r.grad_next_low[part, :] = grad_in.astype(bf16)
        else:
            seen = r.marks[part, 0:1] == 1
            r.grad_next[part, :] = jnp.where(seen, grad_in, 0.0)
            embed_total += jnp.sum(jnp.where(seen, 0.0, grad_in), axis=0, keepdims=True)
    r.write("grad_next")
    if not last:
        put_row(r.small, 4, embed_total)
        head_size = inner // heads
        for idx in range(r.table_rows.shape[0]):
            chosen = jnp.where(r.buckets[...] == idx, r.bias_acc[...], 0.0)
            r.table_rows[idx : idx + 1, :] = jnp.sum(chosen, axis=0, keepdims=True)
        lane = lax.broadcasted_iota(jnp.int32, (r.table_rows.shape[0], 128), 1)
        table = jnp.zeros(lane.shape, f32)
        for head in range(heads):
            cut = r.table_rows[:, head * head_size : (head + 1) * head_size]
            table = jnp.where(lane == head, jnp.sum(cut, axis=1, keepdims=True), table)
        r.small[small_rows(width) :, :] = table
    r.drain("grad_next")
    return gain_total


def last_backward_body(r, sizes, piece_masks, heads):
    r.small[...] = jnp.zeros(r.small.shape, f32)
    put_row(r.small, 3, ff_backward(r, 1, True))
    put_row(r.small, 1, attention_backward(r, sizes, 1, True, piece_masks, heads))
    r.drain("outputs")


def ff_backward_body(r):
    r.small[...] = r.small_before[...]
    put_row(r.small, 2, ff_backward(r, 0, False))


def attention_backward_body(r, sizes, piece_masks, heads):
    r.small[...] = r.small_before[...]
    put_row(r.small, 0, attention_backward(r, sizes, 0, False, piece_masks, heads))


def small_rows(width):
    return -(-5 * width // 1024) * 8


def put_row(packed, which, row):
    lanes = row.shape[1] // 128
    for k in range(lanes):
        packed[which * lanes + k : which * lanes + k + 1, :] = row[:, k * 128 : (k + 1) * 128]


def scatter_pieces(whole, keep, send, masks, place):
    count = len(masks)
    grain = whole.shape[0] // count
    for idx, mask in enumerate(masks):
        target = keep if idx < count // 2 else send
        source = pl.ds(pl.multiple_of((place ^ mask) * grain, grain), grain)
        target[idx % (count // 2)] = whole[source, :].astype(bf16)


def weight_body(r, piece_masks):
    width = r.ff_in.shape[1]
    rows = r.ff_in.shape[0]
    r.fetch("peer_in", "peer_grad")
    r.fetch("ff_in", "grad_gate_up", "hidden", "grad")
    r.need("peer_in", "peer_grad")
    for part in chunks(rows, 256):
        both = dot_nn(r.peer_in[part, :], r.ff_gate_up[0])
        grad_hidden = dot_nt(r.peer_grad[part, :], r.ff_down[0])
        gate_act, up_act = both[:, :width], both[:, width:]
        mixed, slope = gelu_terms(gate_act)
        r.peer_gate_up[part, :width] = (grad_hidden * up_act * slope).astype(bf16)
        r.peer_gate_up[part, width:] = (grad_hidden * mixed).astype(bf16)
        r.peer_hidden[part, :] = (mixed * up_act).astype(bf16)
    r.need("ff_in", "grad_gate_up", "hidden", "grad")
    r.ff_grad[:, : 2 * width] = dot_tn(r.ff_in[...], r.grad_gate_up[...]) + dot_tn(
        r.peer_in[...], r.peer_gate_up[...]
    )
    r.ff_grad[:, 2 * width :] = dot_tn(r.hidden[...], r.grad[...]) + dot_tn(
        r.peer_hidden[...], r.peer_grad[...]
    )
    scatter_pieces(r.ff_grad, r.ff_keep, r.ff_send, piece_masks, r.place[3])
    r.write("ff_send", "ff_keep")
    r.drain("ff_send", "ff_keep")


def finish(pieces, masks, layer_idx, place, shape, before=()):
    grain, width = pieces.shape[1], shape[-1]
    count = len(before)

    def kernel(place_ref, source, *refs):
        outs = refs[count : count + 3]
        stage, out_sem = refs[count + 3 :]
        for idx, mask in enumerate(masks):
            rows = pl.ds(pl.multiple_of((place_ref[3] ^ mask) * grain, grain), grain)
            for k, out in enumerate(outs):
                stage[k, idx] = source[idx, :, k * width : (k + 1) * width].astype(f32)
                pltpu.make_async_copy(stage.at[k, idx], out.at[layer_idx, rows], out_sem).start()
        pltpu.make_async_copy(stage, stage, out_sem).wait()

    return pl.pallas_call(
        kernel,
        name="layer_%d_ff_grads" % layer_idx,
        in_specs=[
            pl.BlockSpec(memory_space=pltpu.SMEM),
            pl.BlockSpec(memory_space=pltpu.VMEM),
        ]
        + [pl.BlockSpec(memory_space=pl.ANY)] * count,
        out_specs=[pl.BlockSpec(memory_space=pl.ANY)] * 3,
        out_shape=[jax.ShapeDtypeStruct(shape, f32)] * 3,
        input_output_aliases={2 + k: k for k in range(count)},
        scratch_shapes=[
            pltpu.VMEM((3, len(masks), grain, width), f32),
            pltpu.SemaphoreType.DMA,
        ],
        compiler_params=pltpu.CompilerParams(vmem_limit_bytes=vmem_bytes),
        cost_estimate=cost(3),
    )(place, pltpu.with_memory_space_constraint(pieces, pltpu.VMEM), *before)


def small_body(r):
    r.fetch("packed")
    r.need("packed")
    lanes = r.embed.shape[1] // 128
    for which in range(5):
        out, row = ((r.gain_attn, which), (r.gain_ff, which - 2), (r.embed, 0))[which // 2]
        for k in range(lanes):
            at = which * lanes + k
            out[row : row + 1, k * 128 : (k + 1) * 128] = r.packed[at : at + 1, :]
    r.table[...] = r.packed[small_rows(r.embed.shape[1]) :, : r.table.shape[1]]
    r.write("gain_attn", "gain_ff", "embed", "table")
    r.drain("gain_attn", "gain_ff", "embed", "table")


def order_masks(hops):
    masks = [0]
    for hop in reversed(hops):
        masks = masks + [mask ^ hop for mask in masks]
    return masks


def tie(value, *others):
    return lax.optimization_barrier((value, *others))[0]


def on_device(
    inputs,
    cotangent,
    attention_mask,
    patch_valid,
    buckets,
    mask_embed,
    w_query,
    w_key,
    w_value,
    w_output,
    w_gate,
    w_up,
    w_down,
    gain_attn,
    gain_ff,
    bias_table,
    dp_size,
):
    series, slots, width = inputs.shape
    heads = bias_table.shape[1]
    inner = w_query.shape[2]
    rows = series * slots
    sizes = (series, slots, inner)
    matrix = (rows, width)
    devices = 2 * dp_size
    dp_at = lax.axis_index("dp")
    device_at = 2 * dp_at + lax.axis_index("tensor")
    cotangent = cotangent.reshape(matrix)

    def swap(array, mask):
        return lax.ppermute(array, axes, [(n, n ^ mask) for n in range(devices)])

    def join(left, right):
        return jnp.concatenate([left, right], axis=0)

    bits = [1 << k for k in range(devices.bit_length() - 1)]

    attn_grain = max(16, width // devices)
    attn_count = width // attn_grain
    ff_grain = max(16, width // dp_size)
    ff_count = width // ff_grain
    quarter_at = lax.rem(dp_at, 4)
    place = jnp.stack(
        [
            device_at,
            quarter_at,
            device_at // (devices // attn_count),
            lax.rem(dp_at, ff_count),
        ]
    ).astype(jnp.int32)

    quarter = width // 4
    packed = jnp.concatenate([w_query, w_key, w_value, jnp.swapaxes(w_output, 1, 2)], axis=2)
    ff_blocks = jnp.concatenate(
        [
            lax.dynamic_slice_in_dim(tie(w, packed), quarter_at * quarter, quarter, axis=1)
            for w in (w_gate, w_up, w_down)
        ],
        axis=0,
    )

    def prepare(token):
        table, marked, kept, near = (
            tie(array, token) for array in (bias_table, patch_valid, attention_mask, buckets)
        )
        wide_buckets = jnp.tile(near.T, (1, heads))
        wide_table = jnp.repeat(table, slots, axis=1)
        marks = jnp.stack([marked.reshape(rows), kept.reshape(rows)], axis=1)
        result = run(
            prepare_body,
            "prepare",
            dict(
                inputs=inputs.reshape(matrix),
                marks=marks,
                embed=mask_embed[None, :],
                gain_attn=gain_attn,
                buckets=wide_buckets,
                table=wide_table,
            ),
            dict(
                x=Kept(matrix, f32),
                a=Kept(matrix, bf16),
                bias=Kept((slots, heads * slots), f32),
                mask=Kept((rows, 128), jnp.int32),
            ),
            {},
            micros=3,
        )
        return result, wide_buckets, marks

    own_rows = packed.shape[1]
    direct = own_rows % 16 == 0
    far = bits[2:]
    if direct:
        hops_0 = [1] + far[2:] + far[:2] + [2]
        hops_1 = far[2:] + far[:2] + [1, 2]
        block_0, block_1 = packed[0], packed[1]
        got_1 = swap(block_1, hops_1[0])
        got_0 = swap(block_0, hops_0[0])
        ff_quarter = swap(tie(ff_blocks, got_0), 1).reshape(3, 2, quarter, width)
        block_0 = join(block_0, got_0)
        block_1 = join(block_1, tie(got_1, block_0))
        for hop_0, hop_1 in zip(hops_0[1:-2], hops_1[1:-2]):
            got_1, got_0 = swap(block_1, hop_1), swap(block_0, hop_0)
            if hop_1 == hops_1[1]:
                start, wide_buckets, marks = prepare(block_1)
            block_0 = join(block_0, got_0)
            block_1 = join(block_1, tie(got_1, block_0))
        got_0 = swap(block_0, hops_0[-2])
        got_1 = swap(block_1, hops_1[-2])
        ff_0 = tie(ff_quarter[:, 0], block_1)
        got_ff_0 = swap(ff_0, 4)
        block_0 = join(block_0, tie(got_0, start.a, got_ff_0))
        block_1 = join(block_1, tie(got_1, block_0))
        ff_0 = join(ff_0, tie(got_ff_0, block_1))
        got_ff_1 = swap(tie(ff_quarter[:, 1], ff_0), 4)
        peer_cotangent = swap(tie(cotangent, ff_0), 1)
        far_0 = swap(block_0, 2)
        attn_pieces = [
            (block_0, far_0, order_masks(hops_0[::-1])),
            (block_1, swap(tie(block_1, far_0), 2), order_masks(hops_1[::-1])),
        ]
        after_first = (attn_pieces[1][1], peer_cotangent)
    else:
        ff_quarter = swap(ff_blocks, 1).reshape(3, 2, quarter, width)
        ff_0 = join(ff_quarter[:, 0], swap(ff_quarter[:, 0], 4))
        start, wide_buckets, marks = prepare(packed)
        whole = lax.all_gather(packed[0], axes, axis=0, tiled=True)
        attn_pieces = [(whole, whole, [0])]
        whole = lax.all_gather(packed[1], axes, axis=0, tiled=True)
        attn_pieces.append((whole, whole, [0]))
        after_first = ()
        peer_cotangent = swap(cotangent, 1)
    ff_pieces = [(ff_0, swap(ff_0, 2))]

    def attn_ins(layer_idx):
        near, far, masks = attn_pieces[layer_idx]
        return dict(attn_near=Kept(near), attn_far=Kept(far)), masks

    def ff_ins(layer_idx):
        near, far = ff_pieces[layer_idx]
        return dict(w_gate=w_gate, w_up=w_up, w_down=w_down, ff_near=Kept(near), ff_far=Kept(far))

    attn_scratch = dict(attn_sem=pltpu.SemaphoreType.DMA)
    ff_scratch = dict(ff_sem=pltpu.SemaphoreType.DMA)
    ff_outs = dict(
        ff_gate_up=Kept((2, width, 2 * width), bf16), ff_down=Kept((2, width, width), bf16)
    )
    grain = own_rows if direct else width
    attn_outs = dict(
        attn_w=Kept((width, 4 * inner), bf16),
        qkv=Kept((rows, 3 * inner), bf16),
        probs=Kept((rows, heads * slots), f32),
        heads=Kept((rows, inner), bf16),
        middle=Kept(matrix, f32),
        ff_in=Kept(matrix, bf16),
    )

    def attention(layer_idx, x, a, after=(), micros=5):
        pieces, masks = attn_ins(layer_idx)
        return run(
            functools.partial(
                attention_body, sizes=sizes, masks=masks, grain=grain, layer_idx=layer_idx
            ),
            "layer_%d_attention" % layer_idx,
            dict(
                place=place,
                x=Kept(x),
                a=Kept(a),
                bias=Kept(start.bias),
                mask=Kept(start.mask),
                gain_ff=gain_ff,
                **pieces,
            ),
            attn_outs,
            attn_scratch,
            after=after,
            micros=micros,
        )

    first = attention(0, start.x, start.a, micros=10)
    peer_in_0 = swap(first.ff_in, 1)
    first_ff = run(
        ff_body,
        "layer_0_ff",
        dict(
            place=place,
            middle=Kept(first.middle),
            ff_in=Kept(first.ff_in),
            gain_attn=gain_attn,
            **ff_ins(0),
        ),
        dict(**ff_outs, x_next=Kept(matrix, f32), a_next=Kept(matrix, bf16)),
        ff_scratch,
        after=after_first,
        micros=0.1,
    )
    if direct:
        ff_1 = join(ff_quarter[:, 1], tie(got_ff_1, first_ff.a_next))
    else:
        ff_1 = join(ff_quarter[:, 1], swap(ff_quarter[:, 1], 4))
    ff_pieces.append((ff_1, swap(ff_1, 2)))
    second = attention(1, first_ff.x_next, first_ff.a_next, micros=0.1)
    peer_in_1 = swap(second.ff_in, 1)

    attn_low = devices // attn_count
    attn_hops = ([2, 1] + bits[2:], [2] + bits[3:] + bits[2:3] + [1])
    attn_split = [[hop for hop in hops if hop >= attn_low] for hops in attn_hops]
    attn_whole = [hop for hop in bits if hop < attn_low]
    attn_masks = [[mask // attn_low for mask in order_masks(hops)] for hops in attn_split]
    ff_hops = (bits[1:], [2] + bits[3:] + bits[2:3])
    ff_split = [[hop for hop in hops if hop // 2 < ff_count] for hops in ff_hops]
    ff_whole = [hop for hop in bits[1:] if hop // 2 >= ff_count]
    ff_masks = [[mask // 2 for mask in order_masks(hops)] for hops in ff_split]
    attn_half = (attn_count // 2, attn_grain, 4 * inner)
    ff_half = (ff_count // 2, ff_grain, 3 * width)
    small_shape = (small_rows(width) + bias_table.shape[0], 128)

    ff_back_outs = dict(
        hidden=Kept(matrix, bf16),
        grad_gate_up=Kept((rows, 2 * width), bf16),
        small=Kept(small_shape, f32),
    )
    attn_back_outs = dict(attn_keep=Kept(attn_half, bf16), attn_send=Kept(attn_half, bf16))
    attn_back_scratch = dict(
        grad_heads=pltpu.VMEM((rows, inner), bf16),
        grad_qkv=pltpu.VMEM((rows, 3 * inner), bf16),
        grad_scores=pltpu.VMEM((rows, heads * slots), bf16),
        attn_grad=pltpu.VMEM((width, 4 * inner), f32),
    )
    mid_scratch = dict(grad_mid=pltpu.VMEM(matrix, f32), branch=pltpu.VMEM(matrix, bf16))
    pulled_scratch = dict(pulled=pltpu.VMEM((256, 2 * width), bf16))
    bias_shape = (slots, heads * slots)

    def attn_back_ins(kept, x, a):
        return dict(
            x=Kept(x),
            a=Kept(a),
            gain_attn=gain_attn,
            attn_w=Kept(kept.attn_w),
            qkv=Kept(kept.qkv),
            probs=Kept(kept.probs),
            heads=Kept(kept.heads),
        )

    def weight_grads(layer_idx, kept, weights, back, grad, peer_in, peer_grad, after, micros):
        return run(
            functools.partial(weight_body, piece_masks=ff_masks[layer_idx]),
            "layer_%d_weight_grads" % layer_idx,
            dict(
                place=place,
                ff_in=Kept(kept.ff_in),
                grad=grad,
                hidden=Kept(back.hidden),
                grad_gate_up=Kept(back.grad_gate_up),
                peer_in=Kept(peer_in),
                peer_grad=Kept(peer_grad),
                ff_gate_up=Kept(weights.ff_gate_up),
                ff_down=Kept(weights.ff_down),
            ),
            dict(ff_keep=Kept(ff_half, bf16), ff_send=Kept(ff_half, bf16)),
            dict(
                peer_gate_up=pltpu.VMEM((rows, 2 * width), bf16),
                peer_hidden=pltpu.VMEM(matrix, bf16),
                ff_grad=pltpu.VMEM((width, 3 * width), f32),
            ),
            after=after,
            micros=micros,
        )

    def add(left, right):
        return (left.astype(f32) + right.astype(f32)).astype(bf16)

    def halving(keep, send, hops, out):
        for step, hop in enumerate(hops):
            got = yield swap(send, hop)
            if step + 1 < len(hops):
                cut = keep.shape[0] // 2
                send = add(keep[cut:], got[cut:])
                keep = add(keep[:cut], got[:cut])
                out["token"] = send
            else:
                out["token"] = keep = add(keep, got)
        out["piece"] = keep

    def summing(piece, hops, out):
        for hop in hops:
            got = yield swap(piece, hop)
            out["token"] = piece = add(piece, got) if piece.dtype == bf16 else piece + got
        out["piece"] = piece

    def sharing(piece, hops, out):
        for step, hop in enumerate(hops):
            got = yield swap(piece, hop)
            if step + 1 < len(hops):
                out["token"] = piece = join(piece, got)
            else:
                out["token"] = got
        out["near"], out["far"] = piece, got

    def attn_chain(part, split, out):
        yield from halving(part.attn_keep, part.attn_send, split, out)
        yield from summing(out["piece"], attn_whole, out)
        piece = out["piece"][0]
        if own_rows < attn_grain:
            first_row = lax.rem(device_at, attn_low) * own_rows
            piece = lax.dynamic_slice_in_dim(piece, first_row, own_rows, axis=0)
        out["done"] = piece.astype(f32)

    def ff_chain(part, split, out):
        yield from halving(part.ff_keep, part.ff_send, split, out)
        yield from summing(out["piece"], ff_whole, out)
        yield from sharing(out["piece"], split[::-1], out)
        out["done"] = True

    class Chain:
        def __init__(self, steps, *args):
            self.out = {}
            self.steps = steps(*args, self.out)
            self.arriving = next(self.steps)

        def step(self, token):
            if self.arriving is not None:
                arrived = tie(self.arriving, token)
                self.arriving = None
                try:
                    self.arriving = self.steps.send(arrived)
                except StopIteration:
                    pass
                return self.out["token"]
            return token

    back_1 = run(
        functools.partial(
            last_backward_body, sizes=sizes, piece_masks=attn_masks[1], heads=heads
        ),
        "layer_1_backward",
        dict(
            place=place,
            grad=cotangent,
            gain_ff=gain_ff,
            middle=Kept(second.middle),
            ff_in=Kept(second.ff_in),
            **ff_ins(1),
            **attn_back_ins(second, first_ff.x_next, first_ff.a_next),
        ),
        dict(
            **ff_outs,
            **ff_back_outs,
            **attn_back_outs,
            outputs=(matrix, bf16),
            grad_next=Kept(matrix, f32),
            grad_next_low=Kept(matrix, bf16),
            bias_acc=Kept(bias_shape, f32),
        ),
        dict(**mid_scratch, **pulled_scratch, **attn_back_scratch, **ff_scratch),
        micros=10,
    )
    peer_grad_0 = swap(back_1.grad_next_low, 1)
    attn_1 = Chain(attn_chain, back_1, attn_split[1])
    back_0 = run(
        ff_backward_body,
        "layer_0_ff_backward",
        dict(
            grad=Kept(back_1.grad_next),
            gain_ff=gain_ff,
            small_before=Kept(back_1.small),
            middle=Kept(first.middle),
            ff_in=Kept(first.ff_in),
            ff_gate_up=Kept(first_ff.ff_gate_up),
            ff_down=Kept(first_ff.ff_down),
        ),
        dict(**ff_back_outs, grad_mid=Kept(matrix, f32), branch=Kept(matrix, bf16)),
        pulled_scratch,
        after=(peer_in_0, peer_in_1),
        micros=10,
    )
    token = attn_1.step(back_0.branch)
    part_1 = weight_grads(
        1, second, back_1, back_1, cotangent, peer_in_1, peer_cotangent, (token,), 0.1
    )
    ff_1 = Chain(ff_chain, part_1, ff_split[1])
    part_0 = weight_grads(
        0,
        first,
        first_ff,
        back_0,
        Kept(back_1.grad_next_low),
        peer_in_0,
        peer_grad_0,
        (part_1.ff_send,),
        4,
    )
    ff_0 = Chain(ff_chain, part_0, ff_split[0])
    token = ff_1.step(part_0.ff_send)
    token = attn_1.step(token)
    token = ff_0.step(token)
    back_attn_0 = run(
        functools.partial(
            attention_backward_body, sizes=sizes, piece_masks=attn_masks[0], heads=heads
        ),
        "layer_0_attention_backward",
        dict(
            place=place,
            bias_before=Kept(back_1.bias_acc),
            marks=marks,
            buckets=wide_buckets,
            small_before=Kept(back_0.small),
            grad_mid=Kept(back_0.grad_mid),
            branch=Kept(back_0.branch),
            **attn_back_ins(first, start.x, start.a),
        ),
        dict(**attn_back_outs, small=Kept(small_shape, f32), grad_next=(matrix, f32)),
        dict(
            bias_acc=pltpu.VMEM(bias_shape, f32),
            table_rows=pltpu.VMEM((bias_table.shape[0], heads * slots), f32),
            **attn_back_scratch,
        ),
        after=(token,),
        micros=7,
    )
    attn_0 = Chain(attn_chain, back_attn_0, attn_split[0])
    small = Chain(summing, back_attn_0.small, attn_hops[0])
    token = back_attn_0.attn_send
    shape = (2, width, width)
    near_masks = ff_masks[0][: ff_count // 2]
    far_masks = ff_masks[0][ff_count // 2 :]
    done_1 = sums = attn_grads = None
    while True:
        for chain in (ff_0, ff_1, attn_0, small, attn_1):
            token = chain.step(token)
        if sums is None and small.arriving is None:
            sums = run(
                small_body,
                "small_sums",
                dict(packed=Kept(tie(small.out["piece"], token))),
                dict(
                    gain_attn=((2, width), f32),
                    gain_ff=((2, width), f32),
                    embed=((1, width), f32),
                    table=(bias_table.shape, f32),
                ),
                {},
            )
            token = sums.embed
        if attn_grads is None and attn_0.arriving is None and attn_1.arriving is None:
            attn_grads = jnp.stack([attn_0.out["done"], tie(attn_1.out["done"], token)])
            token = attn_grads
        if done_1 is None and ff_1.arriving is None:
            pieces = tie(join(ff_1.out["near"], ff_1.out["far"]), token)
            done_1 = finish(pieces, ff_masks[1], 1, place, shape)
            token = done_1[0]
        if ff_0.arriving is None:
            break
    near_0 = finish(ff_0.out["near"], near_masks, 0, place, shape, done_1)
    done = finish(ff_0.out["far"], far_masks, 0, place, shape, near_0)
    return (
        back_1.outputs.reshape(inputs.shape),
        back_attn_0.grad_next.reshape(inputs.shape),
        attn_grads[:, :, :inner],
        attn_grads[:, :, inner : 2 * inner],
        attn_grads[:, :, 2 * inner : 3 * inner],
        jnp.swapaxes(attn_grads[:, :, 3 * inner :], 1, 2),
        *done,
        sums.gain_attn,
        sums.gain_ff,
        sums.table,
        sums.embed[0],
    )


def solution(mesh):
    placed = (
        P(("dp", "tensor"), None, None),
        P(("dp", "tensor"), None, None),
        P(("dp", "tensor"), None),
        P(("dp", "tensor"), None),
        P(),
        P(),
        P(None, ("dp", "tensor"), None),
        P(None, ("dp", "tensor"), None),
        P(None, ("dp", "tensor"), None),
        P(None, None, ("dp", "tensor")),
        P(None, None, "tensor"),
        P(None, None, "tensor"),
        P(None, "tensor", None),
        P(),
        P(),
        P(),
    )
    return jax.shard_map(
        functools.partial(on_device, dp_size=mesh.shape["dp"]),
        mesh=mesh,
        in_specs=placed,
        out_specs=(
            P(("dp", "tensor"), None, None),
            P(("dp", "tensor"), None, None),
            P(None, ("dp", "tensor"), None),
            P(None, ("dp", "tensor"), None),
            P(None, ("dp", "tensor"), None),
            P(None, None, ("dp", "tensor")),
            P(None, None, "tensor"),
            P(None, None, "tensor"),
            P(None, "tensor", None),
            P(),
            P(),
            P(),
            P(),
        ),
        check_vma=False,
    )
```

```python
import functools
import types

import jax
import jax.numpy as jnp
from jax import lax
from jax.experimental import pallas as pl
from jax.experimental.pallas import tpu as pltpu
from jax.sharding import PartitionSpec as P

norm_eps = 1e-06
masked_score = -1e30
bf16 = jnp.bfloat16
f32 = jnp.float32
axes = ("dp", "tensor")
vmem_bytes = 32 * 1024 * 1024
raw_names = ("attn_near", "attn_far", "ff_near", "ff_far", "w_gate", "w_up", "w_down")


def dot_nn(left, right):
    return lax.dot_general(left, right, (((1,), (0,)), ((), ())), preferred_element_type=f32)


def dot_nt(left, right):
    return lax.dot_general(left, right, (((1,), (1,)), ((), ())), preferred_element_type=f32)


def dot_tn(left, right):
    return lax.dot_general(left, right, (((0,), (0,)), ((), ())), preferred_element_type=f32)


def inverse_rms(values):
    return lax.rsqrt(jnp.mean(values * values, axis=-1, keepdims=True) + norm_eps)


def norm_back(values, gain, grad_out):
    scale = inverse_rms(values)
    pulled = grad_out * gain
    mean_part = jnp.mean(pulled * values, axis=-1, keepdims=True)
    grad_in = scale * pulled - values * (scale * scale * scale) * mean_part
    return grad_in, jnp.sum(grad_out * values * scale, axis=0, keepdims=True)


def gelu_terms(gate_act):
    square = gate_act * gate_act
    bent = jnp.tanh(0.7978845608028654 * gate_act * (1.0 + 0.044715 * square))
    half = 0.5 * (1.0 + bent)
    slope = half + 0.5 * gate_act * (1.0 - bent * bent) * (
        0.7978845608028654 * (1.0 + 3.0 * 0.044715 * square)
    )
    return gate_act * half, slope


def cost(micros):
    return pl.CostEstimate(flops=int(micros * 1.15e9), bytes_accessed=0, transcendentals=0)


def run(body, name, ins, outs, scratch, after=(), micros=1):
    in_names, out_names, scratch_names = list(ins), list(outs), list(scratch)
    direct = {n for n in in_names if n == "place" or n in raw_names or isinstance(ins[n], Kept)}
    staged = [n for n in in_names if n not in direct]
    copied = [n for n in out_names if not isinstance(outs[n], Kept)]
    in_sems = {n: i for i, n in enumerate(staged)}
    out_sems = {n: i for i, n in enumerate(copied)}

    def kernel(*refs):
        refs = list(refs)
        sources = dict(zip(in_names, refs))
        refs = refs[len(in_names) + len(after) :]
        targets = dict(zip(out_names, refs))
        refs = refs[len(out_names) :]
        space = dict(zip(scratch_names, refs))
        refs = refs[len(scratch_names) :]
        buffers = dict(zip(staged + copied, refs))
        sems_in, sems_out = refs[len(staged) + len(copied) :]
        kept = {n: ref for n, ref in targets.items() if n not in out_sems}
        r = types.SimpleNamespace(**space, **buffers, **kept)
        for n in direct:
            setattr(r, n, sources[n])

        def copy_in(n):
            return pltpu.make_async_copy(sources[n], buffers[n], sems_in.at[in_sems[n]])

        def copy_out(n):
            return pltpu.make_async_copy(buffers[n], targets[n], sems_out.at[out_sems[n]])

        r.fetch = lambda *names: [copy_in(n).start() for n in names if n in in_sems]
        r.need = lambda *names: [copy_in(n).wait() for n in names if n in in_sems]
        r.write = lambda *names: [copy_out(n).start() for n in names if n in out_sems]
        r.drain = lambda *names: [copy_out(n).wait() for n in names if n in out_sems]
        body(r)

    def in_space(n):
        if n == "place":
            return pltpu.SMEM
        return pltpu.VMEM if isinstance(ins[n], Kept) else pl.ANY

    results = pl.pallas_call(
        kernel,
        name=name,
        in_specs=[pl.BlockSpec(memory_space=in_space(n)) for n in in_names]
        + [pl.BlockSpec(memory_space=pl.ANY) for _ in after],
        out_specs=[
            pl.BlockSpec(memory_space=pltpu.VMEM if isinstance(out, Kept) else pl.ANY)
            for out in outs.values()
        ],
        out_shape=[
            pltpu.VMEM(*out.what) if isinstance(out, Kept) else jax.ShapeDtypeStruct(*out)
            for out in outs.values()
        ],
        scratch_shapes=list(scratch.values())
        + [pltpu.VMEM(ins[n].shape, ins[n].dtype) for n in staged]
        + [pltpu.VMEM(*outs[n]) for n in copied]
        + [
            pltpu.SemaphoreType.DMA((max(1, len(staged)),)),
            pltpu.SemaphoreType.DMA((max(1, len(copied)),)),
        ],
        compiler_params=pltpu.CompilerParams(vmem_limit_bytes=vmem_bytes),
        cost_estimate=cost(micros),
    )(
        *[
            pltpu.with_memory_space_constraint(value.what, pltpu.VMEM)
            if isinstance(value, Kept)
            else value
            for value in ins.values()
        ],
        *after,
    )
    return types.SimpleNamespace(**dict(zip(outs, results)))


class Kept:
    def __init__(self, *what):
        self.what = what[0] if len(what) == 1 else what


def keep_all(names):
    return {name: Kept(value) for name, value in names.items()}


def chunks(extent, size):
    size = min(size, extent)
    return [slice(start, start + size) for start in range(0, extent, size)]


def attention_copies(r, masks, rows):
    copies = []
    for idx, mask in enumerate(masks):
        half, at = divmod(idx, max(1, len(masks) // 2))
        source = (r.attn_near if half == 0 else r.attn_far).at[pl.ds(at * rows, rows)]
        place = (r.place[0] ^ mask) * rows if len(masks) > 1 else 0
        target = r.attn_w.at[pl.ds(pl.multiple_of(place, rows), rows)]
        copies.append(pltpu.make_async_copy(source, target, r.attn_sem))
    return copies


def ff_copies(r, layer_idx):
    width = r.ff_down.shape[-1]
    copies = []
    for k, own in enumerate((r.w_gate, r.w_up)):
        target = r.ff_gate_up.at[0, :, pl.ds(k * width, width)]
        copies.append(pltpu.make_async_copy(own.at[layer_idx], target, r.ff_sem))
    copies.append(pltpu.make_async_copy(r.w_down.at[layer_idx], r.ff_down.at[0], r.ff_sem))
    part = r.ff_near.shape[1]
    for source, base in ((r.ff_near, 0), (r.ff_far, 1)):
        for m in range(2):
            rows = pl.ds(pl.multiple_of((r.place[1] ^ (2 * m + base)) * part, part), part)
            for k in range(2):
                target = r.ff_gate_up.at[1, rows, pl.ds(k * width, width)]
                copies.append(pltpu.make_async_copy(source.at[3 * m + k], target, r.ff_sem))
            copies.append(
                pltpu.make_async_copy(source.at[3 * m + 2], r.ff_down.at[1, rows], r.ff_sem)
            )
    return copies


def start_all(copies):
    for copy in copies:
        copy.start()


def wait_all(sem, *buffers):
    for whole in buffers:
        pltpu.make_async_copy(whole, whole, sem).wait()


def lane_low(rows):
    return lax.broadcasted_iota(jnp.int32, (rows, 128), 1) < 64


def lane_halves():
    low = lane_low(1).astype(f32)
    return low.astype(bf16), (1.0 - low).astype(bf16)


def pair_blocks(rows, low, high):
    return jnp.concatenate([rows * low, rows * high], axis=0)


def own_blocks(both, is_low):
    half = both.shape[0] // 2
    return jnp.where(is_low, both[:half], both[half:]).astype(bf16)


def attention_forward(r, x_ref, a_ref, sizes, layer_idx):
    series, slots, inner = sizes
    rows = series * slots
    for part in chunks(rows, 256):
        r.qkv[part, :] = dot_nn(a_ref[part, :], r.attn_w[:, : 3 * inner]).astype(bf16)
    is_low = lane_low(slots)
    low, high = lane_halves()
    for s in range(series):
        here = slice(s * slots, (s + 1) * slots)
        keep = r.mask[here, :] == 1
        for start in range(0, inner, 128):
            at = slice(start, start + 128)
            query = r.qkv[here, at]
            keys = r.qkv[here, inner + start : inner + start + 128]
            scores = dot_nt(keys, pair_blocks(query, low, high)) + r.bias[:, at]
            scores = jnp.where(keep, scores, masked_score)
            exps = jnp.exp(scores - jnp.max(scores, axis=0, keepdims=True))
            r.probs[here, at] = exps / jnp.sum(exps, axis=0, keepdims=True)
    for s in range(series):
        here = slice(s * slots, (s + 1) * slots)
        for start in range(0, inner, 128):
            at = slice(start, start + 128)
            values = r.qkv[here, 2 * inner + start : 2 * inner + start + 128]
            both = dot_tn(r.probs[here, at].astype(bf16), values)
            r.heads[here, at] = own_blocks(both, is_low)
    gain = r.gain_ff[layer_idx : layer_idx + 1, :]
    for part in chunks(rows, 256):
        middle = x_ref[part, :] + dot_nt(r.heads[part, :], r.attn_w[:, 3 * inner :])
        r.middle[part, :] = middle
        r.ff_in[part, :] = (middle * inverse_rms(middle) * gain).astype(bf16)


def prepare_body(r):
    r.fetch("inputs", "marks", "embed", "gain_attn", "buckets", "table")
    r.need("inputs", "marks", "embed", "gain_attn", "buckets", "table")
    x = jnp.where(r.marks[:, 0:1] == 1, r.inputs[...].astype(f32), r.embed[...])
    r.x[...] = x
    r.a[...] = (x * inverse_rms(x) * r.gain_attn[0:1, :]).astype(bf16)
    buckets = r.buckets[...]
    bias = jnp.zeros(buckets.shape, f32)
    for idx in range(r.table.shape[0]):
        bias = jnp.where(buckets == idx, r.table[idx : idx + 1, :], bias)
    r.bias[...] = bias
    r.mask[...] = jnp.broadcast_to(r.marks[:, 1:2], r.mask.shape)
    r.write("x", "a", "bias", "mask")
    r.drain("x", "a", "bias", "mask")


def attention_body(r, sizes, masks, grain, layer_idx):
    start_all(attention_copies(r, masks, grain))
    r.fetch("gain_ff")
    r.need("gain_ff")
    wait_all(r.attn_sem, r.attn_w)
    attention_forward(r, r.x, r.a, sizes, layer_idx)


def ff_body(r):
    start_all(ff_copies(r, 0))
    r.fetch("gain_attn")
    r.need("gain_attn")
    wait_all(r.ff_sem, r.ff_gate_up, r.ff_down)
    width = r.middle.shape[1]
    for part in chunks(r.middle.shape[0], 256):
        x_next = r.middle[part, :]
        for half in range(2):
            both = dot_nn(r.ff_in[part, :], r.ff_gate_up[half])
            hidden = (gelu_terms(both[:, :width])[0] * both[:, width:]).astype(bf16)
            x_next = x_next + dot_nn(hidden, r.ff_down[half])
        r.x_next[part, :] = x_next
        r.a_next[part, :] = (x_next * inverse_rms(x_next) * r.gain_attn[1:2, :]).astype(bf16)


def ff_backward(r, layer_idx, last):
    rows, width = r.middle.shape
    r.fetch("grad", "gain_ff")
    if last:
        start_all(ff_copies(r, layer_idx))
    r.need("grad", "gain_ff")
    if last:
        wait_all(r.ff_sem, r.ff_gate_up, r.ff_down)
    gain_ff = r.gain_ff[layer_idx : layer_idx + 1, :]
    gain_total = jnp.zeros((1, width), f32)
    for part in chunks(rows, 256):
        grad = r.grad[part, :].astype(f32)
        rounded = grad.astype(bf16)
        ff_rows = r.ff_in[part, :]
        back = None
        middle = r.middle[part, :]
        total = middle
        for half in range(2):
            both = dot_nn(ff_rows, r.ff_gate_up[half])
            grad_hidden = dot_nt(rounded, r.ff_down[half])
            gate_act, up_act = both[:, :width], both[:, width:]
            mixed, slope = gelu_terms(gate_act)
            hidden = (mixed * up_act).astype(bf16)
            if last or half == 0:
                r.hidden[half, part, :] = hidden
                held = r.grad_gate_up.at[half, part]
            else:
                held = r.pulled
            held[:, :width] = (grad_hidden * up_act * slope).astype(bf16)
            held[:, width:] = (grad_hidden * mixed).astype(bf16)
            pulled = held[...]
            if last:
                total = total + dot_nn(hidden, r.ff_down[half])
            term = dot_nt(pulled, r.ff_gate_up[half])
            back = term if back is None else back + term
        if last:
            r.outputs[part, :] = total.astype(bf16)
        grad_mid, gain_part = norm_back(middle, gain_ff, back)
        gain_total += gain_part
        grad_mid = grad + grad_mid
        r.grad_mid[part, :] = grad_mid
        r.branch[part, :] = grad_mid.astype(bf16)
    if last:
        r.write("outputs")
    return gain_total


def attention_backward(r, sizes, layer_idx, last, piece_masks, heads):
    series, slots, inner = sizes
    rows = series * slots
    width = r.x.shape[1]
    r.fetch("gain_attn")
    if not last:
        r.fetch("marks", "buckets")
    for part in chunks(rows, 256):
        r.grad_heads[part, :] = dot_nn(r.branch[part, :], r.attn_w[:, 3 * inner :]).astype(bf16)
    is_low = lane_low(slots)
    low, high = lane_halves()
    for start in range(0, inner, 128):
        at = slice(start, start + 128)
        bias_total = jnp.zeros((slots, 128), f32) if last else r.bias_before[:, at]
        for s in range(series):
            here = slice(s * slots, (s + 1) * slots)
            probs = r.probs[here, at]
            values = r.qkv[here, 2 * inner + start : 2 * inner + start + 128]
            grad_probs = dot_nt(values, pair_blocks(r.grad_heads[here, at], low, high))
            inner_sum = jnp.sum(probs * grad_probs, axis=0, keepdims=True)
            grad_scores = (probs * (grad_probs - inner_sum)).astype(bf16)
            r.grad_scores[here, at] = grad_scores
            bias_total = bias_total + grad_scores.astype(f32)
        r.bias_acc[:, at] = bias_total
    for s in range(series):
        here = slice(s * slots, (s + 1) * slots)
        for start in range(0, inner, 128):
            at = slice(start, start + 128)
            key_at = slice(inner + start, inner + start + 128)
            value_at = slice(2 * inner + start, 2 * inner + start + 128)
            grad_scores = r.grad_scores[here, at]
            r.grad_qkv[here, key_at] = dot_nn(
                grad_scores, pair_blocks(r.qkv[here, at], low, high)
            ).astype(bf16)
            r.grad_qkv[here, value_at] = dot_nn(
                r.probs[here, at].astype(bf16), pair_blocks(r.grad_heads[here, at], low, high)
            ).astype(bf16)
            r.grad_qkv[here, at] = own_blocks(dot_tn(grad_scores, r.qkv[here, key_at]), is_low)
    r.attn_grad[:, : 3 * inner] = dot_tn(r.a[...], r.grad_qkv[...])
    r.attn_grad[:, 3 * inner :] = dot_tn(r.branch[...], r.heads[...])
    scatter_pieces(r.attn_grad, r.attn_keep, r.attn_send, piece_masks, r.place[2])
    r.need("gain_attn")
    if not last:
        r.need("marks", "buckets")
    gain_attn = r.gain_attn[layer_idx : layer_idx + 1, :]
    gain_total = jnp.zeros((1, width), f32)
    embed_total = jnp.zeros((1, width), f32)
    for part in chunks(rows, 256):
        grad_normed = dot_nt(r.grad_qkv[part, :], r.attn_w[:, : 3 * inner])
        grad_in, gain_part = norm_back(r.x[part, :], gain_attn, grad_normed)
        gain_total += gain_part
        grad_in = r.grad_mid[part, :] + grad_in
        if last:
            r.grad_next[part, :] = grad_in
            r.grad_next_low[part, :] = grad_in.astype(bf16)
        else:
            seen = r.marks[part, 0:1] == 1
            r.grad_next[part, :] = jnp.where(seen, grad_in, 0.0)
            embed_total += jnp.sum(jnp.where(seen, 0.0, grad_in), axis=0, keepdims=True)
    r.write("grad_next")
    if not last:
        put_row(r.small, 4, embed_total)
        head_size = inner // heads
        for idx in range(r.table_rows.shape[0]):
            chosen = jnp.where(r.buckets[...] == idx, r.bias_acc[...], 0.0)
            r.table_rows[idx : idx + 1, :] = jnp.sum(chosen, axis=0, keepdims=True)
        lane = lax.broadcasted_iota(jnp.int32, (r.table_rows.shape[0], 128), 1)
        table = jnp.zeros(lane.shape, f32)
        for head in range(heads):
            cut = r.table_rows[:, head * head_size : (head + 1) * head_size]
            table = jnp.where(lane == head, jnp.sum(cut, axis=1, keepdims=True), table)
        r.small[:heads, : table.shape[0]] = jnp.transpose(table)[:heads, :]
    r.drain("grad_next")
    return gain_total


def two_parts(values):
    high = values.astype(bf16).astype(f32)
    return high, (values - high).astype(bf16).astype(f32)


def last_backward_body(r, sizes, piece_masks, ff_masks, heads):
    r.small[...] = jnp.zeros(r.small.shape, f32)
    put_row(r.small, 3, ff_backward(r, 1, True))
    width = r.middle.shape[1]
    for half in range(2):
        r.ff_grad[half, :, : 2 * width] = dot_tn(r.ff_in[...], r.grad_gate_up[half])
        r.ff_grad[half, :, 2 * width :] = dot_tn(r.hidden[half], r.grad[...])
    count = len(ff_masks)
    grain = r.ff_keep.shape[1]
    for idx, mask in enumerate(ff_masks):
        target = r.ff_keep if idx < count // 2 else r.ff_send
        rows = pl.ds(pl.multiple_of((r.place[3] ^ (mask // 2)) * grain, grain), grain)
        target[idx % (count // 2)] = r.ff_grad[mask % 2, rows, :].astype(bf16)
    put_row(r.small, 1, attention_backward(r, sizes, 1, True, piece_masks, heads))
    r.drain("outputs")


def ff_backward_body(r):
    r.small[...] = r.small_before[...]
    put_row(r.small, 2, ff_backward(r, 0, False))


def attention_backward_body(r, sizes, piece_masks, heads):
    r.small[...] = r.small_before[...]
    put_row(r.small, 0, attention_backward(r, sizes, 0, False, piece_masks, heads))
    high, low = two_parts(r.small[...])
    last = r.attn_send.shape[0] - 1
    r.attn_send[last] = jnp.concatenate([high, low], axis=0).astype(bf16)
    r.small[...] = high + low


def put_row(packed, which, row):
    first, width = packed.shape[0] - 2, row.shape[1]
    at = which % 3 * width
    packed[first + which // 3 : first + which // 3 + 1, at : at + width] = row


def scatter_pieces(whole, keep, send, masks, place):
    count = len(masks)
    grain = whole.shape[0] // count
    for idx, mask in enumerate(masks):
        target = keep if idx < count // 2 else send
        source = pl.ds(pl.multiple_of((place ^ mask) * grain, grain), grain)
        target[idx % (count // 2)] = whole[source, :].astype(bf16)


def weight_body(r, piece_masks):
    width = r.ff_in.shape[1]
    rows = r.ff_in.shape[0]
    r.fetch("peer_in", "peer_grad")
    r.fetch("ff_in", "grad_gate_up", "hidden", "grad")
    r.need("peer_in", "peer_grad")
    for part in chunks(rows, 256):
        both = dot_nn(r.peer_in[part, :], r.ff_gate_up[0])
        grad_hidden = dot_nt(r.peer_grad[part, :], r.ff_down[0])
        gate_act, up_act = both[:, :width], both[:, width:]
        mixed, slope = gelu_terms(gate_act)
        r.peer_gate_up[part, :width] = (grad_hidden * up_act * slope).astype(bf16)
        r.peer_gate_up[part, width:] = (grad_hidden * mixed).astype(bf16)
        r.peer_hidden[part, :] = (mixed * up_act).astype(bf16)
    r.need("ff_in", "grad_gate_up", "hidden", "grad")
    r.ff_grad[:, : 2 * width] = dot_tn(r.ff_in[...], r.grad_gate_up[0]) + dot_tn(
        r.peer_in[...], r.peer_gate_up[...]
    )
    r.ff_grad[:, 2 * width :] = dot_tn(r.hidden[0], r.grad[...]) + dot_tn(
        r.peer_hidden[...], r.peer_grad[...]
    )
    scatter_pieces(r.ff_grad, r.ff_keep, r.ff_send, piece_masks, r.place[3])
    r.write("ff_send", "ff_keep")
    r.drain("ff_send", "ff_keep")


def finish(pieces, masks, layer_idx, place, shape, before=()):
    grain, width = pieces.shape[1], shape[-1]
    count = len(before)

    def kernel(place_ref, source, *refs):
        outs = refs[count : count + 3]
        stage, out_sem = refs[count + 3 :]
        for idx, mask in enumerate(masks):
            rows = pl.ds(pl.multiple_of((place_ref[3] ^ mask) * grain, grain), grain)
            for k, out in enumerate(outs):
                stage[k, idx] = source[idx, :, k * width : (k + 1) * width].astype(f32)
                pltpu.make_async_copy(stage.at[k, idx], out.at[layer_idx, rows], out_sem).start()
        pltpu.make_async_copy(stage, stage, out_sem).wait()

    return pl.pallas_call(
        kernel,
        name="layer_%d_ff_grads" % layer_idx,
        in_specs=[
            pl.BlockSpec(memory_space=pltpu.SMEM),
            pl.BlockSpec(memory_space=pltpu.VMEM),
        ]
        + [pl.BlockSpec(memory_space=pl.ANY)] * count,
        out_specs=[pl.BlockSpec(memory_space=pl.ANY)] * 3,
        out_shape=[jax.ShapeDtypeStruct(shape, f32)] * 3,
        input_output_aliases={2 + k: k for k in range(count)},
        scratch_shapes=[
            pltpu.VMEM((3, len(masks), grain, width), f32),
            pltpu.SemaphoreType.DMA,
        ],
        compiler_params=pltpu.CompilerParams(vmem_limit_bytes=vmem_bytes),
        cost_estimate=cost(3),
    )(place, pltpu.with_memory_space_constraint(pieces, pltpu.VMEM), *before)


def small_body(r):
    width = r.embed.shape[1]
    heads = r.table.shape[1]
    outs = ((r.gain_attn, 0), (r.gain_attn, 1), (r.gain_ff, 0), (r.gain_ff, 1), (r.embed, 0))
    for which, (out, row) in enumerate(outs):
        first = r.packed.shape[0] - 2 + which // 3
        at = which % 3 * width
        out[row : row + 1, :] = r.packed[first : first + 1, at : at + width]
    r.table[...] = jnp.transpose(r.packed[:, :128])[: r.table.shape[0], :heads]
    r.write("gain_attn", "gain_ff", "embed", "table")
    r.drain("gain_attn", "gain_ff", "embed", "table")


def cut_body(r):
    rows = r.quarters.shape[2]
    at = pl.ds(pl.multiple_of(r.place[1] * rows, rows), rows)
    copies = [
        pltpu.make_async_copy(w.at[layer_idx, at], r.quarters.at[layer_idx, k], r.cut_sem)
        for layer_idx in range(2)
        for k, w in enumerate((r.w_gate, r.w_up, r.w_down))
    ]
    start_all(copies)
    wait_all(r.cut_sem, r.quarters)


def order_masks(hops):
    masks = [0]
    for hop in reversed(hops):
        masks = masks + [mask ^ hop for mask in masks]
    return masks


def tie(value, *others):
    return lax.optimization_barrier((value, *others))[0]


def on_device(
    inputs,
    cotangent,
    attention_mask,
    patch_valid,
    buckets,
    mask_embed,
    w_query,
    w_key,
    w_value,
    w_output,
    w_gate,
    w_up,
    w_down,
    gain_attn,
    gain_ff,
    bias_table,
    dp_size,
):
    series, slots, width = inputs.shape
    heads = bias_table.shape[1]
    inner = w_query.shape[2]
    rows = series * slots
    sizes = (series, slots, inner)
    matrix = (rows, width)
    devices = 2 * dp_size
    dp_at = lax.axis_index("dp")
    device_at = 2 * dp_at + lax.axis_index("tensor")
    cotangent = cotangent.reshape(matrix)

    def swap(array, mask):
        return lax.ppermute(array, axes, [(n, n ^ mask) for n in range(devices)])

    def join(left, right):
        return jnp.concatenate([left, right], axis=0)

    bits = [1 << k for k in range(devices.bit_length() - 1)]

    attn_grain = max(16, width // devices)
    attn_count = width // attn_grain
    ff_grain = max(16, width // dp_size)
    ff_count = width // ff_grain
    quarter_at = lax.rem(dp_at, 4)
    place = jnp.stack(
        [
            device_at,
            quarter_at,
            device_at // (devices // attn_count),
            lax.rem(dp_at, ff_count),
        ]
    ).astype(jnp.int32)

    quarter = width // 4
    packed = jnp.concatenate([w_query, w_key, w_value, jnp.swapaxes(w_output, 1, 2)], axis=2)
    ff_blocks = run(
        cut_body,
        "cut_quarters",
        dict(place=place, w_gate=w_gate, w_up=w_up, w_down=w_down),
        dict(quarters=Kept((2, 3, quarter, width), bf16)),
        dict(cut_sem=pltpu.SemaphoreType.DMA),
    ).quarters
    own_rows = packed.shape[1]
    direct = own_rows % 16 == 0
    far = bits[2:]

    def prepare(token):
        table, marked, kept, near = (
            tie(array, token) for array in (bias_table, patch_valid, attention_mask, buckets)
        )
        wide_buckets = jnp.tile(near.T, (1, heads))
        wide_table = jnp.repeat(table, slots, axis=1)
        marks = jnp.stack([marked.reshape(rows), kept.reshape(rows)], axis=1)
        result = run(
            prepare_body,
            "prepare",
            dict(
                inputs=inputs.reshape(matrix),
                marks=marks,
                embed=mask_embed[None, :],
                gain_attn=gain_attn,
                buckets=wide_buckets,
                table=wide_table,
            ),
            dict(
                x=Kept(matrix, f32),
                a=Kept(matrix, bf16),
                bias=Kept((slots, heads * slots), f32),
                mask=Kept((rows, 128), jnp.int32),
            ),
            {},
            micros=3,
        )
        return result, wide_buckets, marks

    if direct:
        hops_0 = [1] + far[2:] + far[:2] + [2]
        hops_1 = far[2:] + far[:2] + [1, 2]
        block_0, block_1 = packed[0], packed[1]
        got_1 = swap(block_1, hops_1[0])
        got_0 = swap(block_0, hops_0[0])
        ff_quarter = swap(tie(ff_blocks, got_0), 1)
        block_0 = join(block_0, got_0)
        block_1 = join(block_1, tie(got_1, block_0))
        for hop_0, hop_1 in zip(hops_0[1:-2], hops_1[1:-2]):
            got_1, got_0 = swap(block_1, hop_1), swap(block_0, hop_0)
            if hop_1 == hops_1[1]:
                start, wide_buckets, marks = prepare(block_1)
            block_0 = join(block_0, got_0)
            block_1 = join(block_1, tie(got_1, block_0))
        got_0 = swap(block_0, hops_0[-2])
        got_1 = swap(block_1, hops_1[-2])
        ff_0 = tie(ff_quarter[0], block_1)
        got_ff_0 = swap(ff_0, 4)
        block_0 = join(block_0, tie(got_0, start.a, got_ff_0))
        block_1 = join(block_1, tie(got_1, block_0))
        ff_0 = join(ff_0, tie(got_ff_0, block_1))
        got_ff_1 = swap(tie(ff_quarter[1], ff_0), 4)
        far_0 = swap(block_0, 2)
        attn_pieces = [
            (block_0, far_0, order_masks(hops_0[::-1])),
            (block_1, swap(tie(block_1, far_0), 2), order_masks(hops_1[::-1])),
        ]
        after_first = (attn_pieces[1][1],)
    else:
        ff_quarter = swap(ff_blocks, 1)
        ff_0 = join(ff_quarter[0], swap(ff_quarter[0], 4))
        start, wide_buckets, marks = prepare(packed)
        whole = lax.all_gather(packed[0], axes, axis=0, tiled=True)
        attn_pieces = [(whole, whole, [0])]
        whole = lax.all_gather(packed[1], axes, axis=0, tiled=True)
        attn_pieces.append((whole, whole, [0]))
        after_first = ()
    ff_pieces = [(ff_0, swap(ff_0, 2))]

    def attn_ins(layer_idx):
        near, far, masks = attn_pieces[layer_idx]
        return dict(attn_near=Kept(near), attn_far=Kept(far)), masks

    def ff_ins(layer_idx):
        near, far = ff_pieces[layer_idx]
        return dict(w_gate=w_gate, w_up=w_up, w_down=w_down, ff_near=Kept(near), ff_far=Kept(far))

    attn_scratch = dict(attn_sem=pltpu.SemaphoreType.DMA)
    ff_scratch = dict(ff_sem=pltpu.SemaphoreType.DMA)
    ff_outs = dict(
        ff_gate_up=Kept((2, width, 2 * width), bf16), ff_down=Kept((2, width, width), bf16)
    )
    grain = own_rows if direct else width
    attn_outs = dict(
        attn_w=Kept((width, 4 * inner), bf16),
        qkv=Kept((rows, 3 * inner), bf16),
        probs=Kept((rows, heads * slots), f32),
        heads=Kept((rows, inner), bf16),
        middle=Kept(matrix, f32),
        ff_in=Kept(matrix, bf16),
    )

    def attention(layer_idx, x, a, after=(), micros=5):
        pieces, masks = attn_ins(layer_idx)
        return run(
            functools.partial(
                attention_body, sizes=sizes, masks=masks, grain=grain, layer_idx=layer_idx
            ),
            "layer_%d_attention" % layer_idx,
            dict(
                place=place,
                x=Kept(x),
                a=Kept(a),
                bias=Kept(start.bias),
                mask=Kept(start.mask),
                gain_ff=gain_ff,
                **pieces,
            ),
            attn_outs,
            attn_scratch,
            after=after,
            micros=micros,
        )

    first = attention(0, start.x, start.a, micros=10)
    peer_in_0 = swap(first.ff_in, 1)
    first_ff = run(
        ff_body,
        "layer_0_ff",
        dict(
            place=place,
            middle=Kept(first.middle),
            ff_in=Kept(first.ff_in),
            gain_attn=gain_attn,
            **ff_ins(0),
        ),
        dict(**ff_outs, x_next=Kept(matrix, f32), a_next=Kept(matrix, bf16)),
        ff_scratch,
        after=after_first,
        micros=0.1,
    )
    if direct:
        ff_1 = join(ff_quarter[1], tie(got_ff_1, first_ff.a_next))
    else:
        ff_1 = join(ff_quarter[1], swap(ff_quarter[1], 4))
    ff_pieces.append((ff_1, swap(ff_1, 2)))
    second = attention(1, first_ff.x_next, first_ff.a_next, micros=0.1)

    attn_low = devices // attn_count
    attn_hops = ([2, 1] + bits[2:], [2, 1] + bits[2:])
    attn_split = [[hop for hop in hops if hop >= attn_low] for hops in attn_hops]
    attn_whole = [hop for hop in bits if hop < attn_low]
    attn_masks = [[mask // attn_low for mask in order_masks(hops)] for hops in attn_split]
    ff_hops = ([2] + bits[3:] + bits[2:3], [2] + bits[2:3] + [1] + bits[3:])
    ff_split = [[hop for hop in hops if hop // 2 < ff_count] for hops in ff_hops]
    ff_whole = [hop for hop in bits[1:] if hop // 2 >= ff_count]
    ff_share = [[hop for hop in hops if hop > 1] for hops in ff_split]
    ff_masks = [order_masks(hops) for hops in ff_split]
    place_masks = [[mask // 2 for mask in order_masks(hops)] for hops in ff_share]
    attn_half = (attn_count // 2, attn_grain, 4 * inner)
    ff_half = (ff_count // 2, ff_grain, 3 * width)
    small_shape = (heads + 2, 3 * width)

    attn_back_outs = dict(attn_keep=Kept(attn_half, bf16), attn_send=Kept(attn_half, bf16))
    attn_back_scratch = dict(
        grad_heads=pltpu.VMEM((rows, inner), bf16),
        grad_qkv=pltpu.VMEM((rows, 3 * inner), bf16),
        grad_scores=pltpu.VMEM((rows, heads * slots), bf16),
        attn_grad=pltpu.VMEM((width, 4 * inner), f32),
    )
    mid_scratch = dict(grad_mid=pltpu.VMEM(matrix, f32), branch=pltpu.VMEM(matrix, bf16))
    pulled_scratch = dict(pulled=pltpu.VMEM((256, 2 * width), bf16))
    bias_shape = (slots, heads * slots)

    def attn_back_ins(kept, x, a):
        return dict(
            x=Kept(x),
            a=Kept(a),
            gain_attn=gain_attn,
            attn_w=Kept(kept.attn_w),
            qkv=Kept(kept.qkv),
            probs=Kept(kept.probs),
            heads=Kept(kept.heads),
        )

    def add(left, right):
        return (left.astype(f32) + right.astype(f32)).astype(bf16)

    def halving(keep, send, hops, out):
        for step, hop in enumerate(hops):
            got = yield swap(send, hop)
            if step + 1 < len(hops):
                cut = keep.shape[0] // 2
                send = add(keep[cut:], got[cut:])
                keep = add(keep[:cut], got[:cut])
                out["token"] = send
            else:
                out["token"] = keep = add(keep, got)
        out["piece"] = keep

    def summing(piece, hops, out):
        for hop in hops:
            got = yield swap(piece, hop)
            out["token"] = piece = add(piece, got)
        out["piece"] = piece

    def sharing(piece, hops, out):
        for step, hop in enumerate(hops):
            got = yield swap(piece, hop)
            if step + 1 < len(hops):
                out["token"] = piece = join(piece, got)
            else:
                out["token"] = got
        out["near"], out["far"] = piece, got

    def rounded(values):
        return lax.reduce_precision(values, exponent_bits=8, mantissa_bits=7)

    def with_small(pieces, small):
        high = rounded(small)
        low = rounded(small - high)
        parts = join(high, low).astype(bf16)[None]
        return join(pieces, parts), high + low

    def add_small(small, got):
        parts = got[-1].astype(f32)
        return small + (parts[: small.shape[0]] + parts[small.shape[0] :])

    def attn_chain(part, layer_idx, out):
        small = part.small if layer_idx == 0 else None
        keep, send = part.attn_keep, part.attn_send
        hops = attn_split[layer_idx] + attn_whole
        for step, hop in enumerate(hops):
            got = yield swap(send, hop)
            if small is not None:
                small = add_small(small, got)
                got = got[:-1]
            if step + 1 < len(attn_split[layer_idx]):
                half = keep.shape[0] // 2
                send = add(keep[half:], got[half:])
                keep = add(keep[:half], got[:half])
            else:
                send = keep = add(keep, got)
            if small is not None and step + 1 < len(hops):
                send, small = with_small(send, small)
            out["token"] = send
        piece = keep[0]
        if own_rows < attn_grain:
            first_row = lax.rem(device_at, attn_low) * own_rows
            piece = lax.dynamic_slice_in_dim(piece, first_row, own_rows, axis=0)
        out["done"] = piece.astype(f32)
        out["small"] = small

    def ff_chain(part, layer_idx, out):
        yield from halving(part.ff_keep, part.ff_send, ff_split[layer_idx], out)
        yield from summing(out["piece"], ff_whole, out)
        yield from sharing(out["piece"], ff_share[layer_idx][::-1], out)

    class Chain:
        def __init__(self, steps, *args):
            self.out = {}
            self.steps = steps(*args, self.out)
            self.arriving = next(self.steps)

        def step(self, token, *others):
            if self.arriving is not None:
                arrived = tie(self.arriving, token, *others)
                self.arriving = None
                try:
                    self.arriving = self.steps.send(arrived)
                except StopIteration:
                    pass
                return self.out["token"]
            return token

    back_1 = run(
        functools.partial(
            last_backward_body,
            sizes=sizes,
            piece_masks=attn_masks[1],
            ff_masks=ff_masks[1],
            heads=heads,
        ),
        "layer_1_backward",
        dict(
            place=place,
            grad=cotangent,
            gain_ff=gain_ff,
            middle=Kept(second.middle),
            ff_in=Kept(second.ff_in),
            **ff_ins(1),
            **attn_back_ins(second, first_ff.x_next, first_ff.a_next),
        ),
        dict(
            ff_keep=Kept((ff_count, ff_grain, 3 * width), bf16),
            ff_send=Kept((ff_count, ff_grain, 3 * width), bf16),
            small=Kept(small_shape, f32),
            **attn_back_outs,
            outputs=(matrix, bf16),
            grad_next=Kept(matrix, f32),
            grad_next_low=Kept(matrix, bf16),
            bias_acc=Kept(bias_shape, f32),
        ),
        dict(
            ff_gate_up=pltpu.VMEM((2, width, 2 * width), bf16),
            ff_down=pltpu.VMEM((2, width, width), bf16),
            hidden=pltpu.VMEM((2, rows, width), bf16),
            grad_gate_up=pltpu.VMEM((2, rows, 2 * width), bf16),
            ff_grad=pltpu.VMEM((2, width, 3 * width), f32),
            **mid_scratch,
            **attn_back_scratch,
            **ff_scratch,
        ),
        micros=10,
    )
    peer_grad_0 = swap(back_1.grad_next_low, 1)
    attn_1 = Chain(attn_chain, back_1, 1)
    back_0 = run(
        ff_backward_body,
        "layer_0_ff_backward",
        dict(
            grad=Kept(back_1.grad_next),
            gain_ff=gain_ff,
            small_before=Kept(back_1.small),
            middle=Kept(first.middle),
            ff_in=Kept(first.ff_in),
            ff_gate_up=Kept(first_ff.ff_gate_up),
            ff_down=Kept(first_ff.ff_down),
        ),
        dict(
            hidden=Kept((1, rows, width), bf16),
            grad_gate_up=Kept((1, rows, 2 * width), bf16),
            small=Kept(small_shape, f32),
            grad_mid=Kept(matrix, f32),
            branch=Kept(matrix, bf16),
        ),
        pulled_scratch,
        after=(peer_in_0,),
        micros=10,
    )
    ff_1 = Chain(ff_chain, back_1, 1)
    token = ff_1.step(back_0.branch)
    back_attn_0 = run(
        functools.partial(
            attention_backward_body, sizes=sizes, piece_masks=attn_masks[0], heads=heads
        ),
        "layer_0_attention_backward",
        dict(
            place=place,
            bias_before=Kept(back_1.bias_acc),
            marks=marks,
            buckets=wide_buckets,
            small_before=Kept(back_0.small),
            grad_mid=Kept(back_0.grad_mid),
            branch=Kept(back_0.branch),
            **attn_back_ins(first, start.x, start.a),
        ),
        dict(
            attn_keep=Kept(attn_half, bf16),
            attn_send=Kept((attn_count // 2 + 1, *attn_half[1:]), bf16),
            small=Kept(small_shape, f32),
            grad_next=(matrix, f32),
        ),
        dict(
            bias_acc=pltpu.VMEM(bias_shape, f32),
            table_rows=pltpu.VMEM((bias_table.shape[0], heads * slots), f32),
            **attn_back_scratch,
        ),
        after=(token,),
        micros=7,
    )
    attn_0 = Chain(attn_chain, back_attn_0, 0)
    token = attn_1.step(back_attn_0.attn_send, peer_grad_0)
    part_0 = run(
        functools.partial(weight_body, piece_masks=place_masks[0]),
        "layer_0_weight_grads",
        dict(
            place=place,
            ff_in=Kept(first.ff_in),
            grad=Kept(back_1.grad_next_low),
            hidden=Kept(back_0.hidden),
            grad_gate_up=Kept(back_0.grad_gate_up),
            peer_in=Kept(peer_in_0),
            peer_grad=Kept(peer_grad_0),
            ff_gate_up=Kept(first_ff.ff_gate_up),
            ff_down=Kept(first_ff.ff_down),
        ),
        dict(ff_keep=Kept(ff_half, bf16), ff_send=Kept(ff_half, bf16)),
        dict(
            peer_gate_up=pltpu.VMEM((rows, 2 * width), bf16),
            peer_hidden=pltpu.VMEM(matrix, bf16),
            ff_grad=pltpu.VMEM((width, 3 * width), f32),
        ),
        after=(token,),
        micros=4,
    )
    ff_0 = Chain(ff_chain, part_0, 0)
    token = part_0.ff_send
    shape = (2, width, width)
    near_masks = place_masks[0][: ff_count // 2]
    far_masks = place_masks[0][ff_count // 2 :]
    done_1 = sums = attn_grads = None
    while True:
        for chain in (ff_0, ff_1, attn_0, attn_1):
            token = chain.step(token)
        if sums is None and attn_0.arriving is None:
            sums = run(
                small_body,
                "small_sums",
                dict(packed=Kept(tie(attn_0.out["small"], token))),
                dict(
                    gain_attn=((2, width), f32),
                    gain_ff=((2, width), f32),
                    embed=((1, width), f32),
                    table=(bias_table.shape, f32),
                ),
                {},
            )
            token = sums.embed
        if attn_grads is None and attn_0.arriving is None and attn_1.arriving is None:
            attn_grads = jnp.stack([attn_0.out["done"], tie(attn_1.out["done"], token)])
            token = attn_grads
        if done_1 is None and ff_1.arriving is None:
            pieces = tie(join(ff_1.out["near"], ff_1.out["far"]), token)
            done_1 = finish(pieces, place_masks[1], 1, place, shape)
            token = done_1[0]
        if ff_0.arriving is None:
            break
    near_0 = finish(ff_0.out["near"], near_masks, 0, place, shape, done_1)
    done = finish(ff_0.out["far"], far_masks, 0, place, shape, near_0)
    return (
        back_1.outputs.reshape(inputs.shape),
        back_attn_0.grad_next.reshape(inputs.shape),
        attn_grads[:, :, :inner],
        attn_grads[:, :, inner : 2 * inner],
        attn_grads[:, :, 2 * inner : 3 * inner],
        jnp.swapaxes(attn_grads[:, :, 3 * inner :], 1, 2),
        *done,
        sums.gain_attn,
        sums.gain_ff,
        sums.table,
        sums.embed[0],
    )


def solution(mesh):
    placed = (
        P(("dp", "tensor"), None, None),
        P(("dp", "tensor"), None, None),
        P(("dp", "tensor"), None),
        P(("dp", "tensor"), None),
        P(),
        P(),
        P(None, ("dp", "tensor"), None),
        P(None, ("dp", "tensor"), None),
        P(None, ("dp", "tensor"), None),
        P(None, None, ("dp", "tensor")),
        P(None, None, "tensor"),
        P(None, None, "tensor"),
        P(None, "tensor", None),
        P(),
        P(),
        P(),
    )
    return jax.shard_map(
        functools.partial(on_device, dp_size=mesh.shape["dp"]),
        mesh=mesh,
        in_specs=placed,
        out_specs=(
            P(("dp", "tensor"), None, None),
            P(("dp", "tensor"), None, None),
            P(None, ("dp", "tensor"), None),
            P(None, ("dp", "tensor"), None),
            P(None, ("dp", "tensor"), None),
            P(None, None, ("dp", "tensor")),
            P(None, None, "tensor"),
            P(None, None, "tensor"),
            P(None, "tensor", None),
            P(),
            P(),
            P(),
            P(),
        ),
        check_vma=False,
    )
```

```python
import functools
import types

import jax
import jax.numpy as jnp
from jax import lax
from jax.experimental import pallas as pl
from jax.experimental.pallas import tpu as pltpu
from jax.sharding import PartitionSpec as P

norm_eps = 1e-06
masked_score = -1e30
bf16 = jnp.bfloat16
f32 = jnp.float32
axes = ("dp", "tensor")
vmem_bytes = 32 * 1024 * 1024
raw_names = ("attn_near", "attn_far", "ff_near", "ff_far", "w_gate", "w_up", "w_down")


def dot_nn(left, right):
    return lax.dot_general(left, right, (((1,), (0,)), ((), ())), preferred_element_type=f32)


def dot_nt(left, right):
    return lax.dot_general(left, right, (((1,), (1,)), ((), ())), preferred_element_type=f32)


def dot_tn(left, right):
    return lax.dot_general(left, right, (((0,), (0,)), ((), ())), preferred_element_type=f32)


def inverse_rms(values):
    return lax.rsqrt(jnp.mean(values * values, axis=-1, keepdims=True) + norm_eps)


def norm_back(values, gain, grad_out):
    scale = inverse_rms(values)
    pulled = grad_out * gain
    mean_part = jnp.mean(pulled * values, axis=-1, keepdims=True)
    grad_in = scale * pulled - values * (scale * scale * scale) * mean_part
    return grad_in, jnp.sum(grad_out * values * scale, axis=0, keepdims=True)


def gelu_terms(gate_act):
    square = gate_act * gate_act
    bent = jnp.tanh(0.7978845608028654 * gate_act * (1.0 + 0.044715 * square))
    half = 0.5 * (1.0 + bent)
    slope = half + 0.5 * gate_act * (1.0 - bent * bent) * (
        0.7978845608028654 * (1.0 + 3.0 * 0.044715 * square)
    )
    return gate_act * half, slope


def cost(micros):
    return pl.CostEstimate(flops=int(micros * 1.15e9), bytes_accessed=0, transcendentals=0)


def run(body, name, ins, outs, scratch, after=(), micros=1):
    in_names, out_names, scratch_names = list(ins), list(outs), list(scratch)
    direct = {n for n in in_names if n == "place" or n in raw_names or isinstance(ins[n], Kept)}
    staged = [n for n in in_names if n not in direct]
    copied = [n for n in out_names if not isinstance(outs[n], Kept)]
    in_sems = {n: i for i, n in enumerate(staged)}
    out_sems = {n: i for i, n in enumerate(copied)}

    def kernel(*refs):
        refs = list(refs)
        sources = dict(zip(in_names, refs))
        refs = refs[len(in_names) + len(after) :]
        targets = dict(zip(out_names, refs))
        refs = refs[len(out_names) :]
        space = dict(zip(scratch_names, refs))
        refs = refs[len(scratch_names) :]
        buffers = dict(zip(staged + copied, refs))
        sems_in, sems_out = refs[len(staged) + len(copied) :]
        kept = {n: ref for n, ref in targets.items() if n not in out_sems}
        r = types.SimpleNamespace(**space, **buffers, **kept)
        for n in direct:
            setattr(r, n, sources[n])

        def copy_in(n):
            return pltpu.make_async_copy(sources[n], buffers[n], sems_in.at[in_sems[n]])

        def copy_out(n):
            return pltpu.make_async_copy(buffers[n], targets[n], sems_out.at[out_sems[n]])

        r.fetch = lambda *names: [copy_in(n).start() for n in names if n in in_sems]
        r.need = lambda *names: [copy_in(n).wait() for n in names if n in in_sems]
        r.write = lambda *names: [copy_out(n).start() for n in names if n in out_sems]
        r.drain = lambda *names: [copy_out(n).wait() for n in names if n in out_sems]
        body(r)

    def in_space(n):
        if n == "place":
            return pltpu.SMEM
        return pltpu.VMEM if isinstance(ins[n], Kept) else pl.ANY

    results = pl.pallas_call(
        kernel,
        name=name,
        in_specs=[pl.BlockSpec(memory_space=in_space(n)) for n in in_names]
        + [pl.BlockSpec(memory_space=pl.ANY) for _ in after],
        out_specs=[
            pl.BlockSpec(memory_space=pltpu.VMEM if isinstance(out, Kept) else pl.ANY)
            for out in outs.values()
        ],
        out_shape=[
            pltpu.VMEM(*out.what) if isinstance(out, Kept) else jax.ShapeDtypeStruct(*out)
            for out in outs.values()
        ],
        scratch_shapes=list(scratch.values())
        + [pltpu.VMEM(ins[n].shape, ins[n].dtype) for n in staged]
        + [pltpu.VMEM(*outs[n]) for n in copied]
        + [
            pltpu.SemaphoreType.DMA((max(1, len(staged)),)),
            pltpu.SemaphoreType.DMA((max(1, len(copied)),)),
        ],
        compiler_params=pltpu.CompilerParams(vmem_limit_bytes=vmem_bytes),
        cost_estimate=cost(micros),
    )(
        *[
            pltpu.with_memory_space_constraint(value.what, pltpu.VMEM)
            if isinstance(value, Kept)
            else value
            for value in ins.values()
        ],
        *after,
    )
    return types.SimpleNamespace(**dict(zip(outs, results)))


class Kept:
    def __init__(self, *what):
        self.what = what[0] if len(what) == 1 else what


def keep_all(names):
    return {name: Kept(value) for name, value in names.items()}


def chunks(extent, size):
    size = min(size, extent)
    return [slice(start, start + size) for start in range(0, extent, size)]


def attention_copies(r, masks, rows):
    copies = []
    for idx, mask in enumerate(masks):
        half, at = divmod(idx, max(1, len(masks) // 2))
        source = (r.attn_near if half == 0 else r.attn_far).at[pl.ds(at * rows, rows)]
        place = (r.place[0] ^ mask) * rows if len(masks) > 1 else 0
        target = r.attn_w.at[pl.ds(pl.multiple_of(place, rows), rows)]
        copies.append(pltpu.make_async_copy(source, target, r.attn_sem))
    return copies


def ff_copies(r, layer_idx):
    width = r.ff_down.shape[-1]
    copies = []
    for k, own in enumerate((r.w_gate, r.w_up)):
        target = r.ff_gate_up.at[0, :, pl.ds(k * width, width)]
        copies.append(pltpu.make_async_copy(own.at[layer_idx], target, r.ff_sem))
    copies.append(pltpu.make_async_copy(r.w_down.at[layer_idx], r.ff_down.at[0], r.ff_sem))
    part = r.ff_near.shape[1]
    for source, base in ((r.ff_near, 0), (r.ff_far, 1)):
        for m in range(2):
            rows = pl.ds(pl.multiple_of((r.place[1] ^ (2 * m + base)) * part, part), part)
            for k in range(2):
                target = r.ff_gate_up.at[1, rows, pl.ds(k * width, width)]
                copies.append(pltpu.make_async_copy(source.at[3 * m + k], target, r.ff_sem))
            copies.append(
                pltpu.make_async_copy(source.at[3 * m + 2], r.ff_down.at[1, rows], r.ff_sem)
            )
    return copies


def start_all(copies):
    for copy in copies:
        copy.start()


def wait_all(sem, *buffers):
    for whole in buffers:
        pltpu.make_async_copy(whole, whole, sem).wait()


def lane_low(rows):
    return lax.broadcasted_iota(jnp.int32, (rows, 128), 1) < 64


def lane_halves():
    low = lane_low(1).astype(f32)
    return low.astype(bf16), (1.0 - low).astype(bf16)


def pair_blocks(rows, low, high):
    return jnp.concatenate([rows * low, rows * high], axis=0)


def own_blocks(both, is_low):
    half = both.shape[0] // 2
    return jnp.where(is_low, both[:half], both[half:]).astype(bf16)


def attention_forward(r, x_ref, a_ref, sizes, layer_idx):
    series, slots, inner = sizes
    rows = series * slots
    for part in chunks(rows, 256):
        r.qkv[part, :] = dot_nn(a_ref[part, :], r.attn_w[:, : 3 * inner]).astype(bf16)
    is_low = lane_low(slots)
    low, high = lane_halves()
    for s in range(series):
        here = slice(s * slots, (s + 1) * slots)
        keep = r.mask[here, :] == 1
        for start in range(0, inner, 128):
            at = slice(start, start + 128)
            query = r.qkv[here, at]
            keys = r.qkv[here, inner + start : inner + start + 128]
            scores = dot_nt(keys, pair_blocks(query, low, high)) + r.bias[:, at]
            scores = jnp.where(keep, scores, masked_score)
            exps = jnp.exp(scores - jnp.max(scores, axis=0, keepdims=True))
            r.probs[here, at] = exps / jnp.sum(exps, axis=0, keepdims=True)
    for s in range(series):
        here = slice(s * slots, (s + 1) * slots)
        for start in range(0, inner, 128):
            at = slice(start, start + 128)
            values = r.qkv[here, 2 * inner + start : 2 * inner + start + 128]
            both = dot_tn(r.probs[here, at].astype(bf16), values)
            r.heads[here, at] = own_blocks(both, is_low)
    gain = r.gain_ff[layer_idx : layer_idx + 1, :]
    for part in chunks(rows, 256):
        middle = x_ref[part, :] + dot_nt(r.heads[part, :], r.attn_w[:, 3 * inner :])
        r.middle[part, :] = middle
        r.ff_in[part, :] = (middle * inverse_rms(middle) * gain).astype(bf16)


def prepare_body(r):
    r.fetch("inputs", "marks", "embed", "gain_attn", "buckets", "table")
    r.need("inputs", "marks", "embed", "gain_attn", "buckets", "table")
    x = jnp.where(r.marks[:, 0:1] == 1, r.inputs[...].astype(f32), r.embed[...])
    r.x[...] = x
    r.a[...] = (x * inverse_rms(x) * r.gain_attn[0:1, :]).astype(bf16)
    buckets = r.buckets[...]
    bias = jnp.zeros(buckets.shape, f32)
    for idx in range(r.table.shape[0]):
        bias = jnp.where(buckets == idx, r.table[idx : idx + 1, :], bias)
    r.bias[...] = bias
    r.mask[...] = jnp.broadcast_to(r.marks[:, 1:2], r.mask.shape)
    r.write("x", "a", "bias", "mask")
    r.drain("x", "a", "bias", "mask")


def attention_body(r, sizes, masks, grain, layer_idx):
    start_all(attention_copies(r, masks, grain))
    r.fetch("gain_ff")
    r.need("gain_ff")
    wait_all(r.attn_sem, r.attn_w)
    attention_forward(r, r.x, r.a, sizes, layer_idx)


def ff_body(r):
    start_all(ff_copies(r, 0))
    r.fetch("gain_attn")
    r.need("gain_attn")
    wait_all(r.ff_sem, r.ff_gate_up, r.ff_down)
    width = r.middle.shape[1]
    for part in chunks(r.middle.shape[0], 256):
        x_next = r.middle[part, :]
        for half in range(2):
            both = dot_nn(r.ff_in[part, :], r.ff_gate_up[half])
            hidden = (gelu_terms(both[:, :width])[0] * both[:, width:]).astype(bf16)
            x_next = x_next + dot_nn(hidden, r.ff_down[half])
        r.x_next[part, :] = x_next
        r.a_next[part, :] = (x_next * inverse_rms(x_next) * r.gain_attn[1:2, :]).astype(bf16)


def ff_backward(r, layer_idx, last):
    rows, width = r.middle.shape
    r.fetch("grad", "gain_ff")
    if last:
        start_all(ff_copies(r, layer_idx))
    r.need("grad", "gain_ff")
    if last:
        wait_all(r.ff_sem, r.ff_gate_up, r.ff_down)
    gain_ff = r.gain_ff[layer_idx : layer_idx + 1, :]
    gain_total = jnp.zeros((1, width), f32)
    for part in chunks(rows, 256):
        grad = r.grad[part, :].astype(f32)
        rounded = grad.astype(bf16)
        ff_rows = r.ff_in[part, :]
        back = None
        middle = r.middle[part, :]
        total = middle
        for half in range(2):
            both = dot_nn(ff_rows, r.ff_gate_up[half])
            grad_hidden = dot_nt(rounded, r.ff_down[half])
            gate_act, up_act = both[:, :width], both[:, width:]
            mixed, slope = gelu_terms(gate_act)
            hidden = (mixed * up_act).astype(bf16)
            if last or half == 0:
                r.hidden[half, part, :] = hidden
                held = r.grad_gate_up.at[half, part]
            else:
                held = r.pulled
            held[:, :width] = (grad_hidden * up_act * slope).astype(bf16)
            held[:, width:] = (grad_hidden * mixed).astype(bf16)
            pulled = held[...]
            if last:
                total = total + dot_nn(hidden, r.ff_down[half])
            term = dot_nt(pulled, r.ff_gate_up[half])
            back = term if back is None else back + term
        if last:
            r.outputs[part, :] = total.astype(bf16)
        grad_mid, gain_part = norm_back(middle, gain_ff, back)
        gain_total += gain_part
        grad_mid = grad + grad_mid
        r.grad_mid[part, :] = grad_mid
        r.branch[part, :] = grad_mid.astype(bf16)
    if last:
        r.write("outputs")
    return gain_total


def attention_backward(r, sizes, layer_idx, last, piece_masks, heads):
    series, slots, inner = sizes
    rows = series * slots
    width = r.x.shape[1]
    r.fetch("gain_attn")
    if not last:
        r.fetch("marks", "buckets")
    for part in chunks(rows, 256):
        r.grad_heads[part, :] = dot_nn(r.branch[part, :], r.attn_w[:, 3 * inner :]).astype(bf16)
    is_low = lane_low(slots)
    low, high = lane_halves()
    for start in range(0, inner, 128):
        at = slice(start, start + 128)
        bias_total = jnp.zeros((slots, 128), f32) if last else r.bias_before[:, at]
        for s in range(series):
            here = slice(s * slots, (s + 1) * slots)
            probs = r.probs[here, at]
            values = r.qkv[here, 2 * inner + start : 2 * inner + start + 128]
            grad_probs = dot_nt(values, pair_blocks(r.grad_heads[here, at], low, high))
            inner_sum = jnp.sum(probs * grad_probs, axis=0, keepdims=True)
            grad_scores = (probs * (grad_probs - inner_sum)).astype(bf16)
            r.grad_scores[here, at] = grad_scores
            bias_total = bias_total + grad_scores.astype(f32)
        r.bias_acc[:, at] = bias_total
    for s in range(series):
        here = slice(s * slots, (s + 1) * slots)
        for start in range(0, inner, 128):
            at = slice(start, start + 128)
            key_at = slice(inner + start, inner + start + 128)
            value_at = slice(2 * inner + start, 2 * inner + start + 128)
            grad_scores = r.grad_scores[here, at]
            r.grad_qkv[here, key_at] = dot_nn(
                grad_scores, pair_blocks(r.qkv[here, at], low, high)
            ).astype(bf16)
            r.grad_qkv[here, value_at] = dot_nn(
                r.probs[here, at].astype(bf16), pair_blocks(r.grad_heads[here, at], low, high)
            ).astype(bf16)
            r.grad_qkv[here, at] = own_blocks(dot_tn(grad_scores, r.qkv[here, key_at]), is_low)
    r.attn_grad[:, : 3 * inner] = dot_tn(r.a[...], r.grad_qkv[...])
    r.attn_grad[:, 3 * inner :] = dot_tn(r.branch[...], r.heads[...])
    scatter_pieces(r.attn_grad, r.attn_keep, r.attn_send, piece_masks, r.place[2])
    r.need("gain_attn")
    if not last:
        r.need("marks", "buckets")
    gain_attn = r.gain_attn[layer_idx : layer_idx + 1, :]
    gain_total = jnp.zeros((1, width), f32)
    embed_total = jnp.zeros((1, width), f32)
    for part in chunks(rows, 256):
        grad_normed = dot_nt(r.grad_qkv[part, :], r.attn_w[:, : 3 * inner])
        grad_in, gain_part = norm_back(r.x[part, :], gain_attn, grad_normed)
        gain_total += gain_part
        grad_in = r.grad_mid[part, :] + grad_in
        if last:
            r.grad_next[part, :] = grad_in
            r.grad_next_low[part, :] = grad_in.astype(bf16)
        else:
            seen = r.marks[part, 0:1] == 1
            r.grad_next[part, :] = jnp.where(seen, grad_in, 0.0)
            embed_total += jnp.sum(jnp.where(seen, 0.0, grad_in), axis=0, keepdims=True)
    r.write("grad_next")
    if not last:
        put_row(r.small, 4, embed_total)
        head_size = inner // heads
        for idx in range(r.table_rows.shape[0]):
            chosen = jnp.where(r.buckets[...] == idx, r.bias_acc[...], 0.0)
            r.table_rows[idx : idx + 1, :] = jnp.sum(chosen, axis=0, keepdims=True)
        lane = lax.broadcasted_iota(jnp.int32, (r.table_rows.shape[0], 128), 1)
        table = jnp.zeros(lane.shape, f32)
        for head in range(heads):
            cut = r.table_rows[:, head * head_size : (head + 1) * head_size]
            table = jnp.where(lane == head, jnp.sum(cut, axis=1, keepdims=True), table)
        r.small[:heads, : table.shape[0]] = jnp.transpose(table)[:heads, :]
    r.drain("grad_next")
    return gain_total


def two_parts(values):
    high = values.astype(bf16).astype(f32)
    return high, (values - high).astype(bf16).astype(f32)


def last_backward_body(r, sizes, piece_masks, ff_masks, heads):
    r.small[...] = jnp.zeros(r.small.shape, f32)
    put_row(r.small, 3, ff_backward(r, 1, True))
    width = r.middle.shape[1]
    for half in range(2):
        r.ff_grad[half, :, : 2 * width] = dot_tn(r.ff_in[...], r.grad_gate_up[half])
        r.ff_grad[half, :, 2 * width :] = dot_tn(r.hidden[half], r.grad[...])
    half_count = len(ff_masks[0]) // 2
    grain, columns = r.ff_keep.shape[1:]
    for side, side_masks in enumerate(ff_masks):
        lanes = slice(side * columns, (side + 1) * columns)
        for idx, mask in enumerate(side_masks):
            target = r.ff_keep if idx < half_count else r.ff_send
            rows = pl.ds(pl.multiple_of((r.place[3] ^ (mask // 2)) * grain, grain), grain)
            target[side * half_count + idx % half_count] = r.ff_grad[mask % 2, rows, lanes].astype(
                bf16
            )
    put_row(r.small, 1, attention_backward(r, sizes, 1, True, piece_masks, heads))
    r.drain("outputs")


def ff_backward_body(r):
    r.small[...] = r.small_before[...]
    put_row(r.small, 2, ff_backward(r, 0, False))


def attention_backward_body(r, sizes, piece_masks, heads):
    r.small[...] = r.small_before[...]
    put_row(r.small, 0, attention_backward(r, sizes, 0, False, piece_masks, heads))
    high, low = two_parts(r.small[...])
    last = r.attn_send.shape[0] - 1
    r.attn_send[last] = jnp.concatenate([high, low], axis=0).astype(bf16)
    r.small[...] = high + low


def put_row(packed, which, row):
    first, width = packed.shape[0] - 2, row.shape[1]
    at = which % 3 * width
    packed[first + which // 3 : first + which // 3 + 1, at : at + width] = row


def scatter_pieces(whole, keep, send, masks, place):
    count = len(masks)
    grain = whole.shape[0] // count
    for idx, mask in enumerate(masks):
        target = keep if idx < count // 2 else send
        source = pl.ds(pl.multiple_of((place ^ mask) * grain, grain), grain)
        target[idx % (count // 2)] = whole[source, :].astype(bf16)


def weight_body(r, piece_masks):
    width = r.ff_in.shape[1]
    rows = r.ff_in.shape[0]
    r.fetch("peer_in", "peer_grad")
    r.fetch("ff_in", "grad_gate_up", "hidden", "grad")
    r.need("peer_in", "peer_grad")
    for part in chunks(rows, 256):
        both = dot_nn(r.peer_in[part, :], r.ff_gate_up[0])
        grad_hidden = dot_nt(r.peer_grad[part, :], r.ff_down[0])
        gate_act, up_act = both[:, :width], both[:, width:]
        mixed, slope = gelu_terms(gate_act)
        r.peer_gate_up[part, :width] = (grad_hidden * up_act * slope).astype(bf16)
        r.peer_gate_up[part, width:] = (grad_hidden * mixed).astype(bf16)
        r.peer_hidden[part, :] = (mixed * up_act).astype(bf16)
    r.need("ff_in", "grad_gate_up", "hidden", "grad")
    r.ff_grad[:, : 2 * width] = dot_tn(r.ff_in[...], r.grad_gate_up[0]) + dot_tn(
        r.peer_in[...], r.peer_gate_up[...]
    )
    r.ff_grad[:, 2 * width :] = dot_tn(r.hidden[0], r.grad[...]) + dot_tn(
        r.peer_hidden[...], r.peer_grad[...]
    )
    scatter_pieces(r.ff_grad, r.ff_keep, r.ff_send, piece_masks, r.place[3])
    r.write("ff_send", "ff_keep")
    r.drain("ff_send", "ff_keep")


def finish(pieces, masks, layer_idx, place, shape, before=()):
    grain, width = pieces.shape[1], shape[-1]
    count = len(before)

    def kernel(place_ref, source, *refs):
        outs = refs[count : count + 3]
        stage, out_sem = refs[count + 3 :]
        for idx, mask in enumerate(masks):
            rows = pl.ds(pl.multiple_of((place_ref[3] ^ mask) * grain, grain), grain)
            for k, out in enumerate(outs):
                stage[k, idx] = source[idx, :, k * width : (k + 1) * width].astype(f32)
                pltpu.make_async_copy(stage.at[k, idx], out.at[layer_idx, rows], out_sem).start()
        pltpu.make_async_copy(stage, stage, out_sem).wait()

    return pl.pallas_call(
        kernel,
        name="layer_%d_ff_grads" % layer_idx,
        in_specs=[
            pl.BlockSpec(memory_space=pltpu.SMEM),
            pl.BlockSpec(memory_space=pltpu.VMEM),
        ]
        + [pl.BlockSpec(memory_space=pl.ANY)] * count,
        out_specs=[pl.BlockSpec(memory_space=pl.ANY)] * 3,
        out_shape=[jax.ShapeDtypeStruct(shape, f32)] * 3,
        input_output_aliases={2 + k: k for k in range(count)},
        scratch_shapes=[
            pltpu.VMEM((3, len(masks), grain, width), f32),
            pltpu.SemaphoreType.DMA,
        ],
        compiler_params=pltpu.CompilerParams(vmem_limit_bytes=vmem_bytes),
        cost_estimate=cost(3),
    )(place, pltpu.with_memory_space_constraint(pieces, pltpu.VMEM), *before)


def small_body(r):
    width = r.embed.shape[1]
    heads = r.table.shape[0]
    outs = ((r.gain_attn, 0), (r.gain_attn, 1), (r.gain_ff, 0), (r.gain_ff, 1), (r.embed, 0))
    for which, (out, row) in enumerate(outs):
        first = r.packed.shape[0] - 2 + which // 3
        at = which % 3 * width
        out[row : row + 1, :] = r.packed[first : first + 1, at : at + width]
    r.table[...] = r.packed[:heads, : r.table.shape[1]]
    r.write("gain_attn", "gain_ff", "embed", "table")
    r.drain("gain_attn", "gain_ff", "embed", "table")


def cut_body(r):
    rows = r.quarter_0.shape[1]
    at = pl.ds(pl.multiple_of(r.place[1] * rows, rows), rows)
    outs = (r.quarter_0, r.quarter_1)
    start_all(
        pltpu.make_async_copy(w.at[layer_idx, at], out.at[k], r.cut_sem)
        for layer_idx, out in enumerate(outs)
        for k, w in enumerate((r.w_gate, r.w_up, r.w_down))
    )
    wait_all(r.cut_sem, *outs)


def order_masks(hops):
    masks = [0]
    for hop in reversed(hops):
        masks = masks + [mask ^ hop for mask in masks]
    return masks


def tie(value, *others):
    return lax.optimization_barrier((value, *others))[0]


def on_device(
    inputs,
    cotangent,
    attention_mask,
    patch_valid,
    buckets,
    mask_embed,
    w_query,
    w_key,
    w_value,
    w_output,
    w_gate,
    w_up,
    w_down,
    gain_attn,
    gain_ff,
    bias_table,
    dp_size,
):
    series, slots, width = inputs.shape
    heads = bias_table.shape[1]
    inner = w_query.shape[2]
    rows = series * slots
    sizes = (series, slots, inner)
    matrix = (rows, width)
    devices = 2 * dp_size
    dp_at = lax.axis_index("dp")
    device_at = 2 * dp_at + lax.axis_index("tensor")
    cotangent = cotangent.reshape(matrix)

    def swap(array, mask):
        return lax.ppermute(array, axes, [(n, n ^ mask) for n in range(devices)])

    def join(left, right):
        return jnp.concatenate([left, right], axis=0)

    bits = [1 << k for k in range(devices.bit_length() - 1)]

    attn_grain = max(16, width // devices)
    attn_count = width // attn_grain
    ff_grain = max(16, width // dp_size)
    ff_count = width // ff_grain
    quarter_at = lax.rem(dp_at, 4)
    place = jnp.stack(
        [
            device_at,
            quarter_at,
            device_at // (devices // attn_count),
            lax.rem(dp_at, ff_count),
        ]
    ).astype(jnp.int32)

    quarter = width // 4
    packed = jnp.concatenate([w_query, w_key, w_value, jnp.swapaxes(w_output, 1, 2)], axis=2)
    in_hbm = {
        name: pltpu.with_memory_space_constraint(w, pltpu.HBM)
        for name, w in (("w_gate", w_gate), ("w_up", w_up), ("w_down", w_down))
    }
    ff_blocks = run(
        cut_body,
        "cut_quarters",
        dict(place=place, **in_hbm),
        dict(
            quarter_0=Kept((3, quarter, width), bf16),
            quarter_1=Kept((3, quarter, width), bf16),
        ),
        dict(cut_sem=pltpu.SemaphoreType.DMA),
    )
    own_rows = packed.shape[1]
    direct = own_rows % 16 == 0
    far = bits[2:]

    def prepare(token):
        table, marked, kept, near = (
            tie(array, token) for array in (bias_table, patch_valid, attention_mask, buckets)
        )
        wide_buckets = jnp.tile(near.T, (1, heads))
        wide_table = jnp.repeat(table, slots, axis=1)
        marks = jnp.stack([marked.reshape(rows), kept.reshape(rows)], axis=1)
        result = run(
            prepare_body,
            "prepare",
            dict(
                inputs=inputs.reshape(matrix),
                marks=marks,
                embed=mask_embed[None, :],
                gain_attn=gain_attn,
                buckets=wide_buckets,
                table=wide_table,
            ),
            dict(
                x=Kept(matrix, f32),
                a=Kept(matrix, bf16),
                bias=Kept((slots, heads * slots), f32),
                mask=Kept((rows, 128), jnp.int32),
            ),
            {},
            micros=3,
        )
        return result, wide_buckets, marks

    if direct:
        hops_0 = [1] + far[2:] + far[:2] + [2]
        hops_1 = far[2:] + far[:2] + [1, 2]
        block_0, block_1 = packed[0], packed[1]
        got_1 = swap(block_1, hops_1[0])
        got_0 = swap(block_0, hops_0[0])
        ff_0 = swap(tie(ff_blocks.quarter_0, got_0), 1)
        got_ff_0 = swap(ff_0, 4)
        ff_1 = swap(tie(ff_blocks.quarter_1, ff_0), 1)
        block_0 = join(block_0, got_0)
        block_1 = join(block_1, tie(got_1, block_0))
        for hop_0, hop_1 in zip(hops_0[1:-2], hops_1[1:-2]):
            got_1, got_0 = swap(block_1, hop_1), swap(block_0, hop_0)
            if hop_1 == hops_1[1]:
                start, wide_buckets, marks = prepare(block_1)
            block_0 = join(block_0, got_0)
            block_1 = join(block_1, tie(got_1, block_0))
        got_0 = swap(block_0, hops_0[-2])
        got_1 = swap(block_1, hops_1[-2])
        block_0 = join(block_0, tie(got_0, start.a, got_ff_0))
        block_1 = join(block_1, tie(got_1, block_0))
        ff_0 = join(ff_0, tie(got_ff_0, block_1))
        got_ff_1 = swap(tie(ff_1, ff_0), 4)
        far_0 = swap(block_0, 2)
        attn_pieces = [
            (block_0, far_0, order_masks(hops_0[::-1])),
            (block_1, swap(tie(block_1, far_0), 2), order_masks(hops_1[::-1])),
        ]
        after_first = (attn_pieces[1][1],)
    else:
        ff_0, ff_1 = swap(ff_blocks.quarter_0, 1), swap(ff_blocks.quarter_1, 1)
        ff_0 = join(ff_0, swap(ff_0, 4))
        start, wide_buckets, marks = prepare(packed)
        whole = lax.all_gather(packed[0], axes, axis=0, tiled=True)
        attn_pieces = [(whole, whole, [0])]
        whole = lax.all_gather(packed[1], axes, axis=0, tiled=True)
        attn_pieces.append((whole, whole, [0]))
        after_first = ()
    ff_pieces = [(ff_0, swap(ff_0, 2))]

    def attn_ins(layer_idx):
        near, far, masks = attn_pieces[layer_idx]
        return dict(attn_near=Kept(near), attn_far=Kept(far)), masks

    def ff_ins(layer_idx):
        near, far = ff_pieces[layer_idx]
        return dict(w_gate=w_gate, w_up=w_up, w_down=w_down, ff_near=Kept(near), ff_far=Kept(far))

    attn_scratch = dict(attn_sem=pltpu.SemaphoreType.DMA)
    ff_scratch = dict(ff_sem=pltpu.SemaphoreType.DMA)
    ff_outs = dict(
        ff_gate_up=Kept((2, width, 2 * width), bf16), ff_down=Kept((2, width, width), bf16)
    )
    grain = own_rows if direct else width
    attn_outs = dict(
        attn_w=Kept((width, 4 * inner), bf16),
        qkv=Kept((rows, 3 * inner), bf16),
        probs=Kept((rows, heads * slots), f32),
        heads=Kept((rows, inner), bf16),
        middle=Kept(matrix, f32),
        ff_in=Kept(matrix, bf16),
    )

    def attention(layer_idx, x, a, after=(), micros=5):
        pieces, masks = attn_ins(layer_idx)
        return run(
            functools.partial(
                attention_body, sizes=sizes, masks=masks, grain=grain, layer_idx=layer_idx
            ),
            "layer_%d_attention" % layer_idx,
            dict(
                place=place,
                x=Kept(x),
                a=Kept(a),
                bias=Kept(start.bias),
                mask=Kept(start.mask),
                gain_ff=gain_ff,
                **pieces,
            ),
            attn_outs,
            attn_scratch,
            after=after,
            micros=micros,
        )

    first = attention(0, start.x, start.a, micros=10)
    peer_in_0 = swap(first.ff_in, 1)
    first_ff = run(
        ff_body,
        "layer_0_ff",
        dict(
            place=place,
            middle=Kept(first.middle),
            ff_in=Kept(first.ff_in),
            gain_attn=gain_attn,
            **ff_ins(0),
        ),
        dict(**ff_outs, x_next=Kept(matrix, f32), a_next=Kept(matrix, bf16)),
        ff_scratch,
        after=after_first,
        micros=0.1,
    )
    if direct:
        ff_1 = join(ff_1, tie(got_ff_1, first_ff.a_next))
    else:
        ff_1 = join(ff_1, swap(ff_1, 4))
    ff_pieces.append((ff_1, swap(ff_1, 2)))
    second = attention(1, first_ff.x_next, first_ff.a_next, micros=0.1)

    attn_low = devices // attn_count
    attn_hops = ([2, 1] + bits[2:], [2, 1] + bits[2:])
    attn_split = [[hop for hop in hops if hop >= attn_low] for hops in attn_hops]
    attn_whole = [hop for hop in bits if hop < attn_low]
    attn_masks = [[mask // attn_low for mask in order_masks(hops)] for hops in attn_split]
    ff_hops = (bits[1:], [2, 4, 1] + bits[3:], [2, 1, 4] + bits[3:])
    ff_split = [[hop for hop in hops if hop // 2 < ff_count] for hops in ff_hops]
    ff_whole = [hop for hop in bits[1:] if hop // 2 >= ff_count]
    ff_share = ff_split[0][::-1]
    ff_masks = [order_masks(hops) for hops in ff_split]
    place_masks = [mask // 2 for mask in ff_masks[0]]
    attn_half = (attn_count // 2, attn_grain, 4 * inner)
    ff_half = (ff_count // 2, ff_grain, 3 * width)
    small_shape = (heads + 2, 3 * width)

    attn_back_outs = dict(attn_keep=Kept(attn_half, bf16), attn_send=Kept(attn_half, bf16))
    attn_back_scratch = dict(
        grad_heads=pltpu.VMEM((rows, inner), bf16),
        grad_qkv=pltpu.VMEM((rows, 3 * inner), bf16),
        grad_scores=pltpu.VMEM((rows, heads * slots), bf16),
        attn_grad=pltpu.VMEM((width, 4 * inner), f32),
    )
    mid_scratch = dict(grad_mid=pltpu.VMEM(matrix, f32), branch=pltpu.VMEM(matrix, bf16))
    pulled_scratch = dict(pulled=pltpu.VMEM((256, 2 * width), bf16))
    bias_shape = (slots, heads * slots)

    def attn_back_ins(kept, x, a):
        return dict(
            x=Kept(x),
            a=Kept(a),
            gain_attn=gain_attn,
            attn_w=Kept(kept.attn_w),
            qkv=Kept(kept.qkv),
            probs=Kept(kept.probs),
            heads=Kept(kept.heads),
        )

    def add(left, right):
        return (left.astype(f32) + right.astype(f32)).astype(bf16)

    def halving(keep, send, hops, out):
        for step, hop in enumerate(hops):
            got = yield swap(send, hop)
            if step + 1 < len(hops):
                cut = keep.shape[0] // 2
                send = add(keep[cut:], got[cut:])
                keep = add(keep[:cut], got[:cut])
                out["token"] = send
            else:
                out["token"] = keep = add(keep, got)
        out["piece"] = keep

    def summing(piece, hops, out):
        for hop in hops:
            got = yield swap(piece, hop)
            out["token"] = piece = add(piece, got)
        out["piece"] = piece

    def sharing(piece, hops, out):
        for step, hop in enumerate(hops):
            if step + 1 == len(hops):
                out["near"] = piece
            got = yield swap(piece, hop)
            if step + 1 < len(hops):
                out["token"] = piece = join(piece, got)
            else:
                out["token"] = out["far"] = got

    def rounded(values):
        return lax.reduce_precision(values, exponent_bits=8, mantissa_bits=7)

    def with_small(pieces, small):
        high = rounded(small)
        low = rounded(small - high)
        parts = join(high, low).astype(bf16)[None]
        return join(pieces, parts), high + low

    def add_small(small, got):
        parts = got[-1].astype(f32)
        return small + (parts[: small.shape[0]] + parts[small.shape[0] :])

    def attn_chain(part, layer_idx, out):
        small = part.small if layer_idx == 0 else None
        keep, send = part.attn_keep, part.attn_send
        hops = attn_split[layer_idx] + attn_whole
        for step, hop in enumerate(hops):
            got = yield swap(send, hop)
            if small is not None:
                small = add_small(small, got)
                got = got[:-1]
            if step + 1 < len(attn_split[layer_idx]):
                half = keep.shape[0] // 2
                send = add(keep[half:], got[half:])
                keep = add(keep[:half], got[:half])
            else:
                send = keep = add(keep, got)
            if small is not None and step + 1 < len(hops):
                send, small = with_small(send, small)
            out["token"] = send
        piece = keep[0]
        if own_rows < attn_grain:
            first_row = lax.rem(device_at, attn_low) * own_rows
            piece = lax.dynamic_slice_in_dim(piece, first_row, own_rows, axis=0)
        out["done"] = piece.astype(f32)
        out["small"] = small

    def first_ff_chain(part, out):
        yield from halving(part.ff_keep, part.ff_send, ff_split[0], out)
        yield from summing(out["piece"], ff_whole, out)
        yield from sharing(out["piece"], ff_share, out)

    def second_ff_chain(part, out):
        got = yield swap(part.ff_send, 2)
        count = ff_count
        keeps, sends = [], []
        for side in range(2):
            at, half = side * count, count // 2
            sends.append(add(part.ff_keep[at + half : at + count], got[at + half : at + count]))
            keeps.append(add(part.ff_keep[at : at + half], got[at : at + half]))
        out["token"] = tuple(sends)
        for hops in ((4, 1), (1, 4)):
            got = yield tuple(swap(send, hop) for send, hop in zip(sends, hops))
            count //= 2
            half = count // 2
            sends = [add(keep[half:], one[half:]) for keep, one in zip(keeps, got)]
            keeps = [add(keep[:half], one[:half]) for keep, one in zip(keeps, got)]
            out["token"] = tuple(sends)
        keep, send = (jnp.concatenate(sides, axis=2) for sides in (keeps, sends))
        yield from halving(keep, send, ff_split[1][3:], out)
        yield from summing(out["piece"], ff_whole, out)
        yield from sharing(out["piece"], ff_share, out)

    class Chain:
        def __init__(self, steps, *args):
            self.out = {}
            self.steps = steps(*args, self.out)
            self.arriving = next(self.steps)

        def step(self, token, *others):
            if self.arriving is not None:
                tokens = (*(token if isinstance(token, tuple) else (token,)), *others)
                many = isinstance(self.arriving, tuple)
                arrived = self.arriving if many else (self.arriving,)
                arrived = lax.optimization_barrier((*arrived, *tokens))[: len(arrived)]
                arrived = arrived if many else arrived[0]
                self.arriving = None
                try:
                    self.arriving = self.steps.send(arrived)
                except StopIteration:
                    pass
                return self.out["token"]
            return token

    back_1 = run(
        functools.partial(
            last_backward_body,
            sizes=sizes,
            piece_masks=attn_masks[1],
            ff_masks=ff_masks[1:],
            heads=heads,
        ),
        "layer_1_backward",
        dict(
            place=place,
            grad=cotangent,
            gain_ff=gain_ff,
            middle=Kept(second.middle),
            ff_in=Kept(second.ff_in),
            **ff_ins(1),
            **attn_back_ins(second, first_ff.x_next, first_ff.a_next),
        ),
        dict(
            ff_keep=Kept((2 * ff_count, ff_grain, 3 * width // 2), bf16),
            ff_send=Kept((2 * ff_count, ff_grain, 3 * width // 2), bf16),
            small=Kept(small_shape, f32),
            **attn_back_outs,
            outputs=(matrix, bf16),
            grad_next=Kept(matrix, f32),
            grad_next_low=Kept(matrix, bf16),
            bias_acc=Kept(bias_shape, f32),
        ),
        dict(
            ff_gate_up=pltpu.VMEM((2, width, 2 * width), bf16),
            ff_down=pltpu.VMEM((2, width, width), bf16),
            hidden=pltpu.VMEM((2, rows, width), bf16),
            grad_gate_up=pltpu.VMEM((2, rows, 2 * width), bf16),
            ff_grad=pltpu.VMEM((2, width, 3 * width), f32),
            **mid_scratch,
            **attn_back_scratch,
            **ff_scratch,
        ),
        micros=10,
    )
    peer_grad_0 = swap(back_1.grad_next_low, 1)
    attn_1 = Chain(attn_chain, back_1, 1)
    back_0 = run(
        ff_backward_body,
        "layer_0_ff_backward",
        dict(
            grad=Kept(back_1.grad_next),
            gain_ff=gain_ff,
            small_before=Kept(back_1.small),
            middle=Kept(first.middle),
            ff_in=Kept(first.ff_in),
            ff_gate_up=Kept(first_ff.ff_gate_up),
            ff_down=Kept(first_ff.ff_down),
        ),
        dict(
            hidden=Kept((1, rows, width), bf16),
            grad_gate_up=Kept((1, rows, 2 * width), bf16),
            small=Kept(small_shape, f32),
            grad_mid=Kept(matrix, f32),
            branch=Kept(matrix, bf16),
        ),
        pulled_scratch,
        after=(peer_in_0,),
        micros=10,
    )
    ff_1 = Chain(second_ff_chain, back_1)
    token = ff_1.step(back_0.branch)
    back_attn_0 = run(
        functools.partial(
            attention_backward_body, sizes=sizes, piece_masks=attn_masks[0], heads=heads
        ),
        "layer_0_attention_backward",
        dict(
            place=place,
            bias_before=Kept(back_1.bias_acc),
            marks=marks,
            buckets=wide_buckets,
            small_before=Kept(back_0.small),
            grad_mid=Kept(back_0.grad_mid),
            branch=Kept(back_0.branch),
            **attn_back_ins(first, start.x, start.a),
        ),
        dict(
            attn_keep=Kept(attn_half, bf16),
            attn_send=Kept((attn_count // 2 + 1, *attn_half[1:]), bf16),
            small=Kept(small_shape, f32),
            grad_next=(matrix, f32),
        ),
        dict(
            bias_acc=pltpu.VMEM(bias_shape, f32),
            table_rows=pltpu.VMEM((bias_table.shape[0], heads * slots), f32),
            **attn_back_scratch,
        ),
        after=token,
        micros=7,
    )
    attn_0 = Chain(attn_chain, back_attn_0, 0)
    token = attn_1.step(back_attn_0.attn_send, peer_grad_0)
    part_0 = run(
        functools.partial(weight_body, piece_masks=place_masks),
        "layer_0_weight_grads",
        dict(
            place=place,
            ff_in=Kept(first.ff_in),
            grad=Kept(back_1.grad_next_low),
            hidden=Kept(back_0.hidden),
            grad_gate_up=Kept(back_0.grad_gate_up),
            peer_in=Kept(peer_in_0),
            peer_grad=Kept(peer_grad_0),
            ff_gate_up=Kept(first_ff.ff_gate_up),
            ff_down=Kept(first_ff.ff_down),
        ),
        dict(ff_keep=Kept(ff_half, bf16), ff_send=Kept(ff_half, bf16)),
        dict(
            peer_gate_up=pltpu.VMEM((rows, 2 * width), bf16),
            peer_hidden=pltpu.VMEM(matrix, bf16),
            ff_grad=pltpu.VMEM((width, 3 * width), f32),
        ),
        after=(token,),
        micros=4,
    )
    ff_0 = Chain(first_ff_chain, part_0)
    token = part_0.ff_send
    shape = (2, width, width)
    near_masks = place_masks[: ff_count // 2]
    far_masks = place_masks[ff_count // 2 :]
    done = ()
    ended = False
    sums = attn_grads = None
    while ff_0.arriving is not None:
        token = ff_1.step(token)
        if not done and "near" in ff_1.out:
            done = finish(tie(ff_1.out["near"], token), near_masks, 1, place, shape)
            token = done[0]
        elif not ended and ff_1.arriving is None:
            done = finish(tie(ff_1.out["far"], token), far_masks, 1, place, shape, done)
            token = done[0]
            ended = True
        for chain in (ff_0, attn_0, attn_1):
            token = chain.step(token)
        if sums is None and attn_0.arriving is None:
            sums = run(
                small_body,
                "small_sums",
                dict(packed=Kept(tie(attn_0.out["small"], token))),
                dict(
                    gain_attn=((2, width), f32),
                    gain_ff=((2, width), f32),
                    embed=((1, width), f32),
                    table=(bias_table.shape[::-1], f32),
                ),
                {},
            )
            token = sums.embed
        if attn_grads is None and attn_0.arriving is None and attn_1.arriving is None:
            both = jnp.stack([attn_0.out["done"], tie(attn_1.out["done"], token)])
            attn_grads = [both[:, :, k * inner : (k + 1) * inner] for k in range(4)]
            attn_grads[3] = jnp.swapaxes(attn_grads[3], 1, 2)
            token = tuple(attn_grads)
    if not ended:
        done = finish(ff_1.out["far"], far_masks, 1, place, shape, done)
    for pieces, masks in ((ff_0.out["near"], near_masks), (ff_0.out["far"], far_masks)):
        done = finish(pieces, masks, 0, place, shape, done)
    return (
        back_1.outputs.reshape(inputs.shape),
        back_attn_0.grad_next.reshape(inputs.shape),
        *attn_grads,
        *done,
        sums.gain_attn,
        sums.gain_ff,
        sums.table.T,
        sums.embed[0],
    )


def solution(mesh):
    placed = (
        P(("dp", "tensor"), None, None),
        P(("dp", "tensor"), None, None),
        P(("dp", "tensor"), None),
        P(("dp", "tensor"), None),
        P(),
        P(),
        P(None, ("dp", "tensor"), None),
        P(None, ("dp", "tensor"), None),
        P(None, ("dp", "tensor"), None),
        P(None, None, ("dp", "tensor")),
        P(None, None, "tensor"),
        P(None, None, "tensor"),
        P(None, "tensor", None),
        P(),
        P(),
        P(),
    )
    return jax.shard_map(
        functools.partial(on_device, dp_size=mesh.shape["dp"]),
        mesh=mesh,
        in_specs=placed,
        out_specs=(
            P(("dp", "tensor"), None, None),
            P(("dp", "tensor"), None, None),
            P(None, ("dp", "tensor"), None),
            P(None, ("dp", "tensor"), None),
            P(None, ("dp", "tensor"), None),
            P(None, None, ("dp", "tensor")),
            P(None, None, "tensor"),
            P(None, None, "tensor"),
            P(None, "tensor", None),
            P(),
            P(),
            P(),
            P(),
        ),
        check_vma=False,
    )
```

```python
import functools
import types

import jax
import jax.numpy as jnp
from jax import lax
from jax.experimental import pallas as pl
from jax.experimental.pallas import tpu as pltpu
from jax.sharding import PartitionSpec as P

norm_eps = 1e-06
masked_score = -1e30
bf16 = jnp.bfloat16
f32 = jnp.float32
axes = ("dp", "tensor")
mebibyte = 1024 * 1024
raw_names = ("attn_near", "attn_far", "ff_near", "ff_far", "w_gate", "w_up", "w_down")


def dot_nn(left, right):
    return lax.dot_general(left, right, (((1,), (0,)), ((), ())), preferred_element_type=f32)


def dot_nt(left, right):
    return lax.dot_general(left, right, (((1,), (1,)), ((), ())), preferred_element_type=f32)


def dot_tn(left, right):
    return lax.dot_general(left, right, (((0,), (0,)), ((), ())), preferred_element_type=f32)


def inverse_rms(values):
    return lax.rsqrt(jnp.mean(values * values, axis=-1, keepdims=True) + norm_eps)


def norm_back(values, gain, grad_out):
    scale = inverse_rms(values)
    pulled = grad_out * gain
    mean_part = jnp.mean(pulled * values, axis=-1, keepdims=True)
    grad_in = scale * pulled - values * (scale * scale * scale) * mean_part
    return grad_in, jnp.sum(grad_out * values * scale, axis=0, keepdims=True)


def gelu_terms(gate_act):
    square = gate_act * gate_act
    bent = jnp.tanh(0.7978845608028654 * gate_act * (1.0 + 0.044715 * square))
    half = 0.5 * (1.0 + bent)
    slope = half + 0.5 * gate_act * (1.0 - bent * bent) * (
        0.7978845608028654 * (1.0 + 3.0 * 0.044715 * square)
    )
    return gate_act * half, slope


def cost(micros):
    return pl.CostEstimate(flops=int(micros * 1.15e9), bytes_accessed=0, transcendentals=0)


def run(body, name, ins, outs, scratch, after=(), micros=1, vmem=8):
    in_names, out_names, scratch_names = list(ins), list(outs), list(scratch)
    direct = {n for n in in_names if n == "place" or n in raw_names or isinstance(ins[n], Kept)}
    staged = [n for n in in_names if n not in direct]
    copied = [n for n in out_names if not isinstance(outs[n], Kept)]
    in_sems = {n: i for i, n in enumerate(staged)}
    out_sems = {n: i for i, n in enumerate(copied)}

    def kernel(*refs):
        refs = list(refs)
        sources = dict(zip(in_names, refs))
        refs = refs[len(in_names) + len(after) :]
        targets = dict(zip(out_names, refs))
        refs = refs[len(out_names) :]
        space = dict(zip(scratch_names, refs))
        refs = refs[len(scratch_names) :]
        buffers = dict(zip(staged + copied, refs))
        sems_in, sems_out = refs[len(staged) + len(copied) :]
        kept = {n: ref for n, ref in targets.items() if n not in out_sems}
        r = types.SimpleNamespace(**space, **buffers, **kept)
        for n in direct:
            setattr(r, n, sources[n])

        def copy_in(n):
            return pltpu.make_async_copy(sources[n], buffers[n], sems_in.at[in_sems[n]])

        def copy_out(n):
            return pltpu.make_async_copy(buffers[n], targets[n], sems_out.at[out_sems[n]])

        r.fetch = lambda *names: [copy_in(n).start() for n in names if n in in_sems]
        r.need = lambda *names: [copy_in(n).wait() for n in names if n in in_sems]
        r.write = lambda *names: [copy_out(n).start() for n in names if n in out_sems]
        r.drain = lambda *names: [copy_out(n).wait() for n in names if n in out_sems]
        body(r)

    def in_space(n):
        if n == "place":
            return pltpu.SMEM
        return pltpu.VMEM if isinstance(ins[n], Kept) else pl.ANY

    results = pl.pallas_call(
        kernel,
        name=name,
        in_specs=[pl.BlockSpec(memory_space=in_space(n)) for n in in_names]
        + [pl.BlockSpec(memory_space=pl.ANY) for _ in after],
        out_specs=[
            pl.BlockSpec(memory_space=pltpu.VMEM if isinstance(out, Kept) else pl.ANY)
            for out in outs.values()
        ],
        out_shape=[
            pltpu.VMEM(*out.what) if isinstance(out, Kept) else jax.ShapeDtypeStruct(*out)
            for out in outs.values()
        ],
        scratch_shapes=list(scratch.values())
        + [pltpu.VMEM(ins[n].shape, ins[n].dtype) for n in staged]
        + [pltpu.VMEM(*outs[n]) for n in copied]
        + [
            pltpu.SemaphoreType.DMA((max(1, len(staged)),)),
            pltpu.SemaphoreType.DMA((max(1, len(copied)),)),
        ],
        compiler_params=pltpu.CompilerParams(vmem_limit_bytes=vmem * mebibyte),
        cost_estimate=cost(micros),
    )(
        *[
            pltpu.with_memory_space_constraint(value.what, pltpu.VMEM)
            if isinstance(value, Kept)
            else value
            for value in ins.values()
        ],
        *after,
    )
    return types.SimpleNamespace(**dict(zip(outs, results)))


class Kept:
    def __init__(self, *what):
        self.what = what[0] if len(what) == 1 else what


def keep_all(names):
    return {name: Kept(value) for name, value in names.items()}


def chunks(extent, size):
    size = min(size, extent)
    return [slice(start, start + size) for start in range(0, extent, size)]


def lay_out_attention(r, masks, rows):
    for idx, mask in enumerate(masks):
        half, at = divmod(idx, max(1, len(masks) // 2))
        source = r.attn_near if half == 0 else r.attn_far
        place = pl.multiple_of((r.place[0] ^ mask) * rows, rows) if len(masks) > 1 else 0
        r.attn_w[pl.ds(place, rows), :] = source[at * rows : (at + 1) * rows, :]


def lay_out_ff(r, layer_idx):
    width = r.ff_down.shape[-1]
    for k, own in enumerate((r.w_gate, r.w_up)):
        r.ff_gate_up[0, :, k * width : (k + 1) * width] = own[layer_idx]
    r.ff_down[0] = r.w_down[layer_idx]
    part = r.ff_near.shape[1]
    for source, base in ((r.ff_near, 0), (r.ff_far, 1)):
        for m in range(2):
            rows = pl.ds(pl.multiple_of((r.place[1] ^ (2 * m + base)) * part, part), part)
            for k in range(2):
                r.ff_gate_up[1, rows, k * width : (k + 1) * width] = source[3 * m + k]
            r.ff_down[1, rows, :] = source[3 * m + 2]


def start_all(copies):
    for copy in copies:
        copy.start()


def wait_all(sem, *buffers):
    for whole in buffers:
        pltpu.make_async_copy(whole, whole, sem).wait()


def lane_low(rows):
    return lax.broadcasted_iota(jnp.int32, (rows, 128), 1) < 64


def lane_halves():
    low = lane_low(1).astype(f32)
    return low.astype(bf16), (1.0 - low).astype(bf16)


def pair_blocks(rows, low, high):
    return jnp.concatenate([rows * low, rows * high], axis=0)


def own_blocks(both, is_low):
    half = both.shape[0] // 2
    return jnp.where(is_low, both[:half], both[half:]).astype(bf16)


def attention_forward(r, x_ref, a_ref, sizes, layer_idx):
    series, slots, inner = sizes
    rows = series * slots
    for part in chunks(rows, 256):
        r.qkv[part, :] = dot_nn(a_ref[part, :], r.attn_w[:, : 3 * inner]).astype(bf16)
    is_low = lane_low(slots)
    low, high = lane_halves()
    for s in range(series):
        here = slice(s * slots, (s + 1) * slots)
        keep = r.mask[here, :] == 1
        for start in range(0, inner, 128):
            at = slice(start, start + 128)
            query = r.qkv[here, at]
            keys = r.qkv[here, inner + start : inner + start + 128]
            scores = dot_nt(keys, pair_blocks(query, low, high)) + r.bias[:, at]
            scores = jnp.where(keep, scores, masked_score)
            exps = jnp.exp(scores - jnp.max(scores, axis=0, keepdims=True))
            r.probs[here, at] = exps / jnp.sum(exps, axis=0, keepdims=True)
    for s in range(series):
        here = slice(s * slots, (s + 1) * slots)
        for start in range(0, inner, 128):
            at = slice(start, start + 128)
            values = r.qkv[here, 2 * inner + start : 2 * inner + start + 128]
            both = dot_tn(r.probs[here, at].astype(bf16), values)
            r.heads[here, at] = own_blocks(both, is_low)
    gain = r.gain_ff[layer_idx : layer_idx + 1, :]
    for part in chunks(rows, 256):
        middle = x_ref[part, :] + dot_nt(r.heads[part, :], r.attn_w[:, 3 * inner :])
        r.middle[part, :] = middle
        r.ff_in[part, :] = (middle * inverse_rms(middle) * gain).astype(bf16)


def prepare_body(r):
    r.fetch("inputs", "marks", "embed", "gain_attn", "buckets", "table")
    r.need("inputs", "marks", "embed", "gain_attn", "buckets", "table")
    x = jnp.where(r.marks[:, 0:1] == 1, r.inputs[...].astype(f32), r.embed[...])
    r.x[...] = x
    r.a[...] = (x * inverse_rms(x) * r.gain_attn[0:1, :]).astype(bf16)
    buckets = r.buckets[...]
    bias = jnp.zeros(buckets.shape, f32)
    for idx in range(r.table.shape[0]):
        bias = jnp.where(buckets == idx, r.table[idx : idx + 1, :], bias)
    r.bias[...] = bias
    r.mask[...] = jnp.broadcast_to(r.marks[:, 1:2], r.mask.shape)
    r.write("x", "a", "bias", "mask")
    r.drain("x", "a", "bias", "mask")


def attention_body(r, sizes, masks, grain, layer_idx):
    r.fetch("gain_ff")
    lay_out_attention(r, masks, grain)
    r.need("gain_ff")
    attention_forward(r, r.x, r.a, sizes, layer_idx)


def ff_body(r):
    r.fetch("gain_attn")
    lay_out_ff(r, 0)
    r.need("gain_attn")
    width = r.middle.shape[1]
    for part in chunks(r.middle.shape[0], 256):
        x_next = r.middle[part, :]
        for half in range(2):
            both = dot_nn(r.ff_in[part, :], r.ff_gate_up[half])
            hidden = (gelu_terms(both[:, :width])[0] * both[:, width:]).astype(bf16)
            x_next = x_next + dot_nn(hidden, r.ff_down[half])
        r.x_next[part, :] = x_next
        r.a_next[part, :] = (x_next * inverse_rms(x_next) * r.gain_attn[1:2, :]).astype(bf16)


def ff_backward(r, layer_idx, last, masks):
    rows, width = r.middle.shape
    r.fetch("grad", "gain_ff")
    if last:
        lay_out_ff(r, layer_idx)
    r.need("grad", "gain_ff")
    gain_ff = r.gain_ff[layer_idx : layer_idx + 1, :]
    gain_total = jnp.zeros((1, width), f32)
    for part in chunks(rows, 256):
        grad = r.grad[part, :].astype(f32)
        rounded = grad.astype(bf16)
        ff_rows = r.ff_in[part, :]
        back = None
        middle = r.middle[part, :]
        total = middle
        for half in range(2):
            both = dot_nn(ff_rows, r.ff_gate_up[half])
            grad_hidden = dot_nt(rounded, r.ff_down[half])
            gate_act, up_act = both[:, :width], both[:, width:]
            mixed, slope = gelu_terms(gate_act)
            hidden = (mixed * up_act).astype(bf16)
            r.hidden[half, part, :] = hidden
            r.grad_gate_up[half, part, :width] = (grad_hidden * up_act * slope).astype(bf16)
            r.grad_gate_up[half, part, width:] = (grad_hidden * mixed).astype(bf16)
            pulled = r.grad_gate_up[half, part, :]
            if last:
                total = total + dot_nn(hidden, r.ff_down[half])
            term = dot_nt(pulled, r.ff_gate_up[half])
            back = term if back is None else back + term
        if last:
            r.outputs[part, :] = total.astype(bf16)
        grad_mid, gain_part = norm_back(middle, gain_ff, back)
        gain_total += gain_part
        grad_mid = grad + grad_mid
        r.grad_mid[part, :] = grad_mid
        r.branch[part, :] = grad_mid.astype(bf16)
        r.grad_low[part, :] = rounded
    if last:
        r.write("outputs")
    for half in range(2):
        r.ff_grad[half, :, : 2 * width] = dot_tn(r.ff_in[...], r.grad_gate_up[half])
        r.ff_grad[half, :, 2 * width :] = dot_tn(r.hidden[half], r.grad_low[...])
    half_count = len(masks[0]) // 2
    grain, columns = r.ff_keep.shape[1:]
    for side, side_masks in enumerate(masks):
        lanes = slice(side * columns, (side + 1) * columns)
        for idx, mask in enumerate(side_masks):
            target = r.ff_keep if idx < half_count else r.ff_send
            piece = pl.ds(pl.multiple_of((r.place[3] ^ (mask // 2)) * grain, grain), grain)
            target[side * half_count + idx % half_count] = r.ff_grad[mask % 2, piece, lanes].astype(
                bf16
            )
    if last:
        r.drain("outputs")
    return gain_total


def attention_backward(r, sizes, layer_idx, last, piece_masks, heads):
    series, slots, inner = sizes
    rows = series * slots
    width = r.x.shape[1]
    r.fetch("gain_attn")
    if not last:
        r.fetch("marks", "buckets")
    for part in chunks(rows, 256):
        r.grad_heads[part, :] = dot_nn(r.branch[part, :], r.attn_w[:, 3 * inner :]).astype(bf16)
    is_low = lane_low(slots)
    low, high = lane_halves()
    for start in range(0, inner, 128):
        at = slice(start, start + 128)
        bias_total = jnp.zeros((slots, 128), f32) if last else r.bias_before[:, at]
        for s in range(series):
            here = slice(s * slots, (s + 1) * slots)
            probs = r.probs[here, at]
            values = r.qkv[here, 2 * inner + start : 2 * inner + start + 128]
            grad_probs = dot_nt(values, pair_blocks(r.grad_heads[here, at], low, high))
            inner_sum = jnp.sum(probs * grad_probs, axis=0, keepdims=True)
            grad_scores = (probs * (grad_probs - inner_sum)).astype(bf16)
            r.grad_scores[here, at] = grad_scores
            bias_total = bias_total + grad_scores.astype(f32)
        r.bias_acc[:, at] = bias_total
    for s in range(series):
        here = slice(s * slots, (s + 1) * slots)
        for start in range(0, inner, 128):
            at = slice(start, start + 128)
            key_at = slice(inner + start, inner + start + 128)
            value_at = slice(2 * inner + start, 2 * inner + start + 128)
            grad_scores = r.grad_scores[here, at]
            r.grad_qkv[here, key_at] = dot_nn(
                grad_scores, pair_blocks(r.qkv[here, at], low, high)
            ).astype(bf16)
            r.grad_qkv[here, value_at] = dot_nn(
                r.probs[here, at].astype(bf16), pair_blocks(r.grad_heads[here, at], low, high)
            ).astype(bf16)
            r.grad_qkv[here, at] = own_blocks(dot_tn(grad_scores, r.qkv[here, key_at]), is_low)
    r.attn_grad[:, : 3 * inner] = dot_tn(r.a[...], r.grad_qkv[...])
    r.attn_grad[:, 3 * inner :] = dot_tn(r.branch[...], r.heads[...])
    scatter_pieces(r.attn_grad, r.attn_keep, r.attn_send, piece_masks, r.place[2])
    r.need("gain_attn")
    if not last:
        r.need("marks", "buckets")
    gain_attn = r.gain_attn[layer_idx : layer_idx + 1, :]
    gain_total = jnp.zeros((1, width), f32)
    embed_total = jnp.zeros((1, width), f32)
    for part in chunks(rows, 256):
        grad_normed = dot_nt(r.grad_qkv[part, :], r.attn_w[:, : 3 * inner])
        grad_in, gain_part = norm_back(r.x[part, :], gain_attn, grad_normed)
        gain_total += gain_part
        grad_in = r.grad_mid[part, :] + grad_in
        if last:
            r.grad_next[part, :] = grad_in
        else:
            seen = r.marks[part, 0:1] == 1
            r.grad_next[part, :] = jnp.where(seen, grad_in, 0.0)
            embed_total += jnp.sum(jnp.where(seen, 0.0, grad_in), axis=0, keepdims=True)
    r.write("grad_next")
    if not last:
        put_row(r.small, 4, embed_total)
        head_size = inner // heads
        for idx in range(r.table_rows.shape[0]):
            chosen = jnp.where(r.buckets[...] == idx, r.bias_acc[...], 0.0)
            r.table_rows[idx : idx + 1, :] = jnp.sum(chosen, axis=0, keepdims=True)
        lane = lax.broadcasted_iota(jnp.int32, (r.table_rows.shape[0], 128), 1)
        table = jnp.zeros(lane.shape, f32)
        for head in range(heads):
            cut = r.table_rows[:, head * head_size : (head + 1) * head_size]
            table = jnp.where(lane == head, jnp.sum(cut, axis=1, keepdims=True), table)
        r.small[:heads, : table.shape[0]] = jnp.transpose(table)[:heads, :]
    r.drain("grad_next")
    return gain_total


def two_parts(values):
    high = values.astype(bf16).astype(f32)
    return high, (values - high).astype(bf16).astype(f32)


def last_ff_body(r, masks):
    r.small[...] = jnp.zeros(r.small.shape, f32)
    put_row(r.small, 3, ff_backward(r, 1, True, masks))


def last_attention_body(r, sizes, piece_masks, heads):
    r.small[...] = r.small_before[...]
    put_row(r.small, 1, attention_backward(r, sizes, 1, True, piece_masks, heads))


def ff_backward_body(r, masks):
    r.small[...] = r.small_before[...]
    put_row(r.small, 2, ff_backward(r, 0, False, masks))


def attention_backward_body(r, sizes, piece_masks, heads):
    r.small[...] = r.small_before[...]
    put_row(r.small, 0, attention_backward(r, sizes, 0, False, piece_masks, heads))
    high, low = two_parts(r.small[...])
    last = r.attn_send.shape[0] - 1
    r.attn_send[last] = jnp.concatenate([high, low], axis=0).astype(bf16)
    r.small[...] = high + low


def put_row(packed, which, row):
    first, width = packed.shape[0] - 2, row.shape[1]
    at = which % 3 * width
    packed[first + which // 3 : first + which // 3 + 1, at : at + width] = row


def scatter_pieces(whole, keep, send, masks, place):
    count = len(masks)
    grain = whole.shape[0] // count
    for idx, mask in enumerate(masks):
        target = keep if idx < count // 2 else send
        source = pl.ds(pl.multiple_of((place ^ mask) * grain, grain), grain)
        target[idx % (count // 2)] = whole[source, :].astype(bf16)


def finish(pieces, masks, layer_idx, place, shape, before=()):
    grain, width = pieces.shape[1], shape[-1]
    count = len(before)

    def kernel(place_ref, source, *refs):
        outs = refs[count : count + 3]
        stage, out_sem = refs[count + 3 :]
        for idx, mask in enumerate(masks):
            rows = pl.ds(pl.multiple_of((place_ref[3] ^ mask) * grain, grain), grain)
            for k, out in enumerate(outs):
                stage[k, idx] = source[idx, :, k * width : (k + 1) * width].astype(f32)
                pltpu.make_async_copy(stage.at[k, idx], out.at[layer_idx, rows], out_sem).start()
        pltpu.make_async_copy(stage, stage, out_sem).wait()

    return pl.pallas_call(
        kernel,
        name="layer_%d_ff_grads" % layer_idx,
        in_specs=[
            pl.BlockSpec(memory_space=pltpu.SMEM),
            pl.BlockSpec(memory_space=pltpu.VMEM),
        ]
        + [pl.BlockSpec(memory_space=pl.ANY)] * count,
        out_specs=[pl.BlockSpec(memory_space=pl.ANY)] * 3,
        out_shape=[jax.ShapeDtypeStruct(shape, f32)] * 3,
        input_output_aliases={2 + k: k for k in range(count)},
        scratch_shapes=[
            pltpu.VMEM((3, len(masks), grain, width), f32),
            pltpu.SemaphoreType.DMA,
        ],
        compiler_params=pltpu.CompilerParams(vmem_limit_bytes=6 * mebibyte),
        cost_estimate=cost(3),
    )(place, pltpu.with_memory_space_constraint(pieces, pltpu.VMEM), *before)


def small_body(r):
    width = r.embed.shape[1]
    heads = r.table.shape[0]
    outs = ((r.gain_attn, 0), (r.gain_attn, 1), (r.gain_ff, 0), (r.gain_ff, 1), (r.embed, 0))
    for which, (out, row) in enumerate(outs):
        first = r.packed.shape[0] - 2 + which // 3
        at = which % 3 * width
        out[row : row + 1, :] = r.packed[first : first + 1, at : at + width]
    r.table[...] = r.packed[:heads, : r.table.shape[1]]
    r.write("gain_attn", "gain_ff", "embed", "table")
    r.drain("gain_attn", "gain_ff", "embed", "table")


def cut_body(r):
    rows = r.quarter_0.shape[1]
    at = pl.ds(pl.multiple_of(r.place[1] * rows, rows), rows)
    outs = (r.quarter_0, r.quarter_1)
    start_all(
        pltpu.make_async_copy(w.at[layer_idx, at], out.at[k], r.cut_sem)
        for layer_idx, out in enumerate(outs)
        for k, w in enumerate((r.w_gate, r.w_up, r.w_down))
    )
    wait_all(r.cut_sem, *outs)


def order_masks(hops):
    masks = [0]
    for hop in reversed(hops):
        masks = masks + [mask ^ hop for mask in masks]
    return masks


def tie(value, *others):
    return lax.optimization_barrier((value, *others))[0]


def on_device(
    inputs,
    cotangent,
    attention_mask,
    patch_valid,
    buckets,
    mask_embed,
    w_query,
    w_key,
    w_value,
    w_output,
    w_gate,
    w_up,
    w_down,
    gain_attn,
    gain_ff,
    bias_table,
    dp_size,
):
    series, slots, width = inputs.shape
    heads = bias_table.shape[1]
    inner = w_query.shape[2]
    rows = series * slots
    sizes = (series, slots, inner)
    matrix = (rows, width)
    devices = 2 * dp_size
    dp_at = lax.axis_index("dp")
    device_at = 2 * dp_at + lax.axis_index("tensor")
    cotangent = cotangent.reshape(matrix)

    def swap(array, mask):
        return lax.ppermute(array, axes, [(n, n ^ mask) for n in range(devices)])

    def join(left, right):
        return jnp.concatenate([left, right], axis=0)

    bits = [1 << k for k in range(devices.bit_length() - 1)]

    attn_grain = max(16, width // devices)
    attn_count = width // attn_grain
    ff_grain = max(16, width // dp_size)
    ff_count = width // ff_grain
    quarter_at = lax.rem(dp_at, 4)
    place = jnp.stack(
        [
            device_at,
            quarter_at,
            device_at // (devices // attn_count),
            lax.rem(dp_at, ff_count),
        ]
    ).astype(jnp.int32)

    quarter = width // 4
    packed = jnp.concatenate([w_query, w_key, w_value, jnp.swapaxes(w_output, 1, 2)], axis=2)
    in_hbm = {
        name: pltpu.with_memory_space_constraint(w, pltpu.HBM)
        for name, w in (("w_gate", w_gate), ("w_up", w_up), ("w_down", w_down))
    }
    ff_blocks = run(
        cut_body,
        "cut_quarters",
        dict(place=place, **in_hbm),
        dict(
            quarter_0=Kept((3, quarter, width), bf16),
            quarter_1=Kept((3, quarter, width), bf16),
        ),
        dict(cut_sem=pltpu.SemaphoreType.DMA),
    )
    own_rows = packed.shape[1]
    direct = own_rows % 16 == 0
    far = bits[2:]

    def prepare(token):
        table, marked, kept, near = (
            tie(array, token) for array in (bias_table, patch_valid, attention_mask, buckets)
        )
        wide_buckets = jnp.tile(near.T, (1, heads))
        wide_table = jnp.repeat(table, slots, axis=1)
        marks = jnp.stack([marked.reshape(rows), kept.reshape(rows)], axis=1)
        result = run(
            prepare_body,
            "prepare",
            dict(
                inputs=inputs.reshape(matrix),
                marks=marks,
                embed=mask_embed[None, :],
                gain_attn=gain_attn,
                buckets=wide_buckets,
                table=wide_table,
            ),
            dict(
                x=Kept(matrix, f32),
                a=Kept(matrix, bf16),
                bias=Kept((slots, heads * slots), f32),
                mask=Kept((rows, 128), jnp.int32),
            ),
            {},
            micros=3,
        )
        return result, wide_buckets, marks

    if direct:
        hops_0 = [1] + far[2:] + far[:2] + [2]
        hops_1 = far[2:] + far[:2] + [1, 2]
        block_0, block_1 = packed[0], packed[1]
        got_1 = swap(block_1, hops_1[0])
        got_0 = swap(block_0, hops_0[0])
        ff_0 = swap(tie(ff_blocks.quarter_0, got_0), 1)
        got_ff_0 = swap(ff_0, 4)
        ff_1 = swap(tie(ff_blocks.quarter_1, ff_0), 1)
        block_0 = join(block_0, got_0)
        block_1 = join(block_1, tie(got_1, block_0))
        for hop_0, hop_1 in zip(hops_0[1:-2], hops_1[1:-2]):
            got_1, got_0 = swap(block_1, hop_1), swap(block_0, hop_0)
            if hop_1 == hops_1[1]:
                start, wide_buckets, marks = prepare(block_1)
            block_0 = join(block_0, got_0)
            block_1 = join(block_1, tie(got_1, block_0))
        got_0 = swap(block_0, hops_0[-2])
        got_1 = swap(block_1, hops_1[-2])
        block_0 = join(block_0, tie(got_0, start.a, got_ff_0, ff_1))
        block_1 = join(block_1, tie(got_1, block_0))
        ff_0 = join(ff_0, tie(got_ff_0, block_1))
        got_ff_1 = swap(tie(ff_1, ff_0), 4)
        far_0 = swap(block_0, 2)
        attn_pieces = [
            (block_0, far_0, order_masks(hops_0[::-1])),
            (block_1, swap(tie(block_1, far_0), 2), order_masks(hops_1[::-1])),
        ]
        after_first = (attn_pieces[1][1],)
    else:
        ff_0, ff_1 = swap(ff_blocks.quarter_0, 1), swap(ff_blocks.quarter_1, 1)
        ff_0 = join(ff_0, swap(ff_0, 4))
        start, wide_buckets, marks = prepare(packed)
        whole = lax.all_gather(packed[0], axes, axis=0, tiled=True)
        attn_pieces = [(whole, whole, [0])]
        whole = lax.all_gather(packed[1], axes, axis=0, tiled=True)
        attn_pieces.append((whole, whole, [0]))
        after_first = ()
    ff_pieces = [(ff_0, swap(ff_0, 2))]

    def attn_ins(layer_idx):
        near, far, masks = attn_pieces[layer_idx]
        return dict(attn_near=Kept(near), attn_far=Kept(far)), masks

    def ff_ins(layer_idx):
        near, far = ff_pieces[layer_idx]
        own = keep_all(dict(w_gate=w_gate, w_up=w_up, w_down=w_down))
        return dict(**own, ff_near=Kept(near), ff_far=Kept(far))

    ff_outs = dict(
        ff_gate_up=Kept((2, width, 2 * width), bf16), ff_down=Kept((2, width, width), bf16)
    )
    grain = own_rows if direct else width
    attn_outs = dict(
        attn_w=Kept((width, 4 * inner), bf16),
        qkv=Kept((rows, 3 * inner), bf16),
        probs=Kept((rows, heads * slots), f32),
        heads=Kept((rows, inner), bf16),
        middle=Kept(matrix, f32),
        ff_in=Kept(matrix, bf16),
    )

    def attention(layer_idx, x, a, after=(), micros=5):
        pieces, masks = attn_ins(layer_idx)
        return run(
            functools.partial(
                attention_body, sizes=sizes, masks=masks, grain=grain, layer_idx=layer_idx
            ),
            "layer_%d_attention" % layer_idx,
            dict(
                place=place,
                x=Kept(x),
                a=Kept(a),
                bias=Kept(start.bias),
                mask=Kept(start.mask),
                gain_ff=gain_ff,
                **pieces,
            ),
            attn_outs,
            {},
            after=after,
            micros=micros,
        )

    first = attention(0, start.x, start.a, micros=10)
    first_ff = run(
        ff_body,
        "layer_0_ff",
        dict(
            place=place,
            middle=Kept(first.middle),
            ff_in=Kept(first.ff_in),
            gain_attn=gain_attn,
            **ff_ins(0),
        ),
        dict(**ff_outs, x_next=Kept(matrix, f32), a_next=Kept(matrix, bf16)),
        {},
        after=after_first,
        micros=0.1,
    )
    if direct:
        ff_1 = join(ff_1, tie(got_ff_1, first_ff.a_next))
    else:
        ff_1 = join(ff_1, swap(ff_1, 4))
    ff_pieces.append((ff_1, swap(ff_1, 2)))
    second = attention(1, first_ff.x_next, first_ff.a_next, micros=0.1)

    attn_low = devices // attn_count
    attn_hops = ([2, 1] + bits[2:], [2] + bits[3:] + bits[2:3] + [1])
    attn_split = [[hop for hop in hops if hop >= attn_low] for hops in attn_hops]
    attn_whole = [hop for hop in bits if hop < attn_low]
    attn_masks = [[mask // attn_low for mask in order_masks(hops)] for hops in attn_split]
    ff_hops = ([2, 4, 1] + bits[3:], [2, 1, 4] + bits[3:])
    ff_split = [[hop for hop in hops if hop // 2 < ff_count] for hops in ff_hops]
    ff_whole = [hop for hop in bits[1:] if hop // 2 >= ff_count]
    ff_share = [hop for hop in bits[:0:-1] if hop // 2 < ff_count]
    ff_masks = [order_masks(hops) for hops in ff_split]
    place_masks = [mask // 2 for mask in order_masks(ff_share[::-1])]
    attn_half = (attn_count // 2, attn_grain, 4 * inner)
    small_shape = (heads + 2, 3 * width)

    attn_back_outs = dict(attn_keep=Kept(attn_half, bf16), attn_send=Kept(attn_half, bf16))
    attn_back_scratch = dict(
        grad_heads=pltpu.VMEM((rows, inner), bf16),
        grad_qkv=pltpu.VMEM((rows, 3 * inner), bf16),
        grad_scores=pltpu.VMEM((rows, heads * slots), bf16),
        attn_grad=pltpu.VMEM((width, 4 * inner), f32),
    )
    ff_back_outs = dict(
        ff_keep=Kept((2 * ff_count, ff_grain, 3 * width // 2), bf16),
        ff_send=Kept((2 * ff_count, ff_grain, 3 * width // 2), bf16),
        small=Kept(small_shape, f32),
        grad_mid=Kept(matrix, f32),
        branch=Kept(matrix, bf16),
    )
    ff_back_scratch = dict(
        hidden=pltpu.VMEM((2, rows, width), bf16),
        grad_gate_up=pltpu.VMEM((2, rows, 2 * width), bf16),
        ff_grad=pltpu.VMEM((2, width, 3 * width), f32),
        grad_low=pltpu.VMEM(matrix, bf16),
    )
    bias_shape = (slots, heads * slots)

    def attn_back_ins(kept, x, a):
        return dict(
            x=Kept(x),
            a=Kept(a),
            gain_attn=gain_attn,
            attn_w=Kept(kept.attn_w),
            qkv=Kept(kept.qkv),
            probs=Kept(kept.probs),
            heads=Kept(kept.heads),
        )

    def add(left, right):
        return (left.astype(f32) + right.astype(f32)).astype(bf16)

    def halving(keep, send, hops, out):
        for step, hop in enumerate(hops):
            got = yield swap(send, hop)
            if step + 1 < len(hops):
                cut = keep.shape[0] // 2
                send = add(keep[cut:], got[cut:])
                keep = add(keep[:cut], got[:cut])
                out["token"] = send
            else:
                out["token"] = keep = add(keep, got)
        out["piece"] = keep

    def summing(piece, hops, out):
        for hop in hops:
            got = yield swap(piece, hop)
            out["token"] = piece = add(piece, got)
        out["piece"] = piece

    def sharing(piece, hops, out):
        for step, hop in enumerate(hops):
            if step + 1 == len(hops):
                out["near"] = piece
            got = yield swap(piece, hop)
            if step + 1 < len(hops):
                out["token"] = piece = join(piece, got)
            else:
                out["token"] = out["far"] = got

    def rounded(values):
        return lax.reduce_precision(values, exponent_bits=8, mantissa_bits=7)

    def with_small(pieces, small):
        high = rounded(small)
        low = rounded(small - high)
        parts = join(high, low).astype(bf16)[None]
        return join(pieces, parts), high + low

    def add_small(small, got):
        parts = got[-1].astype(f32)
        return small + (parts[: small.shape[0]] + parts[small.shape[0] :])

    def attn_chain(part, layer_idx, out):
        small = part.small if layer_idx == 0 else None
        keep, send = part.attn_keep, part.attn_send
        hops = attn_split[layer_idx] + attn_whole
        for step, hop in enumerate(hops):
            got = yield swap(send, hop)
            if small is not None:
                small = add_small(small, got)
                got = got[:-1]
            if step + 1 < len(attn_split[layer_idx]):
                half = keep.shape[0] // 2
                send = add(keep[half:], got[half:])
                keep = add(keep[:half], got[:half])
            else:
                send = keep = add(keep, got)
            if small is not None and step + 1 < len(hops):
                send, small = with_small(send, small)
            out["token"] = send
        piece = keep[0]
        if own_rows < attn_grain:
            first_row = lax.rem(device_at, attn_low) * own_rows
            piece = lax.dynamic_slice_in_dim(piece, first_row, own_rows, axis=0)
        out["done"] = piece.astype(f32)
        out["small"] = small

    def ff_chain(part, out):
        got = yield swap(part.ff_send, 2)
        count = ff_count
        keeps, sends = [], []
        for side in range(2):
            at, half = side * count, count // 2
            sends.append(add(part.ff_keep[at + half : at + count], got[at + half : at + count]))
            keeps.append(add(part.ff_keep[at : at + half], got[at : at + half]))
        out["token"] = tuple(sends)
        for hops in zip(ff_split[0][1:3], ff_split[1][1:3]):
            got = yield tuple(swap(send, hop) for send, hop in zip(sends, hops))
            half = keeps[0].shape[0] // 2
            sends = [add(keep[half:], one[half:]) for keep, one in zip(keeps, got)]
            keeps = [add(keep[:half], one[:half]) for keep, one in zip(keeps, got)]
            out["token"] = tuple(sends)
        keep, send = (jnp.concatenate(sides, axis=2) for sides in (keeps, sends))
        yield from halving(keep, send, ff_split[0][3:], out)
        yield from summing(out["piece"], ff_whole, out)
        yield from sharing(out["piece"], ff_share, out)

    class Chain:
        def __init__(self, steps, *args):
            self.out = {}
            self.steps = steps(*args, self.out)
            self.arriving = next(self.steps)

        def step(self, token, *others):
            if self.arriving is not None:
                tokens = (*(token if isinstance(token, tuple) else (token,)), *others)
                many = isinstance(self.arriving, tuple)
                arrived = self.arriving if many else (self.arriving,)
                arrived = lax.optimization_barrier((*arrived, *tokens))[: len(arrived)]
                arrived = arrived if many else arrived[0]
                self.arriving = None
                try:
                    self.arriving = self.steps.send(arrived)
                except StopIteration:
                    pass
                return self.out["token"]
            return token

    back_ff_1 = run(
        functools.partial(last_ff_body, masks=ff_masks),
        "layer_1_ff",
        dict(
            place=place,
            grad=cotangent,
            gain_ff=gain_ff,
            middle=Kept(second.middle),
            ff_in=Kept(second.ff_in),
            **ff_ins(1),
        ),
        dict(**ff_back_outs, outputs=(matrix, bf16)),
        dict(
            ff_gate_up=pltpu.VMEM((2, width, 2 * width), bf16),
            ff_down=pltpu.VMEM((2, width, width), bf16),
            **ff_back_scratch,
        ),
        micros=8,
        vmem=24,
    )
    ff_1 = Chain(ff_chain, back_ff_1)
    back_1 = run(
        functools.partial(
            last_attention_body, sizes=sizes, piece_masks=attn_masks[1], heads=heads
        ),
        "layer_1_attention_backward",
        dict(
            place=place,
            small_before=Kept(back_ff_1.small),
            grad_mid=Kept(back_ff_1.grad_mid),
            branch=Kept(back_ff_1.branch),
            **attn_back_ins(second, first_ff.x_next, first_ff.a_next),
        ),
        dict(
            **attn_back_outs,
            small=Kept(small_shape, f32),
            grad_next=Kept(matrix, f32),
            bias_acc=Kept(bias_shape, f32),
        ),
        attn_back_scratch,
        micros=6,
        vmem=14,
    )
    attn_1 = Chain(attn_chain, back_1, 1)
    token = ff_1.step(back_1.attn_send)
    token = (attn_1.step(token),)
    back_0 = run(
        functools.partial(ff_backward_body, masks=ff_masks),
        "layer_0_ff_backward",
        dict(
            place=place,
            grad=Kept(back_1.grad_next),
            gain_ff=gain_ff,
            small_before=Kept(back_1.small),
            middle=Kept(first.middle),
            ff_in=Kept(first.ff_in),
            ff_gate_up=Kept(first_ff.ff_gate_up),
            ff_down=Kept(first_ff.ff_down),
        ),
        ff_back_outs,
        ff_back_scratch,
        after=token,
        micros=8,
        vmem=20,
    )
    token = ff_1.step(back_0.branch)
    back_0.ff_send = tie(back_0.ff_send, *token)
    ff_0 = Chain(ff_chain, back_0)
    token = ff_0.step(token)
    back_attn_0 = run(
        functools.partial(
            attention_backward_body, sizes=sizes, piece_masks=attn_masks[0], heads=heads
        ),
        "layer_0_attention_backward",
        dict(
            place=place,
            bias_before=Kept(back_1.bias_acc),
            marks=marks,
            buckets=wide_buckets,
            small_before=Kept(back_0.small),
            grad_mid=Kept(back_0.grad_mid),
            branch=Kept(back_0.branch),
            **attn_back_ins(first, start.x, start.a),
        ),
        dict(
            attn_keep=Kept(attn_half, bf16),
            attn_send=Kept((attn_count // 2 + 1, *attn_half[1:]), bf16),
            small=Kept(small_shape, f32),
            grad_next=(matrix, f32),
        ),
        dict(
            bias_acc=pltpu.VMEM(bias_shape, f32),
            table_rows=pltpu.VMEM((bias_table.shape[0], heads * slots), f32),
            **attn_back_scratch,
        ),
        after=token,
        micros=7,
        vmem=14,
    )
    attn_0 = Chain(attn_chain, back_attn_0, 0)
    token = back_attn_0.attn_send
    shape = (2, width, width)
    near_masks = place_masks[: ff_count // 2]
    far_masks = place_masks[ff_count // 2 :]
    done = ()
    ended = False
    turn = 0
    sums = attn_grads = None
    while ff_0.arriving is not None:
        token = ff_1.step(token)
        if not done and "near" in ff_1.out:
            done = finish(tie(ff_1.out["near"], token), near_masks, 1, place, shape)
            token = done[0]
        elif not ended and ff_1.arriving is None:
            done = finish(tie(ff_1.out["far"], token), far_masks, 1, place, shape, done)
            token = done[0]
            ended = True
        turn += 1
        token = ff_0.step(token)
        if turn != 2:
            token = attn_0.step(token)
        token = attn_1.step(token)
        if sums is None and attn_0.arriving is None:
            sums = run(
                small_body,
                "small_sums",
                dict(packed=Kept(tie(attn_0.out["small"], token))),
                dict(
                    gain_attn=((2, width), f32),
                    gain_ff=((2, width), f32),
                    embed=((1, width), f32),
                    table=(bias_table.shape[::-1], f32),
                ),
                {},
            )
            token = sums.embed
        if attn_grads is None and attn_0.arriving is None and attn_1.arriving is None:
            both = jnp.stack([attn_0.out["done"], tie(attn_1.out["done"], token)])
            attn_grads = [both[:, :, k * inner : (k + 1) * inner] for k in range(4)]
            attn_grads[3] = jnp.swapaxes(attn_grads[3], 1, 2)
            token = tuple(attn_grads)
    if not ended:
        done = finish(ff_1.out["far"], far_masks, 1, place, shape, done)
    for pieces, masks in ((ff_0.out["near"], near_masks), (ff_0.out["far"], far_masks)):
        done = finish(pieces, masks, 0, place, shape, done)
    return (
        back_ff_1.outputs.reshape(inputs.shape),
        back_attn_0.grad_next.reshape(inputs.shape),
        *attn_grads,
        *done,
        sums.gain_attn,
        sums.gain_ff,
        sums.table.T,
        sums.embed[0],
    )


def solution(mesh):
    placed = (
        P(("dp", "tensor"), None, None),
        P(("dp", "tensor"), None, None),
        P(("dp", "tensor"), None),
        P(("dp", "tensor"), None),
        P(),
        P(),
        P(None, ("dp", "tensor"), None),
        P(None, ("dp", "tensor"), None),
        P(None, ("dp", "tensor"), None),
        P(None, None, ("dp", "tensor")),
        P(None, None, "tensor"),
        P(None, None, "tensor"),
        P(None, "tensor", None),
        P(),
        P(),
        P(),
    )
    return jax.shard_map(
        functools.partial(on_device, dp_size=mesh.shape["dp"]),
        mesh=mesh,
        in_specs=placed,
        out_specs=(
            P(("dp", "tensor"), None, None),
            P(("dp", "tensor"), None, None),
            P(None, ("dp", "tensor"), None),
            P(None, ("dp", "tensor"), None),
            P(None, ("dp", "tensor"), None),
            P(None, None, ("dp", "tensor")),
            P(None, None, "tensor"),
            P(None, None, "tensor"),
            P(None, "tensor", None),
            P(),
            P(),
            P(),
            P(),
        ),
        check_vma=False,
    )
```

```python
import functools
import types

import jax
import jax.numpy as jnp
from jax import lax
from jax.experimental import pallas as pl
from jax.experimental.pallas import tpu as pltpu
from jax.sharding import PartitionSpec as P

norm_eps = 1e-06
masked_score = -1e30
bf16 = jnp.bfloat16
f32 = jnp.float32
axes = ("dp", "tensor")
mebibyte = 1024 * 1024
raw_names = ("w_query", "w_key", "w_value", "w_out", "w_gate", "w_up", "w_down")
scalar_names = ("place", "table")


def dot_nn(left, right):
    return lax.dot_general(left, right, (((1,), (0,)), ((), ())), preferred_element_type=f32)


def dot_nt(left, right):
    return lax.dot_general(left, right, (((1,), (1,)), ((), ())), preferred_element_type=f32)


def dot_tn(left, right):
    return lax.dot_general(left, right, (((0,), (0,)), ((), ())), preferred_element_type=f32)


def inverse_rms(values):
    return lax.rsqrt(jnp.mean(values * values, axis=-1, keepdims=True) + norm_eps)


def norm_back(values, gain, grad_out):
    scale = inverse_rms(values)
    pulled = grad_out * gain
    mean_part = jnp.mean(pulled * values, axis=-1, keepdims=True)
    grad_in = scale * pulled - values * (scale * scale * scale) * mean_part
    return grad_in, jnp.sum(grad_out * values * scale, axis=0, keepdims=True)


def gelu_terms(gate_act):
    square = gate_act * gate_act
    bent = jnp.tanh(0.7978845608028654 * gate_act * (1.0 + 0.044715 * square))
    half = 0.5 * (1.0 + bent)
    slope = half + 0.5 * gate_act * (1.0 - bent * bent) * (
        0.7978845608028654 * (1.0 + 3.0 * 0.044715 * square)
    )
    return gate_act * half, slope


def cost(micros):
    return pl.CostEstimate(flops=int(micros * 1.15e9), bytes_accessed=0, transcendentals=0)


def run(body, name, ins, outs, scratch, after=(), micros=1, vmem=8):
    in_names, out_names, scratch_names = list(ins), list(outs), list(scratch)
    direct = {n for n in in_names if n in scalar_names + raw_names or isinstance(ins[n], Kept)}
    staged = [n for n in in_names if n not in direct]
    copied = [n for n in out_names if not isinstance(outs[n], Kept)]
    in_sems = {n: i for i, n in enumerate(staged)}
    out_sems = {n: i for i, n in enumerate(copied)}

    def kernel(*refs):
        refs = list(refs)
        sources = dict(zip(in_names, refs))
        refs = refs[len(in_names) + len(after) :]
        targets = dict(zip(out_names, refs))
        refs = refs[len(out_names) :]
        space = dict(zip(scratch_names, refs))
        refs = refs[len(scratch_names) :]
        buffers = dict(zip(staged + copied, refs))
        sems_in, sems_out = refs[len(staged) + len(copied) :]
        kept = {n: ref for n, ref in targets.items() if n not in out_sems}
        r = types.SimpleNamespace(**space, **buffers, **kept)
        for n in direct:
            setattr(r, n, sources[n])

        def copy_in(n):
            return pltpu.make_async_copy(sources[n], buffers[n], sems_in.at[in_sems[n]])

        def copy_out(n):
            return pltpu.make_async_copy(buffers[n], targets[n], sems_out.at[out_sems[n]])

        r.fetch = lambda *names: [copy_in(n).start() for n in names if n in in_sems]
        r.need = lambda *names: [copy_in(n).wait() for n in names if n in in_sems]
        r.write = lambda *names: [copy_out(n).start() for n in names if n in out_sems]
        r.drain = lambda *names: [copy_out(n).wait() for n in names if n in out_sems]
        body(r)

    def in_space(n):
        if n in scalar_names:
            return pltpu.SMEM
        return pltpu.VMEM if isinstance(ins[n], Kept) else pl.ANY

    results = pl.pallas_call(
        kernel,
        name=name,
        in_specs=[pl.BlockSpec(memory_space=in_space(n)) for n in in_names]
        + [pl.BlockSpec(memory_space=pl.ANY) for _ in after],
        out_specs=[
            pl.BlockSpec(memory_space=pltpu.VMEM if isinstance(out, Kept) else pl.ANY)
            for out in outs.values()
        ],
        out_shape=[
            pltpu.VMEM(*out.what) if isinstance(out, Kept) else jax.ShapeDtypeStruct(*out)
            for out in outs.values()
        ],
        scratch_shapes=list(scratch.values())
        + [pltpu.VMEM(ins[n].shape, ins[n].dtype) for n in staged]
        + [pltpu.VMEM(*outs[n]) for n in copied]
        + [
            pltpu.SemaphoreType.DMA((max(1, len(staged)),)),
            pltpu.SemaphoreType.DMA((max(1, len(copied)),)),
        ],
        compiler_params=pltpu.CompilerParams(vmem_limit_bytes=vmem * mebibyte),
        cost_estimate=cost(micros),
    )(
        *[
            pltpu.with_memory_space_constraint(value.what, pltpu.VMEM)
            if isinstance(value, Kept)
            else value
            for value in ins.values()
        ],
        *after,
    )
    return types.SimpleNamespace(**dict(zip(outs, results)))


class Kept:
    def __init__(self, *what):
        self.what = what[0] if len(what) == 1 else what


def keep_all(names):
    return {name: Kept(value) for name, value in names.items()}


def chunks(extent, size):
    size = min(size, extent)
    return [slice(start, start + size) for start in range(0, extent, size)]


def lay_out_attention(r, masks, rows):
    for idx, mask in enumerate(masks):
        half, at = divmod(idx, max(1, len(masks) // 2))
        source = r.attn_near if half == 0 else r.attn_far
        place = pl.multiple_of((r.place[0] ^ mask) * rows, rows) if len(masks) > 1 else 0
        r.attn_w[pl.ds(place, rows), :] = source[at * rows : (at + 1) * rows, :]


def lay_out_ff(r, layer_idx):
    width = r.ff_down.shape[-1]
    for k, own in enumerate((r.w_gate, r.w_up)):
        r.ff_gate_up[0, :, k * width : (k + 1) * width] = own[layer_idx]
    r.ff_down[0] = r.w_down[layer_idx]
    part = r.ff_near.shape[1]
    for source, base in ((r.ff_near, 0), (r.ff_far, 1)):
        for m in range(2):
            rows = pl.ds(pl.multiple_of((r.place[1] ^ (2 * m + base)) * part, part), part)
            for k in range(2):
                r.ff_gate_up[1, rows, k * width : (k + 1) * width] = source[3 * m + k]
            r.ff_down[1, rows, :] = source[3 * m + 2]


def start_all(copies):
    for copy in copies:
        copy.start()


def wait_all(sem, *buffers):
    for whole in buffers:
        pltpu.make_async_copy(whole, whole, sem).wait()


def lane_low(rows):
    return lax.broadcasted_iota(jnp.int32, (rows, 128), 1) < 64


def lane_halves():
    low = lane_low(1).astype(f32)
    return low.astype(bf16), (1.0 - low).astype(bf16)


def pair_blocks(rows, low, high):
    return jnp.concatenate([rows * low, rows * high], axis=0)


def own_blocks(both, is_low):
    half = both.shape[0] // 2
    return jnp.where(is_low, both[:half], both[half:]).astype(bf16)


def attention_forward(r, x_ref, a_ref, sizes, layer_idx):
    series, slots, inner = sizes
    rows = series * slots
    for part in chunks(rows, 256):
        r.qkv[part, :] = dot_nn(a_ref[part, :], r.attn_w[:, : 3 * inner]).astype(bf16)
    is_low = lane_low(slots)
    low, high = lane_halves()
    for s in range(series):
        here = slice(s * slots, (s + 1) * slots)
        keep = r.mask[here, :] == 1
        for start in range(0, inner, 128):
            at = slice(start, start + 128)
            query = r.qkv[here, at]
            keys = r.qkv[here, inner + start : inner + start + 128]
            scores = dot_nt(keys, pair_blocks(query, low, high)) + r.bias[:, at]
            scores = jnp.where(keep, scores, masked_score)
            exps = jnp.exp(scores - jnp.max(scores, axis=0, keepdims=True))
            r.probs[here, at] = exps / jnp.sum(exps, axis=0, keepdims=True)
    for s in range(series):
        here = slice(s * slots, (s + 1) * slots)
        for start in range(0, inner, 128):
            at = slice(start, start + 128)
            values = r.qkv[here, 2 * inner + start : 2 * inner + start + 128]
            both = dot_tn(r.probs[here, at].astype(bf16), values)
            r.heads[here, at] = own_blocks(both, is_low)
    gain = r.gain_ff[layer_idx : layer_idx + 1, :]
    for part in chunks(rows, 256):
        middle = x_ref[part, :] + dot_nt(r.heads[part, :], r.attn_w[:, 3 * inner :])
        r.middle[part, :] = middle
        r.ff_in[part, :] = (middle * inverse_rms(middle) * gain).astype(bf16)


def prepare_body(r):
    names = ("inputs", "valid", "keep", "embed", "gain_attn", "buckets")
    r.fetch(*names)
    r.need(*names)
    series, slots = r.valid.shape
    gain = r.gain_attn[0:1, :]
    valid = jnp.transpose(r.valid[...].astype(f32))
    keep = jnp.transpose(r.keep[...].astype(f32))
    for s in range(series):
        here = slice(s * slots, (s + 1) * slots)
        seen = valid[:, s : s + 1]
        x = jnp.where(seen == 1.0, r.inputs[here, :].astype(f32), r.embed[...])
        r.x[here, :] = x
        r.a[here, :] = (x * inverse_rms(x) * gain).astype(bf16)
        r.seen[here, :] = jnp.broadcast_to(seen, (slots, 128)).astype(jnp.int32)
        r.mask[here, :] = jnp.broadcast_to(keep[:, s : s + 1], (slots, 128)).astype(jnp.int32)
    turned = jnp.transpose(r.buckets[...].astype(f32)).astype(jnp.int32)
    wide = jnp.concatenate([turned, turned], axis=1)
    r.wide[...] = wide
    is_low = lane_low(slots)
    bucket_count, heads = r.table.shape
    for pair in range(heads // 2):
        bias = jnp.zeros((slots, 128), f32)
        for idx in range(bucket_count):
            entry = jnp.where(is_low, r.table[idx, 2 * pair], r.table[idx, 2 * pair + 1])
            bias = jnp.where(wide == idx, entry, bias)
        r.bias[:, pair * 128 : (pair + 1) * 128] = bias


def attention_body(r, sizes, masks, grain, layer_idx):
    r.fetch("gain_ff")
    lay_out_attention(r, masks, grain)
    r.need("gain_ff")
    attention_forward(r, r.x, r.a, sizes, layer_idx)


def ff_body(r):
    r.fetch("gain_attn")
    lay_out_ff(r, 0)
    r.need("gain_attn")
    width = r.middle.shape[1]
    for part in chunks(r.middle.shape[0], 256):
        x_next = r.middle[part, :]
        for half in range(2):
            both = dot_nn(r.ff_in[part, :], r.ff_gate_up[half])
            hidden = (gelu_terms(both[:, :width])[0] * both[:, width:]).astype(bf16)
            x_next = x_next + dot_nn(hidden, r.ff_down[half])
        r.x_next[part, :] = x_next
        r.a_next[part, :] = (x_next * inverse_rms(x_next) * r.gain_attn[1:2, :]).astype(bf16)


def ff_backward(r, layer_idx, last, masks):
    rows, width = r.middle.shape
    r.fetch("grad", "gain_ff")
    if last:
        lay_out_ff(r, layer_idx)
    r.need("grad", "gain_ff")
    gain_ff = r.gain_ff[layer_idx : layer_idx + 1, :]
    gain_total = jnp.zeros((1, width), f32)
    for part in chunks(rows, 256):
        grad = r.grad[part, :].astype(f32)
        rounded = grad.astype(bf16)
        ff_rows = r.ff_in[part, :]
        back = None
        middle = r.middle[part, :]
        total = middle
        for half in range(2):
            both = dot_nn(ff_rows, r.ff_gate_up[half])
            grad_hidden = dot_nt(rounded, r.ff_down[half])
            gate_act, up_act = both[:, :width], both[:, width:]
            mixed, slope = gelu_terms(gate_act)
            hidden = (mixed * up_act).astype(bf16)
            r.hidden[half, part, :] = hidden
            r.grad_gate_up[half, part, :width] = (grad_hidden * up_act * slope).astype(bf16)
            r.grad_gate_up[half, part, width:] = (grad_hidden * mixed).astype(bf16)
            pulled = r.grad_gate_up[half, part, :]
            if last:
                total = total + dot_nn(hidden, r.ff_down[half])
            term = dot_nt(pulled, r.ff_gate_up[half])
            back = term if back is None else back + term
        if last:
            r.outputs[part, :] = total.astype(bf16)
        grad_mid, gain_part = norm_back(middle, gain_ff, back)
        gain_total += gain_part
        grad_mid = grad + grad_mid
        r.grad_mid[part, :] = grad_mid
        r.branch[part, :] = grad_mid.astype(bf16)
        r.grad_low[part, :] = rounded
    if last:
        r.write("outputs")
    for half in range(2):
        r.ff_grad[half, :, : 2 * width] = dot_tn(r.ff_in[...], r.grad_gate_up[half])
        r.ff_grad[half, :, 2 * width :] = dot_tn(r.hidden[half], r.grad_low[...])
    half_count = len(masks[0]) // 2
    grain, columns = r.ff_keep.shape[1:]
    for side, side_masks in enumerate(masks):
        lanes = slice(side * columns, (side + 1) * columns)
        for idx, mask in enumerate(side_masks):
            target = r.ff_keep if idx < half_count else r.ff_send
            piece = pl.ds(pl.multiple_of((r.place[3] ^ (mask // 2)) * grain, grain), grain)
            target[side * half_count + idx % half_count] = r.ff_grad[mask % 2, piece, lanes].astype(
                bf16
            )
    if last:
        r.drain("outputs")
    return gain_total


def attention_backward(r, sizes, layer_idx, last, piece_masks, heads):
    series, slots, inner = sizes
    rows = series * slots
    width = r.x.shape[1]
    r.fetch("gain_attn")
    for part in chunks(rows, 256):
        r.grad_heads[part, :] = dot_nn(r.branch[part, :], r.attn_w[:, 3 * inner :]).astype(bf16)
    is_low = lane_low(slots)
    low, high = lane_halves()
    for start in range(0, inner, 128):
        at = slice(start, start + 128)
        bias_total = jnp.zeros((slots, 128), f32) if last else r.bias_before[:, at]
        for s in range(series):
            here = slice(s * slots, (s + 1) * slots)
            probs = r.probs[here, at]
            values = r.qkv[here, 2 * inner + start : 2 * inner + start + 128]
            grad_probs = dot_nt(values, pair_blocks(r.grad_heads[here, at], low, high))
            inner_sum = jnp.sum(probs * grad_probs, axis=0, keepdims=True)
            grad_scores = (probs * (grad_probs - inner_sum)).astype(bf16)
            r.grad_scores[here, at] = grad_scores
            bias_total = bias_total + grad_scores.astype(f32)
        r.bias_acc[:, at] = bias_total
    for s in range(series):
        here = slice(s * slots, (s + 1) * slots)
        for start in range(0, inner, 128):
            at = slice(start, start + 128)
            key_at = slice(inner + start, inner + start + 128)
            value_at = slice(2 * inner + start, 2 * inner + start + 128)
            grad_scores = r.grad_scores[here, at]
            r.grad_qkv[here, key_at] = dot_nn(
                grad_scores, pair_blocks(r.qkv[here, at], low, high)
            ).astype(bf16)
            r.grad_qkv[here, value_at] = dot_nn(
                r.probs[here, at].astype(bf16), pair_blocks(r.grad_heads[here, at], low, high)
            ).astype(bf16)
            r.grad_qkv[here, at] = own_blocks(dot_tn(grad_scores, r.qkv[here, key_at]), is_low)
    r.attn_grad[:, : 3 * inner] = dot_tn(r.a[...], r.grad_qkv[...])
    r.attn_grad[:, 3 * inner :] = dot_tn(r.branch[...], r.heads[...])
    scatter_pieces(r.attn_grad, r.attn_keep, r.attn_send, piece_masks, r.place[2])
    r.need("gain_attn")
    gain_attn = r.gain_attn[layer_idx : layer_idx + 1, :]
    gain_total = jnp.zeros((1, width), f32)
    embed_total = jnp.zeros((1, width), f32)
    for part in chunks(rows, 256):
        grad_normed = dot_nt(r.grad_qkv[part, :], r.attn_w[:, : 3 * inner])
        grad_in, gain_part = norm_back(r.x[part, :], gain_attn, grad_normed)
        gain_total += gain_part
        grad_in = r.grad_mid[part, :] + grad_in
        if last:
            r.grad_next[part, :] = grad_in
        else:
            seen = r.seen[part, 0:1] == 1
            r.grad_next[part, :] = jnp.where(seen, grad_in, 0.0)
            embed_total += jnp.sum(jnp.where(seen, 0.0, grad_in), axis=0, keepdims=True)
    r.write("grad_next")
    if not last:
        put_row(r.small, 4, embed_total)
        head_size = inner // heads
        for idx in range(r.table_rows.shape[0]):
            for start in range(0, inner, 128):
                at = slice(start, start + 128)
                chosen = jnp.where(r.wide[...] == idx, r.bias_acc[:, at], 0.0)
                r.table_rows[idx : idx + 1, at] = jnp.sum(chosen, axis=0, keepdims=True)
        lane = lax.broadcasted_iota(jnp.int32, (r.table_rows.shape[0], 128), 1)
        table = jnp.zeros(lane.shape, f32)
        for head in range(heads):
            cut = r.table_rows[:, head * head_size : (head + 1) * head_size]
            table = jnp.where(lane == head, jnp.sum(cut, axis=1, keepdims=True), table)
        r.small[:heads, : table.shape[0]] = jnp.transpose(table)[:heads, :]
    r.drain("grad_next")
    return gain_total


def two_parts(values):
    high = values.astype(bf16).astype(f32)
    return high, (values - high).astype(bf16).astype(f32)


def last_ff_body(r, masks):
    r.small[...] = jnp.zeros(r.small.shape, f32)
    put_row(r.small, 3, ff_backward(r, 1, True, masks))


def last_attention_body(r, sizes, piece_masks, heads):
    r.small[...] = r.small_before[...]
    put_row(r.small, 1, attention_backward(r, sizes, 1, True, piece_masks, heads))


def ff_backward_body(r, masks):
    r.small[...] = r.small_before[...]
    put_row(r.small, 2, ff_backward(r, 0, False, masks))


def attention_backward_body(r, sizes, piece_masks, heads):
    r.small[...] = r.small_before[...]
    put_row(r.small, 0, attention_backward(r, sizes, 0, False, piece_masks, heads))
    high, low = two_parts(r.small[...])
    last = r.attn_send.shape[0] - 1
    r.attn_send[last] = jnp.concatenate([high, low], axis=0).astype(bf16)
    r.small[...] = high + low


def put_row(packed, which, row):
    first, width = packed.shape[0] - 2, row.shape[1]
    at = which % 3 * width
    packed[first + which // 3 : first + which // 3 + 1, at : at + width] = row


def scatter_pieces(whole, keep, send, masks, place):
    count = len(masks)
    grain = whole.shape[0] // count
    for idx, mask in enumerate(masks):
        target = keep if idx < count // 2 else send
        source = pl.ds(pl.multiple_of((place ^ mask) * grain, grain), grain)
        target[idx % (count // 2)] = whole[source, :].astype(bf16)


def finish(pieces, masks, layer_idx, place, shape, before=()):
    grain, width = pieces.shape[1], shape[-1]
    count = len(before)

    def kernel(place_ref, source, *refs):
        outs = refs[count : count + 3]
        stage, out_sem = refs[count + 3 :]
        for idx, mask in enumerate(masks):
            rows = pl.ds(pl.multiple_of((place_ref[3] ^ mask) * grain, grain), grain)
            for k, out in enumerate(outs):
                stage[k, idx] = source[idx, :, k * width : (k + 1) * width].astype(f32)
                pltpu.make_async_copy(stage.at[k, idx], out.at[layer_idx, rows], out_sem).start()
        pltpu.make_async_copy(stage, stage, out_sem).wait()

    return pl.pallas_call(
        kernel,
        name="layer_%d_ff_grads" % layer_idx,
        in_specs=[
            pl.BlockSpec(memory_space=pltpu.SMEM),
            pl.BlockSpec(memory_space=pltpu.VMEM),
        ]
        + [pl.BlockSpec(memory_space=pl.ANY)] * count,
        out_specs=[pl.BlockSpec(memory_space=pl.ANY)] * 3,
        out_shape=[jax.ShapeDtypeStruct(shape, f32)] * 3,
        input_output_aliases={2 + k: k for k in range(count)},
        scratch_shapes=[
            pltpu.VMEM((3, len(masks), grain, width), f32),
            pltpu.SemaphoreType.DMA,
        ],
        compiler_params=pltpu.CompilerParams(vmem_limit_bytes=6 * mebibyte),
        cost_estimate=cost(3),
    )(place, pltpu.with_memory_space_constraint(pieces, pltpu.VMEM), *before)


def small_body(r):
    width = r.embed.shape[1]
    heads = r.table.shape[0]
    outs = ((r.gain_attn, 0), (r.gain_attn, 1), (r.gain_ff, 0), (r.gain_ff, 1), (r.embed, 0))
    for which, (out, row) in enumerate(outs):
        first = r.packed.shape[0] - 2 + which // 3
        at = which % 3 * width
        out[row : row + 1, :] = r.packed[first : first + 1, at : at + width]
    r.table[...] = r.packed[:heads, : r.table.shape[1]]
    r.write("gain_attn", "gain_ff", "embed", "table")
    r.drain("gain_attn", "gain_ff", "embed", "table")


def pack_body(r, packs):
    rows = r.quarter_0.shape[1]
    at = pl.ds(pl.multiple_of(r.place[1] * rows, rows), rows)
    copies = []
    outs = [r.quarter_0, r.quarter_1]
    for layer_idx in range(2):
        for k, w in enumerate((r.w_gate, r.w_up, r.w_down)):
            copies.append((w.at[layer_idx, at], outs[layer_idx].at[k]))
    if packs:
        outs += [r.block_0, r.block_1]
        inner = r.w_query.shape[2]
        for layer_idx in range(2):
            for k, w in enumerate((r.w_query, r.w_key, r.w_value, r.w_out)):
                lanes = pl.ds(k * inner, inner)
                copies.append((w.at[layer_idx], outs[2 + layer_idx].at[:, lanes]))
    start_all([pltpu.make_async_copy(*ends, r.pack_sem) for ends in copies])
    wait_all(r.pack_sem, *outs)


def order_masks(hops):
    masks = [0]
    for hop in reversed(hops):
        masks = masks + [mask ^ hop for mask in masks]
    return masks


def tie(value, *others):
    return lax.optimization_barrier((value, *others))[0]


def on_device(
    inputs,
    cotangent,
    attention_mask,
    patch_valid,
    buckets,
    mask_embed,
    w_query,
    w_key,
    w_value,
    w_output,
    w_gate,
    w_up,
    w_down,
    gain_attn,
    gain_ff,
    bias_table,
    dp_size,
):
    series, slots, width = inputs.shape
    heads = bias_table.shape[1]
    inner = w_query.shape[2]
    rows = series * slots
    sizes = (series, slots, inner)
    matrix = (rows, width)
    devices = 2 * dp_size
    dp_at = lax.axis_index("dp")
    device_at = 2 * dp_at + lax.axis_index("tensor")
    cotangent = cotangent.reshape(matrix)

    def swap(array, mask):
        return lax.ppermute(array, axes, [(n, n ^ mask) for n in range(devices)])

    def join(left, right):
        return jnp.concatenate([left, right], axis=0)

    bits = [1 << k for k in range(devices.bit_length() - 1)]

    attn_grain = max(16, width // devices)
    attn_count = width // attn_grain
    ff_grain = max(16, width // dp_size)
    ff_count = width // ff_grain
    quarter_at = lax.rem(dp_at, 4)
    place = jnp.stack(
        [
            device_at,
            quarter_at,
            device_at // (devices // attn_count),
            lax.rem(dp_at, ff_count),
        ]
    ).astype(jnp.int32)

    quarter = width // 4
    own_rows = w_query.shape[1]
    direct = own_rows % 16 == 0
    w_out = jnp.swapaxes(w_output, 1, 2)
    sources = dict(w_gate=w_gate, w_up=w_up, w_down=w_down)
    block_outs = {}
    if direct:
        sources |= dict(w_query=w_query, w_key=w_key, w_value=w_value, w_out=w_out)
        block_outs = {"block_%d" % k: Kept((own_rows, 4 * inner), bf16) for k in range(2)}
    packed = run(
        functools.partial(pack_body, packs=direct),
        "pack",
        dict(
            place=place,
            **{n: pltpu.with_memory_space_constraint(w, pltpu.HBM) for n, w in sources.items()},
        ),
        dict(
            quarter_0=Kept((3, quarter, width), bf16),
            quarter_1=Kept((3, quarter, width), bf16),
            **block_outs,
        ),
        dict(pack_sem=pltpu.SemaphoreType.DMA),
        vmem=4,
    )
    far = bits[2:]

    def prepare(token):
        return run(
            prepare_body,
            "prepare",
            dict(
                inputs=tie(inputs, token).reshape(matrix),
                valid=patch_valid,
                keep=attention_mask,
                embed=mask_embed[None, :],
                gain_attn=gain_attn,
                buckets=buckets,
                table=bias_table,
            ),
            dict(
                x=Kept(matrix, f32),
                a=Kept(matrix, bf16),
                bias=Kept((slots, heads * slots), f32),
                mask=Kept((rows, 128), jnp.int32),
                seen=Kept((rows, 128), jnp.int32),
                wide=Kept((slots, 128), jnp.int32),
            ),
            {},
            micros=3,
        )

    if direct:
        hops_0 = [1] + far[2:] + far[:2] + [2]
        hops_1 = far[2:] + far[1:2] + [1] + far[:1] + [2]
        block_0, block_1 = packed.block_0, packed.block_1
        got_1 = swap(block_1, hops_1[0])
        got_0 = swap(block_0, hops_0[0])
        ff_0 = swap(tie(packed.quarter_0, got_0), 1)
        ff_1 = swap(tie(packed.quarter_1, ff_0), 1)
        got_ff_0 = swap(ff_0, 4)
        block_0 = join(block_0, got_0)
        block_1 = join(block_1, tie(got_1, block_0))
        for hop_0, hop_1 in zip(hops_0[1:-2], hops_1[1:-2]):
            got_1, got_0 = swap(block_1, hop_1), swap(block_0, hop_0)
            if hop_0 == hops_0[1]:
                start = prepare(block_1)
                got_0 = tie(got_0, ff_0)
            block_0 = join(block_0, got_0)
            block_1 = join(block_1, tie(got_1, block_0))
        got_0 = swap(block_0, hops_0[-2])
        got_1 = swap(block_1, hops_1[-2])
        block_0 = join(block_0, tie(got_0, start.a, got_ff_0, ff_1))
        ff_0 = join(ff_0, tie(got_ff_0, block_0))
        got_ff_1 = swap(tie(ff_1, ff_0), 4)
        attn_pieces = [(block_0, swap(block_0, 2), order_masks(hops_0[::-1]))]
    else:
        ff_0, ff_1 = swap(packed.quarter_0, 1), swap(packed.quarter_1, 1)
        ff_0 = join(ff_0, swap(ff_0, 4))
        start = prepare(ff_0)
        attn_pieces = []
        rows_of = jnp.concatenate([w_query, w_key, w_value, w_out], axis=2)
        for layer_idx in range(2):
            whole = lax.all_gather(rows_of[layer_idx], axes, axis=0, tiled=True)
            attn_pieces.append((whole, whole, [0]))
    ff_pieces = [(ff_0, swap(ff_0, 2))]

    def attn_ins(layer_idx):
        near, far, masks = attn_pieces[layer_idx]
        return dict(attn_near=Kept(near), attn_far=Kept(far)), masks

    def ff_ins(layer_idx):
        near, far = ff_pieces[layer_idx]
        own = keep_all(dict(w_gate=w_gate, w_up=w_up, w_down=w_down))
        return dict(**own, ff_near=Kept(near), ff_far=Kept(far))

    ff_outs = dict(
        ff_gate_up=Kept((2, width, 2 * width), bf16), ff_down=Kept((2, width, width), bf16)
    )
    grain = own_rows if direct else width
    attn_outs = dict(
        attn_w=Kept((width, 4 * inner), bf16),
        qkv=Kept((rows, 3 * inner), bf16),
        probs=Kept((rows, heads * slots), f32),
        heads=Kept((rows, inner), bf16),
        middle=Kept(matrix, f32),
        ff_in=Kept(matrix, bf16),
    )

    def attention(layer_idx, x, a, after=(), micros=5):
        pieces, masks = attn_ins(layer_idx)
        return run(
            functools.partial(
                attention_body, sizes=sizes, masks=masks, grain=grain, layer_idx=layer_idx
            ),
            "layer_%d_attention" % layer_idx,
            dict(
                place=place,
                x=Kept(x),
                a=Kept(a),
                bias=Kept(start.bias),
                mask=Kept(start.mask),
                gain_ff=gain_ff,
                **pieces,
            ),
            attn_outs,
            {},
            after=after,
            micros=micros,
        )

    first = attention(0, start.x, start.a, micros=10)
    if direct:
        block_1 = join(block_1, tie(got_1, first.ff_in))
        attn_pieces.append((block_1, swap(block_1, 2), order_masks(hops_1[::-1])))
        ff_1 = join(ff_1, tie(got_ff_1, block_1))
    else:
        ff_1 = join(ff_1, swap(ff_1, 4))
    ff_pieces.append((ff_1, swap(ff_1, 2)))
    first_ff = run(
        ff_body,
        "layer_0_ff",
        dict(
            place=place,
            middle=Kept(first.middle),
            ff_in=Kept(first.ff_in),
            gain_attn=gain_attn,
            **ff_ins(0),
        ),
        dict(**ff_outs, x_next=Kept(matrix, f32), a_next=Kept(matrix, bf16)),
        {},
        after=(block_1, ff_1) if direct else (),
        micros=3,
    )
    second = attention(1, first_ff.x_next, first_ff.a_next, micros=0.1)

    attn_low = devices // attn_count
    attn_hops = ([2, 1] + bits[2:], [2] + bits[3:] + bits[2:3] + [1])
    attn_split = [[hop for hop in hops if hop >= attn_low] for hops in attn_hops]
    attn_whole = [hop for hop in bits if hop < attn_low]
    attn_masks = [[mask // attn_low for mask in order_masks(hops)] for hops in attn_split]
    ff_hops = ([2, 4, 1] + bits[3:], [2, 1, 4] + bits[3:])
    ff_split = [[hop for hop in hops if hop // 2 < ff_count] for hops in ff_hops]
    ff_whole = [hop for hop in bits[1:] if hop // 2 >= ff_count]
    ff_share = [hop for hop in bits[:0:-1] if hop // 2 < ff_count]
    ff_masks = [order_masks(hops) for hops in ff_split]
    place_masks = [mask // 2 for mask in order_masks(ff_share[::-1])]
    attn_half = (attn_count // 2, attn_grain, 4 * inner)
    small_shape = (heads + 2, 3 * width)

    attn_back_outs = dict(attn_keep=Kept(attn_half, bf16), attn_send=Kept(attn_half, bf16))
    attn_back_scratch = dict(
        grad_heads=pltpu.VMEM((rows, inner), bf16),
        grad_qkv=pltpu.VMEM((rows, 3 * inner), bf16),
        grad_scores=pltpu.VMEM((rows, heads * slots), bf16),
        attn_grad=pltpu.VMEM((width, 4 * inner), f32),
    )
    ff_back_outs = dict(
        ff_keep=Kept((2 * ff_count, ff_grain, 3 * width // 2), bf16),
        ff_send=Kept((2 * ff_count, ff_grain, 3 * width // 2), bf16),
        small=Kept(small_shape, f32),
        grad_mid=Kept(matrix, f32),
        branch=Kept(matrix, bf16),
    )
    ff_back_scratch = dict(
        hidden=pltpu.VMEM((2, rows, width), bf16),
        grad_gate_up=pltpu.VMEM((2, rows, 2 * width), bf16),
        ff_grad=pltpu.VMEM((2, width, 3 * width), f32),
        grad_low=pltpu.VMEM(matrix, bf16),
    )
    bias_shape = (slots, heads * slots)

    def attn_back_ins(kept, x, a):
        return dict(
            x=Kept(x),
            a=Kept(a),
            gain_attn=gain_attn,
            attn_w=Kept(kept.attn_w),
            qkv=Kept(kept.qkv),
            probs=Kept(kept.probs),
            heads=Kept(kept.heads),
        )

    def add(left, right):
        return (left.astype(f32) + right.astype(f32)).astype(bf16)

    def halving(keep, send, hops, out):
        for step, hop in enumerate(hops):
            got = yield swap(send, hop)
            if step + 1 < len(hops):
                cut = keep.shape[0] // 2
                send = add(keep[cut:], got[cut:])
                keep = add(keep[:cut], got[:cut])
                out["token"] = send
            else:
                out["token"] = keep = add(keep, got)
        out["piece"] = keep

    def summing(piece, hops, out):
        for hop in hops:
            got = yield swap(piece, hop)
            out["token"] = piece = add(piece, got)
        out["piece"] = piece

    def sharing(piece, hops, out):
        for step, hop in enumerate(hops):
            if step + 1 == len(hops):
                out["near"] = piece
            got = yield swap(piece, hop)
            if step + 1 < len(hops):
                out["token"] = piece = join(piece, got)
            else:
                out["token"] = out["far"] = got

    def rounded(values):
        return lax.reduce_precision(values, exponent_bits=8, mantissa_bits=7)

    def with_small(pieces, small):
        high = rounded(small)
        low = rounded(small - high)
        parts = join(high, low).astype(bf16)[None]
        return join(pieces, parts), high + low

    def add_small(small, got):
        parts = got[-1].astype(f32)
        return small + (parts[: small.shape[0]] + parts[small.shape[0] :])

    def attn_chain(part, layer_idx, out):
        small = part.small if layer_idx == 0 else None
        keep, send = part.attn_keep, part.attn_send
        hops = attn_split[layer_idx] + attn_whole
        for step, hop in enumerate(hops):
            got = yield swap(send, hop)
            if small is not None:
                small = add_small(small, got)
                got = got[:-1]
            if step + 1 < len(attn_split[layer_idx]):
                half = keep.shape[0] // 2
                send = add(keep[half:], got[half:])
                keep = add(keep[:half], got[:half])
            else:
                send = keep = add(keep, got)
            if small is not None and step + 1 < len(hops):
                send, small = with_small(send, small)
            out["token"] = send
        piece = keep[0]
        if own_rows < attn_grain:
            first_row = lax.rem(device_at, attn_low) * own_rows
            piece = lax.dynamic_slice_in_dim(piece, first_row, own_rows, axis=0)
        out["done"] = piece.astype(f32)
        out["small"] = small

    def ff_chain(part, out):
        got = yield swap(part.ff_send, 2)
        count = ff_count
        keeps, sends = [], []
        for side in range(2):
            at, half = side * count, count // 2
            sends.append(add(part.ff_keep[at + half : at + count], got[at + half : at + count]))
            keeps.append(add(part.ff_keep[at : at + half], got[at : at + half]))
        out["token"] = tuple(sends)
        for hops in zip(ff_split[0][1:3], ff_split[1][1:3]):
            got = yield tuple(swap(send, hop) for send, hop in zip(sends, hops))
            half = keeps[0].shape[0] // 2
            sends = [add(keep[half:], one[half:]) for keep, one in zip(keeps, got)]
            keeps = [add(keep[:half], one[:half]) for keep, one in zip(keeps, got)]
            out["token"] = tuple(sends)
        keep, send = (jnp.concatenate(sides, axis=2) for sides in (keeps, sends))
        yield from halving(keep, send, ff_split[0][3:], out)
        yield from summing(out["piece"], ff_whole, out)
        yield from sharing(out["piece"], ff_share, out)

    class Chain:
        def __init__(self, steps, *args):
            self.out = {}
            self.steps = steps(*args, self.out)
            self.arriving = next(self.steps)

        def step(self, token, *others):
            if self.arriving is not None:
                tokens = (*(token if isinstance(token, tuple) else (token,)), *others)
                many = isinstance(self.arriving, tuple)
                arrived = self.arriving if many else (self.arriving,)
                arrived = lax.optimization_barrier((*arrived, *tokens))[: len(arrived)]
                arrived = arrived if many else arrived[0]
                self.arriving = None
                try:
                    self.arriving = self.steps.send(arrived)
                except StopIteration:
                    pass
                return self.out["token"]
            return token

    back_ff_1 = run(
        functools.partial(last_ff_body, masks=ff_masks),
        "layer_1_ff",
        dict(
            place=place,
            grad=cotangent,
            gain_ff=gain_ff,
            middle=Kept(second.middle),
            ff_in=Kept(second.ff_in),
            **ff_ins(1),
        ),
        dict(**ff_back_outs, outputs=(matrix, bf16)),
        dict(
            ff_gate_up=pltpu.VMEM((2, width, 2 * width), bf16),
            ff_down=pltpu.VMEM((2, width, width), bf16),
            **ff_back_scratch,
        ),
        micros=8,
        vmem=24,
    )
    ff_1 = Chain(ff_chain, back_ff_1)
    back_1 = run(
        functools.partial(
            last_attention_body, sizes=sizes, piece_masks=attn_masks[1], heads=heads
        ),
        "layer_1_attention_backward",
        dict(
            place=place,
            small_before=Kept(back_ff_1.small),
            grad_mid=Kept(back_ff_1.grad_mid),
            branch=Kept(back_ff_1.branch),
            **attn_back_ins(second, first_ff.x_next, first_ff.a_next),
        ),
        dict(
            **attn_back_outs,
            small=Kept(small_shape, f32),
            grad_next=Kept(matrix, f32),
            bias_acc=Kept(bias_shape, f32),
        ),
        attn_back_scratch,
        micros=6,
        vmem=14,
    )
    attn_1 = Chain(attn_chain, back_1, 1)
    token = ff_1.step(back_1.attn_send)
    token = (attn_1.step(token),)
    back_0 = run(
        functools.partial(ff_backward_body, masks=ff_masks),
        "layer_0_ff_backward",
        dict(
            place=place,
            grad=Kept(back_1.grad_next),
            gain_ff=gain_ff,
            small_before=Kept(back_1.small),
            middle=Kept(first.middle),
            ff_in=Kept(first.ff_in),
            ff_gate_up=Kept(first_ff.ff_gate_up),
            ff_down=Kept(first_ff.ff_down),
        ),
        ff_back_outs,
        ff_back_scratch,
        after=token,
        micros=8,
        vmem=20,
    )
    token = ff_1.step(back_0.branch)
    back_0.ff_send = tie(back_0.ff_send, *token)
    ff_0 = Chain(ff_chain, back_0)
    token = ff_0.step(token)
    back_attn_0 = run(
        functools.partial(
            attention_backward_body, sizes=sizes, piece_masks=attn_masks[0], heads=heads
        ),
        "layer_0_attention_backward",
        dict(
            place=place,
            bias_before=Kept(back_1.bias_acc),
            seen=Kept(start.seen),
            wide=Kept(start.wide),
            small_before=Kept(back_0.small),
            grad_mid=Kept(back_0.grad_mid),
            branch=Kept(back_0.branch),
            **attn_back_ins(first, start.x, start.a),
        ),
        dict(
            attn_keep=Kept(attn_half, bf16),
            attn_send=Kept((attn_count // 2 + 1, *attn_half[1:]), bf16),
            small=Kept(small_shape, f32),
            grad_next=(matrix, f32),
        ),
        dict(
            bias_acc=pltpu.VMEM(bias_shape, f32),
            table_rows=pltpu.VMEM((bias_table.shape[0], heads * slots), f32),
            **attn_back_scratch,
        ),
        after=token,
        micros=7,
        vmem=14,
    )
    attn_0 = Chain(attn_chain, back_attn_0, 0)
    token = back_attn_0.attn_send
    shape = (2, width, width)
    near_masks = place_masks[: ff_count // 2]
    far_masks = place_masks[ff_count // 2 :]
    done = ()
    ended = False
    turn = 0
    sums = attn_grads = None
    while ff_0.arriving is not None:
        turn += 1
        token = ff_1.step(token)
        if done and not ended:
            done = finish(tie(ff_1.out["far"], token), far_masks, 1, place, shape, done)
            token = done[0]
            ended = True
        token = ff_0.step(token)
        if not done and "near" in ff_1.out:
            done = finish(tie(ff_1.out["near"], token), near_masks, 1, place, shape)
            token = done[0]
        if turn != 2:
            token = attn_0.step(token)
            token = attn_1.step(token)
        if sums is None and attn_0.arriving is None:
            sums = run(
                small_body,
                "small_sums",
                dict(packed=Kept(tie(attn_0.out["small"], token))),
                dict(
                    gain_attn=((2, width), f32),
                    gain_ff=((2, width), f32),
                    embed=((1, width), f32),
                    table=(bias_table.shape[::-1], f32),
                ),
                {},
            )
            token = sums.embed
        if attn_grads is None and attn_0.arriving is None and attn_1.arriving is None:
            both = jnp.stack([attn_0.out["done"], tie(attn_1.out["done"], token)])
            attn_grads = [both[:, :, k * inner : (k + 1) * inner] for k in range(4)]
            attn_grads[3] = jnp.swapaxes(attn_grads[3], 1, 2)
            token = tuple(attn_grads)
    if not ended:
        done = finish(ff_1.out["far"], far_masks, 1, place, shape, done)
    for pieces, masks in ((ff_0.out["near"], near_masks), (ff_0.out["far"], far_masks)):
        done = finish(pieces, masks, 0, place, shape, done)
    return (
        back_ff_1.outputs.reshape(inputs.shape),
        back_attn_0.grad_next.reshape(inputs.shape),
        *attn_grads,
        *done,
        sums.gain_attn,
        sums.gain_ff,
        sums.table.T,
        sums.embed[0],
    )


def solution(mesh):
    placed = (
        P(("dp", "tensor"), None, None),
        P(("dp", "tensor"), None, None),
        P(("dp", "tensor"), None),
        P(("dp", "tensor"), None),
        P(),
        P(),
        P(None, ("dp", "tensor"), None),
        P(None, ("dp", "tensor"), None),
        P(None, ("dp", "tensor"), None),
        P(None, None, ("dp", "tensor")),
        P(None, None, "tensor"),
        P(None, None, "tensor"),
        P(None, "tensor", None),
        P(),
        P(),
        P(),
    )
    return jax.shard_map(
        functools.partial(on_device, dp_size=mesh.shape["dp"]),
        mesh=mesh,
        in_specs=placed,
        out_specs=(
            P(("dp", "tensor"), None, None),
            P(("dp", "tensor"), None, None),
            P(None, ("dp", "tensor"), None),
            P(None, ("dp", "tensor"), None),
            P(None, ("dp", "tensor"), None),
            P(None, None, ("dp", "tensor")),
            P(None, None, "tensor"),
            P(None, None, "tensor"),
            P(None, "tensor", None),
            P(),
            P(),
            P(),
            P(),
        ),
        check_vma=False,
    )
```

```python
import functools
import types

import jax
import jax.numpy as jnp
from jax import lax
from jax.experimental import pallas as pl
from jax.experimental.pallas import tpu as pltpu
from jax.sharding import PartitionSpec as P

norm_eps = 1e-06
masked_score = -1e30
bf16 = jnp.bfloat16
f32 = jnp.float32
axes = ("dp", "tensor")
mebibyte = 1024 * 1024
raw_names = ("w_query", "w_key", "w_value", "w_out", "w_gate", "w_up", "w_down")
scalar_names = ("place", "table")


def dot_nn(left, right):
    return lax.dot_general(left, right, (((1,), (0,)), ((), ())), preferred_element_type=f32)


def dot_nt(left, right):
    return lax.dot_general(left, right, (((1,), (1,)), ((), ())), preferred_element_type=f32)


def dot_tn(left, right):
    return lax.dot_general(left, right, (((0,), (0,)), ((), ())), preferred_element_type=f32)


def inverse_rms(values):
    return lax.rsqrt(jnp.mean(values * values, axis=-1, keepdims=True) + norm_eps)


def norm_back(values, gain, grad_out):
    scale = inverse_rms(values)
    pulled = grad_out * gain
    mean_part = jnp.mean(pulled * values, axis=-1, keepdims=True)
    grad_in = scale * pulled - values * (scale * scale * scale) * mean_part
    return grad_in, jnp.sum(grad_out * values * scale, axis=0, keepdims=True)


def gelu_terms(gate_act):
    square = gate_act * gate_act
    bent = jnp.tanh(0.7978845608028654 * gate_act * (1.0 + 0.044715 * square))
    half = 0.5 * (1.0 + bent)
    slope = half + 0.5 * gate_act * (1.0 - bent * bent) * (
        0.7978845608028654 * (1.0 + 3.0 * 0.044715 * square)
    )
    return gate_act * half, slope


def cost(micros):
    return pl.CostEstimate(flops=int(micros * 1.15e9), bytes_accessed=0, transcendentals=0)


def run(body, name, ins, outs, scratch, after=(), micros=1, vmem=8):
    in_names, out_names, scratch_names = list(ins), list(outs), list(scratch)
    direct = {n for n in in_names if n in scalar_names + raw_names or isinstance(ins[n], Kept)}
    staged = [n for n in in_names if n not in direct]
    copied = [n for n in out_names if not isinstance(outs[n], Kept)]
    in_sems = {n: i for i, n in enumerate(staged)}
    out_sems = {n: i for i, n in enumerate(copied)}

    def kernel(*refs):
        refs = list(refs)
        sources = dict(zip(in_names, refs))
        refs = refs[len(in_names) + len(after) :]
        targets = dict(zip(out_names, refs))
        refs = refs[len(out_names) :]
        space = dict(zip(scratch_names, refs))
        refs = refs[len(scratch_names) :]
        buffers = dict(zip(staged + copied, refs))
        sems_in, sems_out = refs[len(staged) + len(copied) :]
        kept = {n: ref for n, ref in targets.items() if n not in out_sems}
        r = types.SimpleNamespace(**space, **buffers, **kept)
        for n in direct:
            setattr(r, n, sources[n])

        def copy_in(n):
            return pltpu.make_async_copy(sources[n], buffers[n], sems_in.at[in_sems[n]])

        def copy_out(n):
            return pltpu.make_async_copy(buffers[n], targets[n], sems_out.at[out_sems[n]])

        r.fetch = lambda *names: [copy_in(n).start() for n in names if n in in_sems]
        r.need = lambda *names: [copy_in(n).wait() for n in names if n in in_sems]
        r.write = lambda *names: [copy_out(n).start() for n in names if n in out_sems]
        r.drain = lambda *names: [copy_out(n).wait() for n in names if n in out_sems]
        body(r)

    def in_space(n):
        if n in scalar_names:
            return pltpu.SMEM
        return pltpu.VMEM if isinstance(ins[n], Kept) else pl.ANY

    results = pl.pallas_call(
        kernel,
        name=name,
        in_specs=[pl.BlockSpec(memory_space=in_space(n)) for n in in_names]
        + [pl.BlockSpec(memory_space=pl.ANY) for _ in after],
        out_specs=[
            pl.BlockSpec(memory_space=pltpu.VMEM if isinstance(out, Kept) else pl.ANY)
            for out in outs.values()
        ],
        out_shape=[
            pltpu.VMEM(*out.what) if isinstance(out, Kept) else jax.ShapeDtypeStruct(*out)
            for out in outs.values()
        ],
        scratch_shapes=list(scratch.values())
        + [pltpu.VMEM(ins[n].shape, ins[n].dtype) for n in staged]
        + [pltpu.VMEM(*outs[n]) for n in copied]
        + [
            pltpu.SemaphoreType.DMA((max(1, len(staged)),)),
            pltpu.SemaphoreType.DMA((max(1, len(copied)),)),
        ],
        compiler_params=pltpu.CompilerParams(vmem_limit_bytes=vmem * mebibyte),
        cost_estimate=cost(micros),
    )(
        *[
            pltpu.with_memory_space_constraint(value.what, pltpu.VMEM)
            if isinstance(value, Kept)
            else value
            for value in ins.values()
        ],
        *after,
    )
    return types.SimpleNamespace(**dict(zip(outs, results)))


class Kept:
    def __init__(self, *what):
        self.what = what[0] if len(what) == 1 else what


def keep_all(names):
    return {name: Kept(value) for name, value in names.items()}


def chunks(extent, size):
    size = min(size, extent)
    return [slice(start, start + size) for start in range(0, extent, size)]


def lay_out_attention(r, masks, rows):
    for idx, mask in enumerate(masks):
        half, at = divmod(idx, max(1, len(masks) // 2))
        source = r.attn_near if half == 0 else r.attn_far
        place = pl.multiple_of((r.place[0] ^ mask) * rows, rows) if len(masks) > 1 else 0
        r.attn_w[pl.ds(place, rows), :] = source[at * rows : (at + 1) * rows, :]


def lay_out_ff(r, layer_idx):
    width = r.ff_down.shape[-1]
    for k, own in enumerate((r.w_gate, r.w_up)):
        r.ff_gate_up[0, :, k * width : (k + 1) * width] = own[layer_idx]
    r.ff_down[0] = r.w_down[layer_idx]
    part = r.ff_near.shape[1]
    for source, base in ((r.ff_near, 0), (r.ff_far, 1)):
        for m in range(2):
            rows = pl.ds(pl.multiple_of((r.place[1] ^ (2 * m + base)) * part, part), part)
            for k in range(2):
                r.ff_gate_up[1, rows, k * width : (k + 1) * width] = source[3 * m + k]
            r.ff_down[1, rows, :] = source[3 * m + 2]


def start_all(copies):
    for copy in copies:
        copy.start()


def wait_all(sem, *buffers):
    for whole in buffers:
        pltpu.make_async_copy(whole, whole, sem).wait()


def lane_low(rows):
    return lax.broadcasted_iota(jnp.int32, (rows, 128), 1) < 64


def lane_halves():
    low = lane_low(1).astype(f32)
    return low.astype(bf16), (1.0 - low).astype(bf16)


def pair_blocks(rows, low, high):
    return jnp.concatenate([rows * low, rows * high], axis=0)


def own_blocks(both, is_low):
    half = both.shape[0] // 2
    return jnp.where(is_low, both[:half], both[half:]).astype(bf16)


def attention_forward(r, x_ref, a_ref, sizes, layer_idx):
    series, slots, inner = sizes
    rows = series * slots
    for part in chunks(rows, 256):
        r.qkv[part, :] = dot_nn(a_ref[part, :], r.attn_w[:, : 3 * inner]).astype(bf16)
    is_low = lane_low(slots)
    low, high = lane_halves()
    for s in range(series):
        here = slice(s * slots, (s + 1) * slots)
        keep = r.mask[here, :] == 1
        for start in range(0, inner, 128):
            at = slice(start, start + 128)
            query = r.qkv[here, at]
            keys = r.qkv[here, inner + start : inner + start + 128]
            scores = dot_nt(keys, pair_blocks(query, low, high)) + r.bias[:, at]
            scores = jnp.where(keep, scores, masked_score)
            exps = jnp.exp(scores - jnp.max(scores, axis=0, keepdims=True))
            r.probs[here, at] = exps / jnp.sum(exps, axis=0, keepdims=True)
    for s in range(series):
        here = slice(s * slots, (s + 1) * slots)
        for start in range(0, inner, 128):
            at = slice(start, start + 128)
            values = r.qkv[here, 2 * inner + start : 2 * inner + start + 128]
            both = dot_tn(r.probs[here, at].astype(bf16), values)
            r.heads[here, at] = own_blocks(both, is_low)
    gain = r.gain_ff[layer_idx : layer_idx + 1, :]
    for part in chunks(rows, 256):
        middle = x_ref[part, :] + dot_nt(r.heads[part, :], r.attn_w[:, 3 * inner :])
        r.middle[part, :] = middle
        r.ff_in[part, :] = (middle * inverse_rms(middle) * gain).astype(bf16)


def prepare_body(r):
    names = ("inputs", "valid", "keep", "embed", "gain_attn", "buckets")
    r.fetch(*names)
    r.need(*names)
    series, slots = r.valid.shape
    gain = r.gain_attn[0:1, :]
    valid = jnp.transpose(r.valid[...].astype(f32))
    keep = jnp.transpose(r.keep[...].astype(f32))
    for s in range(series):
        here = slice(s * slots, (s + 1) * slots)
        seen = valid[:, s : s + 1]
        x = jnp.where(seen == 1.0, r.inputs[here, :].astype(f32), r.embed[...])
        r.x[here, :] = x
        r.a[here, :] = (x * inverse_rms(x) * gain).astype(bf16)
        r.seen[here, :] = jnp.broadcast_to(seen, (slots, 128)).astype(jnp.int32)
        r.mask[here, :] = jnp.broadcast_to(keep[:, s : s + 1], (slots, 128)).astype(jnp.int32)
    turned = jnp.transpose(r.buckets[...].astype(f32)).astype(jnp.int32)
    wide = jnp.concatenate([turned, turned], axis=1)
    r.wide[...] = wide
    is_low = lane_low(slots)
    bucket_count, heads = r.table.shape
    for pair in range(heads // 2):
        bias = jnp.zeros((slots, 128), f32)
        for idx in range(bucket_count):
            entry = jnp.where(is_low, r.table[idx, 2 * pair], r.table[idx, 2 * pair + 1])
            bias = jnp.where(wide == idx, entry, bias)
        r.bias[:, pair * 128 : (pair + 1) * 128] = bias


def attention_body(r, sizes, masks, grain, layer_idx):
    r.fetch("gain_ff")
    lay_out_attention(r, masks, grain)
    r.need("gain_ff")
    attention_forward(r, r.x, r.a, sizes, layer_idx)


def ff_body(r):
    r.fetch("gain_attn")
    lay_out_ff(r, 0)
    r.need("gain_attn")
    width = r.middle.shape[1]
    for part in chunks(r.middle.shape[0], 256):
        x_next = r.middle[part, :]
        for half in range(2):
            both = dot_nn(r.ff_in[part, :], r.ff_gate_up[half])
            hidden = (gelu_terms(both[:, :width])[0] * both[:, width:]).astype(bf16)
            x_next = x_next + dot_nn(hidden, r.ff_down[half])
        r.x_next[part, :] = x_next
        r.a_next[part, :] = (x_next * inverse_rms(x_next) * r.gain_attn[1:2, :]).astype(bf16)


def ff_backward(r, layer_idx, last, masks):
    rows, width = r.middle.shape
    r.fetch("grad", "gain_ff")
    if last:
        lay_out_ff(r, layer_idx)
    r.need("grad", "gain_ff")
    gain_ff = r.gain_ff[layer_idx : layer_idx + 1, :]
    gain_total = jnp.zeros((1, width), f32)
    for part in chunks(rows, 256):
        grad = r.grad[part, :].astype(f32)
        rounded = grad.astype(bf16)
        ff_rows = r.ff_in[part, :]
        back = None
        middle = r.middle[part, :]
        total = middle
        for half in range(2):
            both = dot_nn(ff_rows, r.ff_gate_up[half])
            grad_hidden = dot_nt(rounded, r.ff_down[half])
            gate_act, up_act = both[:, :width], both[:, width:]
            mixed, slope = gelu_terms(gate_act)
            hidden = (mixed * up_act).astype(bf16)
            r.hidden[half, part, :] = hidden
            r.grad_gate_up[half, part, :width] = (grad_hidden * up_act * slope).astype(bf16)
            r.grad_gate_up[half, part, width:] = (grad_hidden * mixed).astype(bf16)
            pulled = r.grad_gate_up[half, part, :]
            if last:
                total = total + dot_nn(hidden, r.ff_down[half])
            term = dot_nt(pulled, r.ff_gate_up[half])
            back = term if back is None else back + term
        if last:
            r.outputs[part, :] = total.astype(bf16)
        grad_mid, gain_part = norm_back(middle, gain_ff, back)
        gain_total += gain_part
        grad_mid = grad + grad_mid
        r.grad_mid[part, :] = grad_mid
        r.branch[part, :] = grad_mid.astype(bf16)
        r.grad_low[part, :] = rounded
    if last:
        r.write("outputs")
    for half in range(2):
        r.ff_grad[half, :, : 2 * width] = dot_tn(r.ff_in[...], r.grad_gate_up[half])
        r.ff_grad[half, :, 2 * width :] = dot_tn(r.hidden[half], r.grad_low[...])
    half_count = len(masks[0]) // 2
    grain, columns = r.ff_keep.shape[1:]
    for side, side_masks in enumerate(masks):
        lanes = slice(side * columns, (side + 1) * columns)
        for idx, mask in enumerate(side_masks):
            target = r.ff_keep if idx < half_count else r.ff_send
            piece = pl.ds(pl.multiple_of((r.place[3] ^ (mask // 2)) * grain, grain), grain)
            target[side * half_count + idx % half_count] = r.ff_grad[mask % 2, piece, lanes].astype(
                bf16
            )
    if last:
        r.drain("outputs")
    return gain_total


def attention_backward(r, sizes, layer_idx, last, piece_masks, heads):
    series, slots, inner = sizes
    rows = series * slots
    width = r.x.shape[1]
    r.fetch("gain_attn")
    for part in chunks(rows, 256):
        r.grad_heads[part, :] = dot_nn(r.branch[part, :], r.attn_w[:, 3 * inner :]).astype(bf16)
    is_low = lane_low(slots)
    low, high = lane_halves()
    for start in range(0, inner, 128):
        at = slice(start, start + 128)
        bias_total = jnp.zeros((slots, 128), f32) if last else r.bias_before[:, at]
        for s in range(series):
            here = slice(s * slots, (s + 1) * slots)
            probs = r.probs[here, at]
            values = r.qkv[here, 2 * inner + start : 2 * inner + start + 128]
            grad_probs = dot_nt(values, pair_blocks(r.grad_heads[here, at], low, high))
            inner_sum = jnp.sum(probs * grad_probs, axis=0, keepdims=True)
            grad_scores = (probs * (grad_probs - inner_sum)).astype(bf16)
            r.grad_scores[here, at] = grad_scores
            bias_total = bias_total + grad_scores.astype(f32)
        r.bias_acc[:, at] = bias_total
    for s in range(series):
        here = slice(s * slots, (s + 1) * slots)
        for start in range(0, inner, 128):
            at = slice(start, start + 128)
            key_at = slice(inner + start, inner + start + 128)
            value_at = slice(2 * inner + start, 2 * inner + start + 128)
            grad_scores = r.grad_scores[here, at]
            r.grad_qkv[here, key_at] = dot_nn(
                grad_scores, pair_blocks(r.qkv[here, at], low, high)
            ).astype(bf16)
            r.grad_qkv[here, value_at] = dot_nn(
                r.probs[here, at].astype(bf16), pair_blocks(r.grad_heads[here, at], low, high)
            ).astype(bf16)
            r.grad_qkv[here, at] = own_blocks(dot_tn(grad_scores, r.qkv[here, key_at]), is_low)
    r.attn_grad[:, : 3 * inner] = dot_tn(r.a[...], r.grad_qkv[...])
    r.attn_grad[:, 3 * inner :] = dot_tn(r.branch[...], r.heads[...])
    scatter_pieces(r.attn_grad, r.attn_keep, r.attn_send, piece_masks, r.place[2])
    r.need("gain_attn")
    gain_attn = r.gain_attn[layer_idx : layer_idx + 1, :]
    gain_total = jnp.zeros((1, width), f32)
    embed_total = jnp.zeros((1, width), f32)
    for part in chunks(rows, 256):
        grad_normed = dot_nt(r.grad_qkv[part, :], r.attn_w[:, : 3 * inner])
        grad_in, gain_part = norm_back(r.x[part, :], gain_attn, grad_normed)
        gain_total += gain_part
        grad_in = r.grad_mid[part, :] + grad_in
        if last:
            r.grad_next[part, :] = grad_in
        else:
            seen = r.seen[part, 0:1] == 1
            r.grad_next[part, :] = jnp.where(seen, grad_in, 0.0)
            embed_total += jnp.sum(jnp.where(seen, 0.0, grad_in), axis=0, keepdims=True)
    r.write("grad_next")
    if not last:
        put_row(r.small, 4, embed_total)
        head_size = inner // heads
        for idx in range(r.table_rows.shape[0]):
            for start in range(0, inner, 128):
                at = slice(start, start + 128)
                chosen = jnp.where(r.wide[...] == idx, r.bias_acc[:, at], 0.0)
                r.table_rows[idx : idx + 1, at] = jnp.sum(chosen, axis=0, keepdims=True)
        lane = lax.broadcasted_iota(jnp.int32, (r.table_rows.shape[0], 128), 1)
        table = jnp.zeros(lane.shape, f32)
        for head in range(heads):
            cut = r.table_rows[:, head * head_size : (head + 1) * head_size]
            table = jnp.where(lane == head, jnp.sum(cut, axis=1, keepdims=True), table)
        r.small[:heads, : table.shape[0]] = jnp.transpose(table)[:heads, :]
    r.drain("grad_next")
    return gain_total


def two_parts(values):
    high = values.astype(bf16).astype(f32)
    return high, (values - high).astype(bf16).astype(f32)


def last_ff_body(r, masks):
    r.small[...] = jnp.zeros(r.small.shape, f32)
    put_row(r.small, 3, ff_backward(r, 1, True, masks))


def last_attention_body(r, sizes, piece_masks, heads):
    r.small[...] = r.small_before[...]
    put_row(r.small, 1, attention_backward(r, sizes, 1, True, piece_masks, heads))


def ff_backward_body(r, masks):
    r.small[...] = r.small_before[...]
    put_row(r.small, 2, ff_backward(r, 0, False, masks))


def attention_backward_body(r, sizes, piece_masks, heads):
    r.small[...] = r.small_before[...]
    put_row(r.small, 0, attention_backward(r, sizes, 0, False, piece_masks, heads))
    high, low = two_parts(r.small[...])
    last = r.attn_send.shape[0] - 1
    r.attn_send[last] = jnp.concatenate([high, low], axis=0).astype(bf16)
    r.small[...] = high + low


def put_row(packed, which, row):
    first, width = packed.shape[0] - 2, row.shape[1]
    at = which % 3 * width
    packed[first + which // 3 : first + which // 3 + 1, at : at + width] = row


def scatter_pieces(whole, keep, send, masks, place):
    count = len(masks)
    grain = whole.shape[0] // count
    for idx, mask in enumerate(masks):
        target = keep if idx < count // 2 else send
        source = pl.ds(pl.multiple_of((place ^ mask) * grain, grain), grain)
        target[idx % (count // 2)] = whole[source, :].astype(bf16)


def finish(pieces, masks, layer_idx, place, shape, before=()):
    grain, width = pieces.shape[1], shape[-1]
    count = len(before)

    def kernel(place_ref, source, *refs):
        outs = refs[count : count + 3]
        stage, out_sem = refs[count + 3 :]
        for idx, mask in enumerate(masks):
            rows = pl.ds(pl.multiple_of((place_ref[3] ^ mask) * grain, grain), grain)
            for k, out in enumerate(outs):
                stage[k, idx] = source[idx, :, k * width : (k + 1) * width].astype(f32)
                pltpu.make_async_copy(stage.at[k, idx], out.at[layer_idx, rows], out_sem).start()
        pltpu.make_async_copy(stage, stage, out_sem).wait()

    return pl.pallas_call(
        kernel,
        name="layer_%d_ff_grads" % layer_idx,
        in_specs=[
            pl.BlockSpec(memory_space=pltpu.SMEM),
            pl.BlockSpec(memory_space=pltpu.VMEM),
        ]
        + [pl.BlockSpec(memory_space=pl.ANY)] * count,
        out_specs=[pl.BlockSpec(memory_space=pl.ANY)] * 3,
        out_shape=[jax.ShapeDtypeStruct(shape, f32)] * 3,
        input_output_aliases={2 + k: k for k in range(count)},
        scratch_shapes=[
            pltpu.VMEM((3, len(masks), grain, width), f32),
            pltpu.SemaphoreType.DMA,
        ],
        compiler_params=pltpu.CompilerParams(vmem_limit_bytes=6 * mebibyte),
        cost_estimate=cost(3),
    )(place, pltpu.with_memory_space_constraint(pieces, pltpu.VMEM), *before)


def small_body(r):
    width = r.embed.shape[1]
    heads = r.table.shape[0]
    outs = ((r.gain_attn, 0), (r.gain_attn, 1), (r.gain_ff, 0), (r.gain_ff, 1), (r.embed, 0))
    for which, (out, row) in enumerate(outs):
        first = r.packed.shape[0] - 2 + which // 3
        at = which % 3 * width
        out[row : row + 1, :] = r.packed[first : first + 1, at : at + width]
    r.table[...] = r.packed[:heads, : r.table.shape[1]]
    r.write("gain_attn", "gain_ff", "embed", "table")
    r.drain("gain_attn", "gain_ff", "embed", "table")


def pack_body(r, packs):
    rows = r.quarter_0.shape[1]
    at = pl.ds(pl.multiple_of(r.place[1] * rows, rows), rows)
    copies = []
    outs = [r.quarter_0, r.quarter_1]
    for layer_idx in range(2):
        for k, w in enumerate((r.w_gate, r.w_up, r.w_down)):
            copies.append((w.at[layer_idx, at], outs[layer_idx].at[k]))
    if packs:
        outs += [r.block_0, r.block_1]
        inner = r.w_query.shape[2]
        for layer_idx in range(2):
            for k, w in enumerate((r.w_query, r.w_key, r.w_value, r.w_out)):
                lanes = pl.ds(k * inner, inner)
                copies.append((w.at[layer_idx], outs[2 + layer_idx].at[:, lanes]))
    start_all([pltpu.make_async_copy(*ends, r.pack_sem) for ends in copies])
    wait_all(r.pack_sem, *outs)


def order_masks(hops):
    masks = [0]
    for hop in reversed(hops):
        masks = masks + [mask ^ hop for mask in masks]
    return masks


def tie(value, *others):
    return lax.optimization_barrier((value, *others))[0]


def on_device(
    inputs,
    cotangent,
    attention_mask,
    patch_valid,
    buckets,
    mask_embed,
    w_query,
    w_key,
    w_value,
    w_output,
    w_gate,
    w_up,
    w_down,
    gain_attn,
    gain_ff,
    bias_table,
    dp_size,
):
    series, slots, width = inputs.shape
    heads = bias_table.shape[1]
    inner = w_query.shape[2]
    rows = series * slots
    sizes = (series, slots, inner)
    matrix = (rows, width)
    devices = 2 * dp_size
    dp_at = lax.axis_index("dp")
    device_at = 2 * dp_at + lax.axis_index("tensor")
    cotangent = cotangent.reshape(matrix)

    def swap(array, mask):
        return lax.ppermute(array, axes, [(n, n ^ mask) for n in range(devices)])

    def join(left, right):
        return jnp.concatenate([left, right], axis=0)

    bits = [1 << k for k in range(devices.bit_length() - 1)]

    attn_grain = max(16, width // devices)
    attn_count = width // attn_grain
    ff_grain = max(16, width // dp_size)
    ff_count = width // ff_grain
    quarter_at = lax.rem(dp_at, 4)
    place = jnp.stack(
        [
            device_at,
            quarter_at,
            device_at // (devices // attn_count),
            lax.rem(dp_at, ff_count),
        ]
    ).astype(jnp.int32)

    quarter = width // 4
    own_rows = w_query.shape[1]
    direct = own_rows % 16 == 0
    w_out = jnp.swapaxes(w_output, 1, 2)
    sources = dict(w_gate=w_gate, w_up=w_up, w_down=w_down)
    block_outs = {}
    if direct:
        sources |= dict(w_query=w_query, w_key=w_key, w_value=w_value, w_out=w_out)
        block_outs = {"block_%d" % k: Kept((own_rows, 4 * inner), bf16) for k in range(2)}
    packed = run(
        functools.partial(pack_body, packs=direct),
        "pack",
        dict(
            place=place,
            **{n: pltpu.with_memory_space_constraint(w, pltpu.HBM) for n, w in sources.items()},
        ),
        dict(
            quarter_0=Kept((3, quarter, width), bf16),
            quarter_1=Kept((3, quarter, width), bf16),
            **block_outs,
        ),
        dict(pack_sem=pltpu.SemaphoreType.DMA),
        vmem=4,
    )
    far = bits[2:]

    def prepare(token):
        return run(
            prepare_body,
            "prepare",
            dict(
                inputs=tie(inputs, token).reshape(matrix),
                valid=patch_valid,
                keep=attention_mask,
                embed=mask_embed[None, :],
                gain_attn=gain_attn,
                buckets=buckets,
                table=bias_table,
            ),
            dict(
                x=Kept(matrix, f32),
                a=Kept(matrix, bf16),
                bias=Kept((slots, heads * slots), f32),
                mask=Kept((rows, 128), jnp.int32),
                seen=Kept((rows, 128), jnp.int32),
                wide=Kept((slots, 128), jnp.int32),
            ),
            {},
            micros=3,
        )

    if direct:
        hops_0 = [1] + far[2:] + far[:2] + [2]
        hops_1 = far[2:] + far[:2] + [1, 2]
        block_0, block_1 = packed.block_0, packed.block_1
        got_1 = swap(block_1, hops_1[0])
        got_0 = swap(block_0, hops_0[0])
        ff_0 = swap(tie(packed.quarter_0, got_0), 1)
        ff_1 = swap(tie(packed.quarter_1, ff_0), 1)
        got_ff_0 = swap(ff_0, 4)
        block_0 = join(block_0, got_0)
        block_1 = join(block_1, tie(got_1, block_0))
        for hop_0, hop_1 in zip(hops_0[1:-2], hops_1[1:-2]):
            got_1, got_0 = swap(block_1, hop_1), swap(block_0, hop_0)
            if hop_0 == hops_0[1]:
                start = prepare(block_1)
                got_0 = tie(got_0, ff_0)
            block_0 = join(block_0, got_0)
            block_1 = join(block_1, tie(got_1, block_0))
        block_0 = tie(block_0, block_1)
        got_0 = swap(block_0, hops_0[-2])
        got_1 = swap(block_1, hops_1[-2])
        block_0 = join(block_0, tie(got_0, start.a, got_ff_0, ff_1))
        ff_0 = join(ff_0, tie(got_ff_0, block_0))
        got_ff_1 = swap(tie(ff_1, ff_0), 4)
        attn_pieces = [(block_0, swap(block_0, 2), order_masks(hops_0[::-1]))]
    else:
        ff_0, ff_1 = swap(packed.quarter_0, 1), swap(packed.quarter_1, 1)
        ff_0 = join(ff_0, swap(ff_0, 4))
        start = prepare(ff_0)
        attn_pieces = []
        rows_of = jnp.concatenate([w_query, w_key, w_value, w_out], axis=2)
        for layer_idx in range(2):
            whole = lax.all_gather(rows_of[layer_idx], axes, axis=0, tiled=True)
            attn_pieces.append((whole, whole, [0]))
    ff_pieces = [(ff_0, swap(ff_0, 2))]

    def attn_ins(layer_idx):
        near, far, masks = attn_pieces[layer_idx]
        return dict(attn_near=Kept(near), attn_far=Kept(far)), masks

    def ff_ins(layer_idx):
        near, far = ff_pieces[layer_idx]
        own = keep_all(dict(w_gate=w_gate, w_up=w_up, w_down=w_down))
        return dict(**own, ff_near=Kept(near), ff_far=Kept(far))

    ff_outs = dict(
        ff_gate_up=Kept((2, width, 2 * width), bf16), ff_down=Kept((2, width, width), bf16)
    )
    grain = own_rows if direct else width
    attn_outs = dict(
        attn_w=Kept((width, 4 * inner), bf16),
        qkv=Kept((rows, 3 * inner), bf16),
        probs=Kept((rows, heads * slots), f32),
        heads=Kept((rows, inner), bf16),
        middle=Kept(matrix, f32),
        ff_in=Kept(matrix, bf16),
    )

    def attention(layer_idx, x, a, after=(), micros=5):
        pieces, masks = attn_ins(layer_idx)
        return run(
            functools.partial(
                attention_body, sizes=sizes, masks=masks, grain=grain, layer_idx=layer_idx
            ),
            "layer_%d_attention" % layer_idx,
            dict(
                place=place,
                x=Kept(x),
                a=Kept(a),
                bias=Kept(start.bias),
                mask=Kept(start.mask),
                gain_ff=gain_ff,
                **pieces,
            ),
            attn_outs,
            {},
            after=after,
            micros=micros,
        )

    first = attention(0, start.x, start.a, micros=10)
    if direct:
        block_1 = join(block_1, tie(got_1, first.ff_in))
        attn_pieces.append((block_1, swap(block_1, 2), order_masks(hops_1[::-1])))
    first_ff = run(
        ff_body,
        "layer_0_ff",
        dict(
            place=place,
            middle=Kept(first.middle),
            ff_in=Kept(first.ff_in),
            gain_attn=gain_attn,
            **ff_ins(0),
        ),
        dict(**ff_outs, x_next=Kept(matrix, f32), a_next=Kept(matrix, bf16)),
        {},
        after=(block_1,) if direct else (),
        micros=3,
    )
    if direct:
        ff_1 = join(ff_1, tie(got_ff_1, first_ff.x_next))
    else:
        ff_1 = join(ff_1, swap(ff_1, 4))
    ff_pieces.append((ff_1, swap(ff_1, 2)))
    second = attention(1, first_ff.x_next, first_ff.a_next, micros=0.1)

    attn_low = devices // attn_count
    attn_hops = ([2, 1] + bits[2:], [2] + bits[3:4] + bits[2:3] + bits[4:] + [1])
    attn_split = [[hop for hop in hops if hop >= attn_low] for hops in attn_hops]
    attn_whole = [hop for hop in bits if hop < attn_low]
    attn_masks = [[mask // attn_low for mask in order_masks(hops)] for hops in attn_split]
    ff_hops = ([2, 4, 1] + bits[3:], [2, 1, 4] + bits[3:])
    ff_split = [[hop for hop in hops if hop // 2 < ff_count] for hops in ff_hops]
    ff_whole = [hop for hop in bits[1:] if hop // 2 >= ff_count]
    ff_share = [hop for hop in bits[:0:-1] if hop // 2 < ff_count]
    ff_masks = [order_masks(hops) for hops in ff_split]
    place_masks = [mask // 2 for mask in order_masks(ff_share[::-1])]
    attn_half = (attn_count // 2, attn_grain, 4 * inner)
    small_shape = (heads + 2, 3 * width)

    attn_back_outs = dict(attn_keep=Kept(attn_half, bf16), attn_send=Kept(attn_half, bf16))
    attn_back_scratch = dict(
        grad_heads=pltpu.VMEM((rows, inner), bf16),
        grad_qkv=pltpu.VMEM((rows, 3 * inner), bf16),
        grad_scores=pltpu.VMEM((rows, heads * slots), bf16),
        attn_grad=pltpu.VMEM((width, 4 * inner), f32),
    )
    ff_back_outs = dict(
        ff_keep=Kept((2 * ff_count, ff_grain, 3 * width // 2), bf16),
        ff_send=Kept((2 * ff_count, ff_grain, 3 * width // 2), bf16),
        small=Kept(small_shape, f32),
        grad_mid=Kept(matrix, f32),
        branch=Kept(matrix, bf16),
    )
    ff_back_scratch = dict(
        hidden=pltpu.VMEM((2, rows, width), bf16),
        grad_gate_up=pltpu.VMEM((2, rows, 2 * width), bf16),
        ff_grad=pltpu.VMEM((2, width, 3 * width), f32),
        grad_low=pltpu.VMEM(matrix, bf16),
    )
    bias_shape = (slots, heads * slots)

    def attn_back_ins(kept, x, a):
        return dict(
            x=Kept(x),
            a=Kept(a),
            gain_attn=gain_attn,
            attn_w=Kept(kept.attn_w),
            qkv=Kept(kept.qkv),
            probs=Kept(kept.probs),
            heads=Kept(kept.heads),
        )

    def add(left, right):
        return (left.astype(f32) + right.astype(f32)).astype(bf16)

    def halving(keep, send, hops, out):
        for step, hop in enumerate(hops):
            got = yield swap(send, hop)
            if step + 1 < len(hops):
                cut = keep.shape[0] // 2
                send = add(keep[cut:], got[cut:])
                keep = add(keep[:cut], got[:cut])
                out["token"] = send
            else:
                out["token"] = keep = add(keep, got)
        out["piece"] = keep

    def summing(piece, hops, out):
        for hop in hops:
            got = yield swap(piece, hop)
            out["token"] = piece = add(piece, got)
        out["piece"] = piece

    def sharing(piece, hops, out):
        for step, hop in enumerate(hops):
            if step + 1 == len(hops):
                out["near"] = piece
            got = yield swap(piece, hop)
            if step + 1 < len(hops):
                out["token"] = piece = join(piece, got)
            else:
                out["token"] = out["far"] = got

    def rounded(values):
        return lax.reduce_precision(values, exponent_bits=8, mantissa_bits=7)

    def with_small(pieces, small):
        high = rounded(small)
        low = rounded(small - high)
        parts = join(high, low).astype(bf16)[None]
        return join(pieces, parts), high + low

    def add_small(small, got):
        parts = got[-1].astype(f32)
        return small + (parts[: small.shape[0]] + parts[small.shape[0] :])

    def attn_chain(part, layer_idx, out):
        small = part.small if layer_idx == 0 else None
        keep, send = part.attn_keep, part.attn_send
        hops = attn_split[layer_idx] + attn_whole
        for step, hop in enumerate(hops):
            got = yield swap(send, hop)
            if small is not None:
                small = add_small(small, got)
                got = got[:-1]
            if step + 1 < len(attn_split[layer_idx]):
                half = keep.shape[0] // 2
                send = add(keep[half:], got[half:])
                keep = add(keep[:half], got[:half])
            else:
                send = keep = add(keep, got)
            if small is not None and step + 1 < len(hops):
                send, small = with_small(send, small)
            out["token"] = send
            if layer_idx == 1 and step == 0:
                send = tie(send, *(yield None))
        piece = keep[0]
        if own_rows < attn_grain:
            first_row = lax.rem(device_at, attn_low) * own_rows
            piece = lax.dynamic_slice_in_dim(piece, first_row, own_rows, axis=0)
        out["done"] = piece.astype(f32)
        out["small"] = small

    def ff_chain(part, out):
        got = yield swap(part.ff_send, 2)
        count = ff_count
        keeps, sends = [], []
        for side in range(2):
            at, half = side * count, count // 2
            sends.append(add(part.ff_keep[at + half : at + count], got[at + half : at + count]))
            keeps.append(add(part.ff_keep[at : at + half], got[at : at + half]))
        out["token"] = tuple(sends)
        for hops in zip(ff_split[0][1:3], ff_split[1][1:3]):
            got = yield tuple(swap(send, hop) for send, hop in zip(sends, hops))
            half = keeps[0].shape[0] // 2
            sends = [add(keep[half:], one[half:]) for keep, one in zip(keeps, got)]
            keeps = [add(keep[:half], one[:half]) for keep, one in zip(keeps, got)]
            out["token"] = tuple(sends)
        keep, send = (jnp.concatenate(sides, axis=2) for sides in (keeps, sends))
        yield from halving(keep, send, ff_split[0][3:], out)
        yield from summing(out["piece"], ff_whole, out)
        yield from sharing(out["piece"], ff_share, out)

    class Chain:
        def __init__(self, steps, *args):
            self.out = {}
            self.steps = steps(*args, self.out)
            self.arriving = next(self.steps)

        def resume(self, *tokens):
            self.arriving = self.steps.send(tokens)

        def step(self, token, *others):
            if self.arriving is not None:
                tokens = (*(token if isinstance(token, tuple) else (token,)), *others)
                many = isinstance(self.arriving, tuple)
                arrived = self.arriving if many else (self.arriving,)
                arrived = lax.optimization_barrier((*arrived, *tokens))[: len(arrived)]
                arrived = arrived if many else arrived[0]
                self.arriving = None
                try:
                    self.arriving = self.steps.send(arrived)
                except StopIteration:
                    pass
                return self.out["token"]
            return token

    back_ff_1 = run(
        functools.partial(last_ff_body, masks=ff_masks),
        "layer_1_ff",
        dict(
            place=place,
            grad=cotangent,
            gain_ff=gain_ff,
            middle=Kept(second.middle),
            ff_in=Kept(second.ff_in),
            **ff_ins(1),
        ),
        dict(**ff_back_outs, outputs=(matrix, bf16)),
        dict(
            ff_gate_up=pltpu.VMEM((2, width, 2 * width), bf16),
            ff_down=pltpu.VMEM((2, width, width), bf16),
            **ff_back_scratch,
        ),
        micros=8,
        vmem=24,
    )
    ff_1 = Chain(ff_chain, back_ff_1)
    back_1 = run(
        functools.partial(
            last_attention_body, sizes=sizes, piece_masks=attn_masks[1], heads=heads
        ),
        "layer_1_attention_backward",
        dict(
            place=place,
            small_before=Kept(back_ff_1.small),
            grad_mid=Kept(back_ff_1.grad_mid),
            branch=Kept(back_ff_1.branch),
            **attn_back_ins(second, first_ff.x_next, first_ff.a_next),
        ),
        dict(
            **attn_back_outs,
            small=Kept(small_shape, f32),
            grad_next=Kept(matrix, f32),
            bias_acc=Kept(bias_shape, f32),
        ),
        attn_back_scratch,
        micros=6,
        vmem=14,
    )
    attn_1 = Chain(attn_chain, back_1, 1)
    token = ff_1.step(back_1.attn_send)
    token = (attn_1.step(token),)
    back_0 = run(
        functools.partial(ff_backward_body, masks=ff_masks),
        "layer_0_ff_backward",
        dict(
            place=place,
            grad=Kept(back_1.grad_next),
            gain_ff=gain_ff,
            small_before=Kept(back_1.small),
            middle=Kept(first.middle),
            ff_in=Kept(first.ff_in),
            ff_gate_up=Kept(first_ff.ff_gate_up),
            ff_down=Kept(first_ff.ff_down),
        ),
        ff_back_outs,
        ff_back_scratch,
        after=token,
        micros=8,
        vmem=20,
    )
    token = ff_1.step(back_0.branch)
    back_0.ff_send = tie(back_0.ff_send, *token)
    ff_0 = Chain(ff_chain, back_0)
    token = ff_0.step(token)
    back_attn_0 = run(
        functools.partial(
            attention_backward_body, sizes=sizes, piece_masks=attn_masks[0], heads=heads
        ),
        "layer_0_attention_backward",
        dict(
            place=place,
            bias_before=Kept(back_1.bias_acc),
            seen=Kept(start.seen),
            wide=Kept(start.wide),
            small_before=Kept(back_0.small),
            grad_mid=Kept(back_0.grad_mid),
            branch=Kept(back_0.branch),
            **attn_back_ins(first, start.x, start.a),
        ),
        dict(
            attn_keep=Kept(attn_half, bf16),
            attn_send=Kept((attn_count // 2 + 1, *attn_half[1:]), bf16),
            small=Kept(small_shape, f32),
            grad_next=(matrix, f32),
        ),
        dict(
            bias_acc=pltpu.VMEM(bias_shape, f32),
            table_rows=pltpu.VMEM((bias_table.shape[0], heads * slots), f32),
            **attn_back_scratch,
        ),
        after=token,
        micros=7,
        vmem=14,
    )
    attn_0 = Chain(attn_chain, back_attn_0, 0)
    attn_1.resume(back_attn_0.attn_send)
    token = back_attn_0.attn_send
    shape = (2, width, width)
    near_masks = place_masks[: ff_count // 2]
    far_masks = place_masks[ff_count // 2 :]
    done = ()
    ended = False
    turn = 0
    sums = attn_grads = None
    while ff_0.arriving is not None:
        turn += 1
        token = ff_1.step(token)
        if done and not ended:
            done = finish(tie(ff_1.out["far"], token), far_masks, 1, place, shape, done)
            token = done[0]
            ended = True
        token = ff_0.step(token)
        if not done and "near" in ff_1.out:
            done = finish(tie(ff_1.out["near"], token), near_masks, 1, place, shape)
            token = done[0]
        if turn != 2:
            token = attn_0.step(token)
            token = attn_1.step(token)
        if sums is None and attn_0.arriving is None:
            sums = run(
                small_body,
                "small_sums",
                dict(packed=Kept(tie(attn_0.out["small"], token))),
                dict(
                    gain_attn=((2, width), f32),
                    gain_ff=((2, width), f32),
                    embed=((1, width), f32),
                    table=(bias_table.shape[::-1], f32),
                ),
                {},
            )
            token = sums.embed
        if attn_grads is None and attn_0.arriving is None and attn_1.arriving is None:
            both = jnp.stack([attn_0.out["done"], tie(attn_1.out["done"], token)])
            attn_grads = [both[:, :, k * inner : (k + 1) * inner] for k in range(4)]
            attn_grads[3] = jnp.swapaxes(attn_grads[3], 1, 2)
            token = tuple(attn_grads)
    if not ended:
        done = finish(ff_1.out["far"], far_masks, 1, place, shape, done)
    for pieces, masks in ((ff_0.out["near"], near_masks), (ff_0.out["far"], far_masks)):
        done = finish(pieces, masks, 0, place, shape, done)
    return (
        back_ff_1.outputs.reshape(inputs.shape),
        back_attn_0.grad_next.reshape(inputs.shape),
        *attn_grads,
        *done,
        sums.gain_attn,
        sums.gain_ff,
        sums.table.T,
        sums.embed[0],
    )


def solution(mesh):
    placed = (
        P(("dp", "tensor"), None, None),
        P(("dp", "tensor"), None, None),
        P(("dp", "tensor"), None),
        P(("dp", "tensor"), None),
        P(),
        P(),
        P(None, ("dp", "tensor"), None),
        P(None, ("dp", "tensor"), None),
        P(None, ("dp", "tensor"), None),
        P(None, None, ("dp", "tensor")),
        P(None, None, "tensor"),
        P(None, None, "tensor"),
        P(None, "tensor", None),
        P(),
        P(),
        P(),
    )
    return jax.shard_map(
        functools.partial(on_device, dp_size=mesh.shape["dp"]),
        mesh=mesh,
        in_specs=placed,
        out_specs=(
            P(("dp", "tensor"), None, None),
            P(("dp", "tensor"), None, None),
            P(None, ("dp", "tensor"), None),
            P(None, ("dp", "tensor"), None),
            P(None, ("dp", "tensor"), None),
            P(None, None, ("dp", "tensor")),
            P(None, None, "tensor"),
            P(None, None, "tensor"),
            P(None, "tensor", None),
            P(),
            P(),
            P(),
            P(),
        ),
        check_vma=False,
    )
```

```python
import functools
import types

import jax
import jax.numpy as jnp
from jax import lax
from jax.experimental import pallas as pl
from jax.experimental.pallas import tpu as pltpu
from jax.sharding import PartitionSpec as P

norm_eps = 1e-06
masked_score = -1e30
bf16 = jnp.bfloat16
f32 = jnp.float32
axes = ("dp", "tensor")
mebibyte = 1024 * 1024
raw_names = ("w_query", "w_key", "w_value", "w_out", "w_gate", "w_up", "w_down")
scalar_names = ("place", "table")


def dot_nn(left, right):
    return lax.dot_general(left, right, (((1,), (0,)), ((), ())), preferred_element_type=f32)


def dot_nt(left, right):
    return lax.dot_general(left, right, (((1,), (1,)), ((), ())), preferred_element_type=f32)


def dot_tn(left, right):
    return lax.dot_general(left, right, (((0,), (0,)), ((), ())), preferred_element_type=f32)


def inverse_rms(values):
    return lax.rsqrt(jnp.mean(values * values, axis=-1, keepdims=True) + norm_eps)


def norm_back(values, gain, grad_out):
    scale = inverse_rms(values)
    pulled = grad_out * gain
    mean_part = jnp.mean(pulled * values, axis=-1, keepdims=True)
    grad_in = scale * pulled - values * (scale * scale * scale) * mean_part
    return grad_in, jnp.sum(grad_out * values * scale, axis=0, keepdims=True)


def gelu_terms(gate_act):
    square = gate_act * gate_act
    bent = jnp.tanh(0.7978845608028654 * gate_act * (1.0 + 0.044715 * square))
    half = 0.5 * (1.0 + bent)
    slope = half + 0.5 * gate_act * (1.0 - bent * bent) * (
        0.7978845608028654 * (1.0 + 3.0 * 0.044715 * square)
    )
    return gate_act * half, slope


def cost(micros):
    return pl.CostEstimate(flops=int(micros * 1.15e9), bytes_accessed=0, transcendentals=0)


def run(body, name, ins, outs, scratch, after=(), micros=1, vmem=8):
    in_names, out_names, scratch_names = list(ins), list(outs), list(scratch)
    direct = {n for n in in_names if n in scalar_names + raw_names or isinstance(ins[n], Kept)}
    staged = [n for n in in_names if n not in direct]
    copied = [n for n in out_names if not isinstance(outs[n], Kept)]
    in_sems = {n: i for i, n in enumerate(staged)}
    out_sems = {n: i for i, n in enumerate(copied)}

    def kernel(*refs):
        refs = list(refs)
        sources = dict(zip(in_names, refs))
        refs = refs[len(in_names) + len(after) :]
        targets = dict(zip(out_names, refs))
        refs = refs[len(out_names) :]
        space = dict(zip(scratch_names, refs))
        refs = refs[len(scratch_names) :]
        buffers = dict(zip(staged + copied, refs))
        sems_in, sems_out = refs[len(staged) + len(copied) :]
        kept = {n: ref for n, ref in targets.items() if n not in out_sems}
        r = types.SimpleNamespace(**space, **buffers, **kept)
        for n in direct:
            setattr(r, n, sources[n])

        def copy_in(n):
            return pltpu.make_async_copy(sources[n], buffers[n], sems_in.at[in_sems[n]])

        def copy_out(n):
            return pltpu.make_async_copy(buffers[n], targets[n], sems_out.at[out_sems[n]])

        r.fetch = lambda *names: [copy_in(n).start() for n in names if n in in_sems]
        r.need = lambda *names: [copy_in(n).wait() for n in names if n in in_sems]
        r.write = lambda *names: [copy_out(n).start() for n in names if n in out_sems]
        r.drain = lambda *names: [copy_out(n).wait() for n in names if n in out_sems]
        body(r)

    def in_space(n):
        if n in scalar_names:
            return pltpu.SMEM
        return pltpu.VMEM if isinstance(ins[n], Kept) else pl.ANY

    results = pl.pallas_call(
        kernel,
        name=name,
        in_specs=[pl.BlockSpec(memory_space=in_space(n)) for n in in_names]
        + [pl.BlockSpec(memory_space=pl.ANY) for _ in after],
        out_specs=[
            pl.BlockSpec(memory_space=pltpu.VMEM if isinstance(out, Kept) else pl.ANY)
            for out in outs.values()
        ],
        out_shape=[
            pltpu.VMEM(*out.what) if isinstance(out, Kept) else jax.ShapeDtypeStruct(*out)
            for out in outs.values()
        ],
        scratch_shapes=list(scratch.values())
        + [pltpu.VMEM(ins[n].shape, ins[n].dtype) for n in staged]
        + [pltpu.VMEM(*outs[n]) for n in copied]
        + [
            pltpu.SemaphoreType.DMA((max(1, len(staged)),)),
            pltpu.SemaphoreType.DMA((max(1, len(copied)),)),
        ],
        compiler_params=pltpu.CompilerParams(vmem_limit_bytes=vmem * mebibyte),
        cost_estimate=cost(micros),
    )(
        *[
            pltpu.with_memory_space_constraint(value.what, pltpu.VMEM)
            if isinstance(value, Kept)
            else value
            for value in ins.values()
        ],
        *after,
    )
    return types.SimpleNamespace(**dict(zip(outs, results)))


class Kept:
    def __init__(self, *what):
        self.what = what[0] if len(what) == 1 else what


def keep_all(names):
    return {name: Kept(value) for name, value in names.items()}


def chunks(extent, size):
    size = min(size, extent)
    return [slice(start, start + size) for start in range(0, extent, size)]


def lay_out_attention(r, masks, rows):
    for idx, mask in enumerate(masks):
        half, at = divmod(idx, max(1, len(masks) // 2))
        source = r.attn_near if half == 0 else r.attn_far
        place = pl.multiple_of((r.place[0] ^ mask) * rows, rows) if len(masks) > 1 else 0
        r.attn_w[pl.ds(place, rows), :] = source[at * rows : (at + 1) * rows, :]


def lay_out_ff(r, layer_idx):
    width = r.ff_down.shape[-1]
    for k, own in enumerate((r.w_gate, r.w_up)):
        r.ff_gate_up[0, :, k * width : (k + 1) * width] = own[layer_idx]
    r.ff_down[0] = r.w_down[layer_idx]
    part = r.ff_near.shape[1]
    for source, base in ((r.ff_near, 0), (r.ff_far, 1)):
        for m in range(2):
            rows = pl.ds(pl.multiple_of((r.place[1] ^ (2 * m + base)) * part, part), part)
            for k in range(2):
                r.ff_gate_up[1, rows, k * width : (k + 1) * width] = source[3 * m + k]
            r.ff_down[1, rows, :] = source[3 * m + 2]


def start_all(copies):
    for copy in copies:
        copy.start()


def wait_all(sem, *buffers):
    for whole in buffers:
        pltpu.make_async_copy(whole, whole, sem).wait()


def lane_low(rows):
    return lax.broadcasted_iota(jnp.int32, (rows, 128), 1) < 64


def lane_halves():
    low = lane_low(1).astype(f32)
    return low.astype(bf16), (1.0 - low).astype(bf16)


def pair_blocks(rows, low, high):
    return jnp.concatenate([rows * low, rows * high], axis=0)


def own_blocks(both, is_low):
    half = both.shape[0] // 2
    return jnp.where(is_low, both[:half], both[half:]).astype(bf16)


def attention_forward(r, x_ref, a_ref, sizes, layer_idx):
    series, slots, inner = sizes
    rows = series * slots
    for part in chunks(rows, 256):
        r.qkv[part, :] = dot_nn(a_ref[part, :], r.attn_w[:, : 3 * inner]).astype(bf16)
    is_low = lane_low(slots)
    low, high = lane_halves()
    for s in range(series):
        here = slice(s * slots, (s + 1) * slots)
        keep = r.mask[here, :] == 1
        for start in range(0, inner, 128):
            at = slice(start, start + 128)
            query = r.qkv[here, at]
            keys = r.qkv[here, inner + start : inner + start + 128]
            scores = dot_nt(keys, pair_blocks(query, low, high)) + r.bias[:, at]
            scores = jnp.where(keep, scores, masked_score)
            exps = jnp.exp(scores - jnp.max(scores, axis=0, keepdims=True))
            r.probs[here, at] = exps / jnp.sum(exps, axis=0, keepdims=True)
    for s in range(series):
        here = slice(s * slots, (s + 1) * slots)
        for start in range(0, inner, 128):
            at = slice(start, start + 128)
            values = r.qkv[here, 2 * inner + start : 2 * inner + start + 128]
            both = dot_tn(r.probs[here, at].astype(bf16), values)
            r.heads[here, at] = own_blocks(both, is_low)
    gain = r.gain_ff[layer_idx : layer_idx + 1, :]
    for part in chunks(rows, 256):
        middle = x_ref[part, :] + dot_nt(r.heads[part, :], r.attn_w[:, 3 * inner :])
        r.middle[part, :] = middle
        r.ff_in[part, :] = (middle * inverse_rms(middle) * gain).astype(bf16)


def prepare_body(r):
    names = ("inputs", "valid", "keep", "embed", "gain_attn", "buckets")
    r.fetch(*names)
    r.need(*names)
    series, slots = r.valid.shape
    gain = r.gain_attn[0:1, :]
    valid = jnp.transpose(r.valid[...].astype(f32))
    keep = jnp.transpose(r.keep[...].astype(f32))
    for s in range(series):
        here = slice(s * slots, (s + 1) * slots)
        seen = valid[:, s : s + 1]
        x = jnp.where(seen == 1.0, r.inputs[here, :].astype(f32), r.embed[...])
        r.x[here, :] = x
        r.a[here, :] = (x * inverse_rms(x) * gain).astype(bf16)
        r.seen[here, :] = jnp.broadcast_to(seen, (slots, 128)).astype(jnp.int32)
        r.mask[here, :] = jnp.broadcast_to(keep[:, s : s + 1], (slots, 128)).astype(jnp.int32)
    turned = jnp.transpose(r.buckets[...].astype(f32)).astype(jnp.int32)
    wide = jnp.concatenate([turned, turned], axis=1)
    r.wide[...] = wide
    is_low = lane_low(slots)
    bucket_count, heads = r.table.shape
    for pair in range(heads // 2):
        bias = jnp.zeros((slots, 128), f32)
        for idx in range(bucket_count):
            entry = jnp.where(is_low, r.table[idx, 2 * pair], r.table[idx, 2 * pair + 1])
            bias = jnp.where(wide == idx, entry, bias)
        r.bias[:, pair * 128 : (pair + 1) * 128] = bias


def attention_body(r, sizes, masks, grain, layer_idx):
    r.fetch("gain_ff")
    lay_out_attention(r, masks, grain)
    r.need("gain_ff")
    attention_forward(r, r.x, r.a, sizes, layer_idx)


def ff_body(r):
    r.fetch("gain_attn")
    lay_out_ff(r, 0)
    r.need("gain_attn")
    width = r.middle.shape[1]
    for part in chunks(r.middle.shape[0], 256):
        x_next = r.middle[part, :]
        for half in range(2):
            both = dot_nn(r.ff_in[part, :], r.ff_gate_up[half])
            hidden = (gelu_terms(both[:, :width])[0] * both[:, width:]).astype(bf16)
            x_next = x_next + dot_nn(hidden, r.ff_down[half])
        r.x_next[part, :] = x_next
        r.a_next[part, :] = (x_next * inverse_rms(x_next) * r.gain_attn[1:2, :]).astype(bf16)


def ff_backward(r, layer_idx, last, masks):
    rows, width = r.middle.shape
    r.fetch("grad", "gain_ff")
    if last:
        lay_out_ff(r, layer_idx)
    r.need("grad", "gain_ff")
    gain_ff = r.gain_ff[layer_idx : layer_idx + 1, :]
    gain_total = jnp.zeros((1, width), f32)
    for part in chunks(rows, 256):
        grad = r.grad[part, :].astype(f32)
        rounded = grad.astype(bf16)
        ff_rows = r.ff_in[part, :]
        back = None
        middle = r.middle[part, :]
        total = middle
        for half in range(2):
            both = dot_nn(ff_rows, r.ff_gate_up[half])
            grad_hidden = dot_nt(rounded, r.ff_down[half])
            gate_act, up_act = both[:, :width], both[:, width:]
            mixed, slope = gelu_terms(gate_act)
            hidden = (mixed * up_act).astype(bf16)
            r.hidden[half, part, :] = hidden
            r.grad_gate_up[half, part, :width] = (grad_hidden * up_act * slope).astype(bf16)
            r.grad_gate_up[half, part, width:] = (grad_hidden * mixed).astype(bf16)
            pulled = r.grad_gate_up[half, part, :]
            if last:
                total = total + dot_nn(hidden, r.ff_down[half])
            term = dot_nt(pulled, r.ff_gate_up[half])
            back = term if back is None else back + term
        if last:
            r.outputs[part, :] = total.astype(bf16)
        grad_mid, gain_part = norm_back(middle, gain_ff, back)
        gain_total += gain_part
        grad_mid = grad + grad_mid
        r.grad_mid[part, :] = grad_mid
        r.branch[part, :] = grad_mid.astype(bf16)
        r.grad_low[part, :] = rounded
    if last:
        r.write("outputs")
    for half in range(2):
        r.ff_grad[half, :, : 2 * width] = dot_tn(r.ff_in[...], r.grad_gate_up[half])
        r.ff_grad[half, :, 2 * width :] = dot_tn(r.hidden[half], r.grad_low[...])
    half_count = len(masks[0]) // 2
    grain, columns = r.ff_keep.shape[1:]
    for side, side_masks in enumerate(masks):
        lanes = slice(side * columns, (side + 1) * columns)
        for idx, mask in enumerate(side_masks):
            target = r.ff_keep if idx < half_count else r.ff_send
            piece = pl.ds(pl.multiple_of((r.place[3] ^ (mask // 2)) * grain, grain), grain)
            target[side * half_count + idx % half_count] = r.ff_grad[mask % 2, piece, lanes].astype(
                bf16
            )
    if last:
        r.drain("outputs")
    return gain_total


def attention_backward(r, sizes, layer_idx, last, piece_masks, heads):
    series, slots, inner = sizes
    rows = series * slots
    width = r.x.shape[1]
    r.fetch("gain_attn")
    for part in chunks(rows, 256):
        r.grad_heads[part, :] = dot_nn(r.branch[part, :], r.attn_w[:, 3 * inner :]).astype(bf16)
    is_low = lane_low(slots)
    low, high = lane_halves()
    for start in range(0, inner, 128):
        at = slice(start, start + 128)
        bias_total = jnp.zeros((slots, 128), f32) if last else r.bias_before[:, at]
        for s in range(series):
            here = slice(s * slots, (s + 1) * slots)
            probs = r.probs[here, at]
            values = r.qkv[here, 2 * inner + start : 2 * inner + start + 128]
            grad_probs = dot_nt(values, pair_blocks(r.grad_heads[here, at], low, high))
            inner_sum = jnp.sum(probs * grad_probs, axis=0, keepdims=True)
            grad_scores = (probs * (grad_probs - inner_sum)).astype(bf16)
            r.grad_scores[here, at] = grad_scores
            bias_total = bias_total + grad_scores.astype(f32)
        r.bias_acc[:, at] = bias_total
    for s in range(series):
        here = slice(s * slots, (s + 1) * slots)
        for start in range(0, inner, 128):
            at = slice(start, start + 128)
            key_at = slice(inner + start, inner + start + 128)
            value_at = slice(2 * inner + start, 2 * inner + start + 128)
            grad_scores = r.grad_scores[here, at]
            r.grad_qkv[here, key_at] = dot_nn(
                grad_scores, pair_blocks(r.qkv[here, at], low, high)
            ).astype(bf16)
            r.grad_qkv[here, value_at] = dot_nn(
                r.probs[here, at].astype(bf16), pair_blocks(r.grad_heads[here, at], low, high)
            ).astype(bf16)
            r.grad_qkv[here, at] = own_blocks(dot_tn(grad_scores, r.qkv[here, key_at]), is_low)
    r.attn_grad[:, : 3 * inner] = dot_tn(r.a[...], r.grad_qkv[...])
    r.attn_grad[:, 3 * inner :] = dot_tn(r.branch[...], r.heads[...])
    scatter_pieces(r.attn_grad, r.attn_keep, r.attn_send, piece_masks, r.place[2])
    r.need("gain_attn")
    gain_attn = r.gain_attn[layer_idx : layer_idx + 1, :]
    gain_total = jnp.zeros((1, width), f32)
    embed_total = jnp.zeros((1, width), f32)
    for part in chunks(rows, 256):
        grad_normed = dot_nt(r.grad_qkv[part, :], r.attn_w[:, : 3 * inner])
        grad_in, gain_part = norm_back(r.x[part, :], gain_attn, grad_normed)
        gain_total += gain_part
        grad_in = r.grad_mid[part, :] + grad_in
        if last:
            r.grad_next[part, :] = grad_in
        else:
            seen = r.seen[part, 0:1] == 1
            r.grad_next[part, :] = jnp.where(seen, grad_in, 0.0)
            embed_total += jnp.sum(jnp.where(seen, 0.0, grad_in), axis=0, keepdims=True)
    r.write("grad_next")
    if not last:
        put_row(r.small, 4, embed_total)
        head_size = inner // heads
        for idx in range(r.table_rows.shape[0]):
            for start in range(0, inner, 128):
                at = slice(start, start + 128)
                chosen = jnp.where(r.wide[...] == idx, r.bias_acc[:, at], 0.0)
                r.table_rows[idx : idx + 1, at] = jnp.sum(chosen, axis=0, keepdims=True)
        lane = lax.broadcasted_iota(jnp.int32, (r.table_rows.shape[0], 128), 1)
        table = jnp.zeros(lane.shape, f32)
        for head in range(heads):
            cut = r.table_rows[:, head * head_size : (head + 1) * head_size]
            table = jnp.where(lane == head, jnp.sum(cut, axis=1, keepdims=True), table)
        r.small[:heads, : table.shape[0]] = jnp.transpose(table)[:heads, :]
    r.drain("grad_next")
    return gain_total


def two_parts(values):
    high = values.astype(bf16).astype(f32)
    return high, (values - high).astype(bf16).astype(f32)


def last_ff_body(r, masks):
    r.small[...] = jnp.zeros(r.small.shape, f32)
    put_row(r.small, 3, ff_backward(r, 1, True, masks))


def last_attention_body(r, sizes, piece_masks, heads):
    r.small[...] = r.small_before[...]
    put_row(r.small, 1, attention_backward(r, sizes, 1, True, piece_masks, heads))


def ff_backward_body(r, masks):
    r.small[...] = r.small_before[...]
    put_row(r.small, 2, ff_backward(r, 0, False, masks))


def attention_backward_body(r, sizes, piece_masks, heads):
    r.small[...] = r.small_before[...]
    put_row(r.small, 0, attention_backward(r, sizes, 0, False, piece_masks, heads))
    high, low = two_parts(r.small[...])
    last = r.attn_send.shape[0] - 1
    r.attn_send[last] = jnp.concatenate([high, low], axis=0).astype(bf16)
    r.small[...] = high + low


def put_row(packed, which, row):
    first, width = packed.shape[0] - 2, row.shape[1]
    at = which % 3 * width
    packed[first + which // 3 : first + which // 3 + 1, at : at + width] = row


def scatter_pieces(whole, keep, send, masks, place):
    count = len(masks)
    grain = whole.shape[0] // count
    for idx, mask in enumerate(masks):
        target = keep if idx < count // 2 else send
        source = pl.ds(pl.multiple_of((place ^ mask) * grain, grain), grain)
        target[idx % (count // 2)] = whole[source, :].astype(bf16)


def finish(pieces, masks, layer_idx, place, shape, before=()):
    grain, width = pieces.shape[1], shape[-1]
    count = len(before)

    def kernel(place_ref, source, *refs):
        outs = refs[count : count + 3]
        stage, out_sem = refs[count + 3 :]
        for idx, mask in enumerate(masks):
            rows = pl.ds(pl.multiple_of((place_ref[3] ^ mask) * grain, grain), grain)
            for k, out in enumerate(outs):
                stage[k, idx] = source[idx, :, k * width : (k + 1) * width].astype(f32)
                pltpu.make_async_copy(stage.at[k, idx], out.at[layer_idx, rows], out_sem).start()
        pltpu.make_async_copy(stage, stage, out_sem).wait()

    return pl.pallas_call(
        kernel,
        name="layer_%d_ff_grads" % layer_idx,
        in_specs=[
            pl.BlockSpec(memory_space=pltpu.SMEM),
            pl.BlockSpec(memory_space=pltpu.VMEM),
        ]
        + [pl.BlockSpec(memory_space=pl.ANY)] * count,
        out_specs=[pl.BlockSpec(memory_space=pl.ANY)] * 3,
        out_shape=[jax.ShapeDtypeStruct(shape, f32)] * 3,
        input_output_aliases={2 + k: k for k in range(count)},
        scratch_shapes=[
            pltpu.VMEM((3, len(masks), grain, width), f32),
            pltpu.SemaphoreType.DMA,
        ],
        compiler_params=pltpu.CompilerParams(vmem_limit_bytes=6 * mebibyte),
        cost_estimate=cost(3),
    )(place, pltpu.with_memory_space_constraint(pieces, pltpu.VMEM), *before)


def small_body(r):
    width = r.embed.shape[1]
    heads = r.table.shape[0]
    outs = ((r.gain_attn, 0), (r.gain_attn, 1), (r.gain_ff, 0), (r.gain_ff, 1), (r.embed, 0))
    for which, (out, row) in enumerate(outs):
        first = r.packed.shape[0] - 2 + which // 3
        at = which % 3 * width
        out[row : row + 1, :] = r.packed[first : first + 1, at : at + width]
    r.table[...] = r.packed[:heads, : r.table.shape[1]]
    r.write("gain_attn", "gain_ff", "embed", "table")
    r.drain("gain_attn", "gain_ff", "embed", "table")


def pack_body(r, packs):
    rows = r.quarter_0.shape[1]
    at = pl.ds(pl.multiple_of(r.place[1] * rows, rows), rows)
    copies = []
    outs = [r.quarter_0, r.quarter_1]
    for layer_idx in range(2):
        for k, w in enumerate((r.w_gate, r.w_up, r.w_down)):
            copies.append((w.at[layer_idx, at], outs[layer_idx].at[k]))
    if packs:
        outs += [r.block_0, r.block_1]
        inner = r.w_query.shape[2]
        for layer_idx in range(2):
            for k, w in enumerate((r.w_query, r.w_key, r.w_value, r.w_out)):
                lanes = pl.ds(k * inner, inner)
                copies.append((w.at[layer_idx], outs[2 + layer_idx].at[:, lanes]))
    start_all([pltpu.make_async_copy(*ends, r.pack_sem) for ends in copies])
    wait_all(r.pack_sem, *outs)


def order_masks(hops):
    masks = [0]
    for hop in reversed(hops):
        masks = masks + [mask ^ hop for mask in masks]
    return masks


def tie(value, *others):
    return lax.optimization_barrier((value, *others))[0]


def on_device(
    inputs,
    cotangent,
    attention_mask,
    patch_valid,
    buckets,
    mask_embed,
    w_query,
    w_key,
    w_value,
    w_output,
    w_gate,
    w_up,
    w_down,
    gain_attn,
    gain_ff,
    bias_table,
    dp_size,
):
    series, slots, width = inputs.shape
    heads = bias_table.shape[1]
    inner = w_query.shape[2]
    rows = series * slots
    sizes = (series, slots, inner)
    matrix = (rows, width)
    devices = 2 * dp_size
    dp_at = lax.axis_index("dp")
    device_at = 2 * dp_at + lax.axis_index("tensor")
    cotangent = cotangent.reshape(matrix)

    def swap(array, mask):
        return lax.ppermute(array, axes, [(n, n ^ mask) for n in range(devices)])

    def join(left, right):
        return jnp.concatenate([left, right], axis=0)

    bits = [1 << k for k in range(devices.bit_length() - 1)]

    attn_grain = max(16, width // devices)
    attn_count = width // attn_grain
    ff_grain = max(16, width // dp_size)
    ff_count = width // ff_grain
    quarter_at = lax.rem(dp_at, 4)
    place = jnp.stack(
        [
            device_at,
            quarter_at,
            device_at // (devices // attn_count),
            lax.rem(dp_at, ff_count),
        ]
    ).astype(jnp.int32)

    quarter = width // 4
    own_rows = w_query.shape[1]
    direct = own_rows % 16 == 0
    w_out = jnp.swapaxes(w_output, 1, 2)
    sources = dict(w_gate=w_gate, w_up=w_up, w_down=w_down)
    block_outs = {}
    if direct:
        sources |= dict(w_query=w_query, w_key=w_key, w_value=w_value, w_out=w_out)
        block_outs = {"block_%d" % k: Kept((own_rows, 4 * inner), bf16) for k in range(2)}
    packed = run(
        functools.partial(pack_body, packs=direct),
        "pack",
        dict(
            place=place,
            **{n: pltpu.with_memory_space_constraint(w, pltpu.HBM) for n, w in sources.items()},
        ),
        dict(
            quarter_0=Kept((3, quarter, width), bf16),
            quarter_1=Kept((3, quarter, width), bf16),
            **block_outs,
        ),
        dict(pack_sem=pltpu.SemaphoreType.DMA),
        vmem=4,
    )
    far = bits[2:]

    def prepare(token):
        return run(
            prepare_body,
            "prepare",
            dict(
                inputs=tie(inputs, token).reshape(matrix),
                valid=patch_valid,
                keep=attention_mask,
                embed=mask_embed[None, :],
                gain_attn=gain_attn,
                buckets=buckets,
                table=bias_table,
            ),
            dict(
                x=Kept(matrix, f32),
                a=Kept(matrix, bf16),
                bias=Kept((slots, heads * slots), f32),
                mask=Kept((rows, 128), jnp.int32),
                seen=Kept((rows, 128), jnp.int32),
                wide=Kept((slots, 128), jnp.int32),
            ),
            {},
            micros=3,
        )

    if direct:
        hops_0 = [1] + far[2:] + far[:2] + [2]
        hops_1 = far[2:] + far[:2] + [1, 2]
        block_0, block_1 = packed.block_0, packed.block_1
        got_1 = swap(block_1, hops_1[0])
        got_0 = swap(block_0, hops_0[0])
        ff_0 = swap(tie(packed.quarter_0, got_0), 1)
        ff_1 = swap(tie(packed.quarter_1, ff_0), 1)
        got_ff_0 = swap(ff_0, 4)
        block_0 = join(block_0, got_0)
        block_1 = join(block_1, tie(got_1, block_0))
        for hop_0, hop_1 in zip(hops_0[1:-2], hops_1[1:-2]):
            got_1, got_0 = swap(block_1, hop_1), swap(block_0, hop_0)
            if hop_0 == hops_0[1]:
                start = prepare(block_1)
                got_0 = tie(got_0, ff_0)
            block_0 = join(block_0, got_0)
            block_1 = join(block_1, tie(got_1, block_0))
        block_0 = tie(block_0, block_1)
        got_0 = swap(block_0, hops_0[-2])
        got_1 = swap(block_1, hops_1[-2])
        block_0 = join(block_0, tie(got_0, start.a, got_ff_0, ff_1, got_1))
        ff_0 = join(ff_0, tie(got_ff_0, block_0))
        got_ff_1 = swap(tie(ff_1, ff_0), 4)
        attn_pieces = [(block_0, swap(block_0, 2), order_masks(hops_0[::-1]))]
    else:
        ff_0, ff_1 = swap(packed.quarter_0, 1), swap(packed.quarter_1, 1)
        ff_0 = join(ff_0, swap(ff_0, 4))
        start = prepare(ff_0)
        attn_pieces = []
        rows_of = jnp.concatenate([w_query, w_key, w_value, w_out], axis=2)
        for layer_idx in range(2):
            whole = lax.all_gather(rows_of[layer_idx], axes, axis=0, tiled=True)
            attn_pieces.append((whole, whole, [0]))
    ff_pieces = [(ff_0, swap(ff_0, 2))]

    def attn_ins(layer_idx):
        near, far, masks = attn_pieces[layer_idx]
        return dict(attn_near=Kept(near), attn_far=Kept(far)), masks

    def ff_ins(layer_idx):
        near, far = ff_pieces[layer_idx]
        own = keep_all(dict(w_gate=w_gate, w_up=w_up, w_down=w_down))
        return dict(**own, ff_near=Kept(near), ff_far=Kept(far))

    ff_outs = dict(
        ff_gate_up=Kept((2, width, 2 * width), bf16), ff_down=Kept((2, width, width), bf16)
    )
    grain = own_rows if direct else width
    attn_outs = dict(
        attn_w=Kept((width, 4 * inner), bf16),
        qkv=Kept((rows, 3 * inner), bf16),
        probs=Kept((rows, heads * slots), f32),
        heads=Kept((rows, inner), bf16),
        middle=Kept(matrix, f32),
        ff_in=Kept(matrix, bf16),
    )

    def attention(layer_idx, x, a, after=(), micros=5):
        pieces, masks = attn_ins(layer_idx)
        return run(
            functools.partial(
                attention_body, sizes=sizes, masks=masks, grain=grain, layer_idx=layer_idx
            ),
            "layer_%d_attention" % layer_idx,
            dict(
                place=place,
                x=Kept(x),
                a=Kept(a),
                bias=Kept(start.bias),
                mask=Kept(start.mask),
                gain_ff=gain_ff,
                **pieces,
            ),
            attn_outs,
            {},
            after=after,
            micros=micros,
        )

    first = attention(0, start.x, start.a, micros=10)
    if direct:
        block_1 = join(block_1, tie(got_1, first.ff_in))
        attn_pieces.append((block_1, swap(block_1, 2), order_masks(hops_1[::-1])))
    first_ff = run(
        ff_body,
        "layer_0_ff",
        dict(
            place=place,
            middle=Kept(first.middle),
            ff_in=Kept(first.ff_in),
            gain_attn=gain_attn,
            **ff_ins(0),
        ),
        dict(**ff_outs, x_next=Kept(matrix, f32), a_next=Kept(matrix, bf16)),
        {},
        after=(block_1,) if direct else (),
        micros=3,
    )
    if direct:
        ff_1 = join(ff_1, tie(got_ff_1, first_ff.x_next))
    else:
        ff_1 = join(ff_1, swap(ff_1, 4))
    ff_pieces.append((ff_1, swap(ff_1, 2)))
    second = attention(1, first_ff.x_next, first_ff.a_next, micros=0.1)

    attn_low = devices // attn_count
    attn_hops = ([2, 1] + bits[2:], [2] + bits[3:4] + bits[2:3] + bits[4:] + [1])
    attn_split = [[hop for hop in hops if hop >= attn_low] for hops in attn_hops]
    attn_whole = [hop for hop in bits if hop < attn_low]
    attn_masks = [[mask // attn_low for mask in order_masks(hops)] for hops in attn_split]
    ff_hops = ([2, 4, 1] + bits[3:], [2, 1, 4] + bits[3:])
    ff_split = [[hop for hop in hops if hop // 2 < ff_count] for hops in ff_hops]
    ff_whole = [hop for hop in bits[1:] if hop // 2 >= ff_count]
    ff_share = [hop for hop in bits[:0:-1] if hop // 2 < ff_count]
    ff_masks = [order_masks(hops) for hops in ff_split]
    place_masks = [mask // 2 for mask in order_masks(ff_share[::-1])]
    attn_half = (attn_count // 2, attn_grain, 4 * inner)
    small_shape = (heads + 2, 3 * width)

    attn_back_outs = dict(attn_keep=Kept(attn_half, bf16), attn_send=Kept(attn_half, bf16))
    attn_back_scratch = dict(
        grad_heads=pltpu.VMEM((rows, inner), bf16),
        grad_qkv=pltpu.VMEM((rows, 3 * inner), bf16),
        grad_scores=pltpu.VMEM((rows, heads * slots), bf16),
        attn_grad=pltpu.VMEM((width, 4 * inner), f32),
    )
    ff_back_outs = dict(
        ff_keep=Kept((2 * ff_count, ff_grain, 3 * width // 2), bf16),
        ff_send=Kept((2 * ff_count, ff_grain, 3 * width // 2), bf16),
        small=Kept(small_shape, f32),
        grad_mid=Kept(matrix, f32),
        branch=Kept(matrix, bf16),
    )
    ff_back_scratch = dict(
        hidden=pltpu.VMEM((2, rows, width), bf16),
        grad_gate_up=pltpu.VMEM((2, rows, 2 * width), bf16),
        ff_grad=pltpu.VMEM((2, width, 3 * width), f32),
        grad_low=pltpu.VMEM(matrix, bf16),
    )
    bias_shape = (slots, heads * slots)

    def attn_back_ins(kept, x, a):
        return dict(
            x=Kept(x),
            a=Kept(a),
            gain_attn=gain_attn,
            attn_w=Kept(kept.attn_w),
            qkv=Kept(kept.qkv),
            probs=Kept(kept.probs),
            heads=Kept(kept.heads),
        )

    def add(left, right):
        return (left.astype(f32) + right.astype(f32)).astype(bf16)

    def halving(keep, send, hops, out):
        for step, hop in enumerate(hops):
            got = yield swap(send, hop)
            if step + 1 < len(hops):
                cut = keep.shape[0] // 2
                send = add(keep[cut:], got[cut:])
                keep = add(keep[:cut], got[:cut])
                out["token"] = send
            else:
                out["token"] = keep = add(keep, got)
        out["piece"] = keep

    def summing(piece, hops, out):
        for hop in hops:
            got = yield swap(piece, hop)
            out["token"] = piece = add(piece, got)
        out["piece"] = piece

    def sharing(piece, hops, out):
        for step, hop in enumerate(hops):
            if step + 1 == len(hops):
                out["near"] = piece
            got = yield swap(piece, hop)
            if step + 1 < len(hops):
                out["token"] = piece = join(piece, got)
            else:
                out["token"] = out["far"] = got

    def rounded(values):
        return lax.reduce_precision(values, exponent_bits=8, mantissa_bits=7)

    def with_small(pieces, small):
        high = rounded(small)
        low = rounded(small - high)
        parts = join(high, low).astype(bf16)[None]
        return join(pieces, parts), high + low

    def add_small(small, got):
        parts = got[-1].astype(f32)
        return small + (parts[: small.shape[0]] + parts[small.shape[0] :])

    def attn_chain(part, layer_idx, out):
        small = part.small if layer_idx == 0 else None
        keep, send = part.attn_keep, part.attn_send
        hops = attn_split[layer_idx] + attn_whole
        for step, hop in enumerate(hops):
            got = yield swap(send, hop)
            if small is not None:
                small = add_small(small, got)
                got = got[:-1]
            if step + 1 < len(attn_split[layer_idx]):
                half = keep.shape[0] // 2
                send = add(keep[half:], got[half:])
                keep = add(keep[:half], got[:half])
            else:
                send = keep = add(keep, got)
            if small is not None and step + 1 < len(hops):
                send, small = with_small(send, small)
            out["token"] = send
            if layer_idx == 1 and step == 0:
                send = tie(send, *(yield None))
        piece = keep[0]
        if own_rows < attn_grain:
            first_row = lax.rem(device_at, attn_low) * own_rows
            piece = lax.dynamic_slice_in_dim(piece, first_row, own_rows, axis=0)
        out["done"] = piece.astype(f32)
        out["small"] = small

    def ff_chain(part, out):
        got = yield swap(part.ff_send, 2)
        count = ff_count
        keeps, sends = [], []
        for side in range(2):
            at, half = side * count, count // 2
            sends.append(add(part.ff_keep[at + half : at + count], got[at + half : at + count]))
            keeps.append(add(part.ff_keep[at : at + half], got[at : at + half]))
        out["token"] = tuple(sends)
        for hops in zip(ff_split[0][1:3], ff_split[1][1:3]):
            got = yield tuple(swap(send, hop) for send, hop in zip(sends, hops))
            half = keeps[0].shape[0] // 2
            sends = [add(keep[half:], one[half:]) for keep, one in zip(keeps, got)]
            keeps = [add(keep[:half], one[:half]) for keep, one in zip(keeps, got)]
            out["token"] = tuple(sends)
        keep, send = (jnp.concatenate(sides, axis=2) for sides in (keeps, sends))
        yield from halving(keep, send, ff_split[0][3:], out)
        yield from summing(out["piece"], ff_whole, out)
        yield from sharing(out["piece"], ff_share, out)

    class Chain:
        def __init__(self, steps, *args):
            self.out = {}
            self.steps = steps(*args, self.out)
            self.arriving = next(self.steps)

        def resume(self, *tokens):
            self.arriving = self.steps.send(tokens)

        def step(self, token, *others):
            if self.arriving is not None:
                tokens = (*(token if isinstance(token, tuple) else (token,)), *others)
                many = isinstance(self.arriving, tuple)
                arrived = self.arriving if many else (self.arriving,)
                arrived = lax.optimization_barrier((*arrived, *tokens))[: len(arrived)]
                arrived = arrived if many else arrived[0]
                self.arriving = None
                try:
                    self.arriving = self.steps.send(arrived)
                except StopIteration:
                    pass
                return self.out["token"]
            return token

    back_ff_1 = run(
        functools.partial(last_ff_body, masks=ff_masks),
        "layer_1_ff",
        dict(
            place=place,
            grad=cotangent,
            gain_ff=gain_ff,
            middle=Kept(second.middle),
            ff_in=Kept(second.ff_in),
            **ff_ins(1),
        ),
        dict(**ff_back_outs, outputs=(matrix, bf16)),
        dict(
            ff_gate_up=pltpu.VMEM((2, width, 2 * width), bf16),
            ff_down=pltpu.VMEM((2, width, width), bf16),
            **ff_back_scratch,
        ),
        micros=8,
        vmem=24,
    )
    ff_1 = Chain(ff_chain, back_ff_1)
    back_1 = run(
        functools.partial(
            last_attention_body, sizes=sizes, piece_masks=attn_masks[1], heads=heads
        ),
        "layer_1_attention_backward",
        dict(
            place=place,
            small_before=Kept(back_ff_1.small),
            grad_mid=Kept(back_ff_1.grad_mid),
            branch=Kept(back_ff_1.branch),
            **attn_back_ins(second, first_ff.x_next, first_ff.a_next),
        ),
        dict(
            **attn_back_outs,
            small=Kept(small_shape, f32),
            grad_next=Kept(matrix, f32),
            bias_acc=Kept(bias_shape, f32),
        ),
        attn_back_scratch,
        micros=6,
        vmem=14,
    )
    attn_1 = Chain(attn_chain, back_1, 1)
    token = ff_1.step(back_1.attn_send)
    token = (attn_1.step(token),)
    back_0 = run(
        functools.partial(ff_backward_body, masks=ff_masks),
        "layer_0_ff_backward",
        dict(
            place=place,
            grad=Kept(back_1.grad_next),
            gain_ff=gain_ff,
            small_before=Kept(back_1.small),
            middle=Kept(first.middle),
            ff_in=Kept(first.ff_in),
            ff_gate_up=Kept(first_ff.ff_gate_up),
            ff_down=Kept(first_ff.ff_down),
        ),
        ff_back_outs,
        ff_back_scratch,
        after=token,
        micros=8,
        vmem=20,
    )
    token = ff_1.step(back_0.branch)
    back_0.ff_send = tie(back_0.ff_send, *token)
    ff_0 = Chain(ff_chain, back_0)
    token = ff_0.step(token)
    back_attn_0 = run(
        functools.partial(
            attention_backward_body, sizes=sizes, piece_masks=attn_masks[0], heads=heads
        ),
        "layer_0_attention_backward",
        dict(
            place=place,
            bias_before=Kept(back_1.bias_acc),
            seen=Kept(start.seen),
            wide=Kept(start.wide),
            small_before=Kept(back_0.small),
            grad_mid=Kept(back_0.grad_mid),
            branch=Kept(back_0.branch),
            **attn_back_ins(first, start.x, start.a),
        ),
        dict(
            attn_keep=Kept(attn_half, bf16),
            attn_send=Kept((attn_count // 2 + 1, *attn_half[1:]), bf16),
            small=Kept(small_shape, f32),
            grad_next=(matrix, f32),
        ),
        dict(
            bias_acc=pltpu.VMEM(bias_shape, f32),
            table_rows=pltpu.VMEM((bias_table.shape[0], heads * slots), f32),
            **attn_back_scratch,
        ),
        after=token,
        micros=7,
        vmem=14,
    )
    attn_0 = Chain(attn_chain, back_attn_0, 0)
    attn_1.resume(back_attn_0.attn_send)
    token = back_attn_0.attn_send
    shape = (2, width, width)
    near_masks = place_masks[: ff_count // 2]
    far_masks = place_masks[ff_count // 2 :]
    done = ()
    ended = False
    turn = 0
    sums = attn_grads = None
    while ff_0.arriving is not None:
        turn += 1
        token = ff_1.step(token)
        if done and not ended:
            done = finish(tie(ff_1.out["far"], token), far_masks, 1, place, shape, done)
            token = done[0]
            ended = True
        token = ff_0.step(token)
        if not done and "near" in ff_1.out:
            done = finish(tie(ff_1.out["near"], token), near_masks, 1, place, shape)
            token = done[0]
        if turn != 2:
            token = attn_0.step(token)
        if turn > 2:
            token = attn_1.step(token)
        if sums is None and attn_0.arriving is None:
            sums = run(
                small_body,
                "small_sums",
                dict(packed=Kept(tie(attn_0.out["small"], token))),
                dict(
                    gain_attn=((2, width), f32),
                    gain_ff=((2, width), f32),
                    embed=((1, width), f32),
                    table=(bias_table.shape[::-1], f32),
                ),
                {},
            )
            token = sums.embed
        if attn_grads is None and attn_0.arriving is None and attn_1.arriving is None:
            both = jnp.stack([attn_0.out["done"], tie(attn_1.out["done"], token)])
            attn_grads = [both[:, :, k * inner : (k + 1) * inner] for k in range(4)]
            attn_grads[3] = jnp.swapaxes(attn_grads[3], 1, 2)
            token = tuple(attn_grads)
    if not ended:
        done = finish(ff_1.out["far"], far_masks, 1, place, shape, done)
    for pieces, masks in ((ff_0.out["near"], near_masks), (ff_0.out["far"], far_masks)):
        done = finish(pieces, masks, 0, place, shape, done)
    return (
        back_ff_1.outputs.reshape(inputs.shape),
        back_attn_0.grad_next.reshape(inputs.shape),
        *attn_grads,
        *done,
        sums.gain_attn,
        sums.gain_ff,
        sums.table.T,
        sums.embed[0],
    )


def solution(mesh):
    placed = (
        P(("dp", "tensor"), None, None),
        P(("dp", "tensor"), None, None),
        P(("dp", "tensor"), None),
        P(("dp", "tensor"), None),
        P(),
        P(),
        P(None, ("dp", "tensor"), None),
        P(None, ("dp", "tensor"), None),
        P(None, ("dp", "tensor"), None),
        P(None, None, ("dp", "tensor")),
        P(None, None, "tensor"),
        P(None, None, "tensor"),
        P(None, "tensor", None),
        P(),
        P(),
        P(),
    )
    return jax.shard_map(
        functools.partial(on_device, dp_size=mesh.shape["dp"]),
        mesh=mesh,
        in_specs=placed,
        out_specs=(
            P(("dp", "tensor"), None, None),
            P(("dp", "tensor"), None, None),
            P(None, ("dp", "tensor"), None),
            P(None, ("dp", "tensor"), None),
            P(None, ("dp", "tensor"), None),
            P(None, None, ("dp", "tensor")),
            P(None, None, "tensor"),
            P(None, None, "tensor"),
            P(None, "tensor", None),
            P(),
            P(),
            P(),
            P(),
        ),
        check_vma=False,
    )
```

```python
import functools
import types

import jax
import jax.numpy as jnp
from jax import lax
from jax.experimental import pallas as pl
from jax.experimental.pallas import tpu as pltpu
from jax.sharding import PartitionSpec as P

norm_eps = 1e-06
masked_score = -1e30
bf16 = jnp.bfloat16
f32 = jnp.float32
axes = ("dp", "tensor")
mebibyte = 1024 * 1024
raw_names = ("w_query", "w_key", "w_value", "w_out", "w_gate", "w_up", "w_down")
scalar_names = ("place", "table")


def dot_nn(left, right):
    return lax.dot_general(left, right, (((1,), (0,)), ((), ())), preferred_element_type=f32)


def dot_nt(left, right):
    return lax.dot_general(left, right, (((1,), (1,)), ((), ())), preferred_element_type=f32)


def dot_tn(left, right):
    return lax.dot_general(left, right, (((0,), (0,)), ((), ())), preferred_element_type=f32)


def inverse_rms(values):
    return lax.rsqrt(jnp.mean(values * values, axis=-1, keepdims=True) + norm_eps)


def norm_back(values, gain, grad_out):
    scale = inverse_rms(values)
    pulled = grad_out * gain
    mean_part = jnp.mean(pulled * values, axis=-1, keepdims=True)
    grad_in = scale * pulled - values * (scale * scale * scale) * mean_part
    return grad_in, jnp.sum(grad_out * values * scale, axis=0, keepdims=True)


def gelu_terms(gate_act):
    square = gate_act * gate_act
    bent = jnp.tanh(0.7978845608028654 * gate_act * (1.0 + 0.044715 * square))
    half = 0.5 * (1.0 + bent)
    slope = half + 0.5 * gate_act * (1.0 - bent * bent) * (
        0.7978845608028654 * (1.0 + 3.0 * 0.044715 * square)
    )
    return gate_act * half, slope


def cost(micros):
    return pl.CostEstimate(flops=int(micros * 1.15e9), bytes_accessed=0, transcendentals=0)


def run(body, name, ins, outs, scratch, after=(), micros=1, vmem=8):
    in_names, out_names, scratch_names = list(ins), list(outs), list(scratch)
    direct = {n for n in in_names if n in scalar_names + raw_names or isinstance(ins[n], Kept)}
    staged = [n for n in in_names if n not in direct]
    copied = [n for n in out_names if not isinstance(outs[n], Kept)]
    in_sems = {n: i for i, n in enumerate(staged)}
    out_sems = {n: i for i, n in enumerate(copied)}

    def kernel(*refs):
        refs = list(refs)
        sources = dict(zip(in_names, refs))
        refs = refs[len(in_names) + len(after) :]
        targets = dict(zip(out_names, refs))
        refs = refs[len(out_names) :]
        space = dict(zip(scratch_names, refs))
        refs = refs[len(scratch_names) :]
        buffers = dict(zip(staged + copied, refs))
        sems_in, sems_out = refs[len(staged) + len(copied) :]
        kept = {n: ref for n, ref in targets.items() if n not in out_sems}
        r = types.SimpleNamespace(**space, **buffers, **kept)
        for n in direct:
            setattr(r, n, sources[n])

        def copy_in(n):
            return pltpu.make_async_copy(sources[n], buffers[n], sems_in.at[in_sems[n]])

        def copy_out(n):
            return pltpu.make_async_copy(buffers[n], targets[n], sems_out.at[out_sems[n]])

        r.fetch = lambda *names: [copy_in(n).start() for n in names if n in in_sems]
        r.need = lambda *names: [copy_in(n).wait() for n in names if n in in_sems]
        r.write = lambda *names: [copy_out(n).start() for n in names if n in out_sems]
        r.drain = lambda *names: [copy_out(n).wait() for n in names if n in out_sems]
        body(r)

    def in_space(n):
        if n in scalar_names:
            return pltpu.SMEM
        return pltpu.VMEM if isinstance(ins[n], Kept) else pl.ANY

    results = pl.pallas_call(
        kernel,
        name=name,
        in_specs=[pl.BlockSpec(memory_space=in_space(n)) for n in in_names]
        + [pl.BlockSpec(memory_space=pl.ANY) for _ in after],
        out_specs=[
            pl.BlockSpec(memory_space=pltpu.VMEM if isinstance(out, Kept) else pl.ANY)
            for out in outs.values()
        ],
        out_shape=[
            pltpu.VMEM(*out.what) if isinstance(out, Kept) else jax.ShapeDtypeStruct(*out)
            for out in outs.values()
        ],
        scratch_shapes=list(scratch.values())
        + [pltpu.VMEM(ins[n].shape, ins[n].dtype) for n in staged]
        + [pltpu.VMEM(*outs[n]) for n in copied]
        + [
            pltpu.SemaphoreType.DMA((max(1, len(staged)),)),
            pltpu.SemaphoreType.DMA((max(1, len(copied)),)),
        ],
        compiler_params=pltpu.CompilerParams(vmem_limit_bytes=vmem * mebibyte),
        cost_estimate=cost(micros),
    )(
        *[
            pltpu.with_memory_space_constraint(value.what, pltpu.VMEM)
            if isinstance(value, Kept)
            else value
            for value in ins.values()
        ],
        *after,
    )
    return types.SimpleNamespace(**dict(zip(outs, results)))


class Kept:
    def __init__(self, *what):
        self.what = what[0] if len(what) == 1 else what


def keep_all(names):
    return {name: Kept(value) for name, value in names.items()}


def chunks(extent, size):
    size = min(size, extent)
    return [slice(start, start + size) for start in range(0, extent, size)]


def lay_out_attention(r, masks, rows):
    for idx, mask in enumerate(masks):
        half, at = divmod(idx, max(1, len(masks) // 2))
        source = r.attn_near if half == 0 else r.attn_far
        place = pl.multiple_of((r.place[0] ^ mask) * rows, rows) if len(masks) > 1 else 0
        r.attn_w[pl.ds(place, rows), :] = source[at * rows : (at + 1) * rows, :]


def lay_out_ff(r, layer_idx):
    width = r.ff_down.shape[-1]
    for k, own in enumerate((r.w_gate, r.w_up)):
        r.ff_gate_up[0, :, k * width : (k + 1) * width] = own[layer_idx]
    r.ff_down[0] = r.w_down[layer_idx]
    part = r.ff_near.shape[1]
    for source, base in ((r.ff_near, 0), (r.ff_far, 1)):
        for m in range(2):
            rows = pl.ds(pl.multiple_of((r.place[1] ^ (2 * m + base)) * part, part), part)
            for k in range(2):
                r.ff_gate_up[1, rows, k * width : (k + 1) * width] = source[3 * m + k]
            r.ff_down[1, rows, :] = source[3 * m + 2]


def start_all(copies):
    for copy in copies:
        copy.start()


def wait_all(sem, *buffers):
    for whole in buffers:
        pltpu.make_async_copy(whole, whole, sem).wait()


def lane_low(rows):
    return lax.broadcasted_iota(jnp.int32, (rows, 128), 1) < 64


def lane_halves():
    low = lane_low(1).astype(f32)
    return low.astype(bf16), (1.0 - low).astype(bf16)


def pair_blocks(rows, low, high):
    return jnp.concatenate([rows * low, rows * high], axis=0)


def own_blocks(both, is_low):
    half = both.shape[0] // 2
    return jnp.where(is_low, both[:half], both[half:]).astype(bf16)


def attention_forward(r, x_ref, a_ref, sizes, layer_idx):
    series, slots, inner = sizes
    rows = series * slots
    for part in chunks(rows, 256):
        r.qkv[part, :] = dot_nn(a_ref[part, :], r.attn_w[:, : 3 * inner]).astype(bf16)
    is_low = lane_low(slots)
    low, high = lane_halves()
    for s in range(series):
        here = slice(s * slots, (s + 1) * slots)
        keep = r.mask[here, :] == 1
        for start in range(0, inner, 128):
            at = slice(start, start + 128)
            query = r.qkv[here, at]
            keys = r.qkv[here, inner + start : inner + start + 128]
            scores = dot_nt(keys, pair_blocks(query, low, high)) + r.bias[:, at]
            scores = jnp.where(keep, scores, masked_score)
            exps = jnp.exp(scores - jnp.max(scores, axis=0, keepdims=True))
            r.probs[here, at] = exps / jnp.sum(exps, axis=0, keepdims=True)
    for s in range(series):
        here = slice(s * slots, (s + 1) * slots)
        for start in range(0, inner, 128):
            at = slice(start, start + 128)
            values = r.qkv[here, 2 * inner + start : 2 * inner + start + 128]
            both = dot_tn(r.probs[here, at].astype(bf16), values)
            r.heads[here, at] = own_blocks(both, is_low)
    gain = r.gain_ff[layer_idx : layer_idx + 1, :]
    for part in chunks(rows, 256):
        middle = x_ref[part, :] + dot_nt(r.heads[part, :], r.attn_w[:, 3 * inner :])
        r.middle[part, :] = middle
        r.ff_in[part, :] = (middle * inverse_rms(middle) * gain).astype(bf16)


def prepare_body(r):
    names = ("inputs", "valid", "keep", "embed", "gain_attn", "buckets")
    r.fetch(*names)
    r.need(*names)
    series, slots = r.valid.shape
    gain = r.gain_attn[0:1, :]
    valid = jnp.transpose(r.valid[...].astype(f32))
    keep = jnp.transpose(r.keep[...].astype(f32))
    for s in range(series):
        here = slice(s * slots, (s + 1) * slots)
        seen = valid[:, s : s + 1]
        x = jnp.where(seen == 1.0, r.inputs[here, :].astype(f32), r.embed[...])
        r.x[here, :] = x
        r.a[here, :] = (x * inverse_rms(x) * gain).astype(bf16)
        r.seen[here, :] = jnp.broadcast_to(seen, (slots, 128)).astype(jnp.int32)
        r.mask[here, :] = jnp.broadcast_to(keep[:, s : s + 1], (slots, 128)).astype(jnp.int32)
    turned = jnp.transpose(r.buckets[...].astype(f32)).astype(jnp.int32)
    wide = jnp.concatenate([turned, turned], axis=1)
    r.wide[...] = wide
    is_low = lane_low(slots)
    bucket_count, heads = r.table.shape
    for pair in range(heads // 2):
        bias = jnp.zeros((slots, 128), f32)
        for idx in range(bucket_count):
            entry = jnp.where(is_low, r.table[idx, 2 * pair], r.table[idx, 2 * pair + 1])
            bias = jnp.where(wide == idx, entry, bias)
        r.bias[:, pair * 128 : (pair + 1) * 128] = bias


def attention_body(r, sizes, masks, grain, layer_idx):
    r.fetch("gain_ff")
    lay_out_attention(r, masks, grain)
    r.need("gain_ff")
    attention_forward(r, r.x, r.a, sizes, layer_idx)


def ff_body(r):
    r.fetch("gain_attn")
    lay_out_ff(r, 0)
    r.need("gain_attn")
    width = r.middle.shape[1]
    for part in chunks(r.middle.shape[0], 256):
        x_next = r.middle[part, :]
        for half in range(2):
            both = dot_nn(r.ff_in[part, :], r.ff_gate_up[half])
            hidden = (gelu_terms(both[:, :width])[0] * both[:, width:]).astype(bf16)
            x_next = x_next + dot_nn(hidden, r.ff_down[half])
        r.x_next[part, :] = x_next
        r.a_next[part, :] = (x_next * inverse_rms(x_next) * r.gain_attn[1:2, :]).astype(bf16)


def ff_backward(r, layer_idx, last, masks):
    rows, width = r.middle.shape
    r.fetch("grad", "gain_ff")
    if last:
        lay_out_ff(r, layer_idx)
    r.need("grad", "gain_ff")
    gain_ff = r.gain_ff[layer_idx : layer_idx + 1, :]
    gain_total = jnp.zeros((1, width), f32)
    for part in chunks(rows, 256):
        grad = r.grad[part, :].astype(f32)
        rounded = grad.astype(bf16)
        ff_rows = r.ff_in[part, :]
        back = None
        middle = r.middle[part, :]
        total = middle
        for half in range(2):
            both = dot_nn(ff_rows, r.ff_gate_up[half])
            grad_hidden = dot_nt(rounded, r.ff_down[half])
            gate_act, up_act = both[:, :width], both[:, width:]
            mixed, slope = gelu_terms(gate_act)
            hidden = (mixed * up_act).astype(bf16)
            r.hidden[half, part, :] = hidden
            r.grad_gate_up[half, part, :width] = (grad_hidden * up_act * slope).astype(bf16)
            r.grad_gate_up[half, part, width:] = (grad_hidden * mixed).astype(bf16)
            pulled = r.grad_gate_up[half, part, :]
            if last:
                total = total + dot_nn(hidden, r.ff_down[half])
            term = dot_nt(pulled, r.ff_gate_up[half])
            back = term if back is None else back + term
        if last:
            r.outputs[part, :] = total.astype(bf16)
        grad_mid, gain_part = norm_back(middle, gain_ff, back)
        gain_total += gain_part
        grad_mid = grad + grad_mid
        r.grad_mid[part, :] = grad_mid
        r.branch[part, :] = grad_mid.astype(bf16)
        r.grad_low[part, :] = rounded
    if last:
        r.write("outputs")
    for half in range(2):
        r.ff_grad[half, :, : 2 * width] = dot_tn(r.ff_in[...], r.grad_gate_up[half])
        r.ff_grad[half, :, 2 * width :] = dot_tn(r.hidden[half], r.grad_low[...])
    half_count = len(masks[0]) // 2
    grain, columns = r.ff_keep.shape[1:]
    for side, side_masks in enumerate(masks):
        lanes = slice(side * columns, (side + 1) * columns)
        for idx, mask in enumerate(side_masks):
            target = r.ff_keep if idx < half_count else r.ff_send
            piece = pl.ds(pl.multiple_of((r.place[3] ^ (mask // 2)) * grain, grain), grain)
            target[side * half_count + idx % half_count] = r.ff_grad[mask % 2, piece, lanes].astype(
                bf16
            )
    if last:
        r.drain("outputs")
    return gain_total


def attention_backward(r, sizes, layer_idx, last, piece_masks, heads):
    series, slots, inner = sizes
    rows = series * slots
    width = r.x.shape[1]
    r.fetch("gain_attn")
    for part in chunks(rows, 256):
        r.grad_heads[part, :] = dot_nn(r.branch[part, :], r.attn_w[:, 3 * inner :]).astype(bf16)
    is_low = lane_low(slots)
    low, high = lane_halves()
    for start in range(0, inner, 128):
        at = slice(start, start + 128)
        bias_total = jnp.zeros((slots, 128), f32) if last else r.bias_before[:, at]
        for s in range(series):
            here = slice(s * slots, (s + 1) * slots)
            probs = r.probs[here, at]
            values = r.qkv[here, 2 * inner + start : 2 * inner + start + 128]
            grad_probs = dot_nt(values, pair_blocks(r.grad_heads[here, at], low, high))
            inner_sum = jnp.sum(probs * grad_probs, axis=0, keepdims=True)
            grad_scores = (probs * (grad_probs - inner_sum)).astype(bf16)
            r.grad_scores[here, at] = grad_scores
            bias_total = bias_total + grad_scores.astype(f32)
        r.bias_acc[:, at] = bias_total
    for s in range(series):
        here = slice(s * slots, (s + 1) * slots)
        for start in range(0, inner, 128):
            at = slice(start, start + 128)
            key_at = slice(inner + start, inner + start + 128)
            value_at = slice(2 * inner + start, 2 * inner + start + 128)
            grad_scores = r.grad_scores[here, at]
            r.grad_qkv[here, key_at] = dot_nn(
                grad_scores, pair_blocks(r.qkv[here, at], low, high)
            ).astype(bf16)
            r.grad_qkv[here, value_at] = dot_nn(
                r.probs[here, at].astype(bf16), pair_blocks(r.grad_heads[here, at], low, high)
            ).astype(bf16)
            r.grad_qkv[here, at] = own_blocks(dot_tn(grad_scores, r.qkv[here, key_at]), is_low)
    r.attn_grad[:, : 3 * inner] = dot_tn(r.a[...], r.grad_qkv[...])
    r.attn_grad[:, 3 * inner :] = dot_tn(r.branch[...], r.heads[...])
    scatter_pieces(r.attn_grad, r.attn_keep, r.attn_send, piece_masks, r.place[2])
    r.need("gain_attn")
    gain_attn = r.gain_attn[layer_idx : layer_idx + 1, :]
    gain_total = jnp.zeros((1, width), f32)
    embed_total = jnp.zeros((1, width), f32)
    for part in chunks(rows, 256):
        grad_normed = dot_nt(r.grad_qkv[part, :], r.attn_w[:, : 3 * inner])
        grad_in, gain_part = norm_back(r.x[part, :], gain_attn, grad_normed)
        gain_total += gain_part
        grad_in = r.grad_mid[part, :] + grad_in
        if last:
            r.grad_next[part, :] = grad_in
        else:
            seen = r.seen[part, 0:1] == 1
            r.grad_next[part, :] = jnp.where(seen, grad_in, 0.0)
            embed_total += jnp.sum(jnp.where(seen, 0.0, grad_in), axis=0, keepdims=True)
    r.write("grad_next")
    if not last:
        put_row(r.small, 4, embed_total)
        head_size = inner // heads
        for idx in range(r.table_rows.shape[0]):
            for start in range(0, inner, 128):
                at = slice(start, start + 128)
                chosen = jnp.where(r.wide[...] == idx, r.bias_acc[:, at], 0.0)
                r.table_rows[idx : idx + 1, at] = jnp.sum(chosen, axis=0, keepdims=True)
        lane = lax.broadcasted_iota(jnp.int32, (r.table_rows.shape[0], 128), 1)
        table = jnp.zeros(lane.shape, f32)
        for head in range(heads):
            cut = r.table_rows[:, head * head_size : (head + 1) * head_size]
            table = jnp.where(lane == head, jnp.sum(cut, axis=1, keepdims=True), table)
        r.small[:heads, : table.shape[0]] = jnp.transpose(table)[:heads, :]
    r.drain("grad_next")
    return gain_total


def two_parts(values):
    high = values.astype(bf16).astype(f32)
    return high, (values - high).astype(bf16).astype(f32)


def last_ff_body(r, masks):
    r.small[...] = jnp.zeros(r.small.shape, f32)
    put_row(r.small, 3, ff_backward(r, 1, True, masks))


def last_attention_body(r, sizes, piece_masks, heads):
    r.small[...] = r.small_before[...]
    put_row(r.small, 1, attention_backward(r, sizes, 1, True, piece_masks, heads))


def ff_backward_body(r, masks):
    r.small[...] = r.small_before[...]
    put_row(r.small, 2, ff_backward(r, 0, False, masks))


def attention_backward_body(r, sizes, piece_masks, heads):
    r.small[...] = r.small_before[...]
    put_row(r.small, 0, attention_backward(r, sizes, 0, False, piece_masks, heads))
    high, low = two_parts(r.small[...])
    last = r.attn_send.shape[0] - 1
    r.attn_send[last] = jnp.concatenate([high, low], axis=0).astype(bf16)
    r.small[...] = high + low


def put_row(packed, which, row):
    first, width = packed.shape[0] - 2, row.shape[1]
    at = which % 3 * width
    packed[first + which // 3 : first + which // 3 + 1, at : at + width] = row


def scatter_pieces(whole, keep, send, masks, place):
    count = len(masks)
    grain = whole.shape[0] // count
    for idx, mask in enumerate(masks):
        target = keep if idx < count // 2 else send
        source = pl.ds(pl.multiple_of((place ^ mask) * grain, grain), grain)
        target[idx % (count // 2)] = whole[source, :].astype(bf16)


def finish(parts, layer_idx, place, shape, before=()):
    width = shape[-1]
    grain, columns = parts[0][0].shape[1:]
    count = len(before)

    def kernel(place_ref, *refs):
        sources = refs[: len(parts)]
        refs = refs[len(parts) + count :]
        outs, stages, out_sem = refs[:3], refs[3:-1], refs[-1]
        for source, stage, (_, masks, side) in zip(sources, stages, parts):
            for idx, mask in enumerate(masks):
                stage[idx] = source[idx].astype(f32)
                at = idx // (len(masks) // 2) if side is None else side
                rows = pl.ds(pl.multiple_of((place_ref[3] ^ (mask // 2)) * grain, grain), grain)
                for k, out in enumerate(outs):
                    low = max(at * columns, k * width)
                    size = min((at + 1) * columns, (k + 1) * width) - low
                    if size > 0:
                        pltpu.make_async_copy(
                            stage.at[idx, :, pl.ds(low - at * columns, size)],
                            out.at[layer_idx, rows, pl.ds(low - k * width, size)],
                            out_sem,
                        ).start()
        for stage in stages:
            pltpu.make_async_copy(stage, stage, out_sem).wait()

    arrays = [pltpu.with_memory_space_constraint(array, pltpu.VMEM) for array, _, _ in parts]
    return pl.pallas_call(
        kernel,
        name="layer_%d_ff_grads" % layer_idx,
        in_specs=[pl.BlockSpec(memory_space=pltpu.SMEM)]
        + [pl.BlockSpec(memory_space=pltpu.VMEM)] * len(parts)
        + [pl.BlockSpec(memory_space=pl.ANY)] * count,
        out_specs=[pl.BlockSpec(memory_space=pl.ANY)] * 3,
        out_shape=[jax.ShapeDtypeStruct(shape, f32)] * 3,
        input_output_aliases={1 + len(parts) + k: k for k in range(count)},
        scratch_shapes=[pltpu.VMEM(array.shape, f32) for array, _, _ in parts]
        + [pltpu.SemaphoreType.DMA],
        compiler_params=pltpu.CompilerParams(vmem_limit_bytes=6 * mebibyte),
        cost_estimate=cost(2),
    )(place, *arrays, *before)


def small_body(r):
    width = r.embed.shape[1]
    heads = r.table.shape[0]
    outs = ((r.gain_attn, 0), (r.gain_attn, 1), (r.gain_ff, 0), (r.gain_ff, 1), (r.embed, 0))
    for which, (out, row) in enumerate(outs):
        first = r.packed.shape[0] - 2 + which // 3
        at = which % 3 * width
        out[row : row + 1, :] = r.packed[first : first + 1, at : at + width]
    r.table[...] = r.packed[:heads, : r.table.shape[1]]
    r.write("gain_attn", "gain_ff", "embed", "table")
    r.drain("gain_attn", "gain_ff", "embed", "table")


def pack_body(r, packs):
    rows = r.quarter_0.shape[1]
    at = pl.ds(pl.multiple_of(r.place[1] * rows, rows), rows)
    copies = []
    outs = [r.quarter_0, r.quarter_1]
    for layer_idx in range(2):
        for k, w in enumerate((r.w_gate, r.w_up, r.w_down)):
            copies.append((w.at[layer_idx, at], outs[layer_idx].at[k]))
    if packs:
        outs += [r.block_0, r.block_1]
        inner = r.w_query.shape[2]
        for layer_idx in range(2):
            for k, w in enumerate((r.w_query, r.w_key, r.w_value, r.w_out)):
                lanes = pl.ds(k * inner, inner)
                copies.append((w.at[layer_idx], outs[2 + layer_idx].at[:, lanes]))
    start_all([pltpu.make_async_copy(*ends, r.pack_sem) for ends in copies])
    wait_all(r.pack_sem, *outs)


def order_masks(hops):
    masks = [0]
    for hop in reversed(hops):
        masks = masks + [mask ^ hop for mask in masks]
    return masks


def tie(value, *others):
    return lax.optimization_barrier((value, *others))[0]


def on_device(
    inputs,
    cotangent,
    attention_mask,
    patch_valid,
    buckets,
    mask_embed,
    w_query,
    w_key,
    w_value,
    w_output,
    w_gate,
    w_up,
    w_down,
    gain_attn,
    gain_ff,
    bias_table,
    dp_size,
):
    series, slots, width = inputs.shape
    heads = bias_table.shape[1]
    inner = w_query.shape[2]
    rows = series * slots
    sizes = (series, slots, inner)
    matrix = (rows, width)
    devices = 2 * dp_size
    dp_at = lax.axis_index("dp")
    device_at = 2 * dp_at + lax.axis_index("tensor")
    cotangent = cotangent.reshape(matrix)

    def swap(array, mask):
        return lax.ppermute(array, axes, [(n, n ^ mask) for n in range(devices)])

    def join(left, right):
        return jnp.concatenate([left, right], axis=0)

    bits = [1 << k for k in range(devices.bit_length() - 1)]

    attn_grain = max(16, width // devices)
    attn_count = width // attn_grain
    ff_grain = max(16, width // dp_size)
    ff_count = width // ff_grain
    quarter_at = lax.rem(dp_at, 4)
    place = jnp.stack(
        [
            device_at,
            quarter_at,
            device_at // (devices // attn_count),
            lax.rem(dp_at, ff_count),
        ]
    ).astype(jnp.int32)

    quarter = width // 4
    own_rows = w_query.shape[1]
    direct = own_rows % 16 == 0
    w_out = jnp.swapaxes(w_output, 1, 2)
    sources = dict(w_gate=w_gate, w_up=w_up, w_down=w_down)
    block_outs = {}
    if direct:
        sources |= dict(w_query=w_query, w_key=w_key, w_value=w_value, w_out=w_out)
        block_outs = {"block_%d" % k: Kept((own_rows, 4 * inner), bf16) for k in range(2)}
    packed = run(
        functools.partial(pack_body, packs=direct),
        "pack",
        dict(
            place=place,
            **{n: pltpu.with_memory_space_constraint(w, pltpu.HBM) for n, w in sources.items()},
        ),
        dict(
            quarter_0=Kept((3, quarter, width), bf16),
            quarter_1=Kept((3, quarter, width), bf16),
            **block_outs,
        ),
        dict(pack_sem=pltpu.SemaphoreType.DMA),
        vmem=4,
    )
    far = bits[2:]

    def prepare(token):
        return run(
            prepare_body,
            "prepare",
            dict(
                inputs=tie(inputs, token).reshape(matrix),
                valid=patch_valid,
                keep=attention_mask,
                embed=mask_embed[None, :],
                gain_attn=gain_attn,
                buckets=buckets,
                table=bias_table,
            ),
            dict(
                x=Kept(matrix, f32),
                a=Kept(matrix, bf16),
                bias=Kept((slots, heads * slots), f32),
                mask=Kept((rows, 128), jnp.int32),
                seen=Kept((rows, 128), jnp.int32),
                wide=Kept((slots, 128), jnp.int32),
            ),
            {},
            micros=3,
        )

    if direct:
        hops_0 = [1] + far[2:] + far[:2] + [2]
        hops_1 = far[2:] + far[:2] + [1, 2]
        block_0, block_1 = packed.block_0, packed.block_1
        got_1 = swap(block_1, hops_1[0])
        got_0 = swap(block_0, hops_0[0])
        ff_0 = swap(tie(packed.quarter_0, got_0), 1)
        ff_1 = swap(tie(packed.quarter_1, ff_0), 1)
        got_ff_0 = swap(ff_0, 4)
        block_0 = join(block_0, got_0)
        block_1 = join(block_1, tie(got_1, block_0))
        for hop_0, hop_1 in zip(hops_0[1:-2], hops_1[1:-2]):
            got_1, got_0 = swap(block_1, hop_1), swap(block_0, hop_0)
            if hop_0 == hops_0[1]:
                start = prepare(block_1)
                got_0 = tie(got_0, ff_0)
            block_0 = join(block_0, got_0)
            block_1 = join(block_1, tie(got_1, block_0))
        block_0 = tie(block_0, block_1)
        got_0 = swap(block_0, hops_0[-2])
        got_1 = swap(block_1, hops_1[-2])
        block_0 = join(block_0, tie(got_0, start.a, got_ff_0, ff_1, got_1))
        ff_0 = join(ff_0, tie(got_ff_0, block_0))
        got_ff_1 = swap(tie(ff_1, ff_0), 4)
        attn_pieces = [(block_0, swap(block_0, 2), order_masks(hops_0[::-1]))]
    else:
        ff_0, ff_1 = swap(packed.quarter_0, 1), swap(packed.quarter_1, 1)
        ff_0 = join(ff_0, swap(ff_0, 4))
        start = prepare(ff_0)
        attn_pieces = []
        rows_of = jnp.concatenate([w_query, w_key, w_value, w_out], axis=2)
        for layer_idx in range(2):
            whole = lax.all_gather(rows_of[layer_idx], axes, axis=0, tiled=True)
            attn_pieces.append((whole, whole, [0]))
    ff_pieces = [(ff_0, swap(ff_0, 2))]

    def attn_ins(layer_idx):
        near, far, masks = attn_pieces[layer_idx]
        return dict(attn_near=Kept(near), attn_far=Kept(far)), masks

    def ff_ins(layer_idx):
        near, far = ff_pieces[layer_idx]
        own = keep_all(dict(w_gate=w_gate, w_up=w_up, w_down=w_down))
        return dict(**own, ff_near=Kept(near), ff_far=Kept(far))

    ff_outs = dict(
        ff_gate_up=Kept((2, width, 2 * width), bf16), ff_down=Kept((2, width, width), bf16)
    )
    grain = own_rows if direct else width
    attn_outs = dict(
        attn_w=Kept((width, 4 * inner), bf16),
        qkv=Kept((rows, 3 * inner), bf16),
        probs=Kept((rows, heads * slots), f32),
        heads=Kept((rows, inner), bf16),
        middle=Kept(matrix, f32),
        ff_in=Kept(matrix, bf16),
    )

    def attention(layer_idx, x, a, after=(), micros=5):
        pieces, masks = attn_ins(layer_idx)
        return run(
            functools.partial(
                attention_body, sizes=sizes, masks=masks, grain=grain, layer_idx=layer_idx
            ),
            "layer_%d_attention" % layer_idx,
            dict(
                place=place,
                x=Kept(x),
                a=Kept(a),
                bias=Kept(start.bias),
                mask=Kept(start.mask),
                gain_ff=gain_ff,
                **pieces,
            ),
            attn_outs,
            {},
            after=after,
            micros=micros,
        )

    first = attention(0, start.x, start.a, micros=10)
    if direct:
        block_1 = join(block_1, tie(got_1, first.ff_in))
        attn_pieces.append((block_1, swap(block_1, 2), order_masks(hops_1[::-1])))
    first_ff = run(
        ff_body,
        "layer_0_ff",
        dict(
            place=place,
            middle=Kept(first.middle),
            ff_in=Kept(first.ff_in),
            gain_attn=gain_attn,
            **ff_ins(0),
        ),
        dict(**ff_outs, x_next=Kept(matrix, f32), a_next=Kept(matrix, bf16)),
        {},
        after=(block_1,) if direct else (),
        micros=3,
    )
    if direct:
        ff_1 = join(ff_1, tie(got_ff_1, first_ff.x_next))
    else:
        ff_1 = join(ff_1, swap(ff_1, 4))
    ff_pieces.append((ff_1, swap(ff_1, 2)))
    second = attention(1, first_ff.x_next, first_ff.a_next, micros=0.1)

    attn_low = devices // attn_count
    attn_hops = ([2, 1] + bits[2:], [2] + bits[3:4] + bits[2:3] + bits[4:] + [1])
    attn_split = [[hop for hop in hops if hop >= attn_low] for hops in attn_hops]
    attn_whole = [hop for hop in bits if hop < attn_low]
    attn_masks = [[mask // attn_low for mask in order_masks(hops)] for hops in attn_split]
    ff_hops = ([2, 4, 1] + bits[3:], [2, 1, 4] + bits[3:])
    ff_split = [[hop for hop in hops if hop // 2 < ff_count] for hops in ff_hops]
    ff_whole = [hop for hop in bits[1:] if hop // 2 >= ff_count]
    ff_share = [hop for hop in bits[:0:-1] if hop // 2 < ff_count]
    ff_masks = [order_masks(hops) for hops in ff_split]
    attn_half = (attn_count // 2, attn_grain, 4 * inner)
    small_shape = (heads + 2, 3 * width)

    attn_back_outs = dict(attn_keep=Kept(attn_half, bf16), attn_send=Kept(attn_half, bf16))
    attn_back_scratch = dict(
        grad_heads=pltpu.VMEM((rows, inner), bf16),
        grad_qkv=pltpu.VMEM((rows, 3 * inner), bf16),
        grad_scores=pltpu.VMEM((rows, heads * slots), bf16),
        attn_grad=pltpu.VMEM((width, 4 * inner), f32),
    )
    ff_back_outs = dict(
        ff_keep=Kept((2 * ff_count, ff_grain, 3 * width // 2), bf16),
        ff_send=Kept((2 * ff_count, ff_grain, 3 * width // 2), bf16),
        small=Kept(small_shape, f32),
        grad_mid=Kept(matrix, f32),
        branch=Kept(matrix, bf16),
    )
    ff_back_scratch = dict(
        hidden=pltpu.VMEM((2, rows, width), bf16),
        grad_gate_up=pltpu.VMEM((2, rows, 2 * width), bf16),
        ff_grad=pltpu.VMEM((2, width, 3 * width), f32),
        grad_low=pltpu.VMEM(matrix, bf16),
    )
    bias_shape = (slots, heads * slots)

    def attn_back_ins(kept, x, a):
        return dict(
            x=Kept(x),
            a=Kept(a),
            gain_attn=gain_attn,
            attn_w=Kept(kept.attn_w),
            qkv=Kept(kept.qkv),
            probs=Kept(kept.probs),
            heads=Kept(kept.heads),
        )

    def add(left, right):
        return (left.astype(f32) + right.astype(f32)).astype(bf16)

    def halving(keep, send, hops, out):
        for step, hop in enumerate(hops):
            got = yield swap(send, hop)
            if step + 1 < len(hops):
                cut = keep.shape[0] // 2
                send = add(keep[cut:], got[cut:])
                keep = add(keep[:cut], got[:cut])
                out["token"] = send
            else:
                out["token"] = keep = add(keep, got)
        out["piece"] = keep

    def summing(piece, hops, out):
        for hop in hops:
            got = yield swap(piece, hop)
            out["token"] = piece = add(piece, got)
        out["piece"] = piece

    def apart(both, masks):
        return [(both, masks[0] + masks[1], None)]

    def sharing(piece, out):
        columns = piece.shape[2] // 2
        halves = [piece[:, :, :columns], piece[:, :, columns:]]
        masks = [[0], [0]]
        others = ff_share[:-1]
        orders = (others, others[-1:] + others[:-1])
        for step, hops in enumerate(zip(*orders)):
            sent = tuple(swap(half, hop) for half, hop in zip(halves, hops))
            new_masks = [[m ^ hop for m in side] for side, hop in zip(masks, hops)]
            if step + 1 < len(others):
                got = yield sent
                halves = [join(half, one) for half, one in zip(halves, got)]
                masks = [side + new for side, new in zip(masks, new_masks)]
                out["token"] = tuple(halves)
        got = yield swap(join(*halves), 2)
        crossed = [[m ^ 2 for m in side] for side in masks]
        out["early"] = [*zip(halves, masks, (0, 1)), *apart(got, crossed)]
        out["token"] = got
        got = yield sent
        out["near"] = [*zip(got, new_masks, (0, 1))]
        out["token"] = got
        got = yield swap(join(*got), 2)
        out["far"] = apart(got, [[m ^ 2 for m in side] for side in new_masks])
        out["token"] = got

    def rounded(values):
        return lax.reduce_precision(values, exponent_bits=8, mantissa_bits=7)

    def with_small(pieces, small):
        high = rounded(small)
        low = rounded(small - high)
        parts = join(high, low).astype(bf16)[None]
        return join(pieces, parts), high + low

    def add_small(small, got):
        parts = got[-1].astype(f32)
        return small + (parts[: small.shape[0]] + parts[small.shape[0] :])

    def attn_chain(part, layer_idx, out):
        small = part.small if layer_idx == 0 else None
        keep, send = part.attn_keep, part.attn_send
        hops = attn_split[layer_idx] + attn_whole
        for step, hop in enumerate(hops):
            got = yield swap(send, hop)
            if small is not None:
                small = add_small(small, got)
                got = got[:-1]
            if step + 1 < len(attn_split[layer_idx]):
                half = keep.shape[0] // 2
                send = add(keep[half:], got[half:])
                keep = add(keep[:half], got[:half])
            else:
                send = keep = add(keep, got)
            if small is not None and step + 1 < len(hops):
                send, small = with_small(send, small)
            out["token"] = send
            if layer_idx == 1 and step == 0:
                send = tie(send, *(yield None))
        piece = keep[0]
        if own_rows < attn_grain:
            first_row = lax.rem(device_at, attn_low) * own_rows
            piece = lax.dynamic_slice_in_dim(piece, first_row, own_rows, axis=0)
        out["done"] = piece.astype(f32)
        out["small"] = small

    def ff_chain(part, out):
        got = yield swap(part.ff_send, 2)
        count = ff_count
        keeps, sends = [], []
        for side in range(2):
            at, half = side * count, count // 2
            sends.append(add(part.ff_keep[at + half : at + count], got[at + half : at + count]))
            keeps.append(add(part.ff_keep[at : at + half], got[at : at + half]))
        out["token"] = tuple(sends)
        for hops in zip(ff_split[0][1:3], ff_split[1][1:3]):
            got = yield tuple(swap(send, hop) for send, hop in zip(sends, hops))
            half = keeps[0].shape[0] // 2
            sends = [add(keep[half:], one[half:]) for keep, one in zip(keeps, got)]
            keeps = [add(keep[:half], one[:half]) for keep, one in zip(keeps, got)]
            out["token"] = tuple(sends)
        keep, send = (jnp.concatenate(sides, axis=2) for sides in (keeps, sends))
        yield from halving(keep, send, ff_split[0][3:], out)
        yield from summing(out["piece"], ff_whole, out)
        yield from sharing(out["piece"], out)

    class Chain:
        def __init__(self, steps, *args):
            self.out = {}
            self.steps = steps(*args, self.out)
            self.arriving = next(self.steps)

        def resume(self, *tokens):
            self.arriving = self.steps.send(tokens)

        def step(self, token, *others):
            if self.arriving is not None:
                tokens = (*(token if isinstance(token, tuple) else (token,)), *others)
                many = isinstance(self.arriving, tuple)
                arrived = self.arriving if many else (self.arriving,)
                arrived = lax.optimization_barrier((*arrived, *tokens))[: len(arrived)]
                arrived = arrived if many else arrived[0]
                self.arriving = None
                try:
                    self.arriving = self.steps.send(arrived)
                except StopIteration:
                    pass
                return self.out["token"]
            return token

    back_ff_1 = run(
        functools.partial(last_ff_body, masks=ff_masks),
        "layer_1_ff",
        dict(
            place=place,
            grad=cotangent,
            gain_ff=gain_ff,
            middle=Kept(second.middle),
            ff_in=Kept(second.ff_in),
            **ff_ins(1),
        ),
        dict(**ff_back_outs, outputs=(matrix, bf16)),
        dict(
            ff_gate_up=pltpu.VMEM((2, width, 2 * width), bf16),
            ff_down=pltpu.VMEM((2, width, width), bf16),
            **ff_back_scratch,
        ),
        micros=8,
        vmem=24,
    )
    ff_1 = Chain(ff_chain, back_ff_1)
    back_1 = run(
        functools.partial(
            last_attention_body, sizes=sizes, piece_masks=attn_masks[1], heads=heads
        ),
        "layer_1_attention_backward",
        dict(
            place=place,
            small_before=Kept(back_ff_1.small),
            grad_mid=Kept(back_ff_1.grad_mid),
            branch=Kept(back_ff_1.branch),
            **attn_back_ins(second, first_ff.x_next, first_ff.a_next),
        ),
        dict(
            **attn_back_outs,
            small=Kept(small_shape, f32),
            grad_next=Kept(matrix, f32),
            bias_acc=Kept(bias_shape, f32),
        ),
        attn_back_scratch,
        micros=6,
        vmem=14,
    )
    attn_1 = Chain(attn_chain, back_1, 1)
    token = ff_1.step(back_1.attn_send)
    token = (attn_1.step(token),)
    back_0 = run(
        functools.partial(ff_backward_body, masks=ff_masks),
        "layer_0_ff_backward",
        dict(
            place=place,
            grad=Kept(back_1.grad_next),
            gain_ff=gain_ff,
            small_before=Kept(back_1.small),
            middle=Kept(first.middle),
            ff_in=Kept(first.ff_in),
            ff_gate_up=Kept(first_ff.ff_gate_up),
            ff_down=Kept(first_ff.ff_down),
        ),
        ff_back_outs,
        ff_back_scratch,
        after=token,
        micros=8,
        vmem=20,
    )
    token = ff_1.step(back_0.branch)
    back_0.ff_send = tie(back_0.ff_send, *token)
    ff_0 = Chain(ff_chain, back_0)
    token = ff_0.step(token)
    back_attn_0 = run(
        functools.partial(
            attention_backward_body, sizes=sizes, piece_masks=attn_masks[0], heads=heads
        ),
        "layer_0_attention_backward",
        dict(
            place=place,
            bias_before=Kept(back_1.bias_acc),
            seen=Kept(start.seen),
            wide=Kept(start.wide),
            small_before=Kept(back_0.small),
            grad_mid=Kept(back_0.grad_mid),
            branch=Kept(back_0.branch),
            **attn_back_ins(first, start.x, start.a),
        ),
        dict(
            attn_keep=Kept(attn_half, bf16),
            attn_send=Kept((attn_count // 2 + 1, *attn_half[1:]), bf16),
            small=Kept(small_shape, f32),
            grad_next=(matrix, f32),
        ),
        dict(
            bias_acc=pltpu.VMEM(bias_shape, f32),
            table_rows=pltpu.VMEM((bias_table.shape[0], heads * slots), f32),
            **attn_back_scratch,
        ),
        after=token,
        micros=7,
        vmem=14,
    )
    attn_0 = Chain(attn_chain, back_attn_0, 0)
    attn_1.resume(back_attn_0.attn_send)
    token = back_attn_0.attn_send
    shape = (2, width, width)
    done = ()
    written = set()

    def write(chain, layer_idx, key, token):
        nonlocal done
        if key not in chain.out or (layer_idx, key) in written:
            return token
        written.add((layer_idx, key))
        parts = chain.out[key]
        tokens = token if isinstance(token, tuple) else (token,)
        arrays = lax.optimization_barrier((*(part[0] for part in parts), *tokens))
        parts = [(array, *part[1:]) for array, part in zip(arrays, parts)]
        done = finish(parts, layer_idx, place, shape, done)
        return done[0]

    turn = 0
    sums = attn_grads = None
    while ff_0.arriving is not None:
        turn += 1
        last_of_1 = "near" in ff_1.out
        if not last_of_1:
            token = ff_1.step(token)
        for chain, layer_idx, key in ((ff_1, 1, "near"), (ff_0, 0, "near")):
            token = write(chain, layer_idx, key, token)
        token = ff_0.step(token)
        if last_of_1:
            token = ff_1.step(token)
        for chain, layer_idx, key in (
            (ff_1, 1, "early"),
            (ff_0, 0, "early"),
            (ff_1, 1, "far"),
            (ff_0, 0, "far"),
        ):
            token = write(chain, layer_idx, key, token)
        if turn != 2:
            token = attn_0.step(token)
        if turn > 2:
            token = attn_1.step(token)
        if sums is None and attn_0.arriving is None:
            sums = run(
                small_body,
                "small_sums",
                dict(packed=Kept(tie(attn_0.out["small"], token))),
                dict(
                    gain_attn=((2, width), f32),
                    gain_ff=((2, width), f32),
                    embed=((1, width), f32),
                    table=(bias_table.shape[::-1], f32),
                ),
                {},
            )
            token = sums.embed
        if attn_grads is None and attn_0.arriving is None and attn_1.arriving is None:
            both = jnp.stack([attn_0.out["done"], tie(attn_1.out["done"], token)])
            attn_grads = [both[:, :, k * inner : (k + 1) * inner] for k in range(4)]
            attn_grads[3] = jnp.swapaxes(attn_grads[3], 1, 2)
            token = tuple(attn_grads)
    return (
        back_ff_1.outputs.reshape(inputs.shape),
        back_attn_0.grad_next.reshape(inputs.shape),
        *attn_grads,
        *done,
        sums.gain_attn,
        sums.gain_ff,
        sums.table.T,
        sums.embed[0],
    )


def solution(mesh):
    placed = (
        P(("dp", "tensor"), None, None),
        P(("dp", "tensor"), None, None),
        P(("dp", "tensor"), None),
        P(("dp", "tensor"), None),
        P(),
        P(),
        P(None, ("dp", "tensor"), None),
        P(None, ("dp", "tensor"), None),
        P(None, ("dp", "tensor"), None),
        P(None, None, ("dp", "tensor")),
        P(None, None, "tensor"),
        P(None, None, "tensor"),
        P(None, "tensor", None),
        P(),
        P(),
        P(),
    )
    return jax.shard_map(
        functools.partial(on_device, dp_size=mesh.shape["dp"]),
        mesh=mesh,
        in_specs=placed,
        out_specs=(
            P(("dp", "tensor"), None, None),
            P(("dp", "tensor"), None, None),
            P(None, ("dp", "tensor"), None),
            P(None, ("dp", "tensor"), None),
            P(None, ("dp", "tensor"), None),
            P(None, None, ("dp", "tensor")),
            P(None, None, "tensor"),
            P(None, None, "tensor"),
            P(None, "tensor", None),
            P(),
            P(),
            P(),
            P(),
        ),
        check_vma=False,
    )
```

```python
import functools
import types

import jax
import jax.numpy as jnp
from jax import lax
from jax.experimental import pallas as pl
from jax.experimental.pallas import tpu as pltpu
from jax.sharding import PartitionSpec as P

norm_eps = 1e-06
masked_score = -1e30
bf16 = jnp.bfloat16
f32 = jnp.float32
axes = ("dp", "tensor")
mebibyte = 1024 * 1024
raw_names = ("w_query", "w_key", "w_value", "w_out", "w_gate", "w_up", "w_down")
scalar_names = ("place", "table")


def dot_nn(left, right):
    return lax.dot_general(left, right, (((1,), (0,)), ((), ())), preferred_element_type=f32)


def dot_nt(left, right):
    return lax.dot_general(left, right, (((1,), (1,)), ((), ())), preferred_element_type=f32)


def dot_tn(left, right):
    return lax.dot_general(left, right, (((0,), (0,)), ((), ())), preferred_element_type=f32)


def inverse_rms(values):
    return lax.rsqrt(jnp.mean(values * values, axis=-1, keepdims=True) + norm_eps)


def norm_back(values, gain, grad_out):
    scale = inverse_rms(values)
    pulled = grad_out * gain
    mean_part = jnp.mean(pulled * values, axis=-1, keepdims=True)
    grad_in = scale * pulled - values * (scale * scale * scale) * mean_part
    return grad_in, jnp.sum(grad_out * values * scale, axis=0, keepdims=True)


def gelu_terms(gate_act):
    square = gate_act * gate_act
    bent = jnp.tanh(0.7978845608028654 * gate_act * (1.0 + 0.044715 * square))
    half = 0.5 * (1.0 + bent)
    slope = half + 0.5 * gate_act * (1.0 - bent * bent) * (
        0.7978845608028654 * (1.0 + 3.0 * 0.044715 * square)
    )
    return gate_act * half, slope


def cost(micros):
    return pl.CostEstimate(flops=int(micros * 1.15e9), bytes_accessed=0, transcendentals=0)


def run(body, name, ins, outs, scratch, after=(), micros=1, vmem=8):
    in_names, out_names, scratch_names = list(ins), list(outs), list(scratch)
    direct = {n for n in in_names if n in scalar_names + raw_names or isinstance(ins[n], Kept)}
    staged = [n for n in in_names if n not in direct]
    copied = [n for n in out_names if not isinstance(outs[n], Kept)]
    in_sems = {n: i for i, n in enumerate(staged)}
    out_sems = {n: i for i, n in enumerate(copied)}

    def kernel(*refs):
        refs = list(refs)
        sources = dict(zip(in_names, refs))
        refs = refs[len(in_names) + len(after) :]
        targets = dict(zip(out_names, refs))
        refs = refs[len(out_names) :]
        space = dict(zip(scratch_names, refs))
        refs = refs[len(scratch_names) :]
        buffers = dict(zip(staged + copied, refs))
        sems_in, sems_out = refs[len(staged) + len(copied) :]
        kept = {n: ref for n, ref in targets.items() if n not in out_sems}
        r = types.SimpleNamespace(**space, **buffers, **kept)
        for n in direct:
            setattr(r, n, sources[n])

        def copy_in(n):
            return pltpu.make_async_copy(sources[n], buffers[n], sems_in.at[in_sems[n]])

        def copy_out(n):
            return pltpu.make_async_copy(buffers[n], targets[n], sems_out.at[out_sems[n]])

        r.fetch = lambda *names: [copy_in(n).start() for n in names if n in in_sems]
        r.need = lambda *names: [copy_in(n).wait() for n in names if n in in_sems]
        r.write = lambda *names: [copy_out(n).start() for n in names if n in out_sems]
        r.drain = lambda *names: [copy_out(n).wait() for n in names if n in out_sems]
        body(r)

    def in_space(n):
        if n in scalar_names:
            return pltpu.SMEM
        return pltpu.VMEM if isinstance(ins[n], Kept) else pl.ANY

    results = pl.pallas_call(
        kernel,
        name=name,
        in_specs=[pl.BlockSpec(memory_space=in_space(n)) for n in in_names]
        + [pl.BlockSpec(memory_space=pl.ANY) for _ in after],
        out_specs=[
            pl.BlockSpec(memory_space=pltpu.VMEM if isinstance(out, Kept) else pl.ANY)
            for out in outs.values()
        ],
        out_shape=[
            pltpu.VMEM(*out.what) if isinstance(out, Kept) else jax.ShapeDtypeStruct(*out)
            for out in outs.values()
        ],
        scratch_shapes=list(scratch.values())
        + [pltpu.VMEM(ins[n].shape, ins[n].dtype) for n in staged]
        + [pltpu.VMEM(*outs[n]) for n in copied]
        + [
            pltpu.SemaphoreType.DMA((max(1, len(staged)),)),
            pltpu.SemaphoreType.DMA((max(1, len(copied)),)),
        ],
        compiler_params=pltpu.CompilerParams(vmem_limit_bytes=vmem * mebibyte),
        cost_estimate=cost(micros),
    )(
        *[
            pltpu.with_memory_space_constraint(value.what, pltpu.VMEM)
            if isinstance(value, Kept)
            else value
            for value in ins.values()
        ],
        *after,
    )
    return types.SimpleNamespace(**dict(zip(outs, results)))


class Kept:
    def __init__(self, *what):
        self.what = what[0] if len(what) == 1 else what


def keep_all(names):
    return {name: Kept(value) for name, value in names.items()}


def chunks(extent, size):
    size = min(size, extent)
    return [slice(start, start + size) for start in range(0, extent, size)]


def lay_out_attention(r, masks, rows):
    for idx, mask in enumerate(masks):
        half, at = divmod(idx, max(1, len(masks) // 2))
        source = r.attn_near if half == 0 else r.attn_far
        place = pl.multiple_of((r.place[0] ^ mask) * rows, rows) if len(masks) > 1 else 0
        r.attn_w[pl.ds(place, rows), :] = source[at * rows : (at + 1) * rows, :]


def lay_out_ff(r, layer_idx):
    width = r.ff_down.shape[-1]
    for k, own in enumerate((r.w_gate, r.w_up)):
        r.ff_gate_up[0, :, k * width : (k + 1) * width] = own[layer_idx]
    r.ff_down[0] = r.w_down[layer_idx]
    part = r.ff_near.shape[1]
    for source, base in ((r.ff_near, 0), (r.ff_far, 1)):
        for m in range(2):
            rows = pl.ds(pl.multiple_of((r.place[1] ^ (2 * m + base)) * part, part), part)
            for k in range(2):
                r.ff_gate_up[1, rows, k * width : (k + 1) * width] = source[3 * m + k]
            r.ff_down[1, rows, :] = source[3 * m + 2]


def start_all(copies):
    for copy in copies:
        copy.start()


def wait_all(sem, *buffers):
    for whole in buffers:
        pltpu.make_async_copy(whole, whole, sem).wait()


def lane_low(rows):
    return lax.broadcasted_iota(jnp.int32, (rows, 128), 1) < 64


def lane_halves():
    low = lane_low(1).astype(f32)
    return low.astype(bf16), (1.0 - low).astype(bf16)


def pair_blocks(rows, low, high):
    return jnp.concatenate([rows * low, rows * high], axis=0)


def own_blocks(both, is_low):
    half = both.shape[0] // 2
    return jnp.where(is_low, both[:half], both[half:]).astype(bf16)


def attention_forward(r, x_ref, a_ref, sizes, layer_idx):
    series, slots, inner = sizes
    rows = series * slots
    for part in chunks(rows, 256):
        r.qkv[part, :] = dot_nn(a_ref[part, :], r.attn_w[:, : 3 * inner]).astype(bf16)
    is_low = lane_low(slots)
    low, high = lane_halves()
    for s in range(series):
        here = slice(s * slots, (s + 1) * slots)
        keep = r.mask[here, :] == 1
        for start in range(0, inner, 128):
            at = slice(start, start + 128)
            query = r.qkv[here, at]
            keys = r.qkv[here, inner + start : inner + start + 128]
            scores = dot_nt(keys, pair_blocks(query, low, high)) + r.bias[:, at]
            scores = jnp.where(keep, scores, masked_score)
            exps = jnp.exp(scores - jnp.max(scores, axis=0, keepdims=True))
            r.probs[here, at] = exps / jnp.sum(exps, axis=0, keepdims=True)
    for s in range(series):
        here = slice(s * slots, (s + 1) * slots)
        for start in range(0, inner, 128):
            at = slice(start, start + 128)
            values = r.qkv[here, 2 * inner + start : 2 * inner + start + 128]
            both = dot_tn(r.probs[here, at].astype(bf16), values)
            r.heads[here, at] = own_blocks(both, is_low)
    gain = r.gain_ff[layer_idx : layer_idx + 1, :]
    for part in chunks(rows, 256):
        middle = x_ref[part, :] + dot_nt(r.heads[part, :], r.attn_w[:, 3 * inner :])
        r.middle[part, :] = middle
        r.ff_in[part, :] = (middle * inverse_rms(middle) * gain).astype(bf16)


def prepare_body(r):
    names = ("inputs", "valid", "keep", "embed", "gain_attn", "buckets")
    r.fetch(*names)
    r.need(*names)
    series, slots = r.valid.shape
    gain = r.gain_attn[0:1, :]
    valid = jnp.transpose(r.valid[...].astype(f32))
    keep = jnp.transpose(r.keep[...].astype(f32))
    for s in range(series):
        here = slice(s * slots, (s + 1) * slots)
        seen = valid[:, s : s + 1]
        x = jnp.where(seen == 1.0, r.inputs[here, :].astype(f32), r.embed[...])
        r.x[here, :] = x
        r.a[here, :] = (x * inverse_rms(x) * gain).astype(bf16)
        r.seen[here, :] = jnp.broadcast_to(seen, (slots, 128)).astype(jnp.int32)
        r.mask[here, :] = jnp.broadcast_to(keep[:, s : s + 1], (slots, 128)).astype(jnp.int32)
    turned = jnp.transpose(r.buckets[...].astype(f32)).astype(jnp.int32)
    wide = jnp.concatenate([turned, turned], axis=1)
    r.wide[...] = wide
    is_low = lane_low(slots)
    bucket_count, heads = r.table.shape
    for pair in range(heads // 2):
        bias = jnp.zeros((slots, 128), f32)
        for idx in range(bucket_count):
            entry = jnp.where(is_low, r.table[idx, 2 * pair], r.table[idx, 2 * pair + 1])
            bias = jnp.where(wide == idx, entry, bias)
        r.bias[:, pair * 128 : (pair + 1) * 128] = bias


def attention_body(r, sizes, masks, grain, layer_idx):
    r.fetch("gain_ff")
    lay_out_attention(r, masks, grain)
    r.need("gain_ff")
    attention_forward(r, r.x, r.a, sizes, layer_idx)


def ff_body(r):
    r.fetch("gain_attn")
    lay_out_ff(r, 0)
    r.need("gain_attn")
    width = r.middle.shape[1]
    for part in chunks(r.middle.shape[0], 256):
        x_next = r.middle[part, :]
        for half in range(2):
            both = dot_nn(r.ff_in[part, :], r.ff_gate_up[half])
            hidden = (gelu_terms(both[:, :width])[0] * both[:, width:]).astype(bf16)
            x_next = x_next + dot_nn(hidden, r.ff_down[half])
        r.x_next[part, :] = x_next
        r.a_next[part, :] = (x_next * inverse_rms(x_next) * r.gain_attn[1:2, :]).astype(bf16)


def ff_backward(r, layer_idx, last, masks):
    rows, width = r.middle.shape
    r.fetch("grad", "gain_ff")
    if last:
        lay_out_ff(r, layer_idx)
    r.need("grad", "gain_ff")
    gain_ff = r.gain_ff[layer_idx : layer_idx + 1, :]
    gain_total = jnp.zeros((1, width), f32)
    for part in chunks(rows, 256):
        grad = r.grad[part, :].astype(f32)
        rounded = grad.astype(bf16)
        ff_rows = r.ff_in[part, :]
        back = None
        middle = r.middle[part, :]
        total = middle
        for half in range(2):
            both = dot_nn(ff_rows, r.ff_gate_up[half])
            grad_hidden = dot_nt(rounded, r.ff_down[half])
            gate_act, up_act = both[:, :width], both[:, width:]
            mixed, slope = gelu_terms(gate_act)
            hidden = (mixed * up_act).astype(bf16)
            r.hidden[half, part, :] = hidden
            r.grad_gate_up[half, part, :width] = (grad_hidden * up_act * slope).astype(bf16)
            r.grad_gate_up[half, part, width:] = (grad_hidden * mixed).astype(bf16)
            pulled = r.grad_gate_up[half, part, :]
            if last:
                total = total + dot_nn(hidden, r.ff_down[half])
            term = dot_nt(pulled, r.ff_gate_up[half])
            back = term if back is None else back + term
        if last:
            r.outputs[part, :] = total.astype(bf16)
        grad_mid, gain_part = norm_back(middle, gain_ff, back)
        gain_total += gain_part
        grad_mid = grad + grad_mid
        r.grad_mid[part, :] = grad_mid
        r.branch[part, :] = grad_mid.astype(bf16)
        r.grad_low[part, :] = rounded
    if last:
        r.write("outputs")
    for half in range(2):
        r.ff_grad[half, :, : 2 * width] = dot_tn(r.ff_in[...], r.grad_gate_up[half])
        r.ff_grad[half, :, 2 * width :] = dot_tn(r.hidden[half], r.grad_low[...])
    half_count = len(masks[0]) // 2
    grain, columns = r.ff_keep.shape[1:]
    for side, side_masks in enumerate(masks):
        lanes = slice(side * columns, (side + 1) * columns)
        for idx, mask in enumerate(side_masks):
            target = r.ff_keep if idx < half_count else r.ff_send
            piece = pl.ds(pl.multiple_of((r.place[3] ^ (mask // 2)) * grain, grain), grain)
            target[side * half_count + idx % half_count] = r.ff_grad[mask % 2, piece, lanes].astype(
                bf16
            )
    if last:
        r.drain("outputs")
    return gain_total


def attention_backward(r, sizes, layer_idx, last, piece_masks, heads):
    series, slots, inner = sizes
    rows = series * slots
    width = r.x.shape[1]
    r.fetch("gain_attn")
    for part in chunks(rows, 256):
        r.grad_heads[part, :] = dot_nn(r.branch[part, :], r.attn_w[:, 3 * inner :]).astype(bf16)
    is_low = lane_low(slots)
    low, high = lane_halves()
    for start in range(0, inner, 128):
        at = slice(start, start + 128)
        bias_total = jnp.zeros((slots, 128), f32) if last else r.bias_before[:, at]
        for s in range(series):
            here = slice(s * slots, (s + 1) * slots)
            probs = r.probs[here, at]
            values = r.qkv[here, 2 * inner + start : 2 * inner + start + 128]
            grad_probs = dot_nt(values, pair_blocks(r.grad_heads[here, at], low, high))
            inner_sum = jnp.sum(probs * grad_probs, axis=0, keepdims=True)
            grad_scores = (probs * (grad_probs - inner_sum)).astype(bf16)
            r.grad_scores[here, at] = grad_scores
            bias_total = bias_total + grad_scores.astype(f32)
        r.bias_acc[:, at] = bias_total
    for s in range(series):
        here = slice(s * slots, (s + 1) * slots)
        for start in range(0, inner, 128):
            at = slice(start, start + 128)
            key_at = slice(inner + start, inner + start + 128)
            value_at = slice(2 * inner + start, 2 * inner + start + 128)
            grad_scores = r.grad_scores[here, at]
            r.grad_qkv[here, key_at] = dot_nn(
                grad_scores, pair_blocks(r.qkv[here, at], low, high)
            ).astype(bf16)
            r.grad_qkv[here, value_at] = dot_nn(
                r.probs[here, at].astype(bf16), pair_blocks(r.grad_heads[here, at], low, high)
            ).astype(bf16)
            r.grad_qkv[here, at] = own_blocks(dot_tn(grad_scores, r.qkv[here, key_at]), is_low)
    r.attn_grad[:, : 3 * inner] = dot_tn(r.a[...], r.grad_qkv[...])
    r.attn_grad[:, 3 * inner :] = dot_tn(r.branch[...], r.heads[...])
    scatter_pieces(r.attn_grad, r.attn_keep, r.attn_send, piece_masks, r.place[2])
    r.need("gain_attn")
    gain_attn = r.gain_attn[layer_idx : layer_idx + 1, :]
    gain_total = jnp.zeros((1, width), f32)
    embed_total = jnp.zeros((1, width), f32)
    for part in chunks(rows, 256):
        grad_normed = dot_nt(r.grad_qkv[part, :], r.attn_w[:, : 3 * inner])
        grad_in, gain_part = norm_back(r.x[part, :], gain_attn, grad_normed)
        gain_total += gain_part
        grad_in = r.grad_mid[part, :] + grad_in
        if last:
            r.grad_next[part, :] = grad_in
        else:
            seen = r.seen[part, 0:1] == 1
            r.grad_next[part, :] = jnp.where(seen, grad_in, 0.0)
            embed_total += jnp.sum(jnp.where(seen, 0.0, grad_in), axis=0, keepdims=True)
    r.write("grad_next")
    if not last:
        put_row(r.small, 4, embed_total)
        head_size = inner // heads
        for idx in range(r.table_rows.shape[0]):
            for start in range(0, inner, 128):
                at = slice(start, start + 128)
                chosen = jnp.where(r.wide[...] == idx, r.bias_acc[:, at], 0.0)
                r.table_rows[idx : idx + 1, at] = jnp.sum(chosen, axis=0, keepdims=True)
        lane = lax.broadcasted_iota(jnp.int32, (r.table_rows.shape[0], 128), 1)
        table = jnp.zeros(lane.shape, f32)
        for head in range(heads):
            cut = r.table_rows[:, head * head_size : (head + 1) * head_size]
            table = jnp.where(lane == head, jnp.sum(cut, axis=1, keepdims=True), table)
        r.small[:heads, : table.shape[0]] = jnp.transpose(table)[:heads, :]
    r.drain("grad_next")
    return gain_total


def two_parts(values):
    high = values.astype(bf16).astype(f32)
    return high, (values - high).astype(bf16).astype(f32)


def last_ff_body(r, masks):
    r.small[...] = jnp.zeros(r.small.shape, f32)
    put_row(r.small, 3, ff_backward(r, 1, True, masks))


def last_attention_body(r, sizes, piece_masks, heads):
    r.small[...] = r.small_before[...]
    put_row(r.small, 1, attention_backward(r, sizes, 1, True, piece_masks, heads))


def ff_backward_body(r, masks):
    r.small[...] = r.small_before[...]
    put_row(r.small, 2, ff_backward(r, 0, False, masks))


def attention_backward_body(r, sizes, piece_masks, heads):
    r.small[...] = r.small_before[...]
    put_row(r.small, 0, attention_backward(r, sizes, 0, False, piece_masks, heads))
    high, low = two_parts(r.small[...])
    last = r.attn_send.shape[0] - 1
    r.attn_send[last] = jnp.concatenate([high, low], axis=0).astype(bf16)
    r.small[...] = high + low


def put_row(packed, which, row):
    first, width = packed.shape[0] - 2, row.shape[1]
    at = which % 3 * width
    packed[first + which // 3 : first + which // 3 + 1, at : at + width] = row


def scatter_pieces(whole, keep, send, masks, place):
    count = len(masks)
    grain = whole.shape[0] // count
    for idx, mask in enumerate(masks):
        target = keep if idx < count // 2 else send
        source = pl.ds(pl.multiple_of((place ^ mask) * grain, grain), grain)
        target[idx % (count // 2)] = whole[source, :].astype(bf16)


def finish(pieces, masks, layer_idx, place, shape, before=()):
    grain, width = pieces.shape[1], shape[-1]
    count = len(before)

    def kernel(place_ref, source, *refs):
        outs = refs[count : count + 3]
        stage, out_sem = refs[count + 3 :]
        for idx, mask in enumerate(masks):
            rows = pl.ds(pl.multiple_of((place_ref[3] ^ mask) * grain, grain), grain)
            for k, out in enumerate(outs):
                stage[k, idx] = source[idx, :, k * width : (k + 1) * width].astype(f32)
                pltpu.make_async_copy(stage.at[k, idx], out.at[layer_idx, rows], out_sem).start()
        pltpu.make_async_copy(stage, stage, out_sem).wait()

    return pl.pallas_call(
        kernel,
        name="layer_%d_ff_grads" % layer_idx,
        in_specs=[
            pl.BlockSpec(memory_space=pltpu.SMEM),
            pl.BlockSpec(memory_space=pltpu.VMEM),
        ]
        + [pl.BlockSpec(memory_space=pl.ANY)] * count,
        out_specs=[pl.BlockSpec(memory_space=pl.ANY)] * 3,
        out_shape=[jax.ShapeDtypeStruct(shape, f32)] * 3,
        input_output_aliases={2 + k: k for k in range(count)},
        scratch_shapes=[
            pltpu.VMEM((3, len(masks), grain, width), f32),
            pltpu.SemaphoreType.DMA,
        ],
        compiler_params=pltpu.CompilerParams(vmem_limit_bytes=6 * mebibyte),
        cost_estimate=cost(3),
    )(place, pltpu.with_memory_space_constraint(pieces, pltpu.VMEM), *before)


def small_body(r):
    width = r.embed.shape[1]
    heads = r.table.shape[0]
    outs = ((r.gain_attn, 0), (r.gain_attn, 1), (r.gain_ff, 0), (r.gain_ff, 1), (r.embed, 0))
    for which, (out, row) in enumerate(outs):
        first = r.packed.shape[0] - 2 + which // 3
        at = which % 3 * width
        out[row : row + 1, :] = r.packed[first : first + 1, at : at + width]
    r.table[...] = r.packed[:heads, : r.table.shape[1]]
    r.write("gain_attn", "gain_ff", "embed", "table")
    r.drain("gain_attn", "gain_ff", "embed", "table")


def pack_body(r, packs):
    rows = r.quarter_0.shape[1]
    at = pl.ds(pl.multiple_of(r.place[1] * rows, rows), rows)
    copies = []
    outs = [r.quarter_0, r.quarter_1]
    for layer_idx in range(2):
        for k, w in enumerate((r.w_gate, r.w_up, r.w_down)):
            copies.append((w.at[layer_idx, at], outs[layer_idx].at[k]))
    if packs:
        outs += [r.block_0, r.block_1]
        inner = r.w_query.shape[2]
        for layer_idx in range(2):
            for k, w in enumerate((r.w_query, r.w_key, r.w_value, r.w_out)):
                lanes = pl.ds(k * inner, inner)
                copies.append((w.at[layer_idx], outs[2 + layer_idx].at[:, lanes]))
    start_all([pltpu.make_async_copy(*ends, r.pack_sem) for ends in copies])
    wait_all(r.pack_sem, *outs)


def order_masks(hops):
    masks = [0]
    for hop in reversed(hops):
        masks = masks + [mask ^ hop for mask in masks]
    return masks


def tie(value, *others):
    return lax.optimization_barrier((value, *others))[0]


def on_device(
    inputs,
    cotangent,
    attention_mask,
    patch_valid,
    buckets,
    mask_embed,
    w_query,
    w_key,
    w_value,
    w_output,
    w_gate,
    w_up,
    w_down,
    gain_attn,
    gain_ff,
    bias_table,
    dp_size,
):
    series, slots, width = inputs.shape
    heads = bias_table.shape[1]
    inner = w_query.shape[2]
    rows = series * slots
    sizes = (series, slots, inner)
    matrix = (rows, width)
    devices = 2 * dp_size
    dp_at = lax.axis_index("dp")
    device_at = 2 * dp_at + lax.axis_index("tensor")
    cotangent = cotangent.reshape(matrix)

    def swap(array, mask):
        return lax.ppermute(array, axes, [(n, n ^ mask) for n in range(devices)])

    def join(left, right):
        return jnp.concatenate([left, right], axis=0)

    bits = [1 << k for k in range(devices.bit_length() - 1)]

    attn_grain = max(16, width // devices)
    attn_count = width // attn_grain
    ff_grain = max(16, 2 * width // dp_size)
    ff_count = width // ff_grain
    quarter_at = lax.rem(dp_at, 4)
    place = jnp.stack(
        [
            device_at,
            quarter_at,
            device_at // (devices // attn_count),
            lax.rem(dp_at, ff_count),
        ]
    ).astype(jnp.int32)

    quarter = width // 4
    own_rows = w_query.shape[1]
    direct = own_rows % 16 == 0
    w_out = jnp.swapaxes(w_output, 1, 2)
    sources = dict(w_gate=w_gate, w_up=w_up, w_down=w_down)
    block_outs = {}
    if direct:
        sources |= dict(w_query=w_query, w_key=w_key, w_value=w_value, w_out=w_out)
        block_outs = {"block_%d" % k: Kept((own_rows, 4 * inner), bf16) for k in range(2)}
    packed = run(
        functools.partial(pack_body, packs=direct),
        "pack",
        dict(
            place=place,
            **{n: pltpu.with_memory_space_constraint(w, pltpu.HBM) for n, w in sources.items()},
        ),
        dict(
            quarter_0=Kept((3, quarter, width), bf16),
            quarter_1=Kept((3, quarter, width), bf16),
            **block_outs,
        ),
        dict(pack_sem=pltpu.SemaphoreType.DMA),
        vmem=4,
    )
    far = bits[2:]

    def prepare(token):
        return run(
            prepare_body,
            "prepare",
            dict(
                inputs=tie(inputs, token).reshape(matrix),
                valid=patch_valid,
                keep=attention_mask,
                embed=mask_embed[None, :],
                gain_attn=gain_attn,
                buckets=buckets,
                table=bias_table,
            ),
            dict(
                x=Kept(matrix, f32),
                a=Kept(matrix, bf16),
                bias=Kept((slots, heads * slots), f32),
                mask=Kept((rows, 128), jnp.int32),
                seen=Kept((rows, 128), jnp.int32),
                wide=Kept((slots, 128), jnp.int32),
            ),
            {},
            micros=3,
        )

    if direct:
        hops_0 = [1] + far[2:] + far[:2] + [2]
        hops_1 = far[2:] + far[:2] + [1, 2]
        block_0, block_1 = packed.block_0, packed.block_1
        got_1 = swap(block_1, hops_1[0])
        got_0 = swap(block_0, hops_0[0])
        ff_0 = swap(tie(packed.quarter_0, got_0), 1)
        ff_1 = swap(tie(packed.quarter_1, ff_0), 1)
        got_ff_0 = swap(ff_0, 4)
        block_0 = join(block_0, got_0)
        block_1 = join(block_1, tie(got_1, block_0))
        for hop_0, hop_1 in zip(hops_0[1:-2], hops_1[1:-2]):
            got_1, got_0 = swap(block_1, hop_1), swap(block_0, hop_0)
            if hop_0 == hops_0[1]:
                start = prepare(block_1)
                got_0 = tie(got_0, ff_0)
            block_0 = join(block_0, got_0)
            block_1 = join(block_1, tie(got_1, block_0))
        block_0 = tie(block_0, block_1)
        got_0 = swap(block_0, hops_0[-2])
        got_1 = swap(block_1, hops_1[-2])
        block_0 = join(block_0, tie(got_0, start.a, got_ff_0, ff_1, got_1))
        ff_0 = join(ff_0, tie(got_ff_0, block_0))
        got_ff_1 = swap(tie(ff_1, ff_0), 4)
        attn_pieces = [(block_0, swap(block_0, 2), order_masks(hops_0[::-1]))]
    else:
        ff_0, ff_1 = swap(packed.quarter_0, 1), swap(packed.quarter_1, 1)
        ff_0 = join(ff_0, swap(ff_0, 4))
        start = prepare(ff_0)
        attn_pieces = []
        rows_of = jnp.concatenate([w_query, w_key, w_value, w_out], axis=2)
        for layer_idx in range(2):
            whole = lax.all_gather(rows_of[layer_idx], axes, axis=0, tiled=True)
            attn_pieces.append((whole, whole, [0]))
    ff_pieces = [(ff_0, swap(ff_0, 2))]

    def attn_ins(layer_idx):
        near, far, masks = attn_pieces[layer_idx]
        return dict(attn_near=Kept(near), attn_far=Kept(far)), masks

    def ff_ins(layer_idx):
        near, far = ff_pieces[layer_idx]
        own = keep_all(dict(w_gate=w_gate, w_up=w_up, w_down=w_down))
        return dict(**own, ff_near=Kept(near), ff_far=Kept(far))

    ff_outs = dict(
        ff_gate_up=Kept((2, width, 2 * width), bf16), ff_down=Kept((2, width, width), bf16)
    )
    grain = own_rows if direct else width
    attn_outs = dict(
        attn_w=Kept((width, 4 * inner), bf16),
        qkv=Kept((rows, 3 * inner), bf16),
        probs=Kept((rows, heads * slots), f32),
        heads=Kept((rows, inner), bf16),
        middle=Kept(matrix, f32),
        ff_in=Kept(matrix, bf16),
    )

    def attention(layer_idx, x, a, after=(), micros=5):
        pieces, masks = attn_ins(layer_idx)
        return run(
            functools.partial(
                attention_body, sizes=sizes, masks=masks, grain=grain, layer_idx=layer_idx
            ),
            "layer_%d_attention" % layer_idx,
            dict(
                place=place,
                x=Kept(x),
                a=Kept(a),
                bias=Kept(start.bias),
                mask=Kept(start.mask),
                gain_ff=gain_ff,
                **pieces,
            ),
            attn_outs,
            {},
            after=after,
            micros=micros,
        )

    first = attention(0, start.x, start.a, micros=10)
    if direct:
        block_1 = join(block_1, tie(got_1, first.ff_in))
        attn_pieces.append((block_1, swap(block_1, 2), order_masks(hops_1[::-1])))
    first_ff = run(
        ff_body,
        "layer_0_ff",
        dict(
            place=place,
            middle=Kept(first.middle),
            ff_in=Kept(first.ff_in),
            gain_attn=gain_attn,
            **ff_ins(0),
        ),
        dict(**ff_outs, x_next=Kept(matrix, f32), a_next=Kept(matrix, bf16)),
        {},
        after=(block_1,) if direct else (),
        micros=3,
    )
    if direct:
        ff_1 = join(ff_1, tie(got_ff_1, first_ff.x_next))
    else:
        ff_1 = join(ff_1, swap(ff_1, 4))
    ff_pieces.append((ff_1, swap(ff_1, 2)))
    second = attention(1, first_ff.x_next, first_ff.a_next, micros=0.1)

    attn_low = devices // attn_count
    attn_hops = ([2, 1] + bits[2:], [2] + bits[3:4] + bits[2:3] + bits[4:] + [1])
    attn_split = [[hop for hop in hops if hop >= attn_low] for hops in attn_hops]
    attn_whole = [hop for hop in bits if hop < attn_low]
    attn_masks = [[mask // attn_low for mask in order_masks(hops)] for hops in attn_split]
    ff_hops = ([2, 4, 1] + bits[3:], [2, 1, 4] + bits[3:])
    ff_split = [[hop for hop in hops if hop // 2 < ff_count] for hops in ff_hops]
    ff_whole = [hop for hop in bits[1:] if hop // 2 >= ff_count]
    ff_share = [hop for hop in bits[:0:-1] if hop // 2 < ff_count]
    ff_masks = [order_masks(hops) for hops in ff_split]
    place_masks = [mask // 2 for mask in order_masks(ff_share[::-1])]
    attn_half = (attn_count // 2, attn_grain, 4 * inner)
    small_shape = (heads + 2, 3 * width)

    attn_back_outs = dict(attn_keep=Kept(attn_half, bf16), attn_send=Kept(attn_half, bf16))
    attn_back_scratch = dict(
        grad_heads=pltpu.VMEM((rows, inner), bf16),
        grad_qkv=pltpu.VMEM((rows, 3 * inner), bf16),
        grad_scores=pltpu.VMEM((rows, heads * slots), bf16),
        attn_grad=pltpu.VMEM((width, 4 * inner), f32),
    )
    ff_back_outs = dict(
        ff_keep=Kept((2 * ff_count, ff_grain, 3 * width // 2), bf16),
        ff_send=Kept((2 * ff_count, ff_grain, 3 * width // 2), bf16),
        small=Kept(small_shape, f32),
        grad_mid=Kept(matrix, f32),
        branch=Kept(matrix, bf16),
    )
    ff_back_scratch = dict(
        hidden=pltpu.VMEM((2, rows, width), bf16),
        grad_gate_up=pltpu.VMEM((2, rows, 2 * width), bf16),
        ff_grad=pltpu.VMEM((2, width, 3 * width), f32),
        grad_low=pltpu.VMEM(matrix, bf16),
    )
    bias_shape = (slots, heads * slots)

    def attn_back_ins(kept, x, a):
        return dict(
            x=Kept(x),
            a=Kept(a),
            gain_attn=gain_attn,
            attn_w=Kept(kept.attn_w),
            qkv=Kept(kept.qkv),
            probs=Kept(kept.probs),
            heads=Kept(kept.heads),
        )

    def add(left, right):
        return (left.astype(f32) + right.astype(f32)).astype(bf16)

    def halving(keep, send, hops, out):
        for step, hop in enumerate(hops):
            got = yield swap(send, hop)
            if step + 1 < len(hops):
                cut = keep.shape[0] // 2
                send = add(keep[cut:], got[cut:])
                keep = add(keep[:cut], got[:cut])
                out["token"] = send
            else:
                out["token"] = keep = add(keep, got)
        out["piece"] = keep

    def summing(piece, hops, out):
        for hop in hops:
            got = yield swap(piece, hop)
            out["token"] = piece = add(piece, got)
        out["piece"] = piece

    def sharing(piece, hops, out):
        for step, hop in enumerate(hops):
            if step + 1 == len(hops):
                out["near"] = piece
            got = yield swap(piece, hop)
            if step + 1 < len(hops):
                out["token"] = piece = join(piece, got)
            else:
                out["token"] = out["far"] = got

    def rounded(values):
        return lax.reduce_precision(values, exponent_bits=8, mantissa_bits=7)

    def with_small(pieces, small):
        high = rounded(small)
        low = rounded(small - high)
        parts = join(high, low).astype(bf16)[None]
        return join(pieces, parts), high + low

    def add_small(small, got):
        parts = got[-1].astype(f32)
        return small + (parts[: small.shape[0]] + parts[small.shape[0] :])

    def attn_chain(part, layer_idx, out):
        small = part.small if layer_idx == 0 else None
        keep, send = part.attn_keep, part.attn_send
        hops = attn_split[layer_idx] + attn_whole
        for step, hop in enumerate(hops):
            got = yield swap(send, hop)
            if small is not None:
                small = add_small(small, got)
                got = got[:-1]
            if step + 1 < len(attn_split[layer_idx]):
                half = keep.shape[0] // 2
                send = add(keep[half:], got[half:])
                keep = add(keep[:half], got[:half])
            else:
                send = keep = add(keep, got)
            if small is not None and step + 1 < len(hops):
                send, small = with_small(send, small)
            out["token"] = send
            if layer_idx == 1 and step == 0:
                send = tie(send, *(yield None))
        piece = keep[0]
        if own_rows < attn_grain:
            first_row = lax.rem(device_at, attn_low) * own_rows
            piece = lax.dynamic_slice_in_dim(piece, first_row, own_rows, axis=0)
        out["done"] = piece.astype(f32)
        out["small"] = small

    def ff_chain(part, out):
        got = yield swap(part.ff_send, 2)
        count = ff_count
        keeps, sends = [], []
        for side in range(2):
            at, half = side * count, count // 2
            sends.append(add(part.ff_keep[at + half : at + count], got[at + half : at + count]))
            keeps.append(add(part.ff_keep[at : at + half], got[at : at + half]))
        out["token"] = tuple(sends)
        for hops in zip(ff_split[0][1:3], ff_split[1][1:3]):
            got = yield tuple(swap(send, hop) for send, hop in zip(sends, hops))
            half = keeps[0].shape[0] // 2
            sends = [add(keep[half:], one[half:]) for keep, one in zip(keeps, got)]
            keeps = [add(keep[:half], one[:half]) for keep, one in zip(keeps, got)]
            out["token"] = tuple(sends)
        keep, send = (jnp.concatenate(sides, axis=2) for sides in (keeps, sends))
        yield from halving(keep, send, ff_split[0][3:], out)
        yield from summing(out["piece"], ff_whole, out)
        yield from sharing(out["piece"], ff_share, out)

    class Chain:
        def __init__(self, steps, *args):
            self.out = {}
            self.steps = steps(*args, self.out)
            self.arriving = next(self.steps)

        def resume(self, *tokens):
            self.arriving = self.steps.send(tokens)

        def step(self, token, *others):
            if self.arriving is not None:
                tokens = (*(token if isinstance(token, tuple) else (token,)), *others)
                many = isinstance(self.arriving, tuple)
                arrived = self.arriving if many else (self.arriving,)
                arrived = lax.optimization_barrier((*arrived, *tokens))[: len(arrived)]
                arrived = arrived if many else arrived[0]
                self.arriving = None
                try:
                    self.arriving = self.steps.send(arrived)
                except StopIteration:
                    pass
                return self.out["token"]
            return token

    back_ff_1 = run(
        functools.partial(last_ff_body, masks=ff_masks),
        "layer_1_ff",
        dict(
            place=place,
            grad=cotangent,
            gain_ff=gain_ff,
            middle=Kept(second.middle),
            ff_in=Kept(second.ff_in),
            **ff_ins(1),
        ),
        dict(**ff_back_outs, outputs=(matrix, bf16)),
        dict(
            ff_gate_up=pltpu.VMEM((2, width, 2 * width), bf16),
            ff_down=pltpu.VMEM((2, width, width), bf16),
            **ff_back_scratch,
        ),
        micros=8,
        vmem=24,
    )
    ff_1 = Chain(ff_chain, back_ff_1)
    back_1 = run(
        functools.partial(
            last_attention_body, sizes=sizes, piece_masks=attn_masks[1], heads=heads
        ),
        "layer_1_attention_backward",
        dict(
            place=place,
            small_before=Kept(back_ff_1.small),
            grad_mid=Kept(back_ff_1.grad_mid),
            branch=Kept(back_ff_1.branch),
            **attn_back_ins(second, first_ff.x_next, first_ff.a_next),
        ),
        dict(
            **attn_back_outs,
            small=Kept(small_shape, f32),
            grad_next=Kept(matrix, f32),
            bias_acc=Kept(bias_shape, f32),
        ),
        attn_back_scratch,
        micros=6,
        vmem=14,
    )
    attn_1 = Chain(attn_chain, back_1, 1)
    token = ff_1.step(back_1.attn_send)
    token = (attn_1.step(token),)
    back_0 = run(
        functools.partial(ff_backward_body, masks=ff_masks),
        "layer_0_ff_backward",
        dict(
            place=place,
            grad=Kept(back_1.grad_next),
            gain_ff=gain_ff,
            small_before=Kept(back_1.small),
            middle=Kept(first.middle),
            ff_in=Kept(first.ff_in),
            ff_gate_up=Kept(first_ff.ff_gate_up),
            ff_down=Kept(first_ff.ff_down),
        ),
        ff_back_outs,
        ff_back_scratch,
        after=token,
        micros=8,
        vmem=20,
    )
    token = ff_1.step(back_0.branch)
    back_0.ff_send = tie(back_0.ff_send, *token)
    ff_0 = Chain(ff_chain, back_0)
    token = ff_0.step(token)
    back_attn_0 = run(
        functools.partial(
            attention_backward_body, sizes=sizes, piece_masks=attn_masks[0], heads=heads
        ),
        "layer_0_attention_backward",
        dict(
            place=place,
            bias_before=Kept(back_1.bias_acc),
            seen=Kept(start.seen),
            wide=Kept(start.wide),
            small_before=Kept(back_0.small),
            grad_mid=Kept(back_0.grad_mid),
            branch=Kept(back_0.branch),
            **attn_back_ins(first, start.x, start.a),
        ),
        dict(
            attn_keep=Kept(attn_half, bf16),
            attn_send=Kept((attn_count // 2 + 1, *attn_half[1:]), bf16),
            small=Kept(small_shape, f32),
            grad_next=(matrix, f32),
        ),
        dict(
            bias_acc=pltpu.VMEM(bias_shape, f32),
            table_rows=pltpu.VMEM((bias_table.shape[0], heads * slots), f32),
            **attn_back_scratch,
        ),
        after=token,
        micros=7,
        vmem=14,
    )
    attn_0 = Chain(attn_chain, back_attn_0, 0)
    attn_1.resume(back_attn_0.attn_send)
    token = back_attn_0.attn_send
    shape = (2, width, width)
    near_masks = place_masks[: ff_count // 2]
    far_masks = place_masks[ff_count // 2 :]
    done = ()
    ended = False
    turn = 0
    sums = attn_grads = None
    while ff_0.arriving is not None:
        turn += 1
        token = ff_1.step(token)
        if done and not ended:
            done = finish(tie(ff_1.out["far"], token), far_masks, 1, place, shape, done)
            token = done[0]
            ended = True
        token = ff_0.step(token)
        if not done and "near" in ff_1.out:
            done = finish(tie(ff_1.out["near"], token), near_masks, 1, place, shape)
            token = done[0]
        token = attn_0.step(token)
        if turn > 1:
            token = attn_1.step(token)
        if sums is None and attn_0.arriving is None:
            sums = run(
                small_body,
                "small_sums",
                dict(packed=Kept(tie(attn_0.out["small"], token))),
                dict(
                    gain_attn=((2, width), f32),
                    gain_ff=((2, width), f32),
                    embed=((1, width), f32),
                    table=(bias_table.shape[::-1], f32),
                ),
                {},
            )
            token = sums.embed
        if attn_grads is None and attn_0.arriving is None and attn_1.arriving is None:
            both = jnp.stack([attn_0.out["done"], tie(attn_1.out["done"], token)])
            attn_grads = [both[:, :, k * inner : (k + 1) * inner] for k in range(4)]
            attn_grads[3] = jnp.swapaxes(attn_grads[3], 1, 2)
            token = tuple(attn_grads)
    if not ended:
        done = finish(ff_1.out["far"], far_masks, 1, place, shape, done)
    for pieces, masks in ((ff_0.out["near"], near_masks), (ff_0.out["far"], far_masks)):
        done = finish(pieces, masks, 0, place, shape, done)
    return (
        back_ff_1.outputs.reshape(inputs.shape),
        back_attn_0.grad_next.reshape(inputs.shape),
        *attn_grads,
        *done,
        sums.gain_attn,
        sums.gain_ff,
        sums.table.T,
        sums.embed[0],
    )


def solution(mesh):
    placed = (
        P(("dp", "tensor"), None, None),
        P(("dp", "tensor"), None, None),
        P(("dp", "tensor"), None),
        P(("dp", "tensor"), None),
        P(),
        P(),
        P(None, ("dp", "tensor"), None),
        P(None, ("dp", "tensor"), None),
        P(None, ("dp", "tensor"), None),
        P(None, None, ("dp", "tensor")),
        P(None, None, "tensor"),
        P(None, None, "tensor"),
        P(None, "tensor", None),
        P(),
        P(),
        P(),
    )
    return jax.shard_map(
        functools.partial(on_device, dp_size=mesh.shape["dp"]),
        mesh=mesh,
        in_specs=placed,
        out_specs=(
            P(("dp", "tensor"), None, None),
            P(("dp", "tensor"), None, None),
            P(None, ("dp", "tensor"), None),
            P(None, ("dp", "tensor"), None),
            P(None, ("dp", "tensor"), None),
            P(None, None, ("dp", "tensor")),
            P(None, None, "tensor"),
            P(None, None, "tensor"),
            P(None, "tensor", None),
            P(),
            P(),
            P(),
            P(),
        ),
        check_vma=False,
    )
```

```python
import functools
import types

import jax
import jax.numpy as jnp
from jax import lax
from jax.experimental import pallas as pl
from jax.experimental.pallas import tpu as pltpu
from jax.sharding import PartitionSpec as P

norm_eps = 1e-06
masked_score = -1e30
bf16 = jnp.bfloat16
f32 = jnp.float32
axes = ("dp", "tensor")
mebibyte = 1024 * 1024
raw_names = ("w_query", "w_key", "w_value", "w_out", "w_gate", "w_up", "w_down")
scalar_names = ("place", "table")


def dot_nn(left, right):
    return lax.dot_general(left, right, (((1,), (0,)), ((), ())), preferred_element_type=f32)


def dot_nt(left, right):
    return lax.dot_general(left, right, (((1,), (1,)), ((), ())), preferred_element_type=f32)


def dot_tn(left, right):
    return lax.dot_general(left, right, (((0,), (0,)), ((), ())), preferred_element_type=f32)


def inverse_rms(values):
    return lax.rsqrt(jnp.mean(values * values, axis=-1, keepdims=True) + norm_eps)


def norm_back(values, gain, grad_out):
    scale = inverse_rms(values)
    pulled = grad_out * gain
    mean_part = jnp.mean(pulled * values, axis=-1, keepdims=True)
    grad_in = scale * pulled - values * (scale * scale * scale) * mean_part
    return grad_in, jnp.sum(grad_out * values * scale, axis=0, keepdims=True)


def gelu_terms(gate_act):
    square = gate_act * gate_act
    bent = jnp.tanh(0.7978845608028654 * gate_act * (1.0 + 0.044715 * square))
    half = 0.5 * (1.0 + bent)
    slope = half + 0.5 * gate_act * (1.0 - bent * bent) * (
        0.7978845608028654 * (1.0 + 3.0 * 0.044715 * square)
    )
    return gate_act * half, slope


def cost(micros):
    return pl.CostEstimate(flops=int(micros * 1.15e9), bytes_accessed=0, transcendentals=0)


def run(body, name, ins, outs, scratch, after=(), micros=1, vmem=8):
    in_names, out_names, scratch_names = list(ins), list(outs), list(scratch)
    direct = {n for n in in_names if n in scalar_names + raw_names or isinstance(ins[n], Kept)}
    staged = [n for n in in_names if n not in direct]
    copied = [n for n in out_names if not isinstance(outs[n], Kept)]
    in_sems = {n: i for i, n in enumerate(staged)}
    out_sems = {n: i for i, n in enumerate(copied)}

    def kernel(*refs):
        refs = list(refs)
        sources = dict(zip(in_names, refs))
        refs = refs[len(in_names) + len(after) :]
        targets = dict(zip(out_names, refs))
        refs = refs[len(out_names) :]
        space = dict(zip(scratch_names, refs))
        refs = refs[len(scratch_names) :]
        buffers = dict(zip(staged + copied, refs))
        sems_in, sems_out = refs[len(staged) + len(copied) :]
        kept = {n: ref for n, ref in targets.items() if n not in out_sems}
        r = types.SimpleNamespace(**space, **buffers, **kept)
        for n in direct:
            setattr(r, n, sources[n])

        def copy_in(n):
            return pltpu.make_async_copy(sources[n], buffers[n], sems_in.at[in_sems[n]])

        def copy_out(n):
            return pltpu.make_async_copy(buffers[n], targets[n], sems_out.at[out_sems[n]])

        r.fetch = lambda *names: [copy_in(n).start() for n in names if n in in_sems]
        r.need = lambda *names: [copy_in(n).wait() for n in names if n in in_sems]
        r.write = lambda *names: [copy_out(n).start() for n in names if n in out_sems]
        r.drain = lambda *names: [copy_out(n).wait() for n in names if n in out_sems]
        body(r)

    def in_space(n):
        if n in scalar_names:
            return pltpu.SMEM
        return pltpu.VMEM if isinstance(ins[n], Kept) else pl.ANY

    results = pl.pallas_call(
        kernel,
        name=name,
        in_specs=[pl.BlockSpec(memory_space=in_space(n)) for n in in_names]
        + [pl.BlockSpec(memory_space=pl.ANY) for _ in after],
        out_specs=[
            pl.BlockSpec(memory_space=pltpu.VMEM if isinstance(out, Kept) else pl.ANY)
            for out in outs.values()
        ],
        out_shape=[
            pltpu.VMEM(*out.what) if isinstance(out, Kept) else jax.ShapeDtypeStruct(*out)
            for out in outs.values()
        ],
        scratch_shapes=list(scratch.values())
        + [pltpu.VMEM(ins[n].shape, ins[n].dtype) for n in staged]
        + [pltpu.VMEM(*outs[n]) for n in copied]
        + [
            pltpu.SemaphoreType.DMA((max(1, len(staged)),)),
            pltpu.SemaphoreType.DMA((max(1, len(copied)),)),
        ],
        compiler_params=pltpu.CompilerParams(vmem_limit_bytes=vmem * mebibyte),
        cost_estimate=cost(micros),
    )(
        *[
            pltpu.with_memory_space_constraint(value.what, pltpu.VMEM)
            if isinstance(value, Kept)
            else value
            for value in ins.values()
        ],
        *after,
    )
    return types.SimpleNamespace(**dict(zip(outs, results)))


class Kept:
    def __init__(self, *what):
        self.what = what[0] if len(what) == 1 else what


def keep_all(names):
    return {name: Kept(value) for name, value in names.items()}


def chunks(extent, size):
    size = min(size, extent)
    return [slice(start, start + size) for start in range(0, extent, size)]


def lay_out_attention(r, masks, rows):
    for idx, mask in enumerate(masks):
        half, at = divmod(idx, max(1, len(masks) // 2))
        source = r.attn_near if half == 0 else r.attn_far
        place = pl.multiple_of((r.place[0] ^ mask) * rows, rows) if len(masks) > 1 else 0
        r.attn_w[pl.ds(place, rows), :] = source[at * rows : (at + 1) * rows, :]


def lay_out_ff(r, layer_idx):
    width = r.ff_down.shape[-1]
    for k, own in enumerate((r.w_gate, r.w_up)):
        r.ff_gate_up[0, :, k * width : (k + 1) * width] = own[layer_idx]
    r.ff_down[0] = r.w_down[layer_idx]
    part = r.ff_near.shape[1]
    for source, base in ((r.ff_near, 0), (r.ff_far, 1)):
        for m in range(2):
            rows = pl.ds(pl.multiple_of((r.place[1] ^ (2 * m + base)) * part, part), part)
            for k in range(2):
                r.ff_gate_up[1, rows, k * width : (k + 1) * width] = source[3 * m + k]
            r.ff_down[1, rows, :] = source[3 * m + 2]


def start_all(copies):
    for copy in copies:
        copy.start()


def wait_all(sem, *buffers):
    for whole in buffers:
        pltpu.make_async_copy(whole, whole, sem).wait()


def lane_low(rows):
    return lax.broadcasted_iota(jnp.int32, (rows, 128), 1) < 64


def lane_halves():
    low = lane_low(1).astype(f32)
    return low.astype(bf16), (1.0 - low).astype(bf16)


def pair_blocks(rows, low, high):
    return jnp.concatenate([rows * low, rows * high], axis=0)


def own_blocks(both, is_low):
    half = both.shape[0] // 2
    return jnp.where(is_low, both[:half], both[half:]).astype(bf16)


def attention_forward(r, x_ref, a_ref, sizes, layer_idx):
    series, slots, inner = sizes
    rows = series * slots
    for part in chunks(rows, 256):
        r.qkv[part, :] = dot_nn(a_ref[part, :], r.attn_w[:, : 3 * inner]).astype(bf16)
    is_low = lane_low(slots)
    low, high = lane_halves()
    for s in range(series):
        here = slice(s * slots, (s + 1) * slots)
        keep = r.mask[here, :] == 1
        for start in range(0, inner, 128):
            at = slice(start, start + 128)
            query = r.qkv[here, at]
            keys = r.qkv[here, inner + start : inner + start + 128]
            scores = dot_nt(keys, pair_blocks(query, low, high)) + r.bias[:, at]
            scores = jnp.where(keep, scores, masked_score)
            exps = jnp.exp(scores - jnp.max(scores, axis=0, keepdims=True))
            r.probs[here, at] = exps / jnp.sum(exps, axis=0, keepdims=True)
    for s in range(series):
        here = slice(s * slots, (s + 1) * slots)
        for start in range(0, inner, 128):
            at = slice(start, start + 128)
            values = r.qkv[here, 2 * inner + start : 2 * inner + start + 128]
            both = dot_tn(r.probs[here, at].astype(bf16), values)
            r.heads[here, at] = own_blocks(both, is_low)
    gain = r.gain_ff[layer_idx : layer_idx + 1, :]
    for part in chunks(rows, 256):
        middle = x_ref[part, :] + dot_nt(r.heads[part, :], r.attn_w[:, 3 * inner :])
        r.middle[part, :] = middle
        r.ff_in[part, :] = (middle * inverse_rms(middle) * gain).astype(bf16)


def prepare_body(r):
    names = ("inputs", "valid", "keep", "embed", "gain_attn", "buckets")
    r.fetch(*names)
    r.need(*names)
    series, slots = r.valid.shape
    gain = r.gain_attn[0:1, :]
    valid = jnp.transpose(r.valid[...].astype(f32))
    keep = jnp.transpose(r.keep[...].astype(f32))
    for s in range(series):
        here = slice(s * slots, (s + 1) * slots)
        seen = valid[:, s : s + 1]
        x = jnp.where(seen == 1.0, r.inputs[here, :].astype(f32), r.embed[...])
        r.x[here, :] = x
        r.a[here, :] = (x * inverse_rms(x) * gain).astype(bf16)
        r.seen[here, :] = jnp.broadcast_to(seen, (slots, 128)).astype(jnp.int32)
        r.mask[here, :] = jnp.broadcast_to(keep[:, s : s + 1], (slots, 128)).astype(jnp.int32)
    turned = jnp.transpose(r.buckets[...].astype(f32)).astype(jnp.int32)
    wide = jnp.concatenate([turned, turned], axis=1)
    r.wide[...] = wide
    is_low = lane_low(slots)
    bucket_count, heads = r.table.shape
    for pair in range(heads // 2):
        bias = jnp.zeros((slots, 128), f32)
        for idx in range(bucket_count):
            entry = jnp.where(is_low, r.table[idx, 2 * pair], r.table[idx, 2 * pair + 1])
            bias = jnp.where(wide == idx, entry, bias)
        r.bias[:, pair * 128 : (pair + 1) * 128] = bias


def attention_body(r, sizes, masks, grain, layer_idx):
    r.fetch("gain_ff")
    lay_out_attention(r, masks, grain)
    r.need("gain_ff")
    attention_forward(r, r.x, r.a, sizes, layer_idx)


def ff_body(r):
    r.fetch("gain_attn")
    lay_out_ff(r, 0)
    r.need("gain_attn")
    width = r.middle.shape[1]
    for part in chunks(r.middle.shape[0], 256):
        x_next = r.middle[part, :]
        for half in range(2):
            both = dot_nn(r.ff_in[part, :], r.ff_gate_up[half])
            hidden = (gelu_terms(both[:, :width])[0] * both[:, width:]).astype(bf16)
            x_next = x_next + dot_nn(hidden, r.ff_down[half])
        r.x_next[part, :] = x_next
        r.a_next[part, :] = (x_next * inverse_rms(x_next) * r.gain_attn[1:2, :]).astype(bf16)


def ff_backward(r, layer_idx, last, masks):
    rows, width = r.middle.shape
    r.fetch("grad", "gain_ff")
    if last:
        lay_out_ff(r, layer_idx)
    r.need("grad", "gain_ff")
    gain_ff = r.gain_ff[layer_idx : layer_idx + 1, :]
    gain_total = jnp.zeros((1, width), f32)
    for part in chunks(rows, 256):
        grad = r.grad[part, :].astype(f32)
        rounded = grad.astype(bf16)
        ff_rows = r.ff_in[part, :]
        back = None
        middle = r.middle[part, :]
        total = middle
        for half in range(2):
            both = dot_nn(ff_rows, r.ff_gate_up[half])
            grad_hidden = dot_nt(rounded, r.ff_down[half])
            gate_act, up_act = both[:, :width], both[:, width:]
            mixed, slope = gelu_terms(gate_act)
            hidden = (mixed * up_act).astype(bf16)
            r.hidden[half, part, :] = hidden
            r.grad_gate_up[half, part, :width] = (grad_hidden * up_act * slope).astype(bf16)
            r.grad_gate_up[half, part, width:] = (grad_hidden * mixed).astype(bf16)
            pulled = r.grad_gate_up[half, part, :]
            if last:
                total = total + dot_nn(hidden, r.ff_down[half])
            term = dot_nt(pulled, r.ff_gate_up[half])
            back = term if back is None else back + term
        if last:
            r.outputs[part, :] = total.astype(bf16)
        grad_mid, gain_part = norm_back(middle, gain_ff, back)
        gain_total += gain_part
        grad_mid = grad + grad_mid
        r.grad_mid[part, :] = grad_mid
        r.branch[part, :] = grad_mid.astype(bf16)
        r.grad_low[part, :] = rounded
    if last:
        r.write("outputs")
    for half in range(2):
        r.ff_grad[half, :, : 2 * width] = dot_tn(r.ff_in[...], r.grad_gate_up[half])
        r.ff_grad[half, :, 2 * width :] = dot_tn(r.hidden[half], r.grad_low[...])
    half_count = len(masks[0]) // 2
    grain, columns = r.ff_keep.shape[1:]
    for side, side_masks in enumerate(masks):
        lanes = slice(side * columns, (side + 1) * columns)
        for idx, mask in enumerate(side_masks):
            target = r.ff_keep if idx < half_count else r.ff_send
            piece = pl.ds(pl.multiple_of((r.place[3] ^ (mask // 2)) * grain, grain), grain)
            target[side * half_count + idx % half_count] = r.ff_grad[mask % 2, piece, lanes].astype(
                bf16
            )
    if last:
        r.drain("outputs")
    return gain_total


def attention_backward(r, sizes, layer_idx, last, piece_masks, heads):
    series, slots, inner = sizes
    rows = series * slots
    width = r.x.shape[1]
    r.fetch("gain_attn")
    for part in chunks(rows, 256):
        r.grad_heads[part, :] = dot_nn(r.branch[part, :], r.attn_w[:, 3 * inner :]).astype(bf16)
    is_low = lane_low(slots)
    low, high = lane_halves()
    for start in range(0, inner, 128):
        at = slice(start, start + 128)
        bias_total = jnp.zeros((slots, 128), f32) if last else r.bias_before[:, at]
        for s in range(series):
            here = slice(s * slots, (s + 1) * slots)
            probs = r.probs[here, at]
            values = r.qkv[here, 2 * inner + start : 2 * inner + start + 128]
            grad_probs = dot_nt(values, pair_blocks(r.grad_heads[here, at], low, high))
            inner_sum = jnp.sum(probs * grad_probs, axis=0, keepdims=True)
            grad_scores = (probs * (grad_probs - inner_sum)).astype(bf16)
            r.grad_scores[here, at] = grad_scores
            bias_total = bias_total + grad_scores.astype(f32)
        r.bias_acc[:, at] = bias_total
    for s in range(series):
        here = slice(s * slots, (s + 1) * slots)
        for start in range(0, inner, 128):
            at = slice(start, start + 128)
            key_at = slice(inner + start, inner + start + 128)
            value_at = slice(2 * inner + start, 2 * inner + start + 128)
            grad_scores = r.grad_scores[here, at]
            r.grad_qkv[here, key_at] = dot_nn(
                grad_scores, pair_blocks(r.qkv[here, at], low, high)
            ).astype(bf16)
            r.grad_qkv[here, value_at] = dot_nn(
                r.probs[here, at].astype(bf16), pair_blocks(r.grad_heads[here, at], low, high)
            ).astype(bf16)
            r.grad_qkv[here, at] = own_blocks(dot_tn(grad_scores, r.qkv[here, key_at]), is_low)
    r.attn_grad[:, : 3 * inner] = dot_tn(r.a[...], r.grad_qkv[...])
    r.attn_grad[:, 3 * inner :] = dot_tn(r.branch[...], r.heads[...])
    scatter_pieces(r.attn_grad, r.attn_keep, r.attn_send, piece_masks, r.place[2])
    r.need("gain_attn")
    gain_attn = r.gain_attn[layer_idx : layer_idx + 1, :]
    gain_total = jnp.zeros((1, width), f32)
    embed_total = jnp.zeros((1, width), f32)
    for part in chunks(rows, 256):
        grad_normed = dot_nt(r.grad_qkv[part, :], r.attn_w[:, : 3 * inner])
        grad_in, gain_part = norm_back(r.x[part, :], gain_attn, grad_normed)
        gain_total += gain_part
        grad_in = r.grad_mid[part, :] + grad_in
        if last:
            r.grad_next[part, :] = grad_in
        else:
            seen = r.seen[part, 0:1] == 1
            r.grad_next[part, :] = jnp.where(seen, grad_in, 0.0)
            embed_total += jnp.sum(jnp.where(seen, 0.0, grad_in), axis=0, keepdims=True)
    r.write("grad_next")
    if not last:
        put_row(r.small, 4, embed_total)
        head_size = inner // heads
        for idx in range(r.table_rows.shape[0]):
            for start in range(0, inner, 128):
                at = slice(start, start + 128)
                chosen = jnp.where(r.wide[...] == idx, r.bias_acc[:, at], 0.0)
                r.table_rows[idx : idx + 1, at] = jnp.sum(chosen, axis=0, keepdims=True)
        lane = lax.broadcasted_iota(jnp.int32, (r.table_rows.shape[0], 128), 1)
        table = jnp.zeros(lane.shape, f32)
        for head in range(heads):
            cut = r.table_rows[:, head * head_size : (head + 1) * head_size]
            table = jnp.where(lane == head, jnp.sum(cut, axis=1, keepdims=True), table)
        r.small[:heads, : table.shape[0]] = jnp.transpose(table)[:heads, :]
    r.drain("grad_next")
    return gain_total


def two_parts(values):
    high = values.astype(bf16).astype(f32)
    return high, (values - high).astype(bf16).astype(f32)


def last_ff_body(r, masks):
    r.small[...] = jnp.zeros(r.small.shape, f32)
    put_row(r.small, 3, ff_backward(r, 1, True, masks))


def last_attention_body(r, sizes, piece_masks, heads):
    r.small[...] = r.small_before[...]
    put_row(r.small, 1, attention_backward(r, sizes, 1, True, piece_masks, heads))


def ff_backward_body(r, masks):
    r.small[...] = r.small_before[...]
    put_row(r.small, 2, ff_backward(r, 0, False, masks))


def attention_backward_body(r, sizes, piece_masks, heads):
    r.small[...] = r.small_before[...]
    put_row(r.small, 0, attention_backward(r, sizes, 0, False, piece_masks, heads))
    high, low = two_parts(r.small[...])
    last = r.attn_send.shape[0] - 1
    r.attn_send[last] = jnp.concatenate([high, low], axis=0).astype(bf16)
    r.small[...] = high + low


def put_row(packed, which, row):
    first, width = packed.shape[0] - 2, row.shape[1]
    at = which % 3 * width
    packed[first + which // 3 : first + which // 3 + 1, at : at + width] = row


def scatter_pieces(whole, keep, send, masks, place):
    count = len(masks)
    grain = whole.shape[0] // count
    for idx, mask in enumerate(masks):
        target = keep if idx < count // 2 else send
        source = pl.ds(pl.multiple_of((place ^ mask) * grain, grain), grain)
        target[idx % (count // 2)] = whole[source, :].astype(bf16)


def finish(parts, layer_idx, place, shape, before=()):
    width = shape[-1]
    grain = parts[0][0].shape[1]
    count = len(before)

    def kernel(place_ref, *refs):
        sources = refs[: len(parts)]
        refs = refs[len(parts) + count :]
        outs, stages, out_sem = refs[:3], refs[3:-1], refs[-1]
        for source, stage, (_, masks) in zip(sources, stages, parts):
            for idx, mask in enumerate(masks):
                rows = pl.ds(pl.multiple_of((place_ref[3] ^ (mask // 2)) * grain, grain), grain)
                for k, out in enumerate(outs):
                    stage[k, idx] = source[idx, :, k * width : (k + 1) * width].astype(f32)
                    pltpu.make_async_copy(
                        stage.at[k, idx], out.at[layer_idx, rows], out_sem
                    ).start()
        for stage in stages:
            pltpu.make_async_copy(stage, stage, out_sem).wait()

    arrays = [pltpu.with_memory_space_constraint(array, pltpu.VMEM) for array, _ in parts]
    return pl.pallas_call(
        kernel,
        name="layer_%d_ff_grads" % layer_idx,
        in_specs=[pl.BlockSpec(memory_space=pltpu.SMEM)]
        + [pl.BlockSpec(memory_space=pltpu.VMEM)] * len(parts)
        + [pl.BlockSpec(memory_space=pl.ANY)] * count,
        out_specs=[pl.BlockSpec(memory_space=pl.ANY)] * 3,
        out_shape=[jax.ShapeDtypeStruct(shape, f32)] * 3,
        input_output_aliases={1 + len(parts) + k: k for k in range(count)},
        scratch_shapes=[
            pltpu.VMEM((3, array.shape[0], grain, width), f32) for array, _ in parts
        ]
        + [pltpu.SemaphoreType.DMA],
        compiler_params=pltpu.CompilerParams(vmem_limit_bytes=6 * mebibyte),
        cost_estimate=cost(2),
    )(place, *arrays, *before)


def small_body(r):
    width = r.embed.shape[1]
    heads = r.table.shape[0]
    outs = ((r.gain_attn, 0), (r.gain_attn, 1), (r.gain_ff, 0), (r.gain_ff, 1), (r.embed, 0))
    for which, (out, row) in enumerate(outs):
        first = r.packed.shape[0] - 2 + which // 3
        at = which % 3 * width
        out[row : row + 1, :] = r.packed[first : first + 1, at : at + width]
    r.table[...] = r.packed[:heads, : r.table.shape[1]]
    r.write("gain_attn", "gain_ff", "embed", "table")
    r.drain("gain_attn", "gain_ff", "embed", "table")


def pack_body(r, packs):
    rows = r.quarter_0.shape[1]
    at = pl.ds(pl.multiple_of(r.place[1] * rows, rows), rows)
    copies = []
    outs = [r.quarter_0, r.quarter_1]
    for layer_idx in range(2):
        for k, w in enumerate((r.w_gate, r.w_up, r.w_down)):
            copies.append((w.at[layer_idx, at], outs[layer_idx].at[k]))
    if packs:
        outs += [r.block_0, r.block_1]
        inner = r.w_query.shape[2]
        for layer_idx in range(2):
            for k, w in enumerate((r.w_query, r.w_key, r.w_value, r.w_out)):
                lanes = pl.ds(k * inner, inner)
                copies.append((w.at[layer_idx], outs[2 + layer_idx].at[:, lanes]))
    start_all([pltpu.make_async_copy(*ends, r.pack_sem) for ends in copies])
    wait_all(r.pack_sem, *outs)


def order_masks(hops):
    masks = [0]
    for hop in reversed(hops):
        masks = masks + [mask ^ hop for mask in masks]
    return masks


def tie(value, *others):
    return lax.optimization_barrier((value, *others))[0]


def on_device(
    inputs,
    cotangent,
    attention_mask,
    patch_valid,
    buckets,
    mask_embed,
    w_query,
    w_key,
    w_value,
    w_output,
    w_gate,
    w_up,
    w_down,
    gain_attn,
    gain_ff,
    bias_table,
    dp_size,
):
    series, slots, width = inputs.shape
    heads = bias_table.shape[1]
    inner = w_query.shape[2]
    rows = series * slots
    sizes = (series, slots, inner)
    matrix = (rows, width)
    devices = 2 * dp_size
    dp_at = lax.axis_index("dp")
    device_at = 2 * dp_at + lax.axis_index("tensor")
    cotangent = cotangent.reshape(matrix)

    def swap(array, mask):
        return lax.ppermute(array, axes, [(n, n ^ mask) for n in range(devices)])

    def join(left, right):
        return jnp.concatenate([left, right], axis=0)

    bits = [1 << k for k in range(devices.bit_length() - 1)]

    attn_grain = max(16, width // devices)
    attn_count = width // attn_grain
    ff_grain = max(16, 2 * width // dp_size)
    ff_count = width // ff_grain
    quarter_at = lax.rem(dp_at, 4)
    place = jnp.stack(
        [
            device_at,
            quarter_at,
            device_at // (devices // attn_count),
            lax.rem(dp_at, ff_count),
        ]
    ).astype(jnp.int32)

    quarter = width // 4
    own_rows = w_query.shape[1]
    direct = own_rows % 16 == 0
    w_out = jnp.swapaxes(w_output, 1, 2)
    sources = dict(w_gate=w_gate, w_up=w_up, w_down=w_down)
    block_outs = {}
    if direct:
        sources |= dict(w_query=w_query, w_key=w_key, w_value=w_value, w_out=w_out)
        block_outs = {"block_%d" % k: Kept((own_rows, 4 * inner), bf16) for k in range(2)}
    packed = run(
        functools.partial(pack_body, packs=direct),
        "pack",
        dict(
            place=place,
            **{n: pltpu.with_memory_space_constraint(w, pltpu.HBM) for n, w in sources.items()},
        ),
        dict(
            quarter_0=Kept((3, quarter, width), bf16),
            quarter_1=Kept((3, quarter, width), bf16),
            **block_outs,
        ),
        dict(pack_sem=pltpu.SemaphoreType.DMA),
        vmem=4,
    )
    far = bits[2:]

    def prepare(token):
        return run(
            prepare_body,
            "prepare",
            dict(
                inputs=tie(inputs, token).reshape(matrix),
                valid=patch_valid,
                keep=attention_mask,
                embed=mask_embed[None, :],
                gain_attn=gain_attn,
                buckets=buckets,
                table=bias_table,
            ),
            dict(
                x=Kept(matrix, f32),
                a=Kept(matrix, bf16),
                bias=Kept((slots, heads * slots), f32),
                mask=Kept((rows, 128), jnp.int32),
                seen=Kept((rows, 128), jnp.int32),
                wide=Kept((slots, 128), jnp.int32),
            ),
            {},
            micros=3,
        )

    if direct:
        hops_0 = [1] + far[2:] + far[:2] + [2]
        hops_1 = far[2:] + far[:2] + [1, 2]
        block_0, block_1 = packed.block_0, packed.block_1
        got_1 = swap(block_1, hops_1[0])
        got_0 = swap(block_0, hops_0[0])
        ff_0 = swap(tie(packed.quarter_0, got_0), 1)
        ff_1 = swap(tie(packed.quarter_1, ff_0), 1)
        got_ff_0 = swap(ff_0, 4)
        block_0 = join(block_0, got_0)
        block_1 = join(block_1, tie(got_1, block_0))
        for hop_0, hop_1 in zip(hops_0[1:-2], hops_1[1:-2]):
            got_1, got_0 = swap(block_1, hop_1), swap(block_0, hop_0)
            if hop_0 == hops_0[1]:
                start = prepare(block_1)
                got_0 = tie(got_0, ff_0)
            block_0 = join(block_0, got_0)
            block_1 = join(block_1, tie(got_1, block_0))
        block_0 = tie(block_0, block_1)
        got_0 = swap(block_0, hops_0[-2])
        got_1 = swap(block_1, hops_1[-2])
        block_0 = join(block_0, tie(got_0, start.a, got_ff_0, ff_1, got_1))
        ff_0 = join(ff_0, tie(got_ff_0, block_0))
        got_ff_1 = swap(tie(ff_1, ff_0), 4)
        attn_pieces = [(block_0, swap(block_0, 2), order_masks(hops_0[::-1]))]
    else:
        ff_0, ff_1 = swap(packed.quarter_0, 1), swap(packed.quarter_1, 1)
        ff_0 = join(ff_0, swap(ff_0, 4))
        start = prepare(ff_0)
        attn_pieces = []
        rows_of = jnp.concatenate([w_query, w_key, w_value, w_out], axis=2)
        for layer_idx in range(2):
            whole = lax.all_gather(rows_of[layer_idx], axes, axis=0, tiled=True)
            attn_pieces.append((whole, whole, [0]))
    ff_pieces = [(ff_0, swap(ff_0, 2))]

    def attn_ins(layer_idx):
        near, far, masks = attn_pieces[layer_idx]
        return dict(attn_near=Kept(near), attn_far=Kept(far)), masks

    def ff_ins(layer_idx):
        near, far = ff_pieces[layer_idx]
        own = keep_all(dict(w_gate=w_gate, w_up=w_up, w_down=w_down))
        return dict(**own, ff_near=Kept(near), ff_far=Kept(far))

    ff_outs = dict(
        ff_gate_up=Kept((2, width, 2 * width), bf16), ff_down=Kept((2, width, width), bf16)
    )
    grain = own_rows if direct else width
    attn_outs = dict(
        attn_w=Kept((width, 4 * inner), bf16),
        qkv=Kept((rows, 3 * inner), bf16),
        probs=Kept((rows, heads * slots), f32),
        heads=Kept((rows, inner), bf16),
        middle=Kept(matrix, f32),
        ff_in=Kept(matrix, bf16),
    )

    def attention(layer_idx, x, a, after=(), micros=5):
        pieces, masks = attn_ins(layer_idx)
        return run(
            functools.partial(
                attention_body, sizes=sizes, masks=masks, grain=grain, layer_idx=layer_idx
            ),
            "layer_%d_attention" % layer_idx,
            dict(
                place=place,
                x=Kept(x),
                a=Kept(a),
                bias=Kept(start.bias),
                mask=Kept(start.mask),
                gain_ff=gain_ff,
                **pieces,
            ),
            attn_outs,
            {},
            after=after,
            micros=micros,
        )

    first = attention(0, start.x, start.a, micros=10)
    if direct:
        block_1 = join(block_1, tie(got_1, first.ff_in))
        attn_pieces.append((block_1, swap(block_1, 2), order_masks(hops_1[::-1])))
    first_ff = run(
        ff_body,
        "layer_0_ff",
        dict(
            place=place,
            middle=Kept(first.middle),
            ff_in=Kept(first.ff_in),
            gain_attn=gain_attn,
            **ff_ins(0),
        ),
        dict(**ff_outs, x_next=Kept(matrix, f32), a_next=Kept(matrix, bf16)),
        {},
        after=(block_1,) if direct else (),
        micros=3,
    )
    if direct:
        ff_1 = join(ff_1, tie(got_ff_1, first_ff.x_next))
    else:
        ff_1 = join(ff_1, swap(ff_1, 4))
    ff_pieces.append((ff_1, swap(ff_1, 2)))
    second = attention(1, first_ff.x_next, first_ff.a_next, micros=0.1)

    attn_low = devices // attn_count
    attn_hops = ([2, 1] + bits[2:], [2] + bits[3:4] + bits[2:3] + bits[4:] + [1])
    attn_split = [[hop for hop in hops if hop >= attn_low] for hops in attn_hops]
    attn_whole = [hop for hop in bits if hop < attn_low]
    attn_masks = [[mask // attn_low for mask in order_masks(hops)] for hops in attn_split]
    ff_hops = ([2, 4, 1] + bits[3:], [2, 1, 4] + bits[3:])
    ff_split = [[hop for hop in hops if hop // 2 < ff_count] for hops in ff_hops]
    ff_whole = [hop for hop in bits[1:] if hop // 2 >= ff_count]
    ff_share = [hop for hop in bits[:0:-1] if hop // 2 < ff_count]
    ff_masks = [order_masks(hops) for hops in ff_split]
    attn_half = (attn_count // 2, attn_grain, 4 * inner)
    small_shape = (heads + 2, 3 * width)

    attn_back_outs = dict(attn_keep=Kept(attn_half, bf16), attn_send=Kept(attn_half, bf16))
    attn_back_scratch = dict(
        grad_heads=pltpu.VMEM((rows, inner), bf16),
        grad_qkv=pltpu.VMEM((rows, 3 * inner), bf16),
        grad_scores=pltpu.VMEM((rows, heads * slots), bf16),
        attn_grad=pltpu.VMEM((width, 4 * inner), f32),
    )
    ff_back_outs = dict(
        ff_keep=Kept((2 * ff_count, ff_grain, 3 * width // 2), bf16),
        ff_send=Kept((2 * ff_count, ff_grain, 3 * width // 2), bf16),
        small=Kept(small_shape, f32),
        grad_mid=Kept(matrix, f32),
        branch=Kept(matrix, bf16),
    )
    ff_back_scratch = dict(
        hidden=pltpu.VMEM((2, rows, width), bf16),
        grad_gate_up=pltpu.VMEM((2, rows, 2 * width), bf16),
        ff_grad=pltpu.VMEM((2, width, 3 * width), f32),
        grad_low=pltpu.VMEM(matrix, bf16),
    )
    bias_shape = (slots, heads * slots)

    def attn_back_ins(kept, x, a):
        return dict(
            x=Kept(x),
            a=Kept(a),
            gain_attn=gain_attn,
            attn_w=Kept(kept.attn_w),
            qkv=Kept(kept.qkv),
            probs=Kept(kept.probs),
            heads=Kept(kept.heads),
        )

    def add(left, right):
        return (left.astype(f32) + right.astype(f32)).astype(bf16)

    def halving(keep, send, hops, out):
        for step, hop in enumerate(hops):
            got = yield swap(send, hop)
            if step + 1 < len(hops):
                cut = keep.shape[0] // 2
                send = add(keep[cut:], got[cut:])
                keep = add(keep[:cut], got[:cut])
                out["token"] = send
            else:
                out["token"] = keep = add(keep, got)
        out["piece"] = keep

    def summing(piece, hops, out):
        for hop in hops:
            got = yield swap(piece, hop)
            out["token"] = piece = add(piece, got)
        out["piece"] = piece

    def sharing(piece, out):
        masks = [0]
        for hop in ff_share[:-2]:
            got = yield swap(piece, hop)
            out["token"] = piece = join(piece, got)
            masks = masks + [mask ^ hop for mask in masks]
        last, cross = ff_share[-2:]
        sent = swap(piece, last)
        got = yield swap(piece, cross)
        out["early"] = [(piece, masks), (got, [mask ^ cross for mask in masks])]
        out["token"] = got
        masks = [mask ^ last for mask in masks]
        got = yield sent
        out["near"] = [(got, masks)]
        out["token"] = got
        got = yield swap(got, cross)
        out["far"] = [(got, [mask ^ cross for mask in masks])]
        out["token"] = got

    def rounded(values):
        return lax.reduce_precision(values, exponent_bits=8, mantissa_bits=7)

    def with_small(pieces, small):
        high = rounded(small)
        low = rounded(small - high)
        parts = join(high, low).astype(bf16)[None]
        return join(pieces, parts), high + low

    def add_small(small, got):
        parts = got[-1].astype(f32)
        return small + (parts[: small.shape[0]] + parts[small.shape[0] :])

    def attn_chain(part, layer_idx, out):
        small = part.small if layer_idx == 0 else None
        keep, send = part.attn_keep, part.attn_send
        hops = attn_split[layer_idx] + attn_whole
        for step, hop in enumerate(hops):
            got = yield swap(send, hop)
            if small is not None:
                small = add_small(small, got)
                got = got[:-1]
            if step + 1 < len(attn_split[layer_idx]):
                half = keep.shape[0] // 2
                send = add(keep[half:], got[half:])
                keep = add(keep[:half], got[:half])
            else:
                send = keep = add(keep, got)
            if small is not None and step + 1 < len(hops):
                send, small = with_small(send, small)
            out["token"] = send
            if layer_idx == 1 and step == 0:
                send = tie(send, *(yield None))
        piece = keep[0]
        if own_rows < attn_grain:
            first_row = lax.rem(device_at, attn_low) * own_rows
            piece = lax.dynamic_slice_in_dim(piece, first_row, own_rows, axis=0)
        out["done"] = piece.astype(f32)
        out["small"] = small

    def ff_chain(part, out):
        got = yield swap(part.ff_send, 2)
        count = ff_count
        keeps, sends = [], []
        for side in range(2):
            at, half = side * count, count // 2
            sends.append(add(part.ff_keep[at + half : at + count], got[at + half : at + count]))
            keeps.append(add(part.ff_keep[at : at + half], got[at : at + half]))
        out["token"] = tuple(sends)
        for hops in zip(ff_split[0][1:3], ff_split[1][1:3]):
            got = yield tuple(swap(send, hop) for send, hop in zip(sends, hops))
            half = keeps[0].shape[0] // 2
            sends = [add(keep[half:], one[half:]) for keep, one in zip(keeps, got)]
            keeps = [add(keep[:half], one[:half]) for keep, one in zip(keeps, got)]
            out["token"] = tuple(sends)
        keep, send = (jnp.concatenate(sides, axis=2) for sides in (keeps, sends))
        yield from halving(keep, send, ff_split[0][3:], out)
        yield from summing(out["piece"], ff_whole, out)
        yield from sharing(out["piece"], out)

    class Chain:
        def __init__(self, steps, *args):
            self.out = {}
            self.steps = steps(*args, self.out)
            self.arriving = next(self.steps)

        def resume(self, *tokens):
            self.arriving = self.steps.send(tokens)

        def step(self, token, *others):
            if self.arriving is not None:
                tokens = (*(token if isinstance(token, tuple) else (token,)), *others)
                many = isinstance(self.arriving, tuple)
                arrived = self.arriving if many else (self.arriving,)
                arrived = lax.optimization_barrier((*arrived, *tokens))[: len(arrived)]
                arrived = arrived if many else arrived[0]
                self.arriving = None
                try:
                    self.arriving = self.steps.send(arrived)
                except StopIteration:
                    pass
                return self.out["token"]
            return token

    back_ff_1 = run(
        functools.partial(last_ff_body, masks=ff_masks),
        "layer_1_ff",
        dict(
            place=place,
            grad=cotangent,
            gain_ff=gain_ff,
            middle=Kept(second.middle),
            ff_in=Kept(second.ff_in),
            **ff_ins(1),
        ),
        dict(**ff_back_outs, outputs=(matrix, bf16)),
        dict(
            ff_gate_up=pltpu.VMEM((2, width, 2 * width), bf16),
            ff_down=pltpu.VMEM((2, width, width), bf16),
            **ff_back_scratch,
        ),
        micros=8,
        vmem=24,
    )
    ff_1 = Chain(ff_chain, back_ff_1)
    back_1 = run(
        functools.partial(
            last_attention_body, sizes=sizes, piece_masks=attn_masks[1], heads=heads
        ),
        "layer_1_attention_backward",
        dict(
            place=place,
            small_before=Kept(back_ff_1.small),
            grad_mid=Kept(back_ff_1.grad_mid),
            branch=Kept(back_ff_1.branch),
            **attn_back_ins(second, first_ff.x_next, first_ff.a_next),
        ),
        dict(
            **attn_back_outs,
            small=Kept(small_shape, f32),
            grad_next=Kept(matrix, f32),
            bias_acc=Kept(bias_shape, f32),
        ),
        attn_back_scratch,
        micros=6,
        vmem=14,
    )
    attn_1 = Chain(attn_chain, back_1, 1)
    token = ff_1.step(back_1.attn_send)
    token = (attn_1.step(token),)
    back_0 = run(
        functools.partial(ff_backward_body, masks=ff_masks),
        "layer_0_ff_backward",
        dict(
            place=place,
            grad=Kept(back_1.grad_next),
            gain_ff=gain_ff,
            small_before=Kept(back_1.small),
            middle=Kept(first.middle),
            ff_in=Kept(first.ff_in),
            ff_gate_up=Kept(first_ff.ff_gate_up),
            ff_down=Kept(first_ff.ff_down),
        ),
        ff_back_outs,
        ff_back_scratch,
        after=token,
        micros=8,
        vmem=20,
    )
    token = ff_1.step(back_0.branch)
    back_0.ff_send = tie(back_0.ff_send, *token)
    ff_0 = Chain(ff_chain, back_0)
    token = ff_0.step(token)
    back_attn_0 = run(
        functools.partial(
            attention_backward_body, sizes=sizes, piece_masks=attn_masks[0], heads=heads
        ),
        "layer_0_attention_backward",
        dict(
            place=place,
            bias_before=Kept(back_1.bias_acc),
            seen=Kept(start.seen),
            wide=Kept(start.wide),
            small_before=Kept(back_0.small),
            grad_mid=Kept(back_0.grad_mid),
            branch=Kept(back_0.branch),
            **attn_back_ins(first, start.x, start.a),
        ),
        dict(
            attn_keep=Kept(attn_half, bf16),
            attn_send=Kept((attn_count // 2 + 1, *attn_half[1:]), bf16),
            small=Kept(small_shape, f32),
            grad_next=(matrix, f32),
        ),
        dict(
            bias_acc=pltpu.VMEM(bias_shape, f32),
            table_rows=pltpu.VMEM((bias_table.shape[0], heads * slots), f32),
            **attn_back_scratch,
        ),
        after=token,
        micros=7,
        vmem=14,
    )
    attn_0 = Chain(attn_chain, back_attn_0, 0)
    attn_1.resume(back_attn_0.attn_send)
    token = back_attn_0.attn_send
    shape = (2, width, width)
    done = ()
    written = set()

    def write(chain, layer_idx, key, token):
        nonlocal done
        if key not in chain.out or (layer_idx, key) in written:
            return token
        written.add((layer_idx, key))
        parts = chain.out[key]
        tokens = token if isinstance(token, tuple) else (token,)
        arrays = lax.optimization_barrier((*(array for array, _ in parts), *tokens))
        parts = [(array, masks) for array, (_, masks) in zip(arrays, parts)]
        done = finish(parts, layer_idx, place, shape, done)
        return done[0]

    turn = 0
    sums = attn_grads = None
    while ff_0.arriving is not None:
        turn += 1
        chains = (ff_0, ff_1) if turn == 3 or "near" in ff_1.out else (ff_1, ff_0)
        for layer_idx, chain in ((1, ff_1), (0, ff_0)):
            token = write(chain, layer_idx, "near", token)
        for chain in chains:
            token = chain.step(token)
        for key in ("early", "far"):
            for layer_idx, chain in ((1, ff_1), (0, ff_0)):
                token = write(chain, layer_idx, key, token)
        if turn != 2:
            token = attn_0.step(token)
        if turn > 2:
            token = attn_1.step(token)
        if sums is None and attn_0.arriving is None:
            sums = run(
                small_body,
                "small_sums",
                dict(packed=Kept(tie(attn_0.out["small"], token))),
                dict(
                    gain_attn=((2, width), f32),
                    gain_ff=((2, width), f32),
                    embed=((1, width), f32),
                    table=(bias_table.shape[::-1], f32),
                ),
                {},
            )
            token = sums.embed
        if attn_grads is None and attn_0.arriving is None and attn_1.arriving is None:
            both = jnp.stack([attn_0.out["done"], tie(attn_1.out["done"], token)])
            attn_grads = [both[:, :, k * inner : (k + 1) * inner] for k in range(4)]
            attn_grads[3] = jnp.swapaxes(attn_grads[3], 1, 2)
            token = tuple(attn_grads)
    return (
        back_ff_1.outputs.reshape(inputs.shape),
        back_attn_0.grad_next.reshape(inputs.shape),
        *attn_grads,
        *done,
        sums.gain_attn,
        sums.gain_ff,
        sums.table.T,
        sums.embed[0],
    )


def solution(mesh):
    placed = (
        P(("dp", "tensor"), None, None),
        P(("dp", "tensor"), None, None),
        P(("dp", "tensor"), None),
        P(("dp", "tensor"), None),
        P(),
        P(),
        P(None, ("dp", "tensor"), None),
        P(None, ("dp", "tensor"), None),
        P(None, ("dp", "tensor"), None),
        P(None, None, ("dp", "tensor")),
        P(None, None, "tensor"),
        P(None, None, "tensor"),
        P(None, "tensor", None),
        P(),
        P(),
        P(),
    )
    return jax.shard_map(
        functools.partial(on_device, dp_size=mesh.shape["dp"]),
        mesh=mesh,
        in_specs=placed,
        out_specs=(
            P(("dp", "tensor"), None, None),
            P(("dp", "tensor"), None, None),
            P(None, ("dp", "tensor"), None),
            P(None, ("dp", "tensor"), None),
            P(None, ("dp", "tensor"), None),
            P(None, None, ("dp", "tensor")),
            P(None, None, "tensor"),
            P(None, None, "tensor"),
            P(None, "tensor", None),
            P(),
            P(),
            P(),
            P(),
        ),
        check_vma=False,
    )
```

```python
import functools
import types

import jax
import jax.numpy as jnp
from jax import lax
from jax.experimental import pallas as pl
from jax.experimental.pallas import tpu as pltpu
from jax.sharding import PartitionSpec as P

norm_eps = 1e-06
masked_score = -1e30
bf16 = jnp.bfloat16
f32 = jnp.float32
axes = ("dp", "tensor")
mebibyte = 1024 * 1024
raw_names = ("w_query", "w_key", "w_value", "w_out", "w_gate", "w_up", "w_down")
scalar_names = ("place", "table")


def dot_nn(left, right):
    return lax.dot_general(left, right, (((1,), (0,)), ((), ())), preferred_element_type=f32)


def dot_nt(left, right):
    return lax.dot_general(left, right, (((1,), (1,)), ((), ())), preferred_element_type=f32)


def dot_tn(left, right):
    return lax.dot_general(left, right, (((0,), (0,)), ((), ())), preferred_element_type=f32)


def inverse_rms(values):
    return lax.rsqrt(jnp.mean(values * values, axis=-1, keepdims=True) + norm_eps)


def norm_back(values, gain, grad_out):
    scale = inverse_rms(values)
    pulled = grad_out * gain
    mean_part = jnp.mean(pulled * values, axis=-1, keepdims=True)
    grad_in = scale * pulled - values * (scale * scale * scale) * mean_part
    return grad_in, jnp.sum(grad_out * values * scale, axis=0, keepdims=True)


def gelu_terms(gate_act):
    square = gate_act * gate_act
    bent = jnp.tanh(0.7978845608028654 * gate_act * (1.0 + 0.044715 * square))
    half = 0.5 * (1.0 + bent)
    slope = half + 0.5 * gate_act * (1.0 - bent * bent) * (
        0.7978845608028654 * (1.0 + 3.0 * 0.044715 * square)
    )
    return gate_act * half, slope


def cost(micros):
    return pl.CostEstimate(flops=int(micros * 1.15e9), bytes_accessed=0, transcendentals=0)


def run(body, name, ins, outs, scratch, after=(), micros=1, vmem=8):
    in_names, out_names, scratch_names = list(ins), list(outs), list(scratch)
    direct = {n for n in in_names if n in scalar_names + raw_names or isinstance(ins[n], Kept)}
    staged = [n for n in in_names if n not in direct]
    copied = [n for n in out_names if not isinstance(outs[n], Kept)]
    in_sems = {n: i for i, n in enumerate(staged)}
    out_sems = {n: i for i, n in enumerate(copied)}

    def kernel(*refs):
        refs = list(refs)
        sources = dict(zip(in_names, refs))
        refs = refs[len(in_names) + len(after) :]
        targets = dict(zip(out_names, refs))
        refs = refs[len(out_names) :]
        space = dict(zip(scratch_names, refs))
        refs = refs[len(scratch_names) :]
        buffers = dict(zip(staged + copied, refs))
        sems_in, sems_out = refs[len(staged) + len(copied) :]
        kept = {n: ref for n, ref in targets.items() if n not in out_sems}
        r = types.SimpleNamespace(**space, **buffers, **kept)
        for n in direct:
            setattr(r, n, sources[n])

        def copy_in(n):
            return pltpu.make_async_copy(sources[n], buffers[n], sems_in.at[in_sems[n]])

        def copy_out(n):
            return pltpu.make_async_copy(buffers[n], targets[n], sems_out.at[out_sems[n]])

        r.fetch = lambda *names: [copy_in(n).start() for n in names if n in in_sems]
        r.need = lambda *names: [copy_in(n).wait() for n in names if n in in_sems]
        r.write = lambda *names: [copy_out(n).start() for n in names if n in out_sems]
        r.drain = lambda *names: [copy_out(n).wait() for n in names if n in out_sems]
        body(r)

    def in_space(n):
        if n in scalar_names:
            return pltpu.SMEM
        return pltpu.VMEM if isinstance(ins[n], Kept) else pl.ANY

    results = pl.pallas_call(
        kernel,
        name=name,
        in_specs=[pl.BlockSpec(memory_space=in_space(n)) for n in in_names]
        + [pl.BlockSpec(memory_space=pl.ANY) for _ in after],
        out_specs=[
            pl.BlockSpec(memory_space=pltpu.VMEM if isinstance(out, Kept) else pl.ANY)
            for out in outs.values()
        ],
        out_shape=[
            pltpu.VMEM(*out.what) if isinstance(out, Kept) else jax.ShapeDtypeStruct(*out)
            for out in outs.values()
        ],
        scratch_shapes=list(scratch.values())
        + [pltpu.VMEM(ins[n].shape, ins[n].dtype) for n in staged]
        + [pltpu.VMEM(*outs[n]) for n in copied]
        + [
            pltpu.SemaphoreType.DMA((max(1, len(staged)),)),
            pltpu.SemaphoreType.DMA((max(1, len(copied)),)),
        ],
        compiler_params=pltpu.CompilerParams(vmem_limit_bytes=vmem * mebibyte),
        cost_estimate=cost(micros),
    )(
        *[
            pltpu.with_memory_space_constraint(value.what, pltpu.VMEM)
            if isinstance(value, Kept)
            else value
            for value in ins.values()
        ],
        *after,
    )
    return types.SimpleNamespace(**dict(zip(outs, results)))


class Kept:
    def __init__(self, *what):
        self.what = what[0] if len(what) == 1 else what


def keep_all(names):
    return {name: Kept(value) for name, value in names.items()}


def chunks(extent, size):
    size = min(size, extent)
    return [slice(start, start + size) for start in range(0, extent, size)]


def lay_out_attention(r, masks, rows):
    for idx, mask in enumerate(masks):
        half, at = divmod(idx, max(1, len(masks) // 2))
        source = r.attn_near if half == 0 else r.attn_far
        place = pl.multiple_of((r.place[0] ^ mask) * rows, rows) if len(masks) > 1 else 0
        r.attn_w[pl.ds(place, rows), :] = source[at * rows : (at + 1) * rows, :]


def lay_out_ff(r, layer_idx):
    width = r.ff_down.shape[-1]
    for k, own in enumerate((r.w_gate, r.w_up)):
        r.ff_gate_up[0, :, k * width : (k + 1) * width] = own[layer_idx]
    r.ff_down[0] = r.w_down[layer_idx]
    part = r.ff_near.shape[1]
    for source, base in ((r.ff_near, 0), (r.ff_far, 1)):
        for m in range(2):
            rows = pl.ds(pl.multiple_of((r.place[1] ^ (2 * m + base)) * part, part), part)
            for k in range(2):
                r.ff_gate_up[1, rows, k * width : (k + 1) * width] = source[3 * m + k]
            r.ff_down[1, rows, :] = source[3 * m + 2]


def start_all(copies):
    for copy in copies:
        copy.start()


def wait_all(sem, *buffers):
    for whole in buffers:
        pltpu.make_async_copy(whole, whole, sem).wait()


def lane_low(rows):
    return lax.broadcasted_iota(jnp.int32, (rows, 128), 1) < 64


def lane_halves():
    low = lane_low(1).astype(f32)
    return low.astype(bf16), (1.0 - low).astype(bf16)


def pair_blocks(rows, low, high):
    return jnp.concatenate([rows * low, rows * high], axis=0)


def own_blocks(both, is_low):
    half = both.shape[0] // 2
    return jnp.where(is_low, both[:half], both[half:]).astype(bf16)


def attention_forward(r, x_ref, a_ref, sizes, layer_idx):
    series, slots, inner = sizes
    rows = series * slots
    for part in chunks(rows, 256):
        r.qkv[part, :] = dot_nn(a_ref[part, :], r.attn_w[:, : 3 * inner]).astype(bf16)
    is_low = lane_low(slots)
    low, high = lane_halves()
    for s in range(series):
        here = slice(s * slots, (s + 1) * slots)
        keep = r.mask[here, :] == 1
        for start in range(0, inner, 128):
            at = slice(start, start + 128)
            query = r.qkv[here, at]
            keys = r.qkv[here, inner + start : inner + start + 128]
            scores = dot_nt(keys, pair_blocks(query, low, high)) + r.bias[:, at]
            scores = jnp.where(keep, scores, masked_score)
            exps = jnp.exp(scores - jnp.max(scores, axis=0, keepdims=True))
            r.probs[here, at] = exps / jnp.sum(exps, axis=0, keepdims=True)
    for s in range(series):
        here = slice(s * slots, (s + 1) * slots)
        for start in range(0, inner, 128):
            at = slice(start, start + 128)
            values = r.qkv[here, 2 * inner + start : 2 * inner + start + 128]
            both = dot_tn(r.probs[here, at].astype(bf16), values)
            r.heads[here, at] = own_blocks(both, is_low)
    gain = r.gain_ff[layer_idx : layer_idx + 1, :]
    for part in chunks(rows, 256):
        middle = x_ref[part, :] + dot_nt(r.heads[part, :], r.attn_w[:, 3 * inner :])
        r.middle[part, :] = middle
        r.ff_in[part, :] = (middle * inverse_rms(middle) * gain).astype(bf16)


def prepare_body(r):
    names = ("inputs", "valid", "keep", "embed", "gain_attn", "buckets")
    r.fetch(*names)
    r.need(*names)
    series, slots = r.valid.shape
    gain = r.gain_attn[0:1, :]
    valid = jnp.transpose(r.valid[...].astype(f32))
    keep = jnp.transpose(r.keep[...].astype(f32))
    for s in range(series):
        here = slice(s * slots, (s + 1) * slots)
        seen = valid[:, s : s + 1]
        x = jnp.where(seen == 1.0, r.inputs[here, :].astype(f32), r.embed[...])
        r.x[here, :] = x
        r.a[here, :] = (x * inverse_rms(x) * gain).astype(bf16)
        r.seen[here, :] = jnp.broadcast_to(seen, (slots, 128)).astype(jnp.int32)
        r.mask[here, :] = jnp.broadcast_to(keep[:, s : s + 1], (slots, 128)).astype(jnp.int32)
    turned = jnp.transpose(r.buckets[...].astype(f32)).astype(jnp.int32)
    wide = jnp.concatenate([turned, turned], axis=1)
    r.wide[...] = wide
    is_low = lane_low(slots)
    bucket_count, heads = r.table.shape
    for pair in range(heads // 2):
        bias = jnp.zeros((slots, 128), f32)
        for idx in range(bucket_count):
            entry = jnp.where(is_low, r.table[idx, 2 * pair], r.table[idx, 2 * pair + 1])
            bias = jnp.where(wide == idx, entry, bias)
        r.bias[:, pair * 128 : (pair + 1) * 128] = bias


def attention_body(r, sizes, masks, grain, layer_idx):
    r.fetch("gain_ff")
    lay_out_attention(r, masks, grain)
    r.need("gain_ff")
    attention_forward(r, r.x, r.a, sizes, layer_idx)


def ff_body(r):
    r.fetch("gain_attn")
    lay_out_ff(r, 0)
    r.need("gain_attn")
    width = r.middle.shape[1]
    for part in chunks(r.middle.shape[0], 256):
        x_next = r.middle[part, :]
        for half in range(2):
            both = dot_nn(r.ff_in[part, :], r.ff_gate_up[half])
            hidden = (gelu_terms(both[:, :width])[0] * both[:, width:]).astype(bf16)
            x_next = x_next + dot_nn(hidden, r.ff_down[half])
        r.x_next[part, :] = x_next
        r.a_next[part, :] = (x_next * inverse_rms(x_next) * r.gain_attn[1:2, :]).astype(bf16)


def ff_backward(r, layer_idx, last, masks):
    rows, width = r.middle.shape
    r.fetch("grad", "gain_ff")
    if last:
        lay_out_ff(r, layer_idx)
    r.need("grad", "gain_ff")
    gain_ff = r.gain_ff[layer_idx : layer_idx + 1, :]
    gain_total = jnp.zeros((1, width), f32)
    for part in chunks(rows, 256):
        grad = r.grad[part, :].astype(f32)
        rounded = grad.astype(bf16)
        ff_rows = r.ff_in[part, :]
        back = None
        middle = r.middle[part, :]
        total = middle
        for half in range(2):
            both = dot_nn(ff_rows, r.ff_gate_up[half])
            grad_hidden = dot_nt(rounded, r.ff_down[half])
            gate_act, up_act = both[:, :width], both[:, width:]
            mixed, slope = gelu_terms(gate_act)
            hidden = (mixed * up_act).astype(bf16)
            r.hidden[half, part, :] = hidden
            r.grad_gate_up[half, part, :width] = (grad_hidden * up_act * slope).astype(bf16)
            r.grad_gate_up[half, part, width:] = (grad_hidden * mixed).astype(bf16)
            pulled = r.grad_gate_up[half, part, :]
            if last:
                total = total + dot_nn(hidden, r.ff_down[half])
            term = dot_nt(pulled, r.ff_gate_up[half])
            back = term if back is None else back + term
        if last:
            r.outputs[part, :] = total.astype(bf16)
        grad_mid, gain_part = norm_back(middle, gain_ff, back)
        gain_total += gain_part
        grad_mid = grad + grad_mid
        r.grad_mid[part, :] = grad_mid
        r.branch[part, :] = grad_mid.astype(bf16)
        r.grad_low[part, :] = rounded
    if last:
        r.write("outputs")
    for half in range(2):
        r.ff_grad[half, :, : 2 * width] = dot_tn(r.ff_in[...], r.grad_gate_up[half])
        r.ff_grad[half, :, 2 * width :] = dot_tn(r.hidden[half], r.grad_low[...])
    half_count = len(masks[0]) // 2
    grain, columns = r.ff_keep.shape[1:]
    for side, side_masks in enumerate(masks):
        lanes = slice(side * columns, (side + 1) * columns)
        for idx, mask in enumerate(side_masks):
            target = r.ff_keep if idx < half_count else r.ff_send
            piece = pl.ds(pl.multiple_of((r.place[3] ^ (mask // 2)) * grain, grain), grain)
            target[side * half_count + idx % half_count] = r.ff_grad[mask % 2, piece, lanes].astype(
                bf16
            )
    if last:
        r.drain("outputs")
    return gain_total


def attention_backward(r, sizes, layer_idx, last, piece_masks, heads):
    series, slots, inner = sizes
    rows = series * slots
    width = r.x.shape[1]
    r.fetch("gain_attn")
    for part in chunks(rows, 256):
        r.grad_heads[part, :] = dot_nn(r.branch[part, :], r.attn_w[:, 3 * inner :]).astype(bf16)
    is_low = lane_low(slots)
    low, high = lane_halves()
    for start in range(0, inner, 128):
        at = slice(start, start + 128)
        bias_total = jnp.zeros((slots, 128), f32) if last else r.bias_before[:, at]
        for s in range(series):
            here = slice(s * slots, (s + 1) * slots)
            probs = r.probs[here, at]
            values = r.qkv[here, 2 * inner + start : 2 * inner + start + 128]
            grad_probs = dot_nt(values, pair_blocks(r.grad_heads[here, at], low, high))
            inner_sum = jnp.sum(probs * grad_probs, axis=0, keepdims=True)
            grad_scores = (probs * (grad_probs - inner_sum)).astype(bf16)
            r.grad_scores[here, at] = grad_scores
            bias_total = bias_total + grad_scores.astype(f32)
        r.bias_acc[:, at] = bias_total
    for s in range(series):
        here = slice(s * slots, (s + 1) * slots)
        for start in range(0, inner, 128):
            at = slice(start, start + 128)
            key_at = slice(inner + start, inner + start + 128)
            value_at = slice(2 * inner + start, 2 * inner + start + 128)
            grad_scores = r.grad_scores[here, at]
            r.grad_qkv[here, key_at] = dot_nn(
                grad_scores, pair_blocks(r.qkv[here, at], low, high)
            ).astype(bf16)
            r.grad_qkv[here, value_at] = dot_nn(
                r.probs[here, at].astype(bf16), pair_blocks(r.grad_heads[here, at], low, high)
            ).astype(bf16)
            r.grad_qkv[here, at] = own_blocks(dot_tn(grad_scores, r.qkv[here, key_at]), is_low)
    r.attn_grad[:, : 3 * inner] = dot_tn(r.a[...], r.grad_qkv[...])
    r.attn_grad[:, 3 * inner :] = dot_tn(r.branch[...], r.heads[...])
    scatter_pieces(r.attn_grad, r.attn_keep, r.attn_send, piece_masks, r.place[2])
    r.need("gain_attn")
    gain_attn = r.gain_attn[layer_idx : layer_idx + 1, :]
    gain_total = jnp.zeros((1, width), f32)
    embed_total = jnp.zeros((1, width), f32)
    for part in chunks(rows, 256):
        grad_normed = dot_nt(r.grad_qkv[part, :], r.attn_w[:, : 3 * inner])
        grad_in, gain_part = norm_back(r.x[part, :], gain_attn, grad_normed)
        gain_total += gain_part
        grad_in = r.grad_mid[part, :] + grad_in
        if last:
            r.grad_next[part, :] = grad_in
        else:
            seen = r.seen[part, 0:1] == 1
            r.grad_next[part, :] = jnp.where(seen, grad_in, 0.0)
            embed_total += jnp.sum(jnp.where(seen, 0.0, grad_in), axis=0, keepdims=True)
    r.write("grad_next")
    if not last:
        put_row(r.small, 4, embed_total)
        head_size = inner // heads
        for idx in range(r.table_rows.shape[0]):
            for start in range(0, inner, 128):
                at = slice(start, start + 128)
                chosen = jnp.where(r.wide[...] == idx, r.bias_acc[:, at], 0.0)
                r.table_rows[idx : idx + 1, at] = jnp.sum(chosen, axis=0, keepdims=True)
        lane = lax.broadcasted_iota(jnp.int32, (r.table_rows.shape[0], 128), 1)
        table = jnp.zeros(lane.shape, f32)
        for head in range(heads):
            cut = r.table_rows[:, head * head_size : (head + 1) * head_size]
            table = jnp.where(lane == head, jnp.sum(cut, axis=1, keepdims=True), table)
        r.small[:heads, : table.shape[0]] = jnp.transpose(table)[:heads, :]
    r.drain("grad_next")
    return gain_total


def two_parts(values):
    high = values.astype(bf16).astype(f32)
    return high, (values - high).astype(bf16).astype(f32)


def last_ff_body(r, masks):
    r.small[...] = jnp.zeros(r.small.shape, f32)
    put_row(r.small, 3, ff_backward(r, 1, True, masks))


def last_attention_body(r, sizes, piece_masks, heads):
    r.small[...] = r.small_before[...]
    put_row(r.small, 1, attention_backward(r, sizes, 1, True, piece_masks, heads))


def ff_backward_body(r, masks):
    r.small[...] = r.small_before[...]
    put_row(r.small, 2, ff_backward(r, 0, False, masks))


def attention_backward_body(r, sizes, piece_masks, heads):
    r.small[...] = r.small_before[...]
    put_row(r.small, 0, attention_backward(r, sizes, 0, False, piece_masks, heads))
    high, low = two_parts(r.small[...])
    last = r.attn_send.shape[0] - 1
    r.attn_send[last] = jnp.concatenate([high, low], axis=0).astype(bf16)
    r.small[...] = high + low


def put_row(packed, which, row):
    first, width = packed.shape[0] - 2, row.shape[1]
    at = which % 3 * width
    packed[first + which // 3 : first + which // 3 + 1, at : at + width] = row


def scatter_pieces(whole, keep, send, masks, place):
    count = len(masks)
    grain = whole.shape[0] // count
    for idx, mask in enumerate(masks):
        target = keep if idx < count // 2 else send
        source = pl.ds(pl.multiple_of((place ^ mask) * grain, grain), grain)
        target[idx % (count // 2)] = whole[source, :].astype(bf16)


def finish(parts, layer_idx, place, shape, before=()):
    width = shape[-1]
    grain = parts[0][0].shape[1]
    count = len(before)

    def kernel(place_ref, *refs):
        sources = refs[: len(parts)]
        refs = refs[len(parts) + count :]
        outs, stages, out_sem = refs[:3], refs[3:-1], refs[-1]
        for source, stage, (_, masks) in zip(sources, stages, parts):
            for idx, mask in enumerate(masks):
                rows = pl.ds(pl.multiple_of((place_ref[3] ^ (mask // 2)) * grain, grain), grain)
                for k, out in enumerate(outs):
                    stage[k, idx] = source[idx, :, k * width : (k + 1) * width].astype(f32)
                    pltpu.make_async_copy(
                        stage.at[k, idx], out.at[layer_idx, rows], out_sem
                    ).start()
        for stage in stages:
            pltpu.make_async_copy(stage, stage, out_sem).wait()

    arrays = [pltpu.with_memory_space_constraint(array, pltpu.VMEM) for array, _ in parts]
    return pl.pallas_call(
        kernel,
        name="layer_%d_ff_grads" % layer_idx,
        in_specs=[pl.BlockSpec(memory_space=pltpu.SMEM)]
        + [pl.BlockSpec(memory_space=pltpu.VMEM)] * len(parts)
        + [pl.BlockSpec(memory_space=pl.ANY)] * count,
        out_specs=[pl.BlockSpec(memory_space=pl.ANY)] * 3,
        out_shape=[jax.ShapeDtypeStruct(shape, f32)] * 3,
        input_output_aliases={1 + len(parts) + k: k for k in range(count)},
        scratch_shapes=[
            pltpu.VMEM((3, array.shape[0], grain, width), f32) for array, _ in parts
        ]
        + [pltpu.SemaphoreType.DMA],
        compiler_params=pltpu.CompilerParams(vmem_limit_bytes=6 * mebibyte),
        cost_estimate=cost(2),
    )(place, *arrays, *before)


def small_body(r):
    width = r.embed.shape[1]
    heads = r.table.shape[0]
    outs = ((r.gain_attn, 0), (r.gain_attn, 1), (r.gain_ff, 0), (r.gain_ff, 1), (r.embed, 0))
    for which, (out, row) in enumerate(outs):
        first = r.packed.shape[0] - 2 + which // 3
        at = which % 3 * width
        out[row : row + 1, :] = r.packed[first : first + 1, at : at + width]
    r.table[...] = r.packed[:heads, : r.table.shape[1]]
    r.write("gain_attn", "gain_ff", "embed", "table")
    r.drain("gain_attn", "gain_ff", "embed", "table")


def pack_body(r, packs):
    rows = r.quarter_0.shape[1]
    at = pl.ds(pl.multiple_of(r.place[1] * rows, rows), rows)
    copies = []
    outs = [r.quarter_0, r.quarter_1]
    for layer_idx in range(2):
        for k, w in enumerate((r.w_gate, r.w_up, r.w_down)):
            copies.append((w.at[layer_idx, at], outs[layer_idx].at[k]))
    if packs:
        outs += [r.block_0, r.block_1]
        inner = r.w_query.shape[2]
        for layer_idx in range(2):
            for k, w in enumerate((r.w_query, r.w_key, r.w_value, r.w_out)):
                lanes = pl.ds(k * inner, inner)
                copies.append((w.at[layer_idx], outs[2 + layer_idx].at[:, lanes]))
    start_all([pltpu.make_async_copy(*ends, r.pack_sem) for ends in copies])
    wait_all(r.pack_sem, *outs)


def order_masks(hops):
    masks = [0]
    for hop in reversed(hops):
        masks = masks + [mask ^ hop for mask in masks]
    return masks


def tie(value, *others):
    return lax.optimization_barrier((value, *others))[0]


def on_device(
    inputs,
    cotangent,
    attention_mask,
    patch_valid,
    buckets,
    mask_embed,
    w_query,
    w_key,
    w_value,
    w_output,
    w_gate,
    w_up,
    w_down,
    gain_attn,
    gain_ff,
    bias_table,
    dp_size,
):
    series, slots, width = inputs.shape
    heads = bias_table.shape[1]
    inner = w_query.shape[2]
    rows = series * slots
    sizes = (series, slots, inner)
    matrix = (rows, width)
    devices = 2 * dp_size
    dp_at = lax.axis_index("dp")
    device_at = 2 * dp_at + lax.axis_index("tensor")
    cotangent = cotangent.reshape(matrix)

    def swap(array, mask):
        return lax.ppermute(array, axes, [(n, n ^ mask) for n in range(devices)])

    def join(left, right):
        return jnp.concatenate([left, right], axis=0)

    bits = [1 << k for k in range(devices.bit_length() - 1)]

    attn_grain = max(16, width // devices)
    attn_count = width // attn_grain
    ff_grain = max(16, 2 * width // dp_size)
    ff_count = width // ff_grain
    quarter_at = lax.rem(dp_at, 4)
    place = jnp.stack(
        [
            device_at,
            quarter_at,
            device_at // (devices // attn_count),
            lax.rem(dp_at, ff_count),
        ]
    ).astype(jnp.int32)

    quarter = width // 4
    own_rows = w_query.shape[1]
    direct = own_rows % 16 == 0
    w_out = jnp.swapaxes(w_output, 1, 2)
    sources = dict(w_gate=w_gate, w_up=w_up, w_down=w_down)
    block_outs = {}
    if direct:
        sources |= dict(w_query=w_query, w_key=w_key, w_value=w_value, w_out=w_out)
        block_outs = {"block_%d" % k: Kept((own_rows, 4 * inner), bf16) for k in range(2)}
    packed = run(
        functools.partial(pack_body, packs=direct),
        "pack",
        dict(
            place=place,
            **{n: pltpu.with_memory_space_constraint(w, pltpu.HBM) for n, w in sources.items()},
        ),
        dict(
            quarter_0=Kept((3, quarter, width), bf16),
            quarter_1=Kept((3, quarter, width), bf16),
            **block_outs,
        ),
        dict(pack_sem=pltpu.SemaphoreType.DMA),
        vmem=4,
    )
    far = bits[2:]

    def prepare(token):
        return run(
            prepare_body,
            "prepare",
            dict(
                inputs=tie(inputs, token).reshape(matrix),
                valid=patch_valid,
                keep=attention_mask,
                embed=mask_embed[None, :],
                gain_attn=gain_attn,
                buckets=buckets,
                table=bias_table,
            ),
            dict(
                x=Kept(matrix, f32),
                a=Kept(matrix, bf16),
                bias=Kept((slots, heads * slots), f32),
                mask=Kept((rows, 128), jnp.int32),
                seen=Kept((rows, 128), jnp.int32),
                wide=Kept((slots, 128), jnp.int32),
            ),
            {},
            micros=3,
        )

    if direct:
        hops_0 = [1] + far[2:] + far[:2] + [2]
        hops_1 = far[2:] + far[:2] + [1, 2]
        block_0, block_1 = packed.block_0, packed.block_1
        got_1 = swap(block_1, hops_1[0])
        got_0 = swap(block_0, hops_0[0])
        ff_0 = swap(tie(packed.quarter_0, got_0), 1)
        ff_1 = swap(tie(packed.quarter_1, ff_0), 1)
        got_ff_0 = swap(ff_0, 4)
        block_0 = join(block_0, got_0)
        block_1 = join(block_1, tie(got_1, block_0))
        for hop_0, hop_1 in zip(hops_0[1:-2], hops_1[1:-2]):
            got_1, got_0 = swap(block_1, hop_1), swap(block_0, hop_0)
            if hop_0 == hops_0[1]:
                start = prepare(block_1)
                got_0 = tie(got_0, ff_0)
            block_0 = join(block_0, got_0)
            block_1 = join(block_1, tie(got_1, block_0))
        block_0 = tie(block_0, block_1)
        got_0 = swap(block_0, hops_0[-2])
        got_1 = swap(block_1, hops_1[-2])
        block_0 = join(block_0, tie(got_0, start.a, got_ff_0, ff_1, got_1))
        ff_0 = join(ff_0, tie(got_ff_0, block_0))
        got_ff_1 = swap(tie(ff_1, ff_0), 4)
        attn_pieces = [(block_0, swap(block_0, 2), order_masks(hops_0[::-1]))]
    else:
        ff_0, ff_1 = swap(packed.quarter_0, 1), swap(packed.quarter_1, 1)
        ff_0 = join(ff_0, swap(ff_0, 4))
        start = prepare(ff_0)
        attn_pieces = []
        rows_of = jnp.concatenate([w_query, w_key, w_value, w_out], axis=2)
        for layer_idx in range(2):
            whole = lax.all_gather(rows_of[layer_idx], axes, axis=0, tiled=True)
            attn_pieces.append((whole, whole, [0]))
    ff_pieces = [(ff_0, swap(ff_0, 2))]

    def attn_ins(layer_idx):
        near, far, masks = attn_pieces[layer_idx]
        return dict(attn_near=Kept(near), attn_far=Kept(far)), masks

    def ff_ins(layer_idx):
        near, far = ff_pieces[layer_idx]
        own = keep_all(dict(w_gate=w_gate, w_up=w_up, w_down=w_down))
        return dict(**own, ff_near=Kept(near), ff_far=Kept(far))

    ff_outs = dict(
        ff_gate_up=Kept((2, width, 2 * width), bf16), ff_down=Kept((2, width, width), bf16)
    )
    grain = own_rows if direct else width
    attn_outs = dict(
        attn_w=Kept((width, 4 * inner), bf16),
        qkv=Kept((rows, 3 * inner), bf16),
        probs=Kept((rows, heads * slots), f32),
        heads=Kept((rows, inner), bf16),
        middle=Kept(matrix, f32),
        ff_in=Kept(matrix, bf16),
    )

    def attention(layer_idx, x, a, after=(), micros=5):
        pieces, masks = attn_ins(layer_idx)
        return run(
            functools.partial(
                attention_body, sizes=sizes, masks=masks, grain=grain, layer_idx=layer_idx
            ),
            "layer_%d_attention" % layer_idx,
            dict(
                place=place,
                x=Kept(x),
                a=Kept(a),
                bias=Kept(start.bias),
                mask=Kept(start.mask),
                gain_ff=gain_ff,
                **pieces,
            ),
            attn_outs,
            {},
            after=after,
            micros=micros,
        )

    first = attention(0, start.x, start.a, micros=10)
    if direct:
        block_1 = join(block_1, tie(got_1, first.ff_in))
        attn_pieces.append((block_1, swap(block_1, 2), order_masks(hops_1[::-1])))
    first_ff = run(
        ff_body,
        "layer_0_ff",
        dict(
            place=place,
            middle=Kept(first.middle),
            ff_in=Kept(first.ff_in),
            gain_attn=gain_attn,
            **ff_ins(0),
        ),
        dict(**ff_outs, x_next=Kept(matrix, f32), a_next=Kept(matrix, bf16)),
        {},
        after=(block_1,) if direct else (),
        micros=3,
    )
    if direct:
        ff_1 = join(ff_1, tie(got_ff_1, first_ff.x_next))
    else:
        ff_1 = join(ff_1, swap(ff_1, 4))
    ff_pieces.append((ff_1, swap(ff_1, 2)))
    second = attention(1, first_ff.x_next, first_ff.a_next, micros=0.1)

    attn_low = devices // attn_count
    attn_hops = ([2, 1] + bits[2:], [2] + bits[3:4] + bits[2:3] + bits[4:] + [1])
    attn_split = [[hop for hop in hops if hop >= attn_low] for hops in attn_hops]
    attn_whole = [hop for hop in bits if hop < attn_low]
    attn_masks = [[mask // attn_low for mask in order_masks(hops)] for hops in attn_split]
    ff_hops = ([2, 4, 1] + bits[3:], [2, 1, 4] + bits[3:])
    ff_split = [[hop for hop in hops if hop // 2 < ff_count] for hops in ff_hops]
    ff_whole = [hop for hop in bits[1:] if hop // 2 >= ff_count]
    ff_share = [hop for hop in bits[:0:-1] if hop // 2 < ff_count]
    ff_masks = [order_masks(hops) for hops in ff_split]
    attn_half = (attn_count // 2, attn_grain, 4 * inner)
    small_shape = (heads + 2, 3 * width)

    attn_back_outs = dict(attn_keep=Kept(attn_half, bf16), attn_send=Kept(attn_half, bf16))
    attn_back_scratch = dict(
        grad_heads=pltpu.VMEM((rows, inner), bf16),
        grad_qkv=pltpu.VMEM((rows, 3 * inner), bf16),
        grad_scores=pltpu.VMEM((rows, heads * slots), bf16),
        attn_grad=pltpu.VMEM((width, 4 * inner), f32),
    )
    ff_back_outs = dict(
        ff_keep=Kept((2 * ff_count, ff_grain, 3 * width // 2), bf16),
        ff_send=Kept((2 * ff_count, ff_grain, 3 * width // 2), bf16),
        small=Kept(small_shape, f32),
        grad_mid=Kept(matrix, f32),
        branch=Kept(matrix, bf16),
    )
    ff_back_scratch = dict(
        hidden=pltpu.VMEM((2, rows, width), bf16),
        grad_gate_up=pltpu.VMEM((2, rows, 2 * width), bf16),
        ff_grad=pltpu.VMEM((2, width, 3 * width), f32),
        grad_low=pltpu.VMEM(matrix, bf16),
    )
    bias_shape = (slots, heads * slots)

    def attn_back_ins(kept, x, a):
        return dict(
            x=Kept(x),
            a=Kept(a),
            gain_attn=gain_attn,
            attn_w=Kept(kept.attn_w),
            qkv=Kept(kept.qkv),
            probs=Kept(kept.probs),
            heads=Kept(kept.heads),
        )

    def add(left, right):
        return (left.astype(f32) + right.astype(f32)).astype(bf16)

    def halving(keep, send, hops, out):
        for step, hop in enumerate(hops):
            got = yield swap(send, hop)
            if step + 1 < len(hops):
                cut = keep.shape[0] // 2
                send = add(keep[cut:], got[cut:])
                keep = add(keep[:cut], got[:cut])
                out["token"] = send
            else:
                out["token"] = keep = add(keep, got)
        out["piece"] = keep

    def summing(piece, hops, out):
        for hop in hops:
            got = yield swap(piece, hop)
            out["token"] = piece = add(piece, got)
        out["piece"] = piece

    def sharing(piece, out):
        masks = [0]
        for hop in ff_share[:-2]:
            got = yield swap(piece, hop)
            out["token"] = piece = join(piece, got)
            masks = masks + [mask ^ hop for mask in masks]
        last, cross = ff_share[-2:]
        sent = swap(piece, last)
        got = yield swap(piece, cross)
        out["early"] = [(piece, masks), (got, [mask ^ cross for mask in masks])]
        out["token"] = got
        masks = [mask ^ last for mask in masks]
        got = yield sent
        out["near"] = [(got, masks)]
        out["token"] = got
        got = yield swap(got, cross)
        out["far"] = [(got, [mask ^ cross for mask in masks])]
        out["token"] = got

    def rounded(values):
        return lax.reduce_precision(values, exponent_bits=8, mantissa_bits=7)

    def with_small(pieces, small):
        high = rounded(small)
        low = rounded(small - high)
        parts = join(high, low).astype(bf16)[None]
        return join(pieces, parts), high + low

    def add_small(small, got):
        parts = got[-1].astype(f32)
        return small + (parts[: small.shape[0]] + parts[small.shape[0] :])

    def attn_chain(part, layer_idx, out):
        small = part.small if layer_idx == 0 else None
        keep, send = part.attn_keep, part.attn_send
        hops = attn_split[layer_idx] + attn_whole
        for step, hop in enumerate(hops):
            got = yield swap(send, hop)
            if small is not None:
                small = add_small(small, got)
                got = got[:-1]
            if step + 1 < len(attn_split[layer_idx]):
                half = keep.shape[0] // 2
                send = add(keep[half:], got[half:])
                keep = add(keep[:half], got[:half])
            else:
                send = keep = add(keep, got)
            if small is not None and step + 1 < len(hops):
                send, small = with_small(send, small)
            out["token"] = send
            if layer_idx == 1 and step == 0:
                send = tie(send, *(yield None))
        piece = keep[0]
        if own_rows < attn_grain:
            first_row = lax.rem(device_at, attn_low) * own_rows
            piece = lax.dynamic_slice_in_dim(piece, first_row, own_rows, axis=0)
        out["done"] = piece.astype(f32)
        out["small"] = small

    def ff_chain(part, out):
        got = yield swap(part.ff_send, 2)
        count = ff_count
        keeps, sends = [], []
        for side in range(2):
            at, half = side * count, count // 2
            sends.append(add(part.ff_keep[at + half : at + count], got[at + half : at + count]))
            keeps.append(add(part.ff_keep[at : at + half], got[at : at + half]))
        out["token"] = tuple(sends)
        for hops in zip(ff_split[0][1:3], ff_split[1][1:3]):
            got = yield tuple(swap(send, hop) for send, hop in zip(sends, hops))
            half = keeps[0].shape[0] // 2
            sends = [add(keep[half:], one[half:]) for keep, one in zip(keeps, got)]
            keeps = [add(keep[:half], one[:half]) for keep, one in zip(keeps, got)]
            out["token"] = tuple(sends)
        keep, send = (jnp.concatenate(sides, axis=2) for sides in (keeps, sends))
        yield from halving(keep, send, ff_split[0][3:], out)
        yield from summing(out["piece"], ff_whole, out)
        yield from sharing(out["piece"], out)

    class Chain:
        def __init__(self, steps, *args):
            self.out = {}
            self.steps = steps(*args, self.out)
            self.arriving = next(self.steps)

        def resume(self, *tokens):
            self.arriving = self.steps.send(tokens)

        def step(self, token, *others):
            if self.arriving is not None:
                tokens = (*(token if isinstance(token, tuple) else (token,)), *others)
                many = isinstance(self.arriving, tuple)
                arrived = self.arriving if many else (self.arriving,)
                arrived = lax.optimization_barrier((*arrived, *tokens))[: len(arrived)]
                arrived = arrived if many else arrived[0]
                self.arriving = None
                try:
                    self.arriving = self.steps.send(arrived)
                except StopIteration:
                    pass
                return self.out["token"]
            return token

    back_ff_1 = run(
        functools.partial(last_ff_body, masks=ff_masks),
        "layer_1_ff",
        dict(
            place=place,
            grad=cotangent,
            gain_ff=gain_ff,
            middle=Kept(second.middle),
            ff_in=Kept(second.ff_in),
            **ff_ins(1),
        ),
        dict(**ff_back_outs, outputs=(matrix, bf16)),
        dict(
            ff_gate_up=pltpu.VMEM((2, width, 2 * width), bf16),
            ff_down=pltpu.VMEM((2, width, width), bf16),
            **ff_back_scratch,
        ),
        micros=8,
        vmem=24,
    )
    ff_1 = Chain(ff_chain, back_ff_1)
    back_1 = run(
        functools.partial(
            last_attention_body, sizes=sizes, piece_masks=attn_masks[1], heads=heads
        ),
        "layer_1_attention_backward",
        dict(
            place=place,
            small_before=Kept(back_ff_1.small),
            grad_mid=Kept(back_ff_1.grad_mid),
            branch=Kept(back_ff_1.branch),
            **attn_back_ins(second, first_ff.x_next, first_ff.a_next),
        ),
        dict(
            **attn_back_outs,
            small=Kept(small_shape, f32),
            grad_next=Kept(matrix, f32),
            bias_acc=Kept(bias_shape, f32),
        ),
        attn_back_scratch,
        micros=6,
        vmem=14,
    )
    attn_1 = Chain(attn_chain, back_1, 1)
    token = ff_1.step(back_1.attn_send)
    token = (attn_1.step(token),)
    back_0 = run(
        functools.partial(ff_backward_body, masks=ff_masks),
        "layer_0_ff_backward",
        dict(
            place=place,
            grad=Kept(back_1.grad_next),
            gain_ff=gain_ff,
            small_before=Kept(back_1.small),
            middle=Kept(first.middle),
            ff_in=Kept(first.ff_in),
            ff_gate_up=Kept(first_ff.ff_gate_up),
            ff_down=Kept(first_ff.ff_down),
        ),
        ff_back_outs,
        ff_back_scratch,
        after=token,
        micros=8,
        vmem=20,
    )
    token = ff_1.step(back_0.branch)
    back_0.ff_send = tie(back_0.ff_send, *token)
    ff_0 = Chain(ff_chain, back_0)
    token = ff_0.step(token)
    back_attn_0 = run(
        functools.partial(
            attention_backward_body, sizes=sizes, piece_masks=attn_masks[0], heads=heads
        ),
        "layer_0_attention_backward",
        dict(
            place=place,
            bias_before=Kept(back_1.bias_acc),
            seen=Kept(start.seen),
            wide=Kept(start.wide),
            small_before=Kept(back_0.small),
            grad_mid=Kept(back_0.grad_mid),
            branch=Kept(back_0.branch),
            **attn_back_ins(first, start.x, start.a),
        ),
        dict(
            attn_keep=Kept(attn_half, bf16),
            attn_send=Kept((attn_count // 2 + 1, *attn_half[1:]), bf16),
            small=Kept(small_shape, f32),
            grad_next=(matrix, f32),
        ),
        dict(
            bias_acc=pltpu.VMEM(bias_shape, f32),
            table_rows=pltpu.VMEM((bias_table.shape[0], heads * slots), f32),
            **attn_back_scratch,
        ),
        after=token,
        micros=7,
        vmem=14,
    )
    attn_0 = Chain(attn_chain, back_attn_0, 0)
    attn_1.resume(back_attn_0.attn_send)
    token = back_attn_0.attn_send
    shape = (2, width, width)
    done = ()
    written = set()

    def write(chain, layer_idx, key, token):
        nonlocal done
        if key not in chain.out or (layer_idx, key) in written:
            return token
        written.add((layer_idx, key))
        parts = chain.out[key]
        tokens = token if isinstance(token, tuple) else (token,)
        arrays = lax.optimization_barrier((*(array for array, _ in parts), *tokens))
        parts = [(array, masks) for array, (_, masks) in zip(arrays, parts)]
        done = finish(parts, layer_idx, place, shape, done)
        return done[0]

    turn = 0
    sums = attn_grads = None
    while ff_0.arriving is not None:
        turn += 1
        chains = (ff_0, ff_1) if "near" in ff_1.out else (ff_1, ff_0)
        for layer_idx, chain in ((1, ff_1), (0, ff_0)):
            token = write(chain, layer_idx, "near", token)
        for chain in chains:
            token = chain.step(token)
        for key in ("early", "far"):
            for layer_idx, chain in ((1, ff_1), (0, ff_0)):
                token = write(chain, layer_idx, key, token)
        token = attn_0.step(token)
        if turn > 1:
            token = attn_1.step(token)
        if sums is None and attn_0.arriving is None:
            sums = run(
                small_body,
                "small_sums",
                dict(packed=Kept(tie(attn_0.out["small"], token))),
                dict(
                    gain_attn=((2, width), f32),
                    gain_ff=((2, width), f32),
                    embed=((1, width), f32),
                    table=(bias_table.shape[::-1], f32),
                ),
                {},
            )
            token = sums.embed
        if attn_grads is None and attn_0.arriving is None and attn_1.arriving is None:
            both = jnp.stack([attn_0.out["done"], tie(attn_1.out["done"], token)])
            attn_grads = [both[:, :, k * inner : (k + 1) * inner] for k in range(4)]
            attn_grads[3] = jnp.swapaxes(attn_grads[3], 1, 2)
            token = tuple(attn_grads)
    return (
        back_ff_1.outputs.reshape(inputs.shape),
        back_attn_0.grad_next.reshape(inputs.shape),
        *attn_grads,
        *done,
        sums.gain_attn,
        sums.gain_ff,
        sums.table.T,
        sums.embed[0],
    )


def solution(mesh):
    placed = (
        P(("dp", "tensor"), None, None),
        P(("dp", "tensor"), None, None),
        P(("dp", "tensor"), None),
        P(("dp", "tensor"), None),
        P(),
        P(),
        P(None, ("dp", "tensor"), None),
        P(None, ("dp", "tensor"), None),
        P(None, ("dp", "tensor"), None),
        P(None, None, ("dp", "tensor")),
        P(None, None, "tensor"),
        P(None, None, "tensor"),
        P(None, "tensor", None),
        P(),
        P(),
        P(),
    )
    return jax.shard_map(
        functools.partial(on_device, dp_size=mesh.shape["dp"]),
        mesh=mesh,
        in_specs=placed,
        out_specs=(
            P(("dp", "tensor"), None, None),
            P(("dp", "tensor"), None, None),
            P(None, ("dp", "tensor"), None),
            P(None, ("dp", "tensor"), None),
            P(None, ("dp", "tensor"), None),
            P(None, None, ("dp", "tensor")),
            P(None, None, "tensor"),
            P(None, None, "tensor"),
            P(None, "tensor", None),
            P(),
            P(),
            P(),
            P(),
        ),
        check_vma=False,
    )
```

```python
import functools
import types

import jax
import jax.numpy as jnp
from jax import lax
from jax.experimental import pallas as pl
from jax.experimental.pallas import tpu as pltpu
from jax.sharding import PartitionSpec as P

norm_eps = 1e-06
masked_score = -1e30
bf16 = jnp.bfloat16
f32 = jnp.float32
axes = ("dp", "tensor")
mebibyte = 1024 * 1024
raw_names = ("w_query", "w_key", "w_value", "w_out", "w_gate", "w_up", "w_down")
scalar_names = ("place", "table")


def dot_nn(left, right):
    return lax.dot_general(left, right, (((1,), (0,)), ((), ())), preferred_element_type=f32)


def dot_nt(left, right):
    return lax.dot_general(left, right, (((1,), (1,)), ((), ())), preferred_element_type=f32)


def dot_tn(left, right):
    return lax.dot_general(left, right, (((0,), (0,)), ((), ())), preferred_element_type=f32)


def inverse_rms(values):
    return lax.rsqrt(jnp.mean(values * values, axis=-1, keepdims=True) + norm_eps)


def norm_back(values, gain, grad_out):
    scale = inverse_rms(values)
    pulled = grad_out * gain
    mean_part = jnp.mean(pulled * values, axis=-1, keepdims=True)
    grad_in = scale * pulled - values * (scale * scale * scale) * mean_part
    return grad_in, jnp.sum(grad_out * values * scale, axis=0, keepdims=True)


def gelu_terms(gate_act):
    square = gate_act * gate_act
    bent = jnp.tanh(0.7978845608028654 * gate_act * (1.0 + 0.044715 * square))
    half = 0.5 * (1.0 + bent)
    slope = half + 0.5 * gate_act * (1.0 - bent * bent) * (
        0.7978845608028654 * (1.0 + 3.0 * 0.044715 * square)
    )
    return gate_act * half, slope


def cost(micros):
    return pl.CostEstimate(flops=int(micros * 1.15e9), bytes_accessed=0, transcendentals=0)


def run(body, name, ins, outs, scratch, after=(), micros=1, vmem=8):
    in_names, out_names, scratch_names = list(ins), list(outs), list(scratch)
    direct = {n for n in in_names if n in scalar_names + raw_names or isinstance(ins[n], Kept)}
    staged = [n for n in in_names if n not in direct]
    copied = [n for n in out_names if not isinstance(outs[n], Kept)]
    in_sems = {n: i for i, n in enumerate(staged)}
    out_sems = {n: i for i, n in enumerate(copied)}

    def kernel(*refs):
        refs = list(refs)
        sources = dict(zip(in_names, refs))
        refs = refs[len(in_names) + len(after) :]
        targets = dict(zip(out_names, refs))
        refs = refs[len(out_names) :]
        space = dict(zip(scratch_names, refs))
        refs = refs[len(scratch_names) :]
        buffers = dict(zip(staged + copied, refs))
        sems_in, sems_out = refs[len(staged) + len(copied) :]
        kept = {n: ref for n, ref in targets.items() if n not in out_sems}
        r = types.SimpleNamespace(**space, **buffers, **kept)
        for n in direct:
            setattr(r, n, sources[n])

        def copy_in(n):
            return pltpu.make_async_copy(sources[n], buffers[n], sems_in.at[in_sems[n]])

        def copy_out(n):
            return pltpu.make_async_copy(buffers[n], targets[n], sems_out.at[out_sems[n]])

        r.fetch = lambda *names: [copy_in(n).start() for n in names if n in in_sems]
        r.need = lambda *names: [copy_in(n).wait() for n in names if n in in_sems]
        r.write = lambda *names: [copy_out(n).start() for n in names if n in out_sems]
        r.drain = lambda *names: [copy_out(n).wait() for n in names if n in out_sems]
        body(r)

    def in_space(n):
        if n in scalar_names:
            return pltpu.SMEM
        return pltpu.VMEM if isinstance(ins[n], Kept) else pl.ANY

    results = pl.pallas_call(
        kernel,
        name=name,
        in_specs=[pl.BlockSpec(memory_space=in_space(n)) for n in in_names]
        + [pl.BlockSpec(memory_space=pl.ANY) for _ in after],
        out_specs=[
            pl.BlockSpec(memory_space=pltpu.VMEM if isinstance(out, Kept) else pl.ANY)
            for out in outs.values()
        ],
        out_shape=[
            pltpu.VMEM(*out.what) if isinstance(out, Kept) else jax.ShapeDtypeStruct(*out)
            for out in outs.values()
        ],
        scratch_shapes=list(scratch.values())
        + [pltpu.VMEM(ins[n].shape, ins[n].dtype) for n in staged]
        + [pltpu.VMEM(*outs[n]) for n in copied]
        + [
            pltpu.SemaphoreType.DMA((max(1, len(staged)),)),
            pltpu.SemaphoreType.DMA((max(1, len(copied)),)),
        ],
        compiler_params=pltpu.CompilerParams(vmem_limit_bytes=vmem * mebibyte),
        cost_estimate=cost(micros),
    )(
        *[
            pltpu.with_memory_space_constraint(value.what, pltpu.VMEM)
            if isinstance(value, Kept)
            else value
            for value in ins.values()
        ],
        *after,
    )
    return types.SimpleNamespace(**dict(zip(outs, results)))


class Kept:
    def __init__(self, *what):
        self.what = what[0] if len(what) == 1 else what


def keep_all(names):
    return {name: Kept(value) for name, value in names.items()}


def chunks(extent, size):
    size = min(size, extent)
    return [slice(start, start + size) for start in range(0, extent, size)]


def lay_out_attention(r, masks, rows):
    for idx, mask in enumerate(masks):
        half, at = divmod(idx, max(1, len(masks) // 2))
        source = r.attn_near if half == 0 else r.attn_far
        place = pl.multiple_of((r.place[0] ^ mask) * rows, rows) if len(masks) > 1 else 0
        r.attn_w[pl.ds(place, rows), :] = source[at * rows : (at + 1) * rows, :]


def lay_out_ff(r, layer_idx):
    width = r.ff_down.shape[-1]
    for k, own in enumerate((r.w_gate, r.w_up)):
        r.ff_gate_up[0, :, k * width : (k + 1) * width] = own[layer_idx]
    r.ff_down[0] = r.w_down[layer_idx]
    part = r.ff_near.shape[1]
    for source, base in ((r.ff_near, 0), (r.ff_far, 1)):
        for m in range(2):
            rows = pl.ds(pl.multiple_of((r.place[1] ^ (2 * m + base)) * part, part), part)
            for k in range(2):
                r.ff_gate_up[1, rows, k * width : (k + 1) * width] = source[3 * m + k]
            r.ff_down[1, rows, :] = source[3 * m + 2]


def start_all(copies):
    for copy in copies:
        copy.start()


def wait_all(sem, *buffers):
    for whole in buffers:
        pltpu.make_async_copy(whole, whole, sem).wait()


def lane_low(rows):
    return lax.broadcasted_iota(jnp.int32, (rows, 128), 1) < 64


def lane_halves():
    low = lane_low(1).astype(f32)
    return low.astype(bf16), (1.0 - low).astype(bf16)


def pair_blocks(rows, low, high):
    return jnp.concatenate([rows * low, rows * high], axis=0)


def own_blocks(both, is_low):
    half = both.shape[0] // 2
    return jnp.where(is_low, both[:half], both[half:]).astype(bf16)


def attention_forward(r, x_ref, a_ref, sizes, layer_idx):
    series, slots, inner = sizes
    rows = series * slots
    for part in chunks(rows, 256):
        r.qkv[part, :] = dot_nn(a_ref[part, :], r.attn_w[:, : 3 * inner]).astype(bf16)
    is_low = lane_low(slots)
    low, high = lane_halves()
    for s in range(series):
        here = slice(s * slots, (s + 1) * slots)
        keep = r.mask[here, :] == 1
        for start in range(0, inner, 128):
            at = slice(start, start + 128)
            query = r.qkv[here, at]
            keys = r.qkv[here, inner + start : inner + start + 128]
            scores = dot_nt(keys, pair_blocks(query, low, high)) + r.bias[:, at]
            scores = jnp.where(keep, scores, masked_score)
            exps = jnp.exp(scores - jnp.max(scores, axis=0, keepdims=True))
            r.probs[here, at] = exps / jnp.sum(exps, axis=0, keepdims=True)
    for s in range(series):
        here = slice(s * slots, (s + 1) * slots)
        for start in range(0, inner, 128):
            at = slice(start, start + 128)
            values = r.qkv[here, 2 * inner + start : 2 * inner + start + 128]
            both = dot_tn(r.probs[here, at].astype(bf16), values)
            r.heads[here, at] = own_blocks(both, is_low)
    gain = r.gain_ff[layer_idx : layer_idx + 1, :]
    for part in chunks(rows, 256):
        middle = x_ref[part, :] + dot_nt(r.heads[part, :], r.attn_w[:, 3 * inner :])
        r.middle[part, :] = middle
        r.ff_in[part, :] = (middle * inverse_rms(middle) * gain).astype(bf16)


def prepare_body(r):
    names = ("inputs", "valid", "keep", "embed", "gain_attn", "buckets")
    r.fetch(*names)
    r.need(*names)
    series, slots = r.valid.shape
    gain = r.gain_attn[0:1, :]
    valid = jnp.transpose(r.valid[...].astype(f32))
    keep = jnp.transpose(r.keep[...].astype(f32))
    for s in range(series):
        here = slice(s * slots, (s + 1) * slots)
        seen = valid[:, s : s + 1]
        x = jnp.where(seen == 1.0, r.inputs[here, :].astype(f32), r.embed[...])
        r.x[here, :] = x
        r.a[here, :] = (x * inverse_rms(x) * gain).astype(bf16)
        r.seen[here, :] = jnp.broadcast_to(seen, (slots, 128)).astype(jnp.int32)
        r.mask[here, :] = jnp.broadcast_to(keep[:, s : s + 1], (slots, 128)).astype(jnp.int32)
    turned = jnp.transpose(r.buckets[...].astype(f32)).astype(jnp.int32)
    wide = jnp.concatenate([turned, turned], axis=1)
    r.wide[...] = wide
    is_low = lane_low(slots)
    bucket_count, heads = r.table.shape
    for pair in range(heads // 2):
        bias = jnp.zeros((slots, 128), f32)
        for idx in range(bucket_count):
            entry = jnp.where(is_low, r.table[idx, 2 * pair], r.table[idx, 2 * pair + 1])
            bias = jnp.where(wide == idx, entry, bias)
        r.bias[:, pair * 128 : (pair + 1) * 128] = bias


def attention_body(r, sizes, masks, grain, layer_idx):
    r.fetch("gain_ff")
    lay_out_attention(r, masks, grain)
    r.need("gain_ff")
    attention_forward(r, r.x, r.a, sizes, layer_idx)


def ff_body(r):
    r.fetch("gain_attn")
    lay_out_ff(r, 0)
    r.need("gain_attn")
    width = r.middle.shape[1]
    for part in chunks(r.middle.shape[0], 256):
        x_next = r.middle[part, :]
        for half in range(2):
            both = dot_nn(r.ff_in[part, :], r.ff_gate_up[half])
            hidden = (gelu_terms(both[:, :width])[0] * both[:, width:]).astype(bf16)
            x_next = x_next + dot_nn(hidden, r.ff_down[half])
        r.x_next[part, :] = x_next
        r.a_next[part, :] = (x_next * inverse_rms(x_next) * r.gain_attn[1:2, :]).astype(bf16)


def ff_backward(r, layer_idx, last, masks):
    rows, width = r.middle.shape
    r.fetch("grad", "gain_ff")
    if last:
        lay_out_ff(r, layer_idx)
    r.need("grad", "gain_ff")
    gain_ff = r.gain_ff[layer_idx : layer_idx + 1, :]
    gain_total = jnp.zeros((1, width), f32)
    for part in chunks(rows, 256):
        grad = r.grad[part, :].astype(f32)
        rounded = grad.astype(bf16)
        ff_rows = r.ff_in[part, :]
        back = None
        middle = r.middle[part, :]
        total = middle
        for half in range(2):
            both = dot_nn(ff_rows, r.ff_gate_up[half])
            grad_hidden = dot_nt(rounded, r.ff_down[half])
            gate_act, up_act = both[:, :width], both[:, width:]
            mixed, slope = gelu_terms(gate_act)
            hidden = (mixed * up_act).astype(bf16)
            r.hidden[half, part, :] = hidden
            r.grad_gate_up[half, part, :width] = (grad_hidden * up_act * slope).astype(bf16)
            r.grad_gate_up[half, part, width:] = (grad_hidden * mixed).astype(bf16)
            pulled = r.grad_gate_up[half, part, :]
            if last:
                total = total + dot_nn(hidden, r.ff_down[half])
            term = dot_nt(pulled, r.ff_gate_up[half])
            back = term if back is None else back + term
        if last:
            r.outputs[part, :] = total.astype(bf16)
        grad_mid, gain_part = norm_back(middle, gain_ff, back)
        gain_total += gain_part
        grad_mid = grad + grad_mid
        r.grad_mid[part, :] = grad_mid
        r.branch[part, :] = grad_mid.astype(bf16)
        r.grad_low[part, :] = rounded
    if last:
        r.write("outputs")
    for half in range(2):
        r.ff_grad[half, :, : 2 * width] = dot_tn(r.ff_in[...], r.grad_gate_up[half])
        r.ff_grad[half, :, 2 * width :] = dot_tn(r.hidden[half], r.grad_low[...])
    half_count = len(masks[0]) // 2
    grain, columns = r.ff_keep.shape[1:]
    for side, side_masks in enumerate(masks):
        lanes = slice(side * columns, (side + 1) * columns)
        for idx, mask in enumerate(side_masks):
            target = r.ff_keep if idx < half_count else r.ff_send
            piece = pl.ds(pl.multiple_of((r.place[3] ^ (mask // 2)) * grain, grain), grain)
            target[side * half_count + idx % half_count] = r.ff_grad[mask % 2, piece, lanes].astype(
                bf16
            )
    if last:
        r.drain("outputs")
    return gain_total


def attention_backward(r, sizes, layer_idx, last, piece_masks, heads):
    series, slots, inner = sizes
    rows = series * slots
    width = r.x.shape[1]
    r.fetch("gain_attn")
    for part in chunks(rows, 256):
        r.grad_heads[part, :] = dot_nn(r.branch[part, :], r.attn_w[:, 3 * inner :]).astype(bf16)
    is_low = lane_low(slots)
    low, high = lane_halves()
    for start in range(0, inner, 128):
        at = slice(start, start + 128)
        bias_total = jnp.zeros((slots, 128), f32) if last else r.bias_before[:, at]
        for s in range(series):
            here = slice(s * slots, (s + 1) * slots)
            probs = r.probs[here, at]
            values = r.qkv[here, 2 * inner + start : 2 * inner + start + 128]
            grad_probs = dot_nt(values, pair_blocks(r.grad_heads[here, at], low, high))
            inner_sum = jnp.sum(probs * grad_probs, axis=0, keepdims=True)
            grad_scores = (probs * (grad_probs - inner_sum)).astype(bf16)
            r.grad_scores[here, at] = grad_scores
            bias_total = bias_total + grad_scores.astype(f32)
        r.bias_acc[:, at] = bias_total
    for s in range(series):
        here = slice(s * slots, (s + 1) * slots)
        for start in range(0, inner, 128):
            at = slice(start, start + 128)
            key_at = slice(inner + start, inner + start + 128)
            value_at = slice(2 * inner + start, 2 * inner + start + 128)
            grad_scores = r.grad_scores[here, at]
            r.grad_qkv[here, key_at] = dot_nn(
                grad_scores, pair_blocks(r.qkv[here, at], low, high)
            ).astype(bf16)
            r.grad_qkv[here, value_at] = dot_nn(
                r.probs[here, at].astype(bf16), pair_blocks(r.grad_heads[here, at], low, high)
            ).astype(bf16)
            r.grad_qkv[here, at] = own_blocks(dot_tn(grad_scores, r.qkv[here, key_at]), is_low)
    r.attn_grad[:, : 3 * inner] = dot_tn(r.a[...], r.grad_qkv[...])
    r.attn_grad[:, 3 * inner :] = dot_tn(r.branch[...], r.heads[...])
    scatter_pieces(r.attn_grad, r.attn_keep, r.attn_send, piece_masks, r.place[2])
    r.need("gain_attn")
    gain_attn = r.gain_attn[layer_idx : layer_idx + 1, :]
    gain_total = jnp.zeros((1, width), f32)
    embed_total = jnp.zeros((1, width), f32)
    for part in chunks(rows, 256):
        grad_normed = dot_nt(r.grad_qkv[part, :], r.attn_w[:, : 3 * inner])
        grad_in, gain_part = norm_back(r.x[part, :], gain_attn, grad_normed)
        gain_total += gain_part
        grad_in = r.grad_mid[part, :] + grad_in
        if last:
            r.grad_next[part, :] = grad_in
        else:
            seen = r.seen[part, 0:1] == 1
            r.grad_next[part, :] = jnp.where(seen, grad_in, 0.0)
            embed_total += jnp.sum(jnp.where(seen, 0.0, grad_in), axis=0, keepdims=True)
    r.write("grad_next")
    if not last:
        put_row(r.small, 4, embed_total)
        head_size = inner // heads
        for idx in range(r.table_rows.shape[0]):
            for start in range(0, inner, 128):
                at = slice(start, start + 128)
                chosen = jnp.where(r.wide[...] == idx, r.bias_acc[:, at], 0.0)
                r.table_rows[idx : idx + 1, at] = jnp.sum(chosen, axis=0, keepdims=True)
        lane = lax.broadcasted_iota(jnp.int32, (r.table_rows.shape[0], 128), 1)
        table = jnp.zeros(lane.shape, f32)
        for head in range(heads):
            cut = r.table_rows[:, head * head_size : (head + 1) * head_size]
            table = jnp.where(lane == head, jnp.sum(cut, axis=1, keepdims=True), table)
        r.small[:heads, : table.shape[0]] = jnp.transpose(table)[:heads, :]
    r.drain("grad_next")
    return gain_total


def two_parts(values):
    high = values.astype(bf16).astype(f32)
    return high, (values - high).astype(bf16).astype(f32)


def last_ff_body(r, masks):
    r.small[...] = jnp.zeros(r.small.shape, f32)
    put_row(r.small, 3, ff_backward(r, 1, True, masks))


def last_attention_body(r, sizes, piece_masks, heads):
    r.small[...] = r.small_before[...]
    put_row(r.small, 1, attention_backward(r, sizes, 1, True, piece_masks, heads))


def ff_backward_body(r, masks):
    r.small[...] = r.small_before[...]
    put_row(r.small, 2, ff_backward(r, 0, False, masks))


def attention_backward_body(r, sizes, piece_masks, heads):
    r.small[...] = r.small_before[...]
    put_row(r.small, 0, attention_backward(r, sizes, 0, False, piece_masks, heads))
    high, low = two_parts(r.small[...])
    last = r.attn_send.shape[0] - 1
    r.attn_send[last] = jnp.concatenate([high, low], axis=0).astype(bf16)
    r.small[...] = high + low


def put_row(packed, which, row):
    first, width = packed.shape[0] - 2, row.shape[1]
    at = which % 3 * width
    packed[first + which // 3 : first + which // 3 + 1, at : at + width] = row


def scatter_pieces(whole, keep, send, masks, place):
    count = len(masks)
    grain = whole.shape[0] // count
    for idx, mask in enumerate(masks):
        target = keep if idx < count // 2 else send
        source = pl.ds(pl.multiple_of((place ^ mask) * grain, grain), grain)
        target[idx % (count // 2)] = whole[source, :].astype(bf16)


def finish(pieces, masks, layer_idx, place, shape, before=()):
    grain, width = pieces.shape[1], shape[-1]
    count = len(before)

    def kernel(place_ref, source, *refs):
        outs = refs[count : count + 3]
        stage, out_sem = refs[count + 3 :]
        for idx, mask in enumerate(masks):
            rows = pl.ds(pl.multiple_of((place_ref[3] ^ mask) * grain, grain), grain)
            for k, out in enumerate(outs):
                stage[k, idx] = source[idx, :, k * width : (k + 1) * width].astype(f32)
                pltpu.make_async_copy(stage.at[k, idx], out.at[layer_idx, rows], out_sem).start()
        pltpu.make_async_copy(stage, stage, out_sem).wait()

    return pl.pallas_call(
        kernel,
        name="layer_%d_ff_grads" % layer_idx,
        in_specs=[
            pl.BlockSpec(memory_space=pltpu.SMEM),
            pl.BlockSpec(memory_space=pltpu.VMEM),
        ]
        + [pl.BlockSpec(memory_space=pl.ANY)] * count,
        out_specs=[pl.BlockSpec(memory_space=pl.ANY)] * 3,
        out_shape=[jax.ShapeDtypeStruct(shape, f32)] * 3,
        input_output_aliases={2 + k: k for k in range(count)},
        scratch_shapes=[
            pltpu.VMEM((3, len(masks), grain, width), f32),
            pltpu.SemaphoreType.DMA,
        ],
        compiler_params=pltpu.CompilerParams(vmem_limit_bytes=6 * mebibyte),
        cost_estimate=cost(3),
    )(place, pltpu.with_memory_space_constraint(pieces, pltpu.VMEM), *before)


def small_body(r):
    width = r.embed.shape[1]
    heads = r.table.shape[0]
    outs = ((r.gain_attn, 0), (r.gain_attn, 1), (r.gain_ff, 0), (r.gain_ff, 1), (r.embed, 0))
    for which, (out, row) in enumerate(outs):
        first = r.packed.shape[0] - 2 + which // 3
        at = which % 3 * width
        out[row : row + 1, :] = r.packed[first : first + 1, at : at + width]
    r.table[...] = r.packed[:heads, : r.table.shape[1]]
    r.write("gain_attn", "gain_ff", "embed", "table")
    r.drain("gain_attn", "gain_ff", "embed", "table")


def pack_body(r, packs):
    rows = r.quarter_0.shape[1]
    at = pl.ds(pl.multiple_of(r.place[1] * rows, rows), rows)
    copies = []
    outs = [r.quarter_0, r.quarter_1]
    for layer_idx in range(2):
        for k, w in enumerate((r.w_gate, r.w_up, r.w_down)):
            copies.append((w.at[layer_idx, at], outs[layer_idx].at[k]))
    if packs:
        outs += [r.block_0, r.block_1]
        inner = r.w_query.shape[2]
        for layer_idx in range(2):
            for k, w in enumerate((r.w_query, r.w_key, r.w_value, r.w_out)):
                lanes = pl.ds(k * inner, inner)
                copies.append((w.at[layer_idx], outs[2 + layer_idx].at[:, lanes]))
    start_all([pltpu.make_async_copy(*ends, r.pack_sem) for ends in copies])
    wait_all(r.pack_sem, *outs)


def order_masks(hops):
    masks = [0]
    for hop in reversed(hops):
        masks = masks + [mask ^ hop for mask in masks]
    return masks


def tie(value, *others):
    return lax.optimization_barrier((value, *others))[0]


def on_device(
    inputs,
    cotangent,
    attention_mask,
    patch_valid,
    buckets,
    mask_embed,
    w_query,
    w_key,
    w_value,
    w_output,
    w_gate,
    w_up,
    w_down,
    gain_attn,
    gain_ff,
    bias_table,
    dp_size,
):
    series, slots, width = inputs.shape
    heads = bias_table.shape[1]
    inner = w_query.shape[2]
    rows = series * slots
    sizes = (series, slots, inner)
    matrix = (rows, width)
    devices = 2 * dp_size
    dp_at = lax.axis_index("dp")
    device_at = 2 * dp_at + lax.axis_index("tensor")
    cotangent = cotangent.reshape(matrix)

    def swap(array, mask):
        return lax.ppermute(array, axes, [(n, n ^ mask) for n in range(devices)])

    def join(left, right):
        return jnp.concatenate([left, right], axis=0)

    bits = [1 << k for k in range(devices.bit_length() - 1)]

    attn_grain = max(16, width // devices)
    attn_count = width // attn_grain
    ff_grain = max(16, 2 * width // dp_size)
    ff_count = width // ff_grain
    quarter_at = lax.rem(dp_at, 4)
    place = jnp.stack(
        [
            device_at,
            quarter_at,
            device_at // (devices // attn_count),
            lax.rem(dp_at, ff_count),
        ]
    ).astype(jnp.int32)

    quarter = width // 4
    own_rows = w_query.shape[1]
    direct = own_rows % 16 == 0
    w_out = jnp.swapaxes(w_output, 1, 2)
    sources = dict(w_gate=w_gate, w_up=w_up, w_down=w_down)
    block_outs = {}
    if direct:
        sources |= dict(w_query=w_query, w_key=w_key, w_value=w_value, w_out=w_out)
        block_outs = {"block_%d" % k: Kept((own_rows, 4 * inner), bf16) for k in range(2)}
    packed = run(
        functools.partial(pack_body, packs=direct),
        "pack",
        dict(
            place=place,
            **{n: pltpu.with_memory_space_constraint(w, pltpu.HBM) for n, w in sources.items()},
        ),
        dict(
            quarter_0=Kept((3, quarter, width), bf16),
            quarter_1=Kept((3, quarter, width), bf16),
            **block_outs,
        ),
        dict(pack_sem=pltpu.SemaphoreType.DMA),
        vmem=4,
    )
    far = bits[2:]

    def prepare(token):
        return run(
            prepare_body,
            "prepare",
            dict(
                inputs=tie(inputs, token).reshape(matrix),
                valid=patch_valid,
                keep=attention_mask,
                embed=mask_embed[None, :],
                gain_attn=gain_attn,
                buckets=buckets,
                table=bias_table,
            ),
            dict(
                x=Kept(matrix, f32),
                a=Kept(matrix, bf16),
                bias=Kept((slots, heads * slots), f32),
                mask=Kept((rows, 128), jnp.int32),
                seen=Kept((rows, 128), jnp.int32),
                wide=Kept((slots, 128), jnp.int32),
            ),
            {},
            micros=3,
        )

    if direct:
        hops_0 = [1] + far[2:] + far[:2] + [2]
        hops_1 = far[2:] + far[:2] + [1, 2]
        block_0, block_1 = packed.block_0, packed.block_1
        got_1 = swap(block_1, hops_1[0])
        got_0 = swap(block_0, hops_0[0])
        ff_0 = swap(tie(packed.quarter_0, got_0), 1)
        ff_1 = swap(tie(packed.quarter_1, ff_0), 1)
        got_ff_0 = swap(ff_0, 4)
        block_0 = join(block_0, got_0)
        block_1 = join(block_1, tie(got_1, block_0))
        for hop_0, hop_1 in zip(hops_0[1:-2], hops_1[1:-2]):
            got_1, got_0 = swap(block_1, hop_1), swap(block_0, hop_0)
            if hop_0 == hops_0[1]:
                start = prepare(block_1)
                got_0 = tie(got_0, ff_0)
            block_0 = join(block_0, got_0)
            block_1 = join(block_1, tie(got_1, block_0))
        block_0 = tie(block_0, block_1)
        got_0 = swap(block_0, hops_0[-2])
        got_1 = swap(block_1, hops_1[-2])
        block_0 = join(block_0, tie(got_0, start.a, got_ff_0, ff_1, got_1))
        ff_0 = join(ff_0, tie(got_ff_0, block_0))
        got_ff_1 = swap(tie(ff_1, ff_0), 4)
        attn_pieces = [(block_0, swap(block_0, 2), order_masks(hops_0[::-1]))]
    else:
        ff_0, ff_1 = swap(packed.quarter_0, 1), swap(packed.quarter_1, 1)
        ff_0 = join(ff_0, swap(ff_0, 4))
        start = prepare(ff_0)
        attn_pieces = []
        rows_of = jnp.concatenate([w_query, w_key, w_value, w_out], axis=2)
        for layer_idx in range(2):
            whole = lax.all_gather(rows_of[layer_idx], axes, axis=0, tiled=True)
            attn_pieces.append((whole, whole, [0]))
    ff_pieces = [(ff_0, swap(ff_0, 2))]

    def attn_ins(layer_idx):
        near, far, masks = attn_pieces[layer_idx]
        return dict(attn_near=Kept(near), attn_far=Kept(far)), masks

    def ff_ins(layer_idx):
        near, far = ff_pieces[layer_idx]
        own = keep_all(dict(w_gate=w_gate, w_up=w_up, w_down=w_down))
        return dict(**own, ff_near=Kept(near), ff_far=Kept(far))

    ff_outs = dict(
        ff_gate_up=Kept((2, width, 2 * width), bf16), ff_down=Kept((2, width, width), bf16)
    )
    grain = own_rows if direct else width
    attn_outs = dict(
        attn_w=Kept((width, 4 * inner), bf16),
        qkv=Kept((rows, 3 * inner), bf16),
        probs=Kept((rows, heads * slots), f32),
        heads=Kept((rows, inner), bf16),
        middle=Kept(matrix, f32),
        ff_in=Kept(matrix, bf16),
    )

    def attention(layer_idx, x, a, after=(), micros=5):
        pieces, masks = attn_ins(layer_idx)
        return run(
            functools.partial(
                attention_body, sizes=sizes, masks=masks, grain=grain, layer_idx=layer_idx
            ),
            "layer_%d_attention" % layer_idx,
            dict(
                place=place,
                x=Kept(x),
                a=Kept(a),
                bias=Kept(start.bias),
                mask=Kept(start.mask),
                gain_ff=gain_ff,
                **pieces,
            ),
            attn_outs,
            {},
            after=after,
            micros=micros,
        )

    first = attention(0, start.x, start.a, micros=10)
    if direct:
        block_1 = join(block_1, tie(got_1, first.ff_in))
        attn_pieces.append((block_1, swap(block_1, 2), order_masks(hops_1[::-1])))
    first_ff = run(
        ff_body,
        "layer_0_ff",
        dict(
            place=place,
            middle=Kept(first.middle),
            ff_in=Kept(first.ff_in),
            gain_attn=gain_attn,
            **ff_ins(0),
        ),
        dict(**ff_outs, x_next=Kept(matrix, f32), a_next=Kept(matrix, bf16)),
        {},
        after=(block_1,) if direct else (),
        micros=3,
    )
    if direct:
        ff_1 = join(ff_1, tie(got_ff_1, first_ff.x_next))
    else:
        ff_1 = join(ff_1, swap(ff_1, 4))
    ff_pieces.append((ff_1, swap(ff_1, 2)))
    second = attention(1, first_ff.x_next, first_ff.a_next, micros=0.1)

    attn_low = devices // attn_count
    attn_hops = ([2, 1] + bits[2:], [2] + bits[3:4] + bits[2:3] + bits[4:] + [1])
    attn_split = [[hop for hop in hops if hop >= attn_low] for hops in attn_hops]
    attn_whole = [hop for hop in bits if hop < attn_low]
    attn_masks = [[mask // attn_low for mask in order_masks(hops)] for hops in attn_split]
    ff_hops = ([2, 4, 1] + bits[3:], [2, 1, 4] + bits[3:])
    ff_split = [[hop for hop in hops if hop // 2 < ff_count] for hops in ff_hops]
    ff_whole = [hop for hop in bits[1:] if hop // 2 >= ff_count]
    ff_share = [hop for hop in bits[:0:-1] if hop // 2 < ff_count]
    ff_masks = [order_masks(hops) for hops in ff_split]
    place_masks = [mask // 2 for mask in order_masks(ff_share[::-1])]
    attn_half = (attn_count // 2, attn_grain, 4 * inner)
    small_shape = (heads + 2, 3 * width)

    attn_back_outs = dict(attn_keep=Kept(attn_half, bf16), attn_send=Kept(attn_half, bf16))
    attn_back_scratch = dict(
        grad_heads=pltpu.VMEM((rows, inner), bf16),
        grad_qkv=pltpu.VMEM((rows, 3 * inner), bf16),
        grad_scores=pltpu.VMEM((rows, heads * slots), bf16),
        attn_grad=pltpu.VMEM((width, 4 * inner), f32),
    )
    ff_back_outs = dict(
        ff_keep=Kept((2 * ff_count, ff_grain, 3 * width // 2), bf16),
        ff_send=Kept((2 * ff_count, ff_grain, 3 * width // 2), bf16),
        small=Kept(small_shape, f32),
        grad_mid=Kept(matrix, f32),
        branch=Kept(matrix, bf16),
    )
    ff_back_scratch = dict(
        hidden=pltpu.VMEM((2, rows, width), bf16),
        grad_gate_up=pltpu.VMEM((2, rows, 2 * width), bf16),
        ff_grad=pltpu.VMEM((2, width, 3 * width), f32),
        grad_low=pltpu.VMEM(matrix, bf16),
    )
    bias_shape = (slots, heads * slots)

    def attn_back_ins(kept, x, a):
        return dict(
            x=Kept(x),
            a=Kept(a),
            gain_attn=gain_attn,
            attn_w=Kept(kept.attn_w),
            qkv=Kept(kept.qkv),
            probs=Kept(kept.probs),
            heads=Kept(kept.heads),
        )

    def add(left, right):
        return (left.astype(f32) + right.astype(f32)).astype(bf16)

    def halving(keep, send, hops, out):
        for step, hop in enumerate(hops):
            got = yield swap(send, hop)
            if step + 1 < len(hops):
                cut = keep.shape[0] // 2
                send = add(keep[cut:], got[cut:])
                keep = add(keep[:cut], got[:cut])
                out["token"] = send
            else:
                out["token"] = keep = add(keep, got)
        out["piece"] = keep

    def summing(piece, hops, out):
        for hop in hops:
            got = yield swap(piece, hop)
            out["token"] = piece = add(piece, got)
        out["piece"] = piece

    def sharing(piece, hops, out):
        for step, hop in enumerate(hops):
            if step + 1 == len(hops):
                out["near"] = piece
            got = yield swap(piece, hop)
            if step + 1 < len(hops):
                out["token"] = piece = join(piece, got)
            else:
                out["token"] = out["far"] = got

    def rounded(values):
        return lax.reduce_precision(values, exponent_bits=8, mantissa_bits=7)

    def with_small(pieces, small):
        high = rounded(small)
        low = rounded(small - high)
        parts = join(high, low).astype(bf16)[None]
        return join(pieces, parts), high + low

    def add_small(small, got):
        parts = got[-1].astype(f32)
        return small + (parts[: small.shape[0]] + parts[small.shape[0] :])

    def attn_chain(part, layer_idx, out):
        small = part.small if layer_idx == 0 else None
        keep, send = part.attn_keep, part.attn_send
        hops = attn_split[layer_idx] + attn_whole
        for step, hop in enumerate(hops):
            got = yield swap(send, hop)
            if small is not None:
                small = add_small(small, got)
                got = got[:-1]
            if step + 1 < len(attn_split[layer_idx]):
                half = keep.shape[0] // 2
                send = add(keep[half:], got[half:])
                keep = add(keep[:half], got[:half])
            else:
                send = keep = add(keep, got)
            if small is not None and step + 1 < len(hops):
                send, small = with_small(send, small)
            out["token"] = send
            if layer_idx == 1 and step == 0:
                send = tie(send, *(yield None))
        piece = keep[0]
        if own_rows < attn_grain:
            first_row = lax.rem(device_at, attn_low) * own_rows
            piece = lax.dynamic_slice_in_dim(piece, first_row, own_rows, axis=0)
        out["done"] = piece.astype(f32)
        out["small"] = small

    def ff_chain(part, out):
        got = yield swap(part.ff_send, 2)
        count = ff_count
        keeps, sends = [], []
        for side in range(2):
            at, half = side * count, count // 2
            sends.append(add(part.ff_keep[at + half : at + count], got[at + half : at + count]))
            keeps.append(add(part.ff_keep[at : at + half], got[at : at + half]))
        out["token"] = tuple(sends)
        for hops in zip(ff_split[0][1:3], ff_split[1][1:3]):
            got = yield tuple(swap(send, hop) for send, hop in zip(sends, hops))
            half = keeps[0].shape[0] // 2
            sends = [add(keep[half:], one[half:]) for keep, one in zip(keeps, got)]
            keeps = [add(keep[:half], one[:half]) for keep, one in zip(keeps, got)]
            out["token"] = tuple(sends)
        keep, send = (jnp.concatenate(sides, axis=2) for sides in (keeps, sends))
        yield from halving(keep, send, ff_split[0][3:], out)
        yield from summing(out["piece"], ff_whole, out)
        yield from sharing(out["piece"], ff_share, out)

    class Chain:
        def __init__(self, steps, *args):
            self.out = {}
            self.steps = steps(*args, self.out)
            self.arriving = next(self.steps)

        def resume(self, *tokens):
            self.arriving = self.steps.send(tokens)

        def step(self, token, *others):
            if self.arriving is not None:
                tokens = (*(token if isinstance(token, tuple) else (token,)), *others)
                many = isinstance(self.arriving, tuple)
                arrived = self.arriving if many else (self.arriving,)
                arrived = lax.optimization_barrier((*arrived, *tokens))[: len(arrived)]
                arrived = arrived if many else arrived[0]
                self.arriving = None
                try:
                    self.arriving = self.steps.send(arrived)
                except StopIteration:
                    pass
                return self.out["token"]
            return token

    back_ff_1 = run(
        functools.partial(last_ff_body, masks=ff_masks),
        "layer_1_ff",
        dict(
            place=place,
            grad=cotangent,
            gain_ff=gain_ff,
            middle=Kept(second.middle),
            ff_in=Kept(second.ff_in),
            **ff_ins(1),
        ),
        dict(**ff_back_outs, outputs=(matrix, bf16)),
        dict(
            ff_gate_up=pltpu.VMEM((2, width, 2 * width), bf16),
            ff_down=pltpu.VMEM((2, width, width), bf16),
            **ff_back_scratch,
        ),
        micros=8,
        vmem=24,
    )
    ff_1 = Chain(ff_chain, back_ff_1)
    back_1 = run(
        functools.partial(
            last_attention_body, sizes=sizes, piece_masks=attn_masks[1], heads=heads
        ),
        "layer_1_attention_backward",
        dict(
            place=place,
            small_before=Kept(back_ff_1.small),
            grad_mid=Kept(back_ff_1.grad_mid),
            branch=Kept(back_ff_1.branch),
            **attn_back_ins(second, first_ff.x_next, first_ff.a_next),
        ),
        dict(
            **attn_back_outs,
            small=Kept(small_shape, f32),
            grad_next=Kept(matrix, f32),
            bias_acc=Kept(bias_shape, f32),
        ),
        attn_back_scratch,
        micros=6,
        vmem=14,
    )
    attn_1 = Chain(attn_chain, back_1, 1)
    token = ff_1.step(back_1.attn_send)
    token = (attn_1.step(token),)
    back_0 = run(
        functools.partial(ff_backward_body, masks=ff_masks),
        "layer_0_ff_backward",
        dict(
            place=place,
            grad=Kept(back_1.grad_next),
            gain_ff=gain_ff,
            small_before=Kept(back_1.small),
            middle=Kept(first.middle),
            ff_in=Kept(first.ff_in),
            ff_gate_up=Kept(first_ff.ff_gate_up),
            ff_down=Kept(first_ff.ff_down),
        ),
        ff_back_outs,
        ff_back_scratch,
        after=token,
        micros=8,
        vmem=20,
    )
    token = ff_1.step(back_0.branch)
    back_0.ff_send = tie(back_0.ff_send, *token)
    ff_0 = Chain(ff_chain, back_0)
    token = ff_0.step(token)
    back_attn_0 = run(
        functools.partial(
            attention_backward_body, sizes=sizes, piece_masks=attn_masks[0], heads=heads
        ),
        "layer_0_attention_backward",
        dict(
            place=place,
            bias_before=Kept(back_1.bias_acc),
            seen=Kept(start.seen),
            wide=Kept(start.wide),
            small_before=Kept(back_0.small),
            grad_mid=Kept(back_0.grad_mid),
            branch=Kept(back_0.branch),
            **attn_back_ins(first, start.x, start.a),
        ),
        dict(
            attn_keep=Kept(attn_half, bf16),
            attn_send=Kept((attn_count // 2 + 1, *attn_half[1:]), bf16),
            small=Kept(small_shape, f32),
            grad_next=(matrix, f32),
        ),
        dict(
            bias_acc=pltpu.VMEM(bias_shape, f32),
            table_rows=pltpu.VMEM((bias_table.shape[0], heads * slots), f32),
            **attn_back_scratch,
        ),
        after=token,
        micros=7,
        vmem=14,
    )
    attn_0 = Chain(attn_chain, back_attn_0, 0)
    attn_1.resume(back_attn_0.attn_send)
    token = back_attn_0.attn_send
    shape = (2, width, width)
    near_masks = place_masks[: ff_count // 2]
    far_masks = place_masks[ff_count // 2 :]
    done = ()
    ended = False
    turn = 0
    sums = attn_grads = None
    while ff_0.arriving is not None:
        turn += 1
        token = ff_1.step(token)
        if done and not ended:
            done = finish(tie(ff_1.out["far"], token), far_masks, 1, place, shape, done)
            token = done[0]
            ended = True
        token = ff_0.step(token)
        if not done and "near" in ff_1.out:
            done = finish(tie(ff_1.out["near"], token), near_masks, 1, place, shape)
            token = done[0]
        token = attn_0.step(token)
        if turn > 2:
            token = attn_1.step(token)
        if sums is None and attn_0.arriving is None:
            sums = run(
                small_body,
                "small_sums",
                dict(packed=Kept(tie(attn_0.out["small"], token))),
                dict(
                    gain_attn=((2, width), f32),
                    gain_ff=((2, width), f32),
                    embed=((1, width), f32),
                    table=(bias_table.shape[::-1], f32),
                ),
                {},
            )
            token = sums.embed
        if attn_grads is None and attn_0.arriving is None and attn_1.arriving is None:
            both = jnp.stack([attn_0.out["done"], tie(attn_1.out["done"], token)])
            attn_grads = [both[:, :, k * inner : (k + 1) * inner] for k in range(4)]
            attn_grads[3] = jnp.swapaxes(attn_grads[3], 1, 2)
            token = tuple(attn_grads)
    if not ended:
        done = finish(ff_1.out["far"], far_masks, 1, place, shape, done)
    for pieces, masks in ((ff_0.out["near"], near_masks), (ff_0.out["far"], far_masks)):
        done = finish(pieces, masks, 0, place, shape, done)
    return (
        back_ff_1.outputs.reshape(inputs.shape),
        back_attn_0.grad_next.reshape(inputs.shape),
        *attn_grads,
        *done,
        sums.gain_attn,
        sums.gain_ff,
        sums.table.T,
        sums.embed[0],
    )


def solution(mesh):
    placed = (
        P(("dp", "tensor"), None, None),
        P(("dp", "tensor"), None, None),
        P(("dp", "tensor"), None),
        P(("dp", "tensor"), None),
        P(),
        P(),
        P(None, ("dp", "tensor"), None),
        P(None, ("dp", "tensor"), None),
        P(None, ("dp", "tensor"), None),
        P(None, None, ("dp", "tensor")),
        P(None, None, "tensor"),
        P(None, None, "tensor"),
        P(None, "tensor", None),
        P(),
        P(),
        P(),
    )
    return jax.shard_map(
        functools.partial(on_device, dp_size=mesh.shape["dp"]),
        mesh=mesh,
        in_specs=placed,
        out_specs=(
            P(("dp", "tensor"), None, None),
            P(("dp", "tensor"), None, None),
            P(None, ("dp", "tensor"), None),
            P(None, ("dp", "tensor"), None),
            P(None, ("dp", "tensor"), None),
            P(None, None, ("dp", "tensor")),
            P(None, None, "tensor"),
            P(None, None, "tensor"),
            P(None, "tensor", None),
            P(),
            P(),
            P(),
            P(),
        ),
        check_vma=False,
    )
```

```python
import functools
import types

import jax
import jax.numpy as jnp
from jax import lax
from jax.experimental import pallas as pl
from jax.experimental.pallas import tpu as pltpu
from jax.sharding import PartitionSpec as P

norm_eps = 1e-06
masked_score = -1e30
bf16 = jnp.bfloat16
f32 = jnp.float32
axes = ("dp", "tensor")
mebibyte = 1024 * 1024
raw_names = ("w_query", "w_key", "w_value", "w_out", "w_gate", "w_up", "w_down")
scalar_names = ("place", "table")


def dot_nn(left, right):
    return lax.dot_general(left, right, (((1,), (0,)), ((), ())), preferred_element_type=f32)


def dot_nt(left, right):
    return lax.dot_general(left, right, (((1,), (1,)), ((), ())), preferred_element_type=f32)


def dot_tn(left, right):
    return lax.dot_general(left, right, (((0,), (0,)), ((), ())), preferred_element_type=f32)


def inverse_rms(values):
    return lax.rsqrt(jnp.mean(values * values, axis=-1, keepdims=True) + norm_eps)


def norm_back(values, gain, grad_out):
    scale = inverse_rms(values)
    pulled = grad_out * gain
    mean_part = jnp.mean(pulled * values, axis=-1, keepdims=True)
    grad_in = scale * pulled - values * (scale * scale * scale) * mean_part
    return grad_in, jnp.sum(grad_out * values * scale, axis=0, keepdims=True)


def gelu_terms(gate_act):
    square = gate_act * gate_act
    bent = jnp.tanh(0.7978845608028654 * gate_act * (1.0 + 0.044715 * square))
    half = 0.5 * (1.0 + bent)
    slope = half + 0.5 * gate_act * (1.0 - bent * bent) * (
        0.7978845608028654 * (1.0 + 3.0 * 0.044715 * square)
    )
    return gate_act * half, slope


def cost(micros):
    return pl.CostEstimate(flops=int(micros * 1.15e9), bytes_accessed=0, transcendentals=0)


def run(body, name, ins, outs, scratch, after=(), micros=1, vmem=8):
    in_names, out_names, scratch_names = list(ins), list(outs), list(scratch)
    direct = {n for n in in_names if n in scalar_names + raw_names or isinstance(ins[n], Kept)}
    staged = [n for n in in_names if n not in direct]
    copied = [n for n in out_names if not isinstance(outs[n], Kept)]
    in_sems = {n: i for i, n in enumerate(staged)}
    out_sems = {n: i for i, n in enumerate(copied)}

    def kernel(*refs):
        refs = list(refs)
        sources = dict(zip(in_names, refs))
        refs = refs[len(in_names) + len(after) :]
        targets = dict(zip(out_names, refs))
        refs = refs[len(out_names) :]
        space = dict(zip(scratch_names, refs))
        refs = refs[len(scratch_names) :]
        buffers = dict(zip(staged + copied, refs))
        sems_in, sems_out = refs[len(staged) + len(copied) :]
        kept = {n: ref for n, ref in targets.items() if n not in out_sems}
        r = types.SimpleNamespace(**space, **buffers, **kept)
        for n in direct:
            setattr(r, n, sources[n])

        def copy_in(n):
            return pltpu.make_async_copy(sources[n], buffers[n], sems_in.at[in_sems[n]])

        def copy_out(n):
            return pltpu.make_async_copy(buffers[n], targets[n], sems_out.at[out_sems[n]])

        r.fetch = lambda *names: [copy_in(n).start() for n in names if n in in_sems]
        r.need = lambda *names: [copy_in(n).wait() for n in names if n in in_sems]
        r.write = lambda *names: [copy_out(n).start() for n in names if n in out_sems]
        r.drain = lambda *names: [copy_out(n).wait() for n in names if n in out_sems]
        body(r)

    def in_space(n):
        if n in scalar_names:
            return pltpu.SMEM
        return pltpu.VMEM if isinstance(ins[n], Kept) else pl.ANY

    results = pl.pallas_call(
        kernel,
        name=name,
        in_specs=[pl.BlockSpec(memory_space=in_space(n)) for n in in_names]
        + [pl.BlockSpec(memory_space=pl.ANY) for _ in after],
        out_specs=[
            pl.BlockSpec(memory_space=pltpu.VMEM if isinstance(out, Kept) else pl.ANY)
            for out in outs.values()
        ],
        out_shape=[
            pltpu.VMEM(*out.what) if isinstance(out, Kept) else jax.ShapeDtypeStruct(*out)
            for out in outs.values()
        ],
        scratch_shapes=list(scratch.values())
        + [pltpu.VMEM(ins[n].shape, ins[n].dtype) for n in staged]
        + [pltpu.VMEM(*outs[n]) for n in copied]
        + [
            pltpu.SemaphoreType.DMA((max(1, len(staged)),)),
            pltpu.SemaphoreType.DMA((max(1, len(copied)),)),
        ],
        compiler_params=pltpu.CompilerParams(vmem_limit_bytes=vmem * mebibyte),
        cost_estimate=cost(micros),
    )(
        *[
            pltpu.with_memory_space_constraint(value.what, pltpu.VMEM)
            if isinstance(value, Kept)
            else value
            for value in ins.values()
        ],
        *after,
    )
    return types.SimpleNamespace(**dict(zip(outs, results)))


class Kept:
    def __init__(self, *what):
        self.what = what[0] if len(what) == 1 else what


def keep_all(names):
    return {name: Kept(value) for name, value in names.items()}


def chunks(extent, size):
    size = min(size, extent)
    return [slice(start, start + size) for start in range(0, extent, size)]


def lay_out_attention(r, masks, rows):
    for idx, mask in enumerate(masks):
        half, at = divmod(idx, max(1, len(masks) // 2))
        source = r.attn_near if half == 0 else r.attn_far
        place = pl.multiple_of((r.place[0] ^ mask) * rows, rows) if len(masks) > 1 else 0
        r.attn_w[pl.ds(place, rows), :] = source[at * rows : (at + 1) * rows, :]


def lay_out_ff(r, layer_idx):
    width = r.ff_down.shape[-1]
    for k, own in enumerate((r.w_gate, r.w_up)):
        r.ff_gate_up[0, :, k * width : (k + 1) * width] = own[layer_idx]
    r.ff_down[0] = r.w_down[layer_idx]
    part = r.ff_near.shape[1]
    for source, base in ((r.ff_near, 0), (r.ff_far, 1)):
        for m in range(2):
            rows = pl.ds(pl.multiple_of((r.place[1] ^ (2 * m + base)) * part, part), part)
            for k in range(2):
                r.ff_gate_up[1, rows, k * width : (k + 1) * width] = source[3 * m + k]
            r.ff_down[1, rows, :] = source[3 * m + 2]


def start_all(copies):
    for copy in copies:
        copy.start()


def wait_all(sem, *buffers):
    for whole in buffers:
        pltpu.make_async_copy(whole, whole, sem).wait()


def lane_low(rows):
    return lax.broadcasted_iota(jnp.int32, (rows, 128), 1) < 64


def lane_halves():
    low = lane_low(1).astype(f32)
    return low.astype(bf16), (1.0 - low).astype(bf16)


def pair_blocks(rows, low, high):
    return jnp.concatenate([rows * low, rows * high], axis=0)


def own_blocks(both, is_low):
    half = both.shape[0] // 2
    return jnp.where(is_low, both[:half], both[half:]).astype(bf16)


def attention_forward(r, x_ref, a_ref, sizes, layer_idx):
    series, slots, inner = sizes
    rows = series * slots
    for part in chunks(rows, 256):
        r.qkv[part, :] = dot_nn(a_ref[part, :], r.attn_w[:, : 3 * inner]).astype(bf16)
    is_low = lane_low(slots)
    low, high = lane_halves()
    for s in range(series):
        here = slice(s * slots, (s + 1) * slots)
        keep = r.mask[here, :] == 1
        for start in range(0, inner, 128):
            at = slice(start, start + 128)
            query = r.qkv[here, at]
            keys = r.qkv[here, inner + start : inner + start + 128]
            scores = dot_nt(keys, pair_blocks(query, low, high)) + r.bias[:, at]
            scores = jnp.where(keep, scores, masked_score)
            exps = jnp.exp(scores - jnp.max(scores, axis=0, keepdims=True))
            r.probs[here, at] = exps / jnp.sum(exps, axis=0, keepdims=True)
    for s in range(series):
        here = slice(s * slots, (s + 1) * slots)
        for start in range(0, inner, 128):
            at = slice(start, start + 128)
            values = r.qkv[here, 2 * inner + start : 2 * inner + start + 128]
            both = dot_tn(r.probs[here, at].astype(bf16), values)
            r.heads[here, at] = own_blocks(both, is_low)
    gain = r.gain_ff[layer_idx : layer_idx + 1, :]
    for part in chunks(rows, 256):
        middle = x_ref[part, :] + dot_nt(r.heads[part, :], r.attn_w[:, 3 * inner :])
        r.middle[part, :] = middle
        r.ff_in[part, :] = (middle * inverse_rms(middle) * gain).astype(bf16)


def prepare_body(r):
    names = ("inputs", "valid", "keep", "embed", "gain_attn", "buckets")
    r.fetch(*names)
    r.need(*names)
    series, slots = r.valid.shape
    gain = r.gain_attn[0:1, :]
    valid = jnp.transpose(r.valid[...].astype(f32))
    keep = jnp.transpose(r.keep[...].astype(f32))
    for s in range(series):
        here = slice(s * slots, (s + 1) * slots)
        seen = valid[:, s : s + 1]
        x = jnp.where(seen == 1.0, r.inputs[here, :].astype(f32), r.embed[...])
        r.x[here, :] = x
        r.a[here, :] = (x * inverse_rms(x) * gain).astype(bf16)
        r.seen[here, :] = jnp.broadcast_to(seen, (slots, 128)).astype(jnp.int32)
        r.mask[here, :] = jnp.broadcast_to(keep[:, s : s + 1], (slots, 128)).astype(jnp.int32)
    turned = jnp.transpose(r.buckets[...].astype(f32)).astype(jnp.int32)
    wide = jnp.concatenate([turned, turned], axis=1)
    r.wide[...] = wide
    is_low = lane_low(slots)
    bucket_count, heads = r.table.shape
    for pair in range(heads // 2):
        bias = jnp.zeros((slots, 128), f32)
        for idx in range(bucket_count):
            entry = jnp.where(is_low, r.table[idx, 2 * pair], r.table[idx, 2 * pair + 1])
            bias = jnp.where(wide == idx, entry, bias)
        r.bias[:, pair * 128 : (pair + 1) * 128] = bias


def attention_body(r, sizes, masks, grain, layer_idx):
    r.fetch("gain_ff")
    lay_out_attention(r, masks, grain)
    r.need("gain_ff")
    attention_forward(r, r.x, r.a, sizes, layer_idx)


def ff_body(r):
    r.fetch("gain_attn")
    lay_out_ff(r, 0)
    r.need("gain_attn")
    width = r.middle.shape[1]
    for part in chunks(r.middle.shape[0], 256):
        x_next = r.middle[part, :]
        for half in range(2):
            both = dot_nn(r.ff_in[part, :], r.ff_gate_up[half])
            hidden = (gelu_terms(both[:, :width])[0] * both[:, width:]).astype(bf16)
            x_next = x_next + dot_nn(hidden, r.ff_down[half])
        r.x_next[part, :] = x_next
        r.a_next[part, :] = (x_next * inverse_rms(x_next) * r.gain_attn[1:2, :]).astype(bf16)


def ff_backward(r, layer_idx, last, masks):
    rows, width = r.middle.shape
    r.fetch("grad", "gain_ff")
    if last:
        lay_out_ff(r, layer_idx)
    r.need("grad", "gain_ff")
    gain_ff = r.gain_ff[layer_idx : layer_idx + 1, :]
    gain_total = jnp.zeros((1, width), f32)
    for part in chunks(rows, 256):
        grad = r.grad[part, :].astype(f32)
        rounded = grad.astype(bf16)
        ff_rows = r.ff_in[part, :]
        back = None
        middle = r.middle[part, :]
        total = middle
        for half in range(2):
            both = dot_nn(ff_rows, r.ff_gate_up[half])
            grad_hidden = dot_nt(rounded, r.ff_down[half])
            gate_act, up_act = both[:, :width], both[:, width:]
            mixed, slope = gelu_terms(gate_act)
            hidden = (mixed * up_act).astype(bf16)
            r.hidden[half, part, :] = hidden
            r.grad_gate_up[half, part, :width] = (grad_hidden * up_act * slope).astype(bf16)
            r.grad_gate_up[half, part, width:] = (grad_hidden * mixed).astype(bf16)
            pulled = r.grad_gate_up[half, part, :]
            if last:
                total = total + dot_nn(hidden, r.ff_down[half])
            term = dot_nt(pulled, r.ff_gate_up[half])
            back = term if back is None else back + term
        if last:
            r.outputs[part, :] = total.astype(bf16)
        grad_mid, gain_part = norm_back(middle, gain_ff, back)
        gain_total += gain_part
        grad_mid = grad + grad_mid
        r.grad_mid[part, :] = grad_mid
        r.branch[part, :] = grad_mid.astype(bf16)
        r.grad_low[part, :] = rounded
    if last:
        r.write("outputs")
    for half in range(2):
        r.ff_grad[half, :, : 2 * width] = dot_tn(r.ff_in[...], r.grad_gate_up[half])
        r.ff_grad[half, :, 2 * width :] = dot_tn(r.hidden[half], r.grad_low[...])
    half_count = len(masks[0]) // 2
    grain, columns = r.ff_keep.shape[1:]
    for side, side_masks in enumerate(masks):
        lanes = slice(side * columns, (side + 1) * columns)
        for idx, mask in enumerate(side_masks):
            target = r.ff_keep if idx < half_count else r.ff_send
            piece = pl.ds(pl.multiple_of((r.place[3] ^ (mask // 2)) * grain, grain), grain)
            target[side * half_count + idx % half_count] = r.ff_grad[mask % 2, piece, lanes].astype(
                bf16
            )
    if last:
        r.drain("outputs")
    return gain_total


def attention_backward(r, sizes, layer_idx, last, piece_masks, heads):
    series, slots, inner = sizes
    rows = series * slots
    width = r.x.shape[1]
    r.fetch("gain_attn")
    for part in chunks(rows, 256):
        r.grad_heads[part, :] = dot_nn(r.branch[part, :], r.attn_w[:, 3 * inner :]).astype(bf16)
    is_low = lane_low(slots)
    low, high = lane_halves()
    for start in range(0, inner, 128):
        at = slice(start, start + 128)
        bias_total = jnp.zeros((slots, 128), f32) if last else r.bias_before[:, at]
        for s in range(series):
            here = slice(s * slots, (s + 1) * slots)
            probs = r.probs[here, at]
            values = r.qkv[here, 2 * inner + start : 2 * inner + start + 128]
            grad_probs = dot_nt(values, pair_blocks(r.grad_heads[here, at], low, high))
            inner_sum = jnp.sum(probs * grad_probs, axis=0, keepdims=True)
            grad_scores = (probs * (grad_probs - inner_sum)).astype(bf16)
            r.grad_scores[here, at] = grad_scores
            bias_total = bias_total + grad_scores.astype(f32)
        r.bias_acc[:, at] = bias_total
    for s in range(series):
        here = slice(s * slots, (s + 1) * slots)
        for start in range(0, inner, 128):
            at = slice(start, start + 128)
            key_at = slice(inner + start, inner + start + 128)
            value_at = slice(2 * inner + start, 2 * inner + start + 128)
            grad_scores = r.grad_scores[here, at]
            r.grad_qkv[here, key_at] = dot_nn(
                grad_scores, pair_blocks(r.qkv[here, at], low, high)
            ).astype(bf16)
            r.grad_qkv[here, value_at] = dot_nn(
                r.probs[here, at].astype(bf16), pair_blocks(r.grad_heads[here, at], low, high)
            ).astype(bf16)
            r.grad_qkv[here, at] = own_blocks(dot_tn(grad_scores, r.qkv[here, key_at]), is_low)
    r.attn_grad[:, : 3 * inner] = dot_tn(r.a[...], r.grad_qkv[...])
    r.attn_grad[:, 3 * inner :] = dot_tn(r.branch[...], r.heads[...])
    scatter_pieces(r.attn_grad, r.attn_keep, r.attn_send, piece_masks, r.place[2])
    r.need("gain_attn")
    gain_attn = r.gain_attn[layer_idx : layer_idx + 1, :]
    gain_total = jnp.zeros((1, width), f32)
    embed_total = jnp.zeros((1, width), f32)
    for part in chunks(rows, 256):
        grad_normed = dot_nt(r.grad_qkv[part, :], r.attn_w[:, : 3 * inner])
        grad_in, gain_part = norm_back(r.x[part, :], gain_attn, grad_normed)
        gain_total += gain_part
        grad_in = r.grad_mid[part, :] + grad_in
        if last:
            r.grad_next[part, :] = grad_in
        else:
            seen = r.seen[part, 0:1] == 1
            r.grad_next[part, :] = jnp.where(seen, grad_in, 0.0)
            embed_total += jnp.sum(jnp.where(seen, 0.0, grad_in), axis=0, keepdims=True)
    r.write("grad_next")
    if not last:
        put_row(r.small, 4, embed_total)
        head_size = inner // heads
        for idx in range(r.table_rows.shape[0]):
            for start in range(0, inner, 128):
                at = slice(start, start + 128)
                chosen = jnp.where(r.wide[...] == idx, r.bias_acc[:, at], 0.0)
                r.table_rows[idx : idx + 1, at] = jnp.sum(chosen, axis=0, keepdims=True)
        lane = lax.broadcasted_iota(jnp.int32, (r.table_rows.shape[0], 128), 1)
        table = jnp.zeros(lane.shape, f32)
        for head in range(heads):
            cut = r.table_rows[:, head * head_size : (head + 1) * head_size]
            table = jnp.where(lane == head, jnp.sum(cut, axis=1, keepdims=True), table)
        r.small[:heads, : table.shape[0]] = jnp.transpose(table)[:heads, :]
    r.drain("grad_next")
    return gain_total


def two_parts(values):
    high = values.astype(bf16).astype(f32)
    return high, (values - high).astype(bf16).astype(f32)


def last_ff_body(r, masks):
    r.small[...] = jnp.zeros(r.small.shape, f32)
    put_row(r.small, 3, ff_backward(r, 1, True, masks))


def last_attention_body(r, sizes, piece_masks, heads):
    r.small[...] = r.small_before[...]
    put_row(r.small, 1, attention_backward(r, sizes, 1, True, piece_masks, heads))


def ff_backward_body(r, masks):
    r.small[...] = r.small_before[...]
    put_row(r.small, 2, ff_backward(r, 0, False, masks))


def attention_backward_body(r, sizes, piece_masks, heads):
    r.small[...] = r.small_before[...]
    put_row(r.small, 0, attention_backward(r, sizes, 0, False, piece_masks, heads))
    high, low = two_parts(r.small[...])
    last = r.attn_send.shape[0] - 1
    r.attn_send[last] = jnp.concatenate([high, low], axis=0).astype(bf16)
    r.small[...] = high + low


def put_row(packed, which, row):
    first, width = packed.shape[0] - 2, row.shape[1]
    at = which % 3 * width
    packed[first + which // 3 : first + which // 3 + 1, at : at + width] = row


def scatter_pieces(whole, keep, send, masks, place):
    count = len(masks)
    grain = whole.shape[0] // count
    for idx, mask in enumerate(masks):
        target = keep if idx < count // 2 else send
        source = pl.ds(pl.multiple_of((place ^ mask) * grain, grain), grain)
        target[idx % (count // 2)] = whole[source, :].astype(bf16)


def finish(pieces, masks, layer_idx, place, shape, before=()):
    grain, width = pieces.shape[1], shape[-1]
    count = len(before)

    def kernel(place_ref, source, *refs):
        outs = refs[count : count + 3]
        stage, out_sem = refs[count + 3 :]
        for idx, mask in enumerate(masks):
            rows = pl.ds(pl.multiple_of((place_ref[3] ^ mask) * grain, grain), grain)
            for k, out in enumerate(outs):
                stage[k, idx] = source[idx, :, k * width : (k + 1) * width].astype(f32)
                pltpu.make_async_copy(stage.at[k, idx], out.at[layer_idx, rows], out_sem).start()
        pltpu.make_async_copy(stage, stage, out_sem).wait()

    return pl.pallas_call(
        kernel,
        name="layer_%d_ff_grads" % layer_idx,
        in_specs=[
            pl.BlockSpec(memory_space=pltpu.SMEM),
            pl.BlockSpec(memory_space=pltpu.VMEM),
        ]
        + [pl.BlockSpec(memory_space=pl.ANY)] * count,
        out_specs=[pl.BlockSpec(memory_space=pl.ANY)] * 3,
        out_shape=[jax.ShapeDtypeStruct(shape, f32)] * 3,
        input_output_aliases={2 + k: k for k in range(count)},
        scratch_shapes=[
            pltpu.VMEM((3, len(masks), grain, width), f32),
            pltpu.SemaphoreType.DMA,
        ],
        compiler_params=pltpu.CompilerParams(vmem_limit_bytes=6 * mebibyte),
        cost_estimate=cost(3),
    )(place, pltpu.with_memory_space_constraint(pieces, pltpu.VMEM), *before)


def small_body(r):
    width = r.embed.shape[1]
    heads = r.table.shape[0]
    outs = ((r.gain_attn, 0), (r.gain_attn, 1), (r.gain_ff, 0), (r.gain_ff, 1), (r.embed, 0))
    for which, (out, row) in enumerate(outs):
        first = r.packed.shape[0] - 2 + which // 3
        at = which % 3 * width
        out[row : row + 1, :] = r.packed[first : first + 1, at : at + width]
    r.table[...] = r.packed[:heads, : r.table.shape[1]]
    r.write("gain_attn", "gain_ff", "embed", "table")
    r.drain("gain_attn", "gain_ff", "embed", "table")


def pack_body(r, packs):
    rows = r.quarter_0.shape[1]
    at = pl.ds(pl.multiple_of(r.place[1] * rows, rows), rows)
    copies = []
    outs = [r.quarter_0, r.quarter_1]
    for layer_idx in range(2):
        for k, w in enumerate((r.w_gate, r.w_up, r.w_down)):
            copies.append((w.at[layer_idx, at], outs[layer_idx].at[k]))
    if packs:
        outs += [r.block_0, r.block_1]
        inner = r.w_query.shape[2]
        for layer_idx in range(2):
            for k, w in enumerate((r.w_query, r.w_key, r.w_value, r.w_out)):
                lanes = pl.ds(k * inner, inner)
                copies.append((w.at[layer_idx], outs[2 + layer_idx].at[:, lanes]))
    start_all([pltpu.make_async_copy(*ends, r.pack_sem) for ends in copies])
    wait_all(r.pack_sem, *outs)


def order_masks(hops):
    masks = [0]
    for hop in reversed(hops):
        masks = masks + [mask ^ hop for mask in masks]
    return masks


def tie(value, *others):
    return lax.optimization_barrier((value, *others))[0]


def on_device(
    inputs,
    cotangent,
    attention_mask,
    patch_valid,
    buckets,
    mask_embed,
    w_query,
    w_key,
    w_value,
    w_output,
    w_gate,
    w_up,
    w_down,
    gain_attn,
    gain_ff,
    bias_table,
    dp_size,
):
    series, slots, width = inputs.shape
    heads = bias_table.shape[1]
    inner = w_query.shape[2]
    rows = series * slots
    sizes = (series, slots, inner)
    matrix = (rows, width)
    devices = 2 * dp_size
    dp_at = lax.axis_index("dp")
    device_at = 2 * dp_at + lax.axis_index("tensor")
    cotangent = cotangent.reshape(matrix)

    def swap(array, mask):
        return lax.ppermute(array, axes, [(n, n ^ mask) for n in range(devices)])

    def join(left, right):
        return jnp.concatenate([left, right], axis=0)

    bits = [1 << k for k in range(devices.bit_length() - 1)]

    attn_grain = max(16, width // devices)
    attn_count = width // attn_grain
    ff_grain = max(16, 2 * width // dp_size)
    ff_count = width // ff_grain
    quarter_at = lax.rem(dp_at, 4)
    place = jnp.stack(
        [
            device_at,
            quarter_at,
            device_at // (devices // attn_count),
            lax.rem(dp_at, ff_count),
        ]
    ).astype(jnp.int32)

    quarter = width // 4
    own_rows = w_query.shape[1]
    direct = own_rows % 16 == 0
    w_out = jnp.swapaxes(w_output, 1, 2)
    sources = dict(w_gate=w_gate, w_up=w_up, w_down=w_down)
    block_outs = {}
    if direct:
        sources |= dict(w_query=w_query, w_key=w_key, w_value=w_value, w_out=w_out)
        block_outs = {"block_%d" % k: Kept((own_rows, 4 * inner), bf16) for k in range(2)}
    packed = run(
        functools.partial(pack_body, packs=direct),
        "pack",
        dict(
            place=place,
            **{n: pltpu.with_memory_space_constraint(w, pltpu.HBM) for n, w in sources.items()},
        ),
        dict(
            quarter_0=Kept((3, quarter, width), bf16),
            quarter_1=Kept((3, quarter, width), bf16),
            **block_outs,
        ),
        dict(pack_sem=pltpu.SemaphoreType.DMA),
        vmem=4,
    )
    far = bits[2:]

    def prepare(token):
        return run(
            prepare_body,
            "prepare",
            dict(
                inputs=tie(inputs, token).reshape(matrix),
                valid=patch_valid,
                keep=attention_mask,
                embed=mask_embed[None, :],
                gain_attn=gain_attn,
                buckets=buckets,
                table=bias_table,
            ),
            dict(
                x=Kept(matrix, f32),
                a=Kept(matrix, bf16),
                bias=Kept((slots, heads * slots), f32),
                mask=Kept((rows, 128), jnp.int32),
                seen=Kept((rows, 128), jnp.int32),
                wide=Kept((slots, 128), jnp.int32),
            ),
            {},
            micros=3,
        )

    if direct:
        hops_0 = [1] + far[2:] + far[:2] + [2]
        hops_1 = far[2:] + far[:2] + [1, 2]
        block_0, block_1 = packed.block_0, packed.block_1
        got_1 = swap(block_1, hops_1[0])
        got_0 = swap(block_0, hops_0[0])
        ff_0 = swap(tie(packed.quarter_0, got_0), 1)
        ff_1 = swap(tie(packed.quarter_1, ff_0), 1)
        got_ff_0 = swap(ff_0, 4)
        block_0 = join(block_0, got_0)
        block_1 = join(block_1, tie(got_1, block_0))
        for hop_0, hop_1 in zip(hops_0[1:-2], hops_1[1:-2]):
            got_1, got_0 = swap(block_1, hop_1), swap(block_0, hop_0)
            if hop_0 == hops_0[1]:
                start = prepare(block_1)
                got_0 = tie(got_0, ff_0)
            block_0 = join(block_0, got_0)
            block_1 = join(block_1, tie(got_1, block_0))
        block_0 = tie(block_0, block_1)
        got_0 = swap(block_0, hops_0[-2])
        got_1 = swap(block_1, hops_1[-2])
        block_0 = join(block_0, tie(got_0, start.a, got_ff_0, ff_1, got_1))
        ff_0 = join(ff_0, tie(got_ff_0, block_0))
        got_ff_1 = swap(tie(ff_1, ff_0), 4)
        attn_pieces = [(block_0, swap(block_0, 2), order_masks(hops_0[::-1]))]
    else:
        ff_0, ff_1 = swap(packed.quarter_0, 1), swap(packed.quarter_1, 1)
        ff_0 = join(ff_0, swap(ff_0, 4))
        start = prepare(ff_0)
        attn_pieces = []
        rows_of = jnp.concatenate([w_query, w_key, w_value, w_out], axis=2)
        for layer_idx in range(2):
            whole = lax.all_gather(rows_of[layer_idx], axes, axis=0, tiled=True)
            attn_pieces.append((whole, whole, [0]))
    ff_pieces = [(ff_0, swap(ff_0, 2))]

    def attn_ins(layer_idx):
        near, far, masks = attn_pieces[layer_idx]
        return dict(attn_near=Kept(near), attn_far=Kept(far)), masks

    def ff_ins(layer_idx):
        near, far = ff_pieces[layer_idx]
        own = keep_all(dict(w_gate=w_gate, w_up=w_up, w_down=w_down))
        return dict(**own, ff_near=Kept(near), ff_far=Kept(far))

    ff_outs = dict(
        ff_gate_up=Kept((2, width, 2 * width), bf16), ff_down=Kept((2, width, width), bf16)
    )
    grain = own_rows if direct else width
    attn_outs = dict(
        attn_w=Kept((width, 4 * inner), bf16),
        qkv=Kept((rows, 3 * inner), bf16),
        probs=Kept((rows, heads * slots), f32),
        heads=Kept((rows, inner), bf16),
        middle=Kept(matrix, f32),
        ff_in=Kept(matrix, bf16),
    )

    def attention(layer_idx, x, a, after=(), micros=5):
        pieces, masks = attn_ins(layer_idx)
        return run(
            functools.partial(
                attention_body, sizes=sizes, masks=masks, grain=grain, layer_idx=layer_idx
            ),
            "layer_%d_attention" % layer_idx,
            dict(
                place=place,
                x=Kept(x),
                a=Kept(a),
                bias=Kept(start.bias),
                mask=Kept(start.mask),
                gain_ff=gain_ff,
                **pieces,
            ),
            attn_outs,
            {},
            after=after,
            micros=micros,
        )

    first = attention(0, start.x, start.a, micros=10)
    if direct:
        block_1 = join(block_1, tie(got_1, first.ff_in))
        attn_pieces.append((block_1, swap(block_1, 2), order_masks(hops_1[::-1])))
    first_ff = run(
        ff_body,
        "layer_0_ff",
        dict(
            place=place,
            middle=Kept(first.middle),
            ff_in=Kept(first.ff_in),
            gain_attn=gain_attn,
            **ff_ins(0),
        ),
        dict(**ff_outs, x_next=Kept(matrix, f32), a_next=Kept(matrix, bf16)),
        {},
        after=(block_1,) if direct else (),
        micros=3,
    )
    if direct:
        ff_1 = join(ff_1, tie(got_ff_1, first_ff.x_next))
    else:
        ff_1 = join(ff_1, swap(ff_1, 4))
    ff_pieces.append((ff_1, swap(ff_1, 2)))
    second = attention(1, first_ff.x_next, first_ff.a_next, micros=0.1)

    attn_low = devices // attn_count
    attn_hops = ([2, 1] + bits[2:], [2] + bits[3:4] + bits[2:3] + bits[4:] + [1])
    attn_split = [[hop for hop in hops if hop >= attn_low] for hops in attn_hops]
    attn_whole = [hop for hop in bits if hop < attn_low]
    attn_masks = [[mask // attn_low for mask in order_masks(hops)] for hops in attn_split]
    ff_hops = ([2, 4, 1] + bits[3:], [2, 1, 4] + bits[3:])
    ff_split = [[hop for hop in hops if hop // 2 < ff_count] for hops in ff_hops]
    ff_whole = [hop for hop in bits[1:] if hop // 2 >= ff_count]
    ff_share = [hop for hop in bits[:0:-1] if hop // 2 < ff_count]
    ff_masks = [order_masks(hops) for hops in ff_split]
    place_masks = [mask // 2 for mask in order_masks(ff_share[::-1])]
    attn_half = (attn_count // 2, attn_grain, 4 * inner)
    small_shape = (heads + 2, 3 * width)

    attn_back_outs = dict(attn_keep=Kept(attn_half, bf16), attn_send=Kept(attn_half, bf16))
    attn_back_scratch = dict(
        grad_heads=pltpu.VMEM((rows, inner), bf16),
        grad_qkv=pltpu.VMEM((rows, 3 * inner), bf16),
        grad_scores=pltpu.VMEM((rows, heads * slots), bf16),
        attn_grad=pltpu.VMEM((width, 4 * inner), f32),
    )
    ff_back_outs = dict(
        ff_keep=Kept((2 * ff_count, ff_grain, 3 * width // 2), bf16),
        ff_send=Kept((2 * ff_count, ff_grain, 3 * width // 2), bf16),
        small=Kept(small_shape, f32),
        grad_mid=Kept(matrix, f32),
        branch=Kept(matrix, bf16),
    )
    ff_back_scratch = dict(
        hidden=pltpu.VMEM((2, rows, width), bf16),
        grad_gate_up=pltpu.VMEM((2, rows, 2 * width), bf16),
        ff_grad=pltpu.VMEM((2, width, 3 * width), f32),
        grad_low=pltpu.VMEM(matrix, bf16),
    )
    bias_shape = (slots, heads * slots)

    def attn_back_ins(kept, x, a):
        return dict(
            x=Kept(x),
            a=Kept(a),
            gain_attn=gain_attn,
            attn_w=Kept(kept.attn_w),
            qkv=Kept(kept.qkv),
            probs=Kept(kept.probs),
            heads=Kept(kept.heads),
        )

    def add(left, right):
        return (left.astype(f32) + right.astype(f32)).astype(bf16)

    def halving(keep, send, hops, out):
        for step, hop in enumerate(hops):
            got = yield swap(send, hop)
            if step + 1 < len(hops):
                cut = keep.shape[0] // 2
                send = add(keep[cut:], got[cut:])
                keep = add(keep[:cut], got[:cut])
                out["token"] = send
            else:
                out["token"] = keep = add(keep, got)
        out["piece"] = keep

    def summing(piece, hops, out):
        for hop in hops:
            got = yield swap(piece, hop)
            out["token"] = piece = add(piece, got)
        out["piece"] = piece

    def sharing(piece, hops, out):
        for step, hop in enumerate(hops):
            if step + 1 == len(hops):
                out["near"] = piece
            got = yield swap(piece, hop)
            if step + 1 < len(hops):
                out["token"] = piece = join(piece, got)
            else:
                out["token"] = out["far"] = got

    def rounded(values):
        return lax.reduce_precision(values, exponent_bits=8, mantissa_bits=7)

    def with_small(pieces, small):
        high = rounded(small)
        low = rounded(small - high)
        parts = join(high, low).astype(bf16)[None]
        return join(pieces, parts), high + low

    def add_small(small, got):
        parts = got[-1].astype(f32)
        return small + (parts[: small.shape[0]] + parts[small.shape[0] :])

    def attn_chain(part, layer_idx, out):
        small = part.small if layer_idx == 0 else None
        keep, send = part.attn_keep, part.attn_send
        hops = attn_split[layer_idx] + attn_whole
        for step, hop in enumerate(hops):
            got = yield swap(send, hop)
            if small is not None:
                small = add_small(small, got)
                got = got[:-1]
            if step + 1 < len(attn_split[layer_idx]):
                half = keep.shape[0] // 2
                send = add(keep[half:], got[half:])
                keep = add(keep[:half], got[:half])
            else:
                send = keep = add(keep, got)
            if small is not None and step + 1 < len(hops):
                send, small = with_small(send, small)
            out["token"] = send
            if layer_idx == 1 and step == 0:
                send = tie(send, *(yield None))
        piece = keep[0]
        if own_rows < attn_grain:
            first_row = lax.rem(device_at, attn_low) * own_rows
            piece = lax.dynamic_slice_in_dim(piece, first_row, own_rows, axis=0)
        out["done"] = piece.astype(f32)
        out["small"] = small

    def ff_chain(part, out):
        got = yield swap(part.ff_send, 2)
        count = ff_count
        keeps, sends = [], []
        for side in range(2):
            at, half = side * count, count // 2
            sends.append(add(part.ff_keep[at + half : at + count], got[at + half : at + count]))
            keeps.append(add(part.ff_keep[at : at + half], got[at : at + half]))
        out["token"] = tuple(sends)
        for hops in zip(ff_split[0][1:3], ff_split[1][1:3]):
            got = yield tuple(swap(send, hop) for send, hop in zip(sends, hops))
            half = keeps[0].shape[0] // 2
            sends = [add(keep[half:], one[half:]) for keep, one in zip(keeps, got)]
            keeps = [add(keep[:half], one[:half]) for keep, one in zip(keeps, got)]
            out["token"] = tuple(sends)
        keep, send = (jnp.concatenate(sides, axis=2) for sides in (keeps, sends))
        yield from halving(keep, send, ff_split[0][3:], out)
        yield from summing(out["piece"], ff_whole, out)
        yield from sharing(out["piece"], ff_share, out)

    class Chain:
        def __init__(self, steps, *args):
            self.out = {}
            self.steps = steps(*args, self.out)
            self.arriving = next(self.steps)

        def resume(self, *tokens):
            self.arriving = self.steps.send(tokens)

        def step(self, token, *others):
            if self.arriving is not None:
                tokens = (*(token if isinstance(token, tuple) else (token,)), *others)
                many = isinstance(self.arriving, tuple)
                arrived = self.arriving if many else (self.arriving,)
                arrived = lax.optimization_barrier((*arrived, *tokens))[: len(arrived)]
                arrived = arrived if many else arrived[0]
                self.arriving = None
                try:
                    self.arriving = self.steps.send(arrived)
                except StopIteration:
                    pass
                return self.out["token"]
            return token

    back_ff_1 = run(
        functools.partial(last_ff_body, masks=ff_masks),
        "layer_1_ff",
        dict(
            place=place,
            grad=cotangent,
            gain_ff=gain_ff,
            middle=Kept(second.middle),
            ff_in=Kept(second.ff_in),
            **ff_ins(1),
        ),
        dict(**ff_back_outs, outputs=(matrix, bf16)),
        dict(
            ff_gate_up=pltpu.VMEM((2, width, 2 * width), bf16),
            ff_down=pltpu.VMEM((2, width, width), bf16),
            **ff_back_scratch,
        ),
        micros=8,
        vmem=24,
    )
    ff_1 = Chain(ff_chain, back_ff_1)
    back_1 = run(
        functools.partial(
            last_attention_body, sizes=sizes, piece_masks=attn_masks[1], heads=heads
        ),
        "layer_1_attention_backward",
        dict(
            place=place,
            small_before=Kept(back_ff_1.small),
            grad_mid=Kept(back_ff_1.grad_mid),
            branch=Kept(back_ff_1.branch),
            **attn_back_ins(second, first_ff.x_next, first_ff.a_next),
        ),
        dict(
            **attn_back_outs,
            small=Kept(small_shape, f32),
            grad_next=Kept(matrix, f32),
            bias_acc=Kept(bias_shape, f32),
        ),
        attn_back_scratch,
        micros=6,
        vmem=14,
    )
    attn_1 = Chain(attn_chain, back_1, 1)
    token = ff_1.step(back_1.attn_send)
    token = (attn_1.step(token),)
    back_0 = run(
        functools.partial(ff_backward_body, masks=ff_masks),
        "layer_0_ff_backward",
        dict(
            place=place,
            grad=Kept(back_1.grad_next),
            gain_ff=gain_ff,
            small_before=Kept(back_1.small),
            middle=Kept(first.middle),
            ff_in=Kept(first.ff_in),
            ff_gate_up=Kept(first_ff.ff_gate_up),
            ff_down=Kept(first_ff.ff_down),
        ),
        ff_back_outs,
        ff_back_scratch,
        after=token,
        micros=8,
        vmem=20,
    )
    token = ff_1.step(back_0.branch)
    back_0.ff_send = tie(back_0.ff_send, *token)
    ff_0 = Chain(ff_chain, back_0)
    token = ff_0.step(token)
    back_attn_0 = run(
        functools.partial(
            attention_backward_body, sizes=sizes, piece_masks=attn_masks[0], heads=heads
        ),
        "layer_0_attention_backward",
        dict(
            place=place,
            bias_before=Kept(back_1.bias_acc),
            seen=Kept(start.seen),
            wide=Kept(start.wide),
            small_before=Kept(back_0.small),
            grad_mid=Kept(back_0.grad_mid),
            branch=Kept(back_0.branch),
            **attn_back_ins(first, start.x, start.a),
        ),
        dict(
            attn_keep=Kept(attn_half, bf16),
            attn_send=Kept((attn_count // 2 + 1, *attn_half[1:]), bf16),
            small=Kept(small_shape, f32),
            grad_next=(matrix, f32),
        ),
        dict(
            bias_acc=pltpu.VMEM(bias_shape, f32),
            table_rows=pltpu.VMEM((bias_table.shape[0], heads * slots), f32),
            **attn_back_scratch,
        ),
        after=token,
        micros=7,
        vmem=14,
    )
    attn_0 = Chain(attn_chain, back_attn_0, 0)
    attn_1.resume(back_attn_0.attn_send)
    token = back_attn_0.attn_send
    shape = (2, width, width)
    near_masks = place_masks[: ff_count // 2]
    far_masks = place_masks[ff_count // 2 :]
    done = ()
    ended = False
    turn = 0
    sums = attn_grads = None
    while ff_0.arriving is not None:
        turn += 1
        token = ff_1.step(token)
        if done and not ended:
            done = finish(tie(ff_1.out["far"], token), far_masks, 1, place, shape, done)
            token = done[0]
            ended = True
        if turn == 3:
            token = attn_0.step(token)
        token = ff_0.step(token)
        if not done and "near" in ff_1.out:
            done = finish(tie(ff_1.out["near"], token), near_masks, 1, place, shape)
            token = done[0]
        if turn != 2:
            token = attn_0.step(token)
        if turn > 2:
            token = attn_1.step(token)
        if sums is None and attn_0.arriving is None:
            sums = run(
                small_body,
                "small_sums",
                dict(packed=Kept(tie(attn_0.out["small"], token))),
                dict(
                    gain_attn=((2, width), f32),
                    gain_ff=((2, width), f32),
                    embed=((1, width), f32),
                    table=(bias_table.shape[::-1], f32),
                ),
                {},
            )
            token = sums.embed
        if attn_grads is None and attn_0.arriving is None and attn_1.arriving is None:
            both = jnp.stack([attn_0.out["done"], tie(attn_1.out["done"], token)])
            attn_grads = [both[:, :, k * inner : (k + 1) * inner] for k in range(4)]
            attn_grads[3] = jnp.swapaxes(attn_grads[3], 1, 2)
            token = tuple(attn_grads)
    if not ended:
        done = finish(ff_1.out["far"], far_masks, 1, place, shape, done)
    for pieces, masks in ((ff_0.out["near"], near_masks), (ff_0.out["far"], far_masks)):
        done = finish(pieces, masks, 0, place, shape, done)
    return (
        back_ff_1.outputs.reshape(inputs.shape),
        back_attn_0.grad_next.reshape(inputs.shape),
        *attn_grads,
        *done,
        sums.gain_attn,
        sums.gain_ff,
        sums.table.T,
        sums.embed[0],
    )


def solution(mesh):
    placed = (
        P(("dp", "tensor"), None, None),
        P(("dp", "tensor"), None, None),
        P(("dp", "tensor"), None),
        P(("dp", "tensor"), None),
        P(),
        P(),
        P(None, ("dp", "tensor"), None),
        P(None, ("dp", "tensor"), None),
        P(None, ("dp", "tensor"), None),
        P(None, None, ("dp", "tensor")),
        P(None, None, "tensor"),
        P(None, None, "tensor"),
        P(None, "tensor", None),
        P(),
        P(),
        P(),
    )
    return jax.shard_map(
        functools.partial(on_device, dp_size=mesh.shape["dp"]),
        mesh=mesh,
        in_specs=placed,
        out_specs=(
            P(("dp", "tensor"), None, None),
            P(("dp", "tensor"), None, None),
            P(None, ("dp", "tensor"), None),
            P(None, ("dp", "tensor"), None),
            P(None, ("dp", "tensor"), None),
            P(None, None, ("dp", "tensor")),
            P(None, None, "tensor"),
            P(None, None, "tensor"),
            P(None, "tensor", None),
            P(),
            P(),
            P(),
            P(),
        ),
        check_vma=False,
    )
```
